32 devices in a mesh: row: 8 (over z, y), col: 4 (over x, core).
Axes of the slice: x: 2, y: 2, z: 4, core: 2. Of those that a mesh axis runs over, the one named last changes fastest.
Arguments:
- hidden_in: bfloat16 [16384, 2048], P('row', 'col'), may hold values from -6 to 6
- lengths: int32 [16], P('row'), may hold values from 256 to 1024
- routes: int32 [16384, 8], P('row'), may hold values from 0 to 15, all different within a row; in each aligned block of 2048 rows (0 to 2047, 2048 to 4095, ...) at most 1152 rows name the same one
- attn_gain: float32 [2048], P('col'), may hold values from 0.5 to 1.5
- query_gain: float32 [128], replicated, may hold values from 0.5 to 1.5
- key_gain: float32 [128], replicated, may hold values from 0.5 to 1.5
- query_weight: float32 [2048, 2048], P('row', 'col'), may hold values from -0.125 to 0.125
- key_weight: float32 [2048, 2048], P('row', 'col'), may hold values from -0.125 to 0.125
- value_weight: float32 [2048, 2048], P('row', 'col'), may hold values from -0.125 to 0.125
- out_weight: float32 [2048, 2048], P('col', 'row'), may hold values from -1.5 to 1.5
- moe_gain: float32 [2048], P('col'), may hold values from 0.5 to 1.5
- router: float32 [2048, 16], P('row'), may hold values from -0.0625 to 0.0625
- gate_weight: float32 [16, 2048, 1024], P('col', 'row'), may hold values from -0.125 to 0.125
- up_weight: float32 [16, 2048, 1024], P('col', 'row'), may hold values from -0.125 to 0.125
- down_weight: float32 [16, 1024, 2048], P('col', None, 'row'), may hold values from -0.75 to 0.75
- cotangent: bfloat16 [16384, 2048], P('row', 'col'), may hold values from -6 to 6
Outputs:
- output: bfloat16 [16384, 2048], P('row', 'col')
- input_grad: float32 [16384, 2048], P('row', 'col')
- attn_gain_grad: float32 [2048], P('col')
- query_gain_grad: float32 [128], replicated
- key_gain_grad: float32 [128], replicated
- query_grad: float32 [2048, 2048], P('row', 'col')
- key_grad: float32 [2048, 2048], P('row', 'col')
- value_grad: float32 [2048, 2048], P('row', 'col')
- out_grad: float32 [2048, 2048], P('col', 'row')
- moe_gain_grad: float32 [2048], P('col')
- router_grad: float32 [2048, 16], P('row')
- gate_grad: float32 [16, 2048, 1024], P('col', 'row')
- up_grad: float32 [16, 2048, 1024], P('col', 'row')
- down_grad: float32 [16, 1024, 2048], P('col', None, 'row')
The draws below stay inside these ranges and needn't reach their ends.
Inputs may be any that keep to these rules, and one draw needn't show every extreme that they name: `routes`: each token names 8 different experts. Among the 2048 tokens of each aligned block of rows (the tokens of one index of row), no expert is named by more than 1152 tokens, and in some block one expert is named by exactly 1152.
All inputs are finite; a program needn't handle non-finite values.
Results may differ from the reference program's by a relative error of at most 0.02.
Values may be sent and summed in bfloat16 or wider, within the bound.
No kernel may reach another device: no remote copies, remote signals or barrier semaphores. Data moves between devices by JAX's collectives and lax.ppermute only.
A program may use at most 512 MiB of HBM per device.

```python
import math
import jax
import jax.numpy as jnp
import numpy as np
from jax import lax

D = 2048
HEADS = 16
HD = 128
F = 1024
EXPERTS = 16
TOP = 8
SEQ_LEN = 1024
TOK_ROW = 2048
NSEQ = 16
TOKENS = 16384
CAP = 1152
N_ROW = 8


def with_ends(values, rng, least, top_value):
    shape = values.shape
    spot = [jax.random.randint(jax.random.fold_in(rng, axis), (), 0, shape[axis]) for axis in range(len(shape))]
    values = values.at[tuple(spot)].set(least)
    longest = shape.index(max(shape))
    spot[longest] = (spot[longest] + 1) % shape[longest]
    return values.at[tuple(spot)].set(top_value)


def levels(key, dims, shards, low, largest):
    factor_of = 1.0
    for position, parts in shards:
        draws = jax.random.uniform(jax.random.fold_in(jax.random.fold_in(key, 6), position), (parts,), jnp.float32, low / len(shards), largest / len(shards))
        factor_of = factor_of * jnp.repeat(jnp.exp(draws), dims[position] // parts).reshape((-1,) + (1,) * (len(dims) - 1 - position))
    return factor_of


def deal_out(rng, own, number, rows, number_of, top, limit, skew):
    order = jax.random.permutation(rng, number_of)
    packed, common = shares(number_of, rows * top, limit, skew, True), shares(number_of, rows * top, limit, skew, False)
    places = jnp.arange(number_of)

    def named(sizes, turn):
        used = int((sizes > 0).sum())
        fixed = max(1, used // 4)
        moved = fixed + (places - fixed + turn * (used - fixed)) % max(1, number_of - fixed)
        return jnp.zeros((number_of,), jnp.int32).at[order[jnp.where(places < fixed, places, moved)]].set(jnp.asarray(sizes, jnp.int32))

    sizes = jnp.where(number % 4 == 0, named(packed, number // 4), named(common, number - number // 4 - 1))
    mixed = jax.random.permutation(jax.random.fold_in(own, 3), number_of)
    source_of, taker = mixed[0:number_of // 2 * 2:2], mixed[1:number_of // 2 * 2:2]
    margin = jnp.minimum(sizes[source_of] - 1, limit - sizes[taker]) // 2
    margin = jnp.where((source_of == order[0]) | (taker == order[0]) | (sizes[taker] == 0), 0, jnp.maximum(margin, 0))
    moved = jax.random.randint(jax.random.fold_in(own, 4), (number_of // 2,), 0, 1 << 20) % (margin + 1)
    sizes = sizes.at[source_of].add(-moved).at[taker].add(moved)
    members = jnp.searchsorted(jnp.cumsum(sizes), jnp.arange(rows * top), side="right").astype(jnp.int32)
    listing = members.reshape(top, rows).T
    listing = listing[jax.random.permutation(jax.random.fold_in(own, 1), rows)]
    turn = jax.random.randint(jax.random.fold_in(own, 2), (rows, 1), 0, top)
    return jnp.take_along_axis(listing, (jnp.arange(top)[None, :] + turn) % top, axis=1)


def shares(amount, total, most, slope, full):
    loads = [(1 << 20) // math.isqrt(standing ** slope) + 1 for standing in range(1, amount + 1)]
    largest = most if full else min(most, max(-(-total // amount), total * loads[0] // sum(loads)))
    least = 1 if total - largest >= amount - 1 else 0
    counts, rest = [largest] + [least] * (amount - 1), total - largest - least * (amount - 1)
    while rest > 0:
        movable = [i for i in range(1, amount) if counts[i] < largest] or [i for i in range(1, amount) if counts[i] < most]
        whole, remaining = sum([loads[i] for i in movable]), rest
        for i in movable:
            addition = min(most - counts[i], max(1, remaining * loads[i] // whole), rest)
            counts[i] = counts[i] + addition
            rest = rest - addition
    return np.array(counts)


def bell_draw(own_key, shape, scale, reach, split=(), kind=jnp.bfloat16):
    values = jax.random.normal(own_key, shape, jnp.float32) * scale
    if len(split) > 0:
        values = levels(own_key, shape, split, -0.22, 0.18) * values
    return jnp.clip(values, min=-reach, max=reach).astype(kind)


def setup_inputs(seed: int = 0) -> dict:
    splits = jax.random.split(jax.random.key(seed), 17)
    hidden_in = bell_draw(splits[0], (TOKENS, D), 1.0, 6.0, ((0, 8), (1, 4)))
    lengths = with_ends(jax.random.randint(splits[1], (NSEQ,), SEQ_LEN // 4, SEQ_LEN + 1), jax.random.fold_in(splits[1], 1), SEQ_LEN // 4, SEQ_LEN).astype(jnp.int32)
    routes_keys = jax.random.split(jax.random.fold_in(splits[2], 1), TOKENS // TOK_ROW)
    routes_turns = jax.random.permutation(jax.random.fold_in(splits[2], 3), TOKENS // TOK_ROW)
    routes = jax.vmap(lambda own, number: deal_out(jax.random.fold_in(splits[2], 2), own, number, TOK_ROW, EXPERTS, TOP, CAP, 1))(routes_keys, routes_turns).reshape((TOKENS, TOP))
    attn_gain = jnp.clip(1.0 + 0.1 * jax.random.normal(splits[3], (D,), jnp.float32), 0.5, 1.5)
    query_gain = jnp.clip(1.0 + 0.1 * jax.random.normal(splits[4], (HD,), jnp.float32), 0.5, 1.5)
    key_gain = jnp.clip(1.0 + 0.1 * jax.random.normal(splits[5], (HD,), jnp.float32), 0.5, 1.5)
    query_weight = bell_draw(splits[6], (D, D), D ** -0.5, 0.125, ((0, 8), (1, 4)), jnp.float32)
    key_weight = bell_draw(splits[7], (D, D), D ** -0.5, 0.125, ((0, 8), (1, 4)), jnp.float32)
    value_weight = bell_draw(splits[8], (D, D), D ** -0.5, 0.125, ((0, 8), (1, 4)), jnp.float32)
    out_weight = bell_draw(splits[9], (D, D), (D * 8 // SEQ_LEN) ** -0.5, 1.5, ((0, 4), (1, 8)), jnp.float32)
    moe_gain = jnp.clip(1.0 + 0.1 * jax.random.normal(splits[10], (D,), jnp.float32), 0.5, 1.5)
    router = bell_draw(splits[11], (D, EXPERTS), (4 * D) ** -0.5, 0.0625, ((0, 8),), jnp.float32)
    gate_weight = bell_draw(splits[12], (EXPERTS, D, F), D ** -0.5, 0.125, ((0, 4), (1, 8)), jnp.float32)
    up_weight = bell_draw(splits[13], (EXPERTS, D, F), D ** -0.5, 0.125, ((0, 4), (1, 8)), jnp.float32)
    down_weight = bell_draw(splits[14], (EXPERTS, F, D), (F // 16) ** -0.5, 0.75, ((0, 4), (2, 8)), jnp.float32)
    cotangent = bell_draw(splits[15], (TOKENS, D), 1.0, 6.0, ((0, 8), (1, 4)))
    return {"hidden_in": hidden_in, "lengths": lengths, "routes": routes, "attn_gain": attn_gain, "query_gain": query_gain, "key_gain": key_gain, "query_weight": query_weight, "key_weight": key_weight, "value_weight": value_weight, "out_weight": out_weight, "moe_gain": moe_gain, "router": router, "gate_weight": gate_weight, "up_weight": up_weight, "down_weight": down_weight, "cotangent": cotangent}


epsilon = 1e-06
rope_base = 10000.0
masked_score = -1e+30
highest = lax.Precision.HIGHEST

@jax.custom_vjp
def low(v):
    return lax.optimization_barrier(v.astype(jnp.bfloat16)).astype(jnp.float32)

@jax.custom_vjp
def low_back(v):
    return v

def low_keep(v):
    return (low(v), None)

def low_pass(kept, grad):
    return (grad,)

def back_keep(v):
    return (v, None)

def back_low(kept, grad):
    return (low(grad),)
low.defvjp(low_keep, low_pass)
low_back.defvjp(back_keep, back_low)

def rms_scale(values):
    return lax.rsqrt(lax.optimization_barrier(jnp.mean(values * values, axis=-1, keepdims=True)) + epsilon)

def rotary_tables(row_count):
    places = (jnp.arange(row_count) % SEQ_LEN).astype(jnp.float32)
    powers = jnp.arange(HD // 2).astype(jnp.float32) * (2.0 / HD)
    angles = places[:, None] * jnp.exp(-powers * math.log(rope_base))[None, :]
    return (jnp.cos(angles)[:, None, :], jnp.sin(angles)[:, None, :])

def rotate(values, cosine, sine_table):
    half_width = values.shape[-1] // 2
    front_half = values[..., :half_width]
    back_half = values[..., half_width:]
    return jnp.concatenate([front_half * cosine - back_half * sine_table, back_half * cosine + front_half * sine_table], axis=-1)

def head_norm(values, scaling):
    return values * rms_scale(values) * scaling

def attend(inputs_block):
    queries, keys_in, values_in, key_live = inputs_block
    products = jnp.einsum('qhd,khd->hqk', queries, keys_in, precision=highest)
    scores = low_back(products) * (1.0 / math.sqrt(HD))
    scores = jnp.where(key_live[None, None, :], scores, masked_score)
    highest_score = lax.optimization_barrier(jnp.max(scores, axis=-1, keepdims=True))
    shifted_exp = jnp.exp(scores - highest_score)
    probabilities = low(shifted_exp / lax.optimization_barrier(jnp.sum(shifted_exp, axis=-1, keepdims=True)))
    mixture = jnp.einsum('hqk,khd->qhd', probabilities, values_in, precision=highest)
    return low(low_back(mixture))

def expert_block(inputs_block, gate_low, up_low, down_low):
    normed, gate_values, route_rows = inputs_block
    summed = jnp.zeros((normed.shape[0], D), jnp.float32)
    for expert in range(EXPERTS):
        member = route_rows == expert
        chosen = jnp.any(member, axis=1)
        token_gate = lax.optimization_barrier(jnp.sum(jnp.where(member, gate_values, 0.0), axis=1))
        picked = jnp.nonzero(chosen, size=CAP, fill_value=0)[0].astype(jnp.int32)
        filled = jnp.arange(CAP) < jnp.sum(chosen.astype(jnp.int32))
        gathered = normed[picked]
        gate_pre = low_back(jnp.dot(gathered, gate_low[expert], precision=highest))
        up_pre = low_back(jnp.dot(gathered, up_low[expert], precision=highest))
        active = low(gate_pre * jax.nn.sigmoid(gate_pre) * up_pre)
        result = low_back(jnp.dot(active, down_low[expert], precision=highest))
        row_gate = jnp.where(filled, token_gate[picked], 0.0)
        summed = summed.at[picked].add(row_gate[:, None] * result)
    return summed

def forward(hidden, attn_gain, query_gain, key_gain, query_weight, key_weight, value_weight, out_weight, moe_gain, router, gate_weight, up_weight, down_weight, lengths, routes):
    tokens = hidden.shape[0]
    normed_attn = low(hidden * rms_scale(hidden) * attn_gain)
    query_pre = low_back(jnp.dot(normed_attn, low(query_weight), precision=highest))
    key_pre = low_back(jnp.dot(normed_attn, low(key_weight), precision=highest))
    value_low = low(low_back(jnp.dot(normed_attn, low(value_weight), precision=highest)))
    cosine, sine_table = rotary_tables(tokens)
    query_low = low(rotate(head_norm(query_pre.reshape(tokens, HEADS, HD), query_gain), cosine, sine_table))
    key_low = low(rotate(head_norm(key_pre.reshape(tokens, HEADS, HD), key_gain), cosine, sine_table))
    key_live = jnp.arange(SEQ_LEN)[None, :] < lengths[:, None]
    shaped = (query_low.reshape(NSEQ, SEQ_LEN, HEADS, HD), key_low.reshape(NSEQ, SEQ_LEN, HEADS, HD), value_low.reshape(NSEQ, SEQ_LEN, HEADS, HD), key_live)
    mixture = lax.map(jax.checkpoint(attend), shaped).reshape(tokens, D)
    attn_branch = low_back(jnp.dot(mixture, low(out_weight), precision=highest))
    middle = hidden + attn_branch
    normed_moe = low(middle * rms_scale(middle) * moe_gain)
    logits = low_back(jnp.dot(normed_moe, low(router), precision=highest))
    chosen_logits = jnp.take_along_axis(logits, routes, axis=1)
    top_logit = lax.optimization_barrier(jnp.max(chosen_logits, axis=1, keepdims=True))
    shifted_exp = jnp.exp(chosen_logits - top_logit)
    gate_values = shifted_exp / lax.optimization_barrier(jnp.sum(shifted_exp, axis=1, keepdims=True))
    gate_low = low(gate_weight)
    up_low = low(up_weight)
    down_low = low(down_weight)

    def run_experts(inputs_block):
        return expert_block(inputs_block, gate_low, up_low, down_low)
    groups = (normed_moe.reshape(N_ROW, TOK_ROW, D), gate_values.reshape(N_ROW, TOK_ROW, TOP), routes.reshape(N_ROW, TOK_ROW, TOP))
    moe_branch = lax.map(jax.checkpoint(run_experts), groups).reshape(tokens, D)
    return middle + low_back(moe_branch)

def reference(hidden_in, lengths, routes, attn_gain, query_gain, key_gain, query_weight, key_weight, value_weight, out_weight, moe_gain, router, gate_weight, up_weight, down_weight, cotangent):
    places = jnp.arange(TOKENS) % SEQ_LEN
    owners = jnp.arange(TOKENS) // SEQ_LEN
    live_rows = (places < lengths[owners]).astype(jnp.float32)

    def layer(hidden, attn_scale, query_scale, key_scale, query_proj, key_proj, value_proj, out_proj, moe_scale, router_proj, gate_proj, up_proj, down_proj):
        return forward(hidden, attn_scale, query_scale, key_scale, query_proj, key_proj, value_proj, out_proj, moe_scale, router_proj, gate_proj, up_proj, down_proj, lengths, routes)
    output, pullback = jax.vjp(layer, hidden_in.astype(jnp.float32), attn_gain, query_gain, key_gain, query_weight, key_weight, value_weight, out_weight, moe_gain, router, gate_weight, up_weight, down_weight)
    grads = pullback(cotangent.astype(jnp.float32) * live_rows[:, None])
    return (output.astype(jnp.bfloat16), grads[0], grads[1], grads[2], grads[3], grads[4], grads[5], grads[6], grads[7], grads[8], grads[9], grads[10], grads[11], grads[12])
```

```python
import functools
import math

import jax
import jax.numpy as jnp
from jax import lax
from jax.experimental import pallas as pl
from jax.experimental.pallas import tpu as pltpu
from jax.sharding import Mesh, PartitionSpec as P

D = 2048
HD = 128
EXPERTS = 16
SEQ_LEN = 1024
CAP = 1152

BLOCK = 128
WINDOW = 144
EDGE = 16
TILE = 384

epsilon = 1e-06
rope_base = 10000.0
masked_score = -1e30

F32 = jnp.float32
BF16 = jnp.bfloat16
ANY = pl.ANY
VMEM_LIMIT = 56 * 1024 * 1024


def dot_of(a, b, da, db):
    return lax.dot_general(a, b, (((da,), (db,)), ((), ())), preferred_element_type=F32)


def params(*semantics):
    return pltpu.CompilerParams(
        vmem_limit_bytes=VMEM_LIMIT, dimension_semantics=semantics or None
    )


def cost(flops, bytes_accessed, transcendentals=0):
    return pl.CostEstimate(
        flops=int(flops), bytes_accessed=int(bytes_accessed), transcendentals=int(transcendentals)
    )


def turn(values, cosine, sine):
    return values * cosine + pltpu.roll(values, HD // 2, 1) * sine


def attend_forward_kernel(
    live_ref, q_ref, k_ref, v_ref, cos_ref, sin_ref, qg_ref, kg_ref, mix_ref, ql_ref, kl_ref, vl_ref
):
    live = live_ref[0]
    cosine = cos_ref[...]
    sine = sin_ref[...]

    def normed(values, gain):
        inverse = lax.rsqrt(jnp.mean(values * values, axis=1, keepdims=True) + epsilon)
        return turn(values * inverse * gain, cosine, sine).astype(BF16)

    ql_ref[...] = normed(q_ref[...], qg_ref[...])
    kl_ref[...] = normed(k_ref[...], kg_ref[...])
    vl_ref[...] = v_ref[...].astype(BF16)
    keys = kl_ref[...]
    values = vl_ref[...]
    rows = 256
    place = lax.broadcasted_iota(jnp.int32, (rows, SEQ_LEN), 1)
    for part in range(SEQ_LEN // rows):
        here = pl.ds(part * rows, rows)
        scores = dot_of(ql_ref[here, :], keys, 1, 1) * (1.0 / math.sqrt(HD))
        scores = jnp.where(place < live, scores, masked_score)
        top = jnp.max(scores, axis=1, keepdims=True)
        shifted = jnp.exp(scores - top)
        total = jnp.sum(shifted, axis=1, keepdims=True)
        probs = (shifted * (1.0 / total)).astype(BF16)
        mix_ref[here, :] = dot_of(probs, values, 1, 0).astype(BF16)


def attend_forward(seq, live, qkv, tables, query_gain, key_gain, heads):
    width = heads * HD

    def pick(offset):
        return pl.BlockSpec((SEQ_LEN, HD), lambda h, live, o=offset: (seq, o + h))

    def whole(shape):
        return pl.BlockSpec(shape, lambda h, live: (0, 0))

    out = pl.BlockSpec((SEQ_LEN, HD), lambda h, live: (0, h))
    return pl.pallas_call(
        attend_forward_kernel,
        grid_spec=pltpu.PrefetchScalarGridSpec(
            num_scalar_prefetch=1,
            grid=(heads,),
            in_specs=[
                pick(0),
                pick(heads),
                pick(2 * heads),
                whole((SEQ_LEN, HD)),
                whole((SEQ_LEN, HD)),
                whole((1, HD)),
                whole((1, HD)),
            ],
            out_specs=[out] * 4,
        ),
        out_shape=[jax.ShapeDtypeStruct((SEQ_LEN, width), BF16)] * 4,
        compiler_params=params("arbitrary"),
        cost_estimate=cost(
            heads * 8 * SEQ_LEN * SEQ_LEN * HD, 20 * SEQ_LEN * width, heads * SEQ_LEN * SEQ_LEN
        ),
        name="attend_forward",
    )(live, qkv, qkv, qkv, tables[0], tables[1], query_gain, key_gain)


def attend_backward_kernel(
    live_ref,
    ql_ref,
    kl_ref,
    vl_ref,
    do_ref,
    q_ref,
    k_ref,
    cos_ref,
    sin_ref,
    qg_ref,
    kg_ref,
    qc_ref,
    kc_ref,
    vc_ref,
    qpart_ref,
    kpart_ref,
    inner_ref,
    dq_ref,
    dk_ref,
    dv_ref,
):
    head = pl.program_id(0)
    live = live_ref[0]
    scale = 1.0 / math.sqrt(HD)
    keys = kl_ref[...]
    values = vl_ref[...]
    rows = 256
    place = lax.broadcasted_iota(jnp.int32, (SEQ_LEN, rows), 0)
    for part in range(SEQ_LEN // rows):
        here = pl.ds(part * rows, rows)
        queries = ql_ref[here, :]
        incoming = do_ref[here, :]
        scores = dot_of(keys, queries, 1, 1) * scale
        scores = jnp.where(place < live, scores, masked_score)
        top = jnp.max(scores, axis=0, keepdims=True)
        shifted = jnp.exp(scores - top)
        total = jnp.sum(shifted, axis=0, keepdims=True)
        probs = shifted * (1.0 / total)
        dv = dot_of(probs.astype(BF16), incoming, 1, 0)
        probs_cot = dot_of(values, incoming, 1, 1)
        weighted = probs * probs_cot
        centre = jnp.sum(weighted, axis=0, keepdims=True)
        raw = ((weighted - probs * centre) * scale).astype(BF16)
        dk = dot_of(raw, queries, 1, 0)
        dq_ref[here, :] = dot_of(raw, keys, 0, 0)
        if part == 0:
            dv_ref[...] = dv
            dk_ref[...] = dk
        else:
            dv_ref[...] += dv
            dk_ref[...] += dk
    cosine = cos_ref[...]
    sine = -sin_ref[...]

    def back(values, gain, rotated_cot):
        incoming = turn(rotated_cot, cosine, sine)
        inverse = lax.rsqrt(jnp.mean(values * values, axis=1, keepdims=True) + epsilon)
        scaled = incoming * gain
        inner = jnp.mean(scaled * values, axis=1, keepdims=True)
        grad = inverse * scaled - values * (inverse * inverse * inverse * inner)
        part = jnp.sum(incoming * values * inverse, axis=0, keepdims=True)
        return grad.astype(BF16), part, jnp.sum(grad * values, axis=1, keepdims=True)

    qc_ref[...], qpart, inner = back(q_ref[...], qg_ref[...], dq_ref[...])
    kc_ref[...], kpart, key_inner = back(k_ref[...], kg_ref[...], dk_ref[...])
    vc_ref[...] = dv_ref[...].astype(BF16)
    inner += key_inner
    inner += jnp.sum(dv_ref[...] * values.astype(F32), axis=1, keepdims=True)

    @pl.when(head == 0)
    def _():
        qpart_ref[...] = qpart
        kpart_ref[...] = kpart
        inner_ref[...] = inner

    @pl.when(head > 0)
    def _():
        qpart_ref[...] += qpart
        kpart_ref[...] += kpart
        inner_ref[...] += inner


def attend_backward(seq, live, lows, mixture_cot, qkv, tables, query_gain, key_gain, heads):
    width = heads * HD
    block = pl.BlockSpec((SEQ_LEN, HD), lambda h, live: (0, h))

    def pick(offset):
        return pl.BlockSpec((SEQ_LEN, HD), lambda h, live, o=offset: (seq, o + h))

    def whole(shape):
        return pl.BlockSpec(shape, lambda h, live: (0, 0))

    return pl.pallas_call(
        attend_backward_kernel,
        grid_spec=pltpu.PrefetchScalarGridSpec(
            num_scalar_prefetch=1,
            grid=(heads,),
            in_specs=[block] * 4
            + [
                pick(0),
                pick(heads),
                whole((SEQ_LEN, HD)),
                whole((SEQ_LEN, HD)),
                whole((1, HD)),
                whole((1, HD)),
            ],
            out_specs=[block] * 3 + [whole((1, HD))] * 2 + [whole((SEQ_LEN, 1))],
            scratch_shapes=[pltpu.VMEM((SEQ_LEN, HD), F32)] * 3,
        ),
        out_shape=[jax.ShapeDtypeStruct((SEQ_LEN, width), BF16)] * 3
        + [jax.ShapeDtypeStruct((1, HD), F32)] * 2
        + [jax.ShapeDtypeStruct((SEQ_LEN, 1), F32)],
        compiler_params=params("arbitrary"),
        cost_estimate=cost(
            heads * 20 * SEQ_LEN * SEQ_LEN * HD, 24 * SEQ_LEN * width, heads * SEQ_LEN * SEQ_LEN
        ),
        name="attend_backward",
    )(live, *lows, mixture_cot, qkv, qkv, tables[0], tables[1], query_gain, key_gain)


def compact_kernel(start_ref, where_ref, pos_ref, source_ref, *outs):
    group, groups = pl.program_id(0), pl.num_programs(0)
    row_of = lax.broadcasted_iota(jnp.int32, (WINDOW, BLOCK), 0)
    for out in outs:
        out[...] = jnp.zeros_like(out)
    for number in range(source_ref.shape[1] // BLOCK):
        here = slice(number * BLOCK, (number + 1) * BLOCK)
        for expert, out in enumerate(outs):
            start = pl.multiple_of(start_ref[expert * groups + group, number], EDGE)
            place = pos_ref[expert, 0, :, here]
            choice = jnp.where(row_of + start == place, 1.0, 0.0).astype(BF16)
            rows = dot_of(choice, source_ref[0, here, :], 1, 0)
            out[pl.ds(start, WINDOW), :] += rows.astype(BF16)


def compact(starts, where, pos_row, source, groups, cols):
    tokens, width = source.shape[1:]
    count = pos_row.shape[0] // groups
    return pl.pallas_call(
        compact_kernel,
        grid_spec=pltpu.PrefetchScalarGridSpec(
            num_scalar_prefetch=2,
            grid=(groups, cols),
            in_specs=[
                pl.BlockSpec((count, 1, 1, tokens), lambda q, j, s, w: (0, q, 0, 0)),
                pl.BlockSpec(
                    (1, tokens, width), lambda q, j, s, w: ((w[0] ^ q) * cols + j, 0, 0)
                ),
            ],
            out_specs=[pl.BlockSpec((CAP, width), lambda q, j, s, w: (q, j))] * count,
        ),
        out_shape=[jax.ShapeDtypeStruct((groups * CAP, cols * width), BF16)] * count,
        compiler_params=params("arbitrary", "arbitrary"),
        cost_estimate=cost(
            count * groups * cols * 2 * tokens * WINDOW * width * 2,
            groups * cols * 2 * width * (tokens + count * CAP),
        ),
        name="compact",
    )(starts, where, pos_row.reshape(count, groups, 1, tokens), source)


def compact_scalars_kernel(start_ref, pos_ref, *refs):
    count = len(refs) // 2
    group = pl.program_id(0)
    row_of = lax.broadcasted_iota(jnp.int32, (WINDOW, BLOCK), 0)
    for number in range(count):
        refs[count + number][...] = jnp.zeros_like(refs[count + number])
    for number in range(pos_ref.shape[2] // BLOCK):
        start = pl.multiple_of(start_ref[group, number], EDGE)
        here = slice(number * BLOCK, (number + 1) * BLOCK)
        choice = row_of + start == pos_ref[0, :, here]
        for source, out in zip(refs[:count], refs[count:]):
            picked = jnp.sum(jnp.where(choice, source[0, :, here], 0.0), axis=1, keepdims=True)
            out[pl.ds(start, WINDOW), :] += picked


def compact_scalars(starts, pos_row, sources):
    groups, _, tokens = pos_row.shape
    block = pl.BlockSpec((1, 1, tokens), lambda q, s: (q, 0, 0))
    return pl.pallas_call(
        compact_scalars_kernel,
        grid_spec=pltpu.PrefetchScalarGridSpec(
            num_scalar_prefetch=1,
            grid=(groups,),
            in_specs=[block] * (1 + len(sources)),
            out_specs=[pl.BlockSpec((CAP, 1), lambda q, s: (q, 0))] * len(sources),
        ),
        out_shape=[jax.ShapeDtypeStruct((groups * CAP, 1), F32)] * len(sources),
        compiler_params=params("arbitrary"),
        cost_estimate=cost(0, 4 * groups * CAP * 128 * len(sources)),
        name="compact_scalars",
    )(starts, pos_row, *sources)


def expand_scalars_kernel(start_ref, pos_ref, *refs):
    count = len(refs) // 2
    group = pl.program_id(0)
    row_of = lax.broadcasted_iota(jnp.int32, (WINDOW, BLOCK), 0)
    for number in range(pos_ref.shape[2] // BLOCK):
        start = pl.multiple_of(start_ref[group, number], EDGE)
        here = slice(number * BLOCK, (number + 1) * BLOCK)
        choice = row_of + start == pos_ref[0, :, here]
        for source, out in zip(refs[:count], refs[count:]):
            held = source[pl.ds(start, WINDOW), :]
            out[0, :, here] = jnp.sum(jnp.where(choice, held, 0.0), axis=0, keepdims=True)


def expand_scalars(starts, pos_row, sources):
    groups, _, tokens = pos_row.shape
    block = pl.BlockSpec((1, 1, tokens), lambda q, s: (q, 0, 0))
    return pl.pallas_call(
        expand_scalars_kernel,
        grid_spec=pltpu.PrefetchScalarGridSpec(
            num_scalar_prefetch=1,
            grid=(groups,),
            in_specs=[block] + [pl.BlockSpec((CAP, 1), lambda q, s: (q, 0))] * len(sources),
            out_specs=[block] * len(sources),
        ),
        out_shape=[jax.ShapeDtypeStruct((groups, 1, tokens), F32)] * len(sources),
        compiler_params=params("arbitrary"),
        cost_estimate=cost(0, 4 * groups * CAP * 128 * len(sources)),
        name="expand_scalars",
    )(starts, pos_row, *sources)


def expand_kernel(sizes, count, start_ref, where_ref, pos_ref, *refs):
    group, groups = pl.program_id(0), pl.num_programs(0)
    sides = len(refs) // (count + len(sizes))
    sources, outs = refs[: count * sides], refs[count * sides :]
    column_of = lax.broadcasted_iota(jnp.int32, (BLOCK, WINDOW), 1)
    number = 0
    for part, size in enumerate(sizes):
        for step in range(size // BLOCK):
            totals = [None] * sides
            for expert in range(count):
                start = pl.multiple_of(start_ref[expert * groups + group, number], EDGE)
                place = pos_ref[expert, 0, number * BLOCK : (number + 1) * BLOCK, :]
                choice = jnp.where(column_of + start == place, 1.0, 0.0).astype(BF16)
                for side in range(sides):
                    held = sources[expert * sides + side][pl.ds(start, WINDOW), :]
                    rows = dot_of(choice, held, 1, 0)
                    totals[side] = rows if totals[side] is None else totals[side] + rows
            here = slice(step * BLOCK, (step + 1) * BLOCK)
            for side in range(sides):
                outs[part * sides + side][0, 0, here, :] = totals[side].astype(BF16)
            number += 1


def expand(starts, where, pos_col, sources, sizes, groups, cols):
    width = sources[0].shape[1] // cols
    tokens = sum(sizes)
    count = len(sources)

    def side(odd):
        return pl.BlockSpec((CAP, width), lambda q, j, s, w: (q, w[1] ^ (2 * j + odd)))

    outs = pl.pallas_call(
        functools.partial(expand_kernel, sizes, count),
        grid_spec=pltpu.PrefetchScalarGridSpec(
            num_scalar_prefetch=2,
            grid=(groups, cols // 2),
            in_specs=[pl.BlockSpec((count, 1, tokens, 1), lambda q, j, s, w: (0, q, 0, 0))]
            + [side(0), side(1)] * count,
            out_specs=[
                pl.BlockSpec((1, 1, size, width), lambda q, j, s, w: (q, j, 0, 0))
                for size in sizes
                for _ in range(2)
            ],
        ),
        out_shape=[
            jax.ShapeDtypeStruct((groups, cols // 2, size, width), BF16)
            for size in sizes
            for _ in range(2)
        ],
        compiler_params=params("arbitrary", "arbitrary"),
        cost_estimate=cost(
            4 * count * groups * cols * tokens * WINDOW * width,
            groups * cols * width * (2 * tokens + 2 * count * CAP),
        ),
        name="expand",
    )(
        starts,
        where,
        pos_col.reshape(count, groups, tokens, 1),
        *[source for source in sources for _ in range(2)],
    )
    return list(zip(outs[::2], outs[1::2]))


def expand_all(starts, where, pos_col, sources, groups, cols):
    width = sources[0].shape[1] // cols
    tokens = pos_col.shape[1]
    count = len(sources)
    return pl.pallas_call(
        functools.partial(expand_kernel, [tokens], count),
        grid_spec=pltpu.PrefetchScalarGridSpec(
            num_scalar_prefetch=2,
            grid=(groups, cols),
            in_specs=[pl.BlockSpec((count, 1, tokens, 1), lambda q, j, s, w: (0, q, 0, 0))]
            + [pl.BlockSpec((CAP, width), lambda q, j, s, w: (q, j))] * count,
            out_specs=pl.BlockSpec((1, 1, tokens, width), lambda q, j, s, w: (w[0] ^ q, j, 0, 0)),
        ),
        out_shape=jax.ShapeDtypeStruct((groups, cols, tokens, width), BF16),
        compiler_params=params("arbitrary", "arbitrary"),
        cost_estimate=cost(
            4 * count * groups * cols * tokens * WINDOW * width,
            groups * cols * width * (2 * tokens + 2 * count * CAP),
        ),
        name="expand_all",
    )(starts, where, pos_col.reshape(count, groups, tokens, 1), *sources)


def pack_kernel(where_ref, gate_ref, up_ref, down_ref, out_ref):
    hidden = gate_ref.shape[2]
    out_ref[0, :, :hidden] = gate_ref[0].astype(BF16)
    out_ref[0, :, hidden : 2 * hidden] = up_ref[0].astype(BF16)
    out_ref[0, :, 2 * hidden :] = down_ref[0].T.astype(BF16)


def pack_weights(where, gate, up, down, each):
    experts, depth, hidden = gate.shape

    def pick(shape):
        return pl.BlockSpec(shape, lambda q, w: ((w[0] ^ (q // each)) * each + q % each, 0, 0))

    return pl.pallas_call(
        pack_kernel,
        grid_spec=pltpu.PrefetchScalarGridSpec(
            num_scalar_prefetch=1,
            grid=(experts,),
            in_specs=[pick((1, depth, hidden)), pick((1, depth, hidden)), pick((1, hidden, depth))],
            out_specs=pl.BlockSpec((1, depth, 3 * hidden), lambda q, w: (q, 0, 0)),
        ),
        out_shape=jax.ShapeDtypeStruct((experts, depth, 3 * hidden), BF16),
        compiler_params=params("arbitrary"),
        cost_estimate=cost(0, 18 * experts * depth * hidden),
        name="pack_weights",
    )(where, gate, up, down)


def unpack_kernel(where_ref, *refs):
    sources, (gate_ref, up_ref, down_ref) = refs[:-3], refs[-3:]
    hidden = gate_ref.shape[2]
    for number, source in enumerate(sources):

        @pl.when(pl.program_id(0) == number)
        def _(source=source):
            gate_ref[0] = source[:, :hidden].astype(F32)
            up_ref[0] = source[:, hidden : 2 * hidden].astype(F32)
            down_ref[0] = source[:, 2 * hidden :].astype(F32).T


def unpack_grads(where, sources, each):
    count = len(sources)
    depth, wide = sources[0].shape
    hidden = wide // 3

    def pick(shape):
        return pl.BlockSpec(shape, lambda q, w: ((w[0] ^ (q // each)) * each + q % each, 0, 0))

    shapes = [(count, depth, hidden), (count, depth, hidden), (count, hidden, depth)]
    return pl.pallas_call(
        unpack_kernel,
        grid_spec=pltpu.PrefetchScalarGridSpec(
            num_scalar_prefetch=1,
            grid=(count,),
            in_specs=[pl.BlockSpec((depth, wide), lambda q, w: (0, 0))] * count,
            out_specs=[pick((1,) + shape[1:]) for shape in shapes],
        ),
        out_shape=[jax.ShapeDtypeStruct(shape, F32) for shape in shapes],
        compiler_params=params("arbitrary"),
        cost_estimate=cost(0, 18 * count * depth * hidden),
        name="unpack_grads",
    )(where, *sources)


def expert_kernel(count, hidden, row_ref, x_ref, m_ref, gate_ref, scale_ref, *refs):
    pieces = refs[:count]
    rows_ref, pre_ref, act_ref, cot_ref, inner_ref, result_ref, held, sems = refs[count:]
    depth = pieces[0].shape[0]

    @pl.when(pl.program_id(0) == 0)
    def _():
        copies = []
        for number, piece in enumerate(pieces):
            place = pl.ds(pl.multiple_of(row_ref[number] * depth, depth), depth)
            copies.append(pltpu.make_async_copy(piece, held.at[place, :], sems.at[number]))
        for copy in copies:
            copy.start()
        for copy in copies:
            copy.wait()

    gate = gate_ref[...]
    scale = scale_ref[...]
    wide = 256
    cot_ref[...] = jnp.zeros_like(cot_ref)
    inner_ref[...] = jnp.zeros_like(inner_ref)

    @pl.loop(0, hidden // wide)
    def _(step):
        first = pl.multiple_of(step * wide, wide)
        gate_pre = dot_of(x_ref[...], held[:, pl.ds(first, wide)], 1, 0) * scale
        up_pre = dot_of(x_ref[...], held[:, pl.ds(hidden + first, wide)], 1, 0) * scale
        back = dot_of(m_ref[...], held[:, pl.ds(2 * hidden + first, wide)], 1, 0)
        squash = 1.0 / (1.0 + jnp.exp(-gate_pre))
        silu = gate_pre * squash
        active = silu * up_pre
        cot_ref[...] += jnp.sum(active.astype(BF16).astype(F32) * back, axis=1, keepdims=True)
        act_ref[:, pl.ds(first, wide)] = (active * gate).astype(BF16)
        back = back * gate
        slope = squash * (1.0 + gate_pre * (1.0 - squash))
        gate_cot = back * up_pre * slope
        up_cot = back * silu
        inner_ref[...] += jnp.sum(gate_cot * gate_pre + up_cot * up_pre, axis=1, keepdims=True)
        pre_ref[:, pl.ds(first, wide)] = (gate_cot * scale).astype(BF16)
        pre_ref[:, pl.ds(hidden + first, wide)] = (up_cot * scale).astype(BF16)

    @pl.loop(0, held.shape[0] // wide)
    def _(step):
        first = pl.multiple_of(step * wide, wide)
        here = pl.ds(first, wide)
        rows_ref[:, here] = dot_of(pre_ref[...], held[here, : 2 * hidden], 1, 1).astype(BF16)
        result_ref[:, here] = dot_of(act_ref[...], held[here, 2 * hidden :], 1, 1).astype(BF16)


def expert_step(row_numbers, x, m, gate, scale, pieces):
    total, wide = x.shape
    hidden = pieces[0].shape[1] // 3
    count = len(pieces)

    def tile(columns):
        return pl.BlockSpec((TILE, columns), lambda i, r: (i, 0))

    return pl.pallas_call(
        functools.partial(expert_kernel, count, hidden),
        grid_spec=pltpu.PrefetchScalarGridSpec(
            num_scalar_prefetch=1,
            grid=(total // TILE,),
            in_specs=[tile(wide), tile(wide), tile(1), tile(1)]
            + [pl.BlockSpec(memory_space=ANY)] * count,
            out_specs=[tile(wide), tile(2 * hidden), tile(hidden), tile(1), tile(1), tile(wide)],
            scratch_shapes=[
                pltpu.VMEM((wide, 3 * hidden), BF16),
                pltpu.SemaphoreType.DMA((count,)),
            ],
        ),
        out_shape=[
            jax.ShapeDtypeStruct((total, wide), BF16),
            jax.ShapeDtypeStruct((total, 2 * hidden), BF16),
            jax.ShapeDtypeStruct((total, hidden), BF16),
            jax.ShapeDtypeStruct((total, 1), F32),
            jax.ShapeDtypeStruct((total, 1), F32),
            jax.ShapeDtypeStruct((total, wide), BF16),
        ],
        compiler_params=params("arbitrary"),
        cost_estimate=cost(
            2 * total * wide * hidden * 6, 2 * total * (4 * wide + 3 * hidden), total * hidden
        ),
        name="expert_step",
    )(row_numbers, x, m, gate, scale, *pieces)


def weight_grad_kernel(row_ref, x_ref, m_ref, pre_ref, act_ref, out_ref, turned_ref):
    wide = 512
    first = pre_ref.shape[1]
    turned_ref[0] = x_ref[...].T
    turned_ref[1] = m_ref[...].T

    @pl.loop(0, first // wide)
    def _(step):
        here = pl.ds(pl.multiple_of(step * wide, wide), wide)
        out_ref[0, :, here] = dot_of(turned_ref[0], pre_ref[:, here], 1, 0).astype(BF16)

    @pl.loop(0, act_ref.shape[1] // wide)
    def _(step):
        here = pl.ds(pl.multiple_of(step * wide, wide), wide)
        there = pl.ds(pl.multiple_of(first + step * wide, wide), wide)
        out_ref[0, :, there] = dot_of(turned_ref[1], act_ref[:, here], 1, 0).astype(BF16)


def weight_grads(row_numbers, x, m, pre, act, depth):
    total = x.shape[0]
    wide = pre.shape[1] + act.shape[1]
    count = row_numbers.shape[0]

    def column(array):
        return pl.BlockSpec((total, depth), lambda i, r: (0, r[i]))

    def whole(array):
        return pl.BlockSpec(array.shape, lambda i, r: (0, 0), pipeline_mode=pl.Buffered(1))

    return pl.pallas_call(
        weight_grad_kernel,
        grid_spec=pltpu.PrefetchScalarGridSpec(
            num_scalar_prefetch=1,
            grid=(count,),
            in_specs=[column(x), column(m), whole(pre), whole(act)],
            out_specs=pl.BlockSpec((1, depth, wide), lambda i, r: (i, 0, 0)),
            scratch_shapes=[pltpu.VMEM((2, depth, total), BF16)],
        ),
        out_shape=jax.ShapeDtypeStruct((count, depth, wide), BF16),
        compiler_params=params("arbitrary"),
        cost_estimate=cost(
            2 * total * depth * count * wide, 2 * total * (2 * depth * count + wide)
        ),
        name="weight_grads",
    )(row_numbers, x, m, pre, act)


def bits_of(size):
    return [1 << n for n in range(size.bit_length() - 1)]


def swap(values, axis, bit):
    size = lax.axis_size(axis)
    return lax.ppermute(values, axis, [(n, n ^ bit) for n in range(size)])


class Flow:
    def __init__(self, steps):
        self.steps = steps
        self.result = None
        self.sends = next(steps)

    def advance(self, got):
        try:
            self.sends = self.steps.send(got)
        except StopIteration as stop:
            self.sends = None
            self.result = stop.value

    def finish(self):
        while self.sends is not None:
            self.advance([swap(*send) for send in self.sends])
        return self.result


def stage(live, flows=(), work=(), slow=()):
    waiting = live.pop("slow", [])
    busy = [flow for flow, _ in waiting]
    slow = [flow for flow in slow if flow.sends is not None and flow not in busy]
    busy += slow
    slow = [(flow, [swap(*send) for send in flow.sends]) for flow in slow]
    flows = [flow for flow in flows if flow.sends is not None and flow not in busy]
    got = [[swap(*send) for send in flow.sends] for flow in flows]
    done = [each() for each in work]
    late = [arrays for _, arrays in waiting]
    got, late, done, kept = lax.optimization_barrier((got, late, done, dict(live)))
    live.update(kept)
    for flow, arrays in zip(flows + [flow for flow, _ in waiting], got + late):
        flow.advance(arrays)
    live["slow"] = slow
    return done


def spread_steps(values, axis, bits):
    blocks = {0: values}
    for bit in bits:
        places = sorted(blocks)
        got = yield [(blocks[place], axis, bit) for place in places]
        blocks.update({place | bit: block for place, block in zip(places, got)})
    return [blocks[place] for place in sorted(blocks)]


def spread_rows_steps(values, row_bits, strides):
    held = values[None]
    places = [0]
    for axis, bit in row_bits:
        (got,) = yield [(held, axis, bit)]
        held = jnp.concatenate([held, got], axis=0)
        places += [place | (bit * strides[axis]) for place in places]
    return jnp.stack([held[places.index(place)] for place in range(len(places))])


def spread_cube_steps(values, groups, cols):
    held = values[None]
    for axis, bits in (("col", bits_of(cols)), ("lo", bits_of(groups))):
        for bit in bits:
            (got,) = yield [(held, axis, bit)]
            held = jnp.concatenate([held, got], axis=0)
    return held.reshape((groups, cols) + values.shape)


def col_reduce_steps(blocks, cols):
    held = dict(enumerate(blocks))
    for bit in bits_of(cols):
        away = [place for place in sorted(held) if place & bit]
        (got,) = yield [(jnp.stack([held[place].astype(BF16) for place in away]), "col", bit)]
        held = {
            place & ~bit: held[place & ~bit] + got[number].astype(F32)
            for number, place in enumerate(away)
        }
    return held[0]


def total_steps(values, axis, bits):
    for bit in bits:
        (got,) = yield [(values, axis, bit)]
        values = values + got
    return values


def links_of(groups, cols):
    return [("col", bit) for bit in bits_of(cols)[1:]] + [("lo", bit) for bit in bits_of(groups)]


def turned(links, number):
    number %= len(links)
    return links[number:] + links[:number]


def reduce_steps(parts, groups, cols):
    links = links_of(groups, cols)
    got = yield [(away, "col", 1) for _, away in parts]
    held = []
    for number, (keep, _) in enumerate(parts):
        shape = (2,) * len(links) + keep.shape[2:]
        names = [("lo", bit) for bit in reversed(bits_of(groups))]
        names += [("col", bit) for bit in reversed(bits_of(cols)[1:])]
        held.append((keep.reshape(shape), got[number].reshape(shape), names))
    for step in range(len(links)):
        sends, rest = [], []
        for number, (keep, more, names) in enumerate(held):
            link = turned(links, number)[step]
            axis = names.index(link)

            def half(place):
                total = lax.index_in_dim(keep, place, axis, False).astype(F32)
                return total + lax.index_in_dim(more, place, axis, False).astype(F32)

            sends.append((half(1).astype(BF16), *link))
            kept = half(0)
            rest.append(
                (
                    kept if step + 1 == len(links) else kept.astype(BF16),
                    [name for name in names if name != link],
                )
            )
        got = yield sends
        held = [(keep, more, names) for (keep, names), more in zip(rest, got)]
    return jnp.concatenate([keep.astype(F32) + more.astype(F32) for keep, more, _ in held], axis=0)


def part_sizes(tokens, count):
    whole = tokens // BLOCK
    return [BLOCK * ((whole + count - 1 - n) // count) for n in range(count)]


def expert_weight_steps(piece, far, bits):
    if far:
        (piece,) = yield [(piece, "lo", far)]
    held = {(): piece}
    fresh = [()]
    while True:
        ways = [
            (place, number)
            for place in fresh
            for number in range(place[-1] + 1 if place else 0, len(bits))
        ]
        if not ways:
            return held
        got = yield [(held[place], *bits[number]) for place, number in ways]
        fresh = [place + (number,) for place, number in ways]
        held.update(zip(fresh, got))


def expert_grad_steps(blocks, far, bits):
    for number in reversed(range(len(bits))):
        half = blocks.shape[0] // 2
        (got,) = yield [(blocks[half:], *bits[number])]
        blocks = blocks[:half].astype(F32) + got.astype(F32)
        if number or far:
            blocks = blocks.astype(BF16)
    total = blocks[0]
    if far:
        (total,) = yield [(total, "lo", far)]
    return total


def per_device(
    hidden_in,
    lengths,
    routes,
    attn_gain,
    query_gain,
    key_gain,
    query_weight,
    key_weight,
    value_weight,
    out_weight,
    moe_gain,
    router,
    gate_weight,
    up_weight,
    down_weight,
    cotangent,
):
    tok_rows, width = hidden_in.shape
    cols = lax.axis_size("col")
    groups = lax.axis_size("lo")
    high = lax.axis_size("hi")
    mids = lax.axis_size("mid")
    col = lax.axis_index("col")
    lo = lax.axis_index("lo")
    hi = lax.axis_index("hi")
    mid = lax.axis_index("mid")
    row = (hi * groups + lo) * mids + mid
    where = jnp.stack([lo, col])
    heads = width // HD
    seqs = lengths.shape[0]
    depth = gate_weight.shape[1]
    each = gate_weight.shape[0] // groups
    cube = ("lo", "col")
    rows_axes = ("hi", "lo", "mid")
    strides = {"hi": groups * mids, "lo": mids, "mid": 1}
    seq_rows = [slice(s * SEQ_LEN, (s + 1) * SEQ_LEN) for s in range(seqs)]
    links = links_of(groups, cols)
    col_bits = list(reversed(bits_of(cols)))
    hi_bits = [("hi", bit) for bit in bits_of(high)]
    mid_bits = [("mid", bit) for bit in bits_of(mids)]
    row_bits = hi_bits + [("lo", bit) for bit in bits_of(groups)] + mid_bits
    far_bits = hi_bits + mid_bits
    live = {}

    def row_of_set(place, far):
        other = row ^ (far * mids)
        for number in place:
            axis, bit = far_bits[number]
            other = other ^ (bit * strides[axis])
        return other

    hidden_flow = Flow(spread_steps(hidden_in, "col", col_bits))
    gain_flow = Flow(spread_steps(attn_gain, "col", col_bits))
    routes_flow = Flow(spread_steps(routes.T, "lo", bits_of(groups)))
    router_flow = Flow(spread_rows_steps(router.T.astype(BF16), row_bits, strides))
    out_flow = Flow(spread_rows_steps(out_weight.T.astype(BF16), row_bits, strides))
    qkv_local = jnp.concatenate([query_weight, key_weight, value_weight], axis=1).astype(BF16)
    qkv_full = lax.all_gather(qkv_local, rows_axes, axis=0, tiled=True)
    live_key = jnp.arange(SEQ_LEN)[None, :] < lengths[:, None]
    out_cot = jnp.where(live_key.reshape(tok_rows, 1), cotangent, jnp.zeros_like(cotangent))
    packed = pack_weights(where, gate_weight, up_weight, down_weight, each)
    units = [(expert, far) for expert in range(each) for far in range(groups)]
    live["packed"] = packed

    def rotary_tables():
        places = jnp.arange(SEQ_LEN).astype(F32)
        powers = jnp.arange(HD // 2).astype(F32) * (2.0 / HD)
        angles = places[:, None] * jnp.exp(-powers * math.log(rope_base))[None, :]
        cosine, sine = jnp.cos(angles), jnp.sin(angles)
        return (
            jnp.concatenate([cosine, cosine], axis=1),
            jnp.concatenate([-sine, sine], axis=1),
        )

    live["out_cot"] = out_cot
    (tables,) = stage(
        live,
        [hidden_flow, gain_flow, routes_flow, router_flow, out_flow],
        [rotary_tables],
    )

    hidden = hidden_in.astype(F32)

    def norm_attn():
        blocks = hidden_flow.finish()
        gains = gain_flow.finish()
        square = sum(jnp.sum(jnp.square(block.astype(F32)), axis=1) for block in blocks)
        inverse = lax.rsqrt(square / D + epsilon)[:, None]
        normed = jnp.zeros((tok_rows, D), BF16)
        for place, (block, gain) in enumerate(zip(blocks, gains)):
            piece = (block.astype(F32) * inverse * gain).astype(BF16)
            normed = lax.dynamic_update_slice_in_dim(normed, piece, (col ^ place) * width, 1)
        return normed, inverse

    def routing():
        rel = jnp.stack(routes_flow.finish())
        named = jnp.any(rel[:, :, None, :] == jnp.arange(EXPERTS)[None, None, :, None], axis=1)
        first = (col * groups + lo) * each
        member = lax.dynamic_slice_in_dim(named, first, each, 1)
        member = jnp.swapaxes(member, 0, 1).reshape(each * groups, tok_rows)
        count = member.astype(jnp.int32)
        rank = jnp.cumsum(count, axis=1) - count
        pos = jnp.where(member, rank, -(1 << 20))
        starts = jnp.minimum(rank[:, ::BLOCK] // EDGE * EDGE, CAP - WINDOW)
        return named, starts, pos[:, None, :], pos[:, :, None]

    live["qkv_full"] = qkv_full
    ((live["normed_attn"], attn_inverse),) = stage(live, [router_flow, out_flow], [norm_attn])
    weight_flows = {
        (expert, far): Flow(
            expert_weight_steps(live["packed"][far * each + expert], far, far_bits)
        )
        for expert, far in units
    }
    fars = [weight_flows[unit] for unit in units if unit[1]]
    moe_cot = lax.all_gather(live["out_cot"], cube, axis=0, tiled=False)
    hidden_blocks = hidden_flow.result
    query_scale, key_scale = query_gain[None, :], key_gain[None, :]

    def attend(s):
        return attend_forward(
            s, lengths[s : s + 1], live["qkv"], tables, query_scale, key_scale, heads
        )

    live["qkv"] = dot_of(live["normed_attn"], live["qkv_full"], 1, 0)
    first_seq, (named, starts, pos_row, pos_col) = stage(
        live,
        [router_flow, out_flow],
        [functools.partial(attend, 0), routing],
        slow=[weight_flows[0, 0]] + fars,
    )
    attended = [first_seq]

    span = width // depth

    def col_rows(blocks, place, axis):
        first = (col ^ place) * span
        return jnp.concatenate(
            [
                lax.dynamic_index_in_dim(blocks, (first + n) ^ row, 0, False)
                for n in range(span)
            ],
            axis=axis,
        )

    out_spread = out_flow.finish()
    out_rel = jnp.concatenate([col_rows(out_spread, place, 0) for place in range(cols)], axis=0)
    router_rows = col_rows(router_flow.finish(), 0, 1)

    def branch_flow(s):
        partial = dot_of(attended[s][0], out_rel, 1, 1)
        return Flow(
            col_reduce_steps([partial[:, n * width : (n + 1) * width] for n in range(cols)], cols)
        )

    branches = [branch_flow(0)]
    attended += stage(
        live, branches, [functools.partial(attend, s) for s in range(1, seqs)]
    )
    branches += [branch_flow(s) for s in range(1, seqs)]
    middle, scaled_rows = [], []

    def after_branch(s):
        branch = branches[s].finish()
        middle.append(hidden[seq_rows[s]] + branch)
        scaled_rows.append((middle[s] * moe_gain).astype(BF16))

    stage(live, branches, slow=[weight_flows[0, 0], fars[0]])
    (live["cot_rows"],) = stage(
        live,
        branches,
        [lambda: compact(starts, where, pos_row, moe_cot, groups, cols)],
    )
    for s in range(seqs):
        after_branch(s)
    middle = jnp.concatenate(middle, axis=0)
    scaled_rows = jnp.concatenate(scaled_rows, axis=0)
    moe_in = lax.all_gather(scaled_rows, cube, axis=0, tiled=False)
    square = jnp.sum(middle * middle, axis=1)[None, :]
    stat = jnp.concatenate([dot_of(router_rows, scaled_rows, 1, 1), square], axis=0)
    stat = Flow(spread_cube_steps(stat, groups, cols)).finish()

    stat = jnp.sum(stat, axis=1)
    moe_inverse = lax.rsqrt(stat[:, EXPERTS] / D + epsilon)
    all_logits = stat[:, :EXPERTS] * moe_inverse[:, None, :]
    logits = jnp.where(named, all_logits, masked_score)
    shifted = jnp.where(named, jnp.exp(logits - jnp.max(logits, axis=1, keepdims=True)), 0.0)
    gates = shifted / jnp.sum(shifted, axis=1, keepdims=True)
    own_gate = lax.dynamic_slice_in_dim(gates, (col * groups + lo) * each, each, 1)
    own_gate = jnp.swapaxes(own_gate, 0, 1).reshape(each * groups, 1, tok_rows)
    row_gate, row_scale = compact_scalars(
        starts, pos_row, (own_gate, jnp.tile(moe_inverse, (each, 1))[:, None, :])
    )
    total_rows = groups * CAP

    live["moe_rows"] = compact(starts, where, pos_row, moe_in, groups, cols)

    def run_expert(expert):
        pieces, row_numbers = [], []
        for far in range(groups):
            for place, piece in weight_flows[expert, far].finish().items():
                pieces.append(piece)
                row_numbers.append(row_of_set(place, far))
        here = slice(expert * total_rows, (expert + 1) * total_rows)
        return expert_step(
            jnp.stack(row_numbers),
            live["moe_rows"][expert],
            live["cot_rows"][expert],
            row_gate[here],
            row_scale[here],
            pieces,
        )

    set_rows = [
        [number for number in range(len(far_bits)) if index >> number & 1]
        for index in range(1 << len(far_bits))
    ]
    grad_rows = jnp.stack(
        [row_of_set(place, far) for far in reversed(range(groups)) for place in set_rows]
    )
    grad_flows = {}

    def start_grads(expert, outs):
        grads = weight_grads(
            grad_rows,
            live["moe_rows"][expert],
            live["cot_rows"][expert],
            outs[1],
            outs[2],
            depth,
        )
        return grads.reshape((groups, len(set_rows)) + grads.shape[1:])

    def grad_flow(expert, grads):
        for number, far in enumerate(reversed(range(groups))):
            grad_flows[expert, far] = Flow(expert_grad_steps(grads[number], far, far_bits))

    def running():
        return list(grad_flows.values())

    ran = []
    for expert in range(each):
        (outs,) = stage(live, running(), [functools.partial(run_expert, expert)])
        ran.append(outs)
        if expert + 1 < each:
            (grads,) = stage(live, [], [functools.partial(start_grads, expert, outs)])
            grad_flow(expert, grads)
    live["result"] = [outs[5] for outs in ran]
    last = ran[-1]
    gate_cot = jnp.concatenate([outs[3] for outs in ran], axis=0)
    row_inner = jnp.concatenate([outs[4] for outs in ran], axis=0)
    sizes = part_sizes(tok_rows, len(links))
    rows_parts, (gate_cot, row_inner) = stage(
        live,
        [],
        [
            lambda: expand(
                starts, where, pos_col, [outs[0] for outs in ran], sizes, groups, cols
            ),
            lambda: expand_scalars(starts, pos_row, (gate_cot, row_inner)),
        ],
    )
    gate_cot = gate_cot.reshape(each, groups, tok_rows)
    row_inner = jnp.sum(row_inner.reshape(each, groups, tok_rows), axis=0)[None]
    scalars = jnp.concatenate([gate_cot, row_inner], axis=0)
    scalars = scalars.reshape((each + 1) * groups, tok_rows)
    scalar_flow = Flow(spread_cube_steps(scalars, groups, cols))
    moe_in_flow = Flow(reduce_steps(rows_parts, groups, cols))

    (grads,) = stage(
        live,
        [moe_in_flow, scalar_flow],
        [functools.partial(start_grads, each - 1, last)],
        slow=running(),
    )
    grad_flow(each - 1, grads)
    (branch_parts,) = stage(
        live,
        [moe_in_flow, scalar_flow],
        [lambda: expand_all(starts, where, pos_col, live["result"], groups, cols)],
    )
    branch_parts = branch_parts.reshape(groups * cols, tok_rows, width)
    moe_branch = lax.psum_scatter(branch_parts, cube, scatter_dimension=0, tiled=True)[0]
    stage(live, [moe_in_flow, scalar_flow], slow=running())
    while moe_in_flow.sends is not None or scalar_flow.sends is not None:
        stage(live, [moe_in_flow, scalar_flow])

    scalar_all = scalar_flow.finish().reshape(groups, cols, each + 1, groups, tok_rows)
    scalar_all = jnp.stack([scalar_all[place, :, :, place] for place in range(groups)])
    by_expert = jnp.stack(
        [
            ((lo ^ (number // each % groups)) * cols + (col ^ (number // (each * groups)))) * each
            + number % each
            for number in range(EXPERTS)
        ]
    )
    gate_cot = jnp.take(scalar_all[:, :, :each].reshape(EXPERTS, tok_rows), by_expert, axis=0)
    my_gates, my_logits = gates[0], all_logits[0]
    logit_cot = my_gates * (gate_cot - jnp.sum(my_gates * gate_cot, axis=0, keepdims=True))
    inner = jnp.sum(scalar_all[:, :, each], axis=(0, 1)) + jnp.sum(logit_cot * my_logits, axis=0)
    scaled_logit = (logit_cot * moe_inverse[0][None, :]).astype(BF16)
    logit_cot = logit_cot.astype(BF16)
    my_inverse = moe_inverse[0][:, None]

    back = moe_in_flow.finish() + my_inverse * dot_of(logit_cot, router_rows, 0, 0)
    middle_cot = (
        out_cot.astype(F32)
        + back * moe_gain
        - middle * (my_inverse * my_inverse * (inner[:, None] / D))
    )
    cot_flow = Flow(spread_steps(middle_cot.astype(BF16), "col", col_bits))
    router_part, moe_gain_part = stage(
        live,
        [cot_flow],
        [
            lambda: dot_of(scaled_logit, scaled_rows, 1, 0),
            lambda: jnp.sum(back * middle, axis=0)[None],
        ],
        slow=running(),
    )
    cot_blocks = cot_flow.finish()

    def out_weight_grad():
        grad = jnp.zeros((D, width), F32)
        mixture = jnp.concatenate([each[0] for each in attended], axis=0)
        for place, block in enumerate(cot_blocks):
            piece = dot_of(block, mixture, 0, 0)
            grad = lax.dynamic_update_slice_in_dim(grad, piece, (col ^ place) * width, 0)
        return grad.astype(BF16)

    def row_sum(values):
        return lax.psum_scatter(values, rows_axes, scatter_dimension=0, tiled=True).astype(F32)

    out_sum = row_sum(out_weight_grad())

    def attend_back(s):
        rows = seq_rows[s]
        cots = jnp.concatenate([block[rows] for block in cot_blocks], axis=1)
        mixture_cot = dot_of(cots, out_rel, 1, 0).astype(BF16)
        *cots, query_part, key_part, token_inner = attend_backward(
            s,
            lengths[s : s + 1],
            attended[s][1:],
            mixture_cot,
            live["qkv"],
            tables,
            query_scale,
            key_scale,
            heads,
        )
        cots = jnp.concatenate(cots, axis=1)
        return cots, query_part, key_part, token_inner[:, 0]

    qkv_rel = jnp.concatenate(
        [
            lax.dynamic_slice_in_dim(live["qkv_full"], (col ^ place) * width, width, 0)
            for place in range(cols)
        ],
        axis=0,
    )
    live["moe_branch"] = moe_branch
    done = stage(
        live,
        running(),
        [functools.partial(attend_back, s) for s in range(seqs)],
    )
    qkv_cot = jnp.concatenate([each[0] for each in done], axis=0)
    token_inner = jnp.concatenate([each[3] for each in done], axis=0)
    inner_flow = Flow(total_steps(token_inner, "col", bits_of(cols)))
    weight_sum = row_sum(dot_of(live["normed_attn"], qkv_cot, 0, 0).astype(BF16))
    partial = dot_of(qkv_cot, qkv_rel, 1, 1)
    backs = [partial[:, n * width : (n + 1) * width] for n in range(cols)]
    attn_gain_parts = [
        jnp.sum(part * (block.astype(F32) * attn_inverse), axis=0)[None]
        for part, block in zip(backs, hidden_blocks)
    ]
    attn_flow = Flow(col_reduce_steps(backs, cols))

    def widen(blocks):
        full = jnp.zeros((blocks[0].shape[0], D), F32)
        for place, block in enumerate(blocks):
            full = lax.dynamic_update_slice_in_dim(full, block, (col ^ place) * width, 1)
        return full

    head_parts = jnp.concatenate([sum(each[1] for each in done), sum(each[2] for each in done)], 1)
    small = jnp.concatenate(
        [
            widen([router_part]),
            widen([moe_gain_part]),
            widen(attn_gain_parts),
            jnp.pad(head_parts, ((0, 0), (0, D - 2 * HD))),
        ],
        axis=0,
    )

    def total_everywhere(values):
        for axis, bit in [("col", bit) for bit in bits_of(cols)] + row_bits:
            (got,) = yield [(values, axis, bit)]
            values = values + got
        return values

    small_flow = Flow(total_everywhere(small))
    flows = [attn_flow, inner_flow, small_flow] + running()
    while any(flow.sends is not None for flow in flows):
        stage(live, flows)

    input_grad = (
        middle_cot
        + attn_inverse * (attn_flow.finish() * attn_gain)
        - hidden * (attn_inverse * attn_inverse * (inner_flow.finish()[:, None] / D))
    )
    output = (middle + live["moe_branch"].astype(F32)).astype(BF16)
    gate_grad, up_grad, down_grad = unpack_grads(
        where,
        [grad_flows[expert, far].finish() for far in range(groups) for expert in range(each)],
        each,
    )
    small = small_flow.finish()
    own = lax.dynamic_slice_in_dim(small, col * width, width, 1)
    router_grad = lax.dynamic_slice_in_dim(small[:EXPERTS], row * depth, depth, 1).T
    return (
        output,
        input_grad,
        own[EXPERTS + 1],
        small[EXPERTS + 2, :HD],
        small[EXPERTS + 2, HD : 2 * HD],
        weight_sum[:, :width],
        weight_sum[:, width : 2 * width],
        weight_sum[:, 2 * width : 3 * width],
        out_sum.T,
        own[EXPERTS],
        router_grad,
        gate_grad,
        up_grad,
        down_grad,
    )


def solution(mesh):
    row_count, col_count = mesh.shape["row"], mesh.shape["col"]
    groups = 2
    between = EXPERTS // col_count // groups
    shape = (row_count // (groups * between), groups, between, col_count)
    inner = Mesh(mesh.devices.reshape(shape), ("hi", "lo", "mid", "col"))
    row = ("hi", "lo", "mid")
    return jax.shard_map(
        per_device,
        mesh=inner,
        in_specs=(
            P(row, "col"),
            P(row),
            P(row, None),
            P("col"),
            P(),
            P(),
            P(row, "col"),
            P(row, "col"),
            P(row, "col"),
            P("col", row),
            P("col"),
            P(row, None),
            P("col", row, None),
            P("col", row, None),
            P("col", None, row),
            P(row, "col"),
        ),
        out_specs=(
            P(row, "col"),
            P(row, "col"),
            P("col"),
            P(),
            P(),
            P(row, "col"),
            P(row, "col"),
            P(row, "col"),
            P("col", row),
            P("col"),
            P(row, None),
            P("col", row, None),
            P("col", row, None),
            P("col", None, row),
        ),
        check_vma=False,
    )
```

```python
import functools
import math

import jax
import jax.numpy as jnp
from jax import lax
from jax.experimental import pallas as pl
from jax.experimental.pallas import tpu as pltpu
from jax.sharding import Mesh, PartitionSpec as P

D = 2048
HD = 128
EXPERTS = 16
SEQ_LEN = 1024
CAP = 1152

BLOCK = 128
WINDOW = 144
EDGE = 16
TILE = 384
COST_SHARE = 50
EXPERT_WIDE, EXPERT_UNROLL = 512, 2
GRAD_WIDE, GRAD_UNROLL = 512, 1

epsilon = 1e-06
rope_base = 10000.0
masked_score = -1e30

F32 = jnp.float32
BF16 = jnp.bfloat16
ANY = pl.ANY
VMEM_LIMIT = 56 * 1024 * 1024


def dot_of(a, b, da, db):
    return lax.dot_general(a, b, (((da,), (db,)), ((), ())), preferred_element_type=F32)


def params(*semantics):
    return pltpu.CompilerParams(
        vmem_limit_bytes=VMEM_LIMIT, dimension_semantics=semantics or None
    )


def cost(flops, bytes_accessed, transcendentals=0):
    return pl.CostEstimate(
        flops=int(flops) // COST_SHARE,
        bytes_accessed=int(bytes_accessed) // COST_SHARE,
        transcendentals=int(transcendentals) // COST_SHARE,
    )


def turn(values, cosine, sine):
    return values * cosine + pltpu.roll(values, HD // 2, 1) * sine


def attend_forward_kernel(
    live_ref, q_ref, k_ref, v_ref, cos_ref, sin_ref, qg_ref, kg_ref, mix_ref, ql_ref, kl_ref, vl_ref
):
    live = live_ref[0]
    cosine = cos_ref[...]
    sine = sin_ref[...]

    def normed(values, gain):
        inverse = lax.rsqrt(jnp.mean(values * values, axis=1, keepdims=True) + epsilon)
        return turn(values * inverse * gain, cosine, sine).astype(BF16)

    ql_ref[...] = normed(q_ref[...], qg_ref[...])
    kl_ref[...] = normed(k_ref[...], kg_ref[...])
    vl_ref[...] = v_ref[...].astype(BF16)
    keys = kl_ref[...]
    values = vl_ref[...]
    rows = 256
    place = lax.broadcasted_iota(jnp.int32, (rows, SEQ_LEN), 1)
    for part in range(SEQ_LEN // rows):
        here = pl.ds(part * rows, rows)
        scores = dot_of(ql_ref[here, :], keys, 1, 1) * (1.0 / math.sqrt(HD))
        scores = jnp.where(place < live, scores, masked_score)
        top = jnp.max(scores, axis=1, keepdims=True)
        shifted = jnp.exp(scores - top)
        total = jnp.sum(shifted, axis=1, keepdims=True)
        probs = (shifted * (1.0 / total)).astype(BF16)
        mix_ref[here, :] = dot_of(probs, values, 1, 0).astype(BF16)


def attend_forward(seq, live, qkv, tables, query_gain, key_gain, heads):
    width = heads * HD

    def pick(offset):
        return pl.BlockSpec((SEQ_LEN, HD), lambda h, live, o=offset: (seq, o + h))

    def whole(shape):
        return pl.BlockSpec(shape, lambda h, live: (0, 0))

    out = pl.BlockSpec((SEQ_LEN, HD), lambda h, live: (0, h))
    return pl.pallas_call(
        attend_forward_kernel,
        grid_spec=pltpu.PrefetchScalarGridSpec(
            num_scalar_prefetch=1,
            grid=(heads,),
            in_specs=[
                pick(0),
                pick(heads),
                pick(2 * heads),
                whole((SEQ_LEN, HD)),
                whole((SEQ_LEN, HD)),
                whole((1, HD)),
                whole((1, HD)),
            ],
            out_specs=[out] * 4,
        ),
        out_shape=[jax.ShapeDtypeStruct((SEQ_LEN, width), BF16)] * 4,
        compiler_params=params("arbitrary"),
        cost_estimate=cost(
            heads * 8 * SEQ_LEN * SEQ_LEN * HD, 20 * SEQ_LEN * width, heads * SEQ_LEN * SEQ_LEN
        ),
        name="attend_forward",
    )(live, qkv, qkv, qkv, tables[0], tables[1], query_gain, key_gain)


def attend_backward_kernel(
    live_ref,
    ql_ref,
    kl_ref,
    vl_ref,
    do_ref,
    q_ref,
    k_ref,
    cos_ref,
    sin_ref,
    qg_ref,
    kg_ref,
    qc_ref,
    kc_ref,
    vc_ref,
    qpart_ref,
    kpart_ref,
    inner_ref,
    dq_ref,
    dk_ref,
    dv_ref,
):
    head = pl.program_id(0)
    live = live_ref[0]
    scale = 1.0 / math.sqrt(HD)
    keys = kl_ref[...]
    values = vl_ref[...]
    rows = 256
    place = lax.broadcasted_iota(jnp.int32, (SEQ_LEN, rows), 0)
    for part in range(SEQ_LEN // rows):
        here = pl.ds(part * rows, rows)
        queries = ql_ref[here, :]
        incoming = do_ref[here, :]
        scores = dot_of(keys, queries, 1, 1) * scale
        scores = jnp.where(place < live, scores, masked_score)
        top = jnp.max(scores, axis=0, keepdims=True)
        shifted = jnp.exp(scores - top)
        total = jnp.sum(shifted, axis=0, keepdims=True)
        probs = shifted * (1.0 / total)
        dv = dot_of(probs.astype(BF16), incoming, 1, 0)
        probs_cot = dot_of(values, incoming, 1, 1)
        weighted = probs * probs_cot
        centre = jnp.sum(weighted, axis=0, keepdims=True)
        raw = ((weighted - probs * centre) * scale).astype(BF16)
        dk = dot_of(raw, queries, 1, 0)
        dq_ref[here, :] = dot_of(raw, keys, 0, 0)
        if part == 0:
            dv_ref[...] = dv
            dk_ref[...] = dk
        else:
            dv_ref[...] += dv
            dk_ref[...] += dk
    cosine = cos_ref[...]
    sine = -sin_ref[...]

    def back(values, gain, rotated_cot):
        incoming = turn(rotated_cot, cosine, sine)
        inverse = lax.rsqrt(jnp.mean(values * values, axis=1, keepdims=True) + epsilon)
        scaled = incoming * gain
        inner = jnp.mean(scaled * values, axis=1, keepdims=True)
        grad = inverse * scaled - values * (inverse * inverse * inverse * inner)
        part = jnp.sum(incoming * values * inverse, axis=0, keepdims=True)
        return grad.astype(BF16), part, jnp.sum(grad * values, axis=1, keepdims=True)

    qc_ref[...], qpart, inner = back(q_ref[...], qg_ref[...], dq_ref[...])
    kc_ref[...], kpart, key_inner = back(k_ref[...], kg_ref[...], dk_ref[...])
    vc_ref[...] = dv_ref[...].astype(BF16)
    inner += key_inner
    inner += jnp.sum(dv_ref[...] * values.astype(F32), axis=1, keepdims=True)

    @pl.when(head == 0)
    def _():
        qpart_ref[...] = qpart
        kpart_ref[...] = kpart
        inner_ref[...] = inner

    @pl.when(head > 0)
    def _():
        qpart_ref[...] += qpart
        kpart_ref[...] += kpart
        inner_ref[...] += inner


def attend_backward(seq, live, lows, mixture_cot, qkv, tables, query_gain, key_gain, heads):
    width = heads * HD
    block = pl.BlockSpec((SEQ_LEN, HD), lambda h, live: (0, h))

    def pick(offset):
        return pl.BlockSpec((SEQ_LEN, HD), lambda h, live, o=offset: (seq, o + h))

    def whole(shape):
        return pl.BlockSpec(shape, lambda h, live: (0, 0))

    return pl.pallas_call(
        attend_backward_kernel,
        grid_spec=pltpu.PrefetchScalarGridSpec(
            num_scalar_prefetch=1,
            grid=(heads,),
            in_specs=[block] * 4
            + [
                pick(0),
                pick(heads),
                whole((SEQ_LEN, HD)),
                whole((SEQ_LEN, HD)),
                whole((1, HD)),
                whole((1, HD)),
            ],
            out_specs=[block] * 3 + [whole((1, HD))] * 2 + [whole((SEQ_LEN, 1))],
            scratch_shapes=[pltpu.VMEM((SEQ_LEN, HD), F32)] * 3,
        ),
        out_shape=[jax.ShapeDtypeStruct((SEQ_LEN, width), BF16)] * 3
        + [jax.ShapeDtypeStruct((1, HD), F32)] * 2
        + [jax.ShapeDtypeStruct((SEQ_LEN, 1), F32)],
        compiler_params=params("arbitrary"),
        cost_estimate=cost(
            heads * 20 * SEQ_LEN * SEQ_LEN * HD, 24 * SEQ_LEN * width, heads * SEQ_LEN * SEQ_LEN
        ),
        name="attend_backward",
    )(live, *lows, mixture_cot, qkv, qkv, tables[0], tables[1], query_gain, key_gain)


def compact_kernel(start_ref, where_ref, pos_ref, source_ref, *outs):
    group, groups = pl.program_id(0), pl.num_programs(0)
    row_of = lax.broadcasted_iota(jnp.int32, (WINDOW, BLOCK), 0)
    for out in outs:
        out[...] = jnp.zeros_like(out)
    for number in range(source_ref.shape[1] // BLOCK):
        here = slice(number * BLOCK, (number + 1) * BLOCK)
        for expert, out in enumerate(outs):
            start = pl.multiple_of(start_ref[expert * groups + group, number], EDGE)
            place = pos_ref[expert, 0, :, here]
            choice = jnp.where(row_of + start == place, 1.0, 0.0).astype(BF16)
            rows = dot_of(choice, source_ref[0, here, :], 1, 0)
            out[pl.ds(start, WINDOW), :] += rows.astype(BF16)


def compact(starts, where, pos_row, source, groups, cols):
    tokens, width = source.shape[1:]
    count = pos_row.shape[0] // groups
    return pl.pallas_call(
        compact_kernel,
        grid_spec=pltpu.PrefetchScalarGridSpec(
            num_scalar_prefetch=2,
            grid=(groups, cols),
            in_specs=[
                pl.BlockSpec((count, 1, 1, tokens), lambda q, j, s, w: (0, q, 0, 0)),
                pl.BlockSpec(
                    (1, tokens, width), lambda q, j, s, w: ((w[0] ^ q) * cols + j, 0, 0)
                ),
            ],
            out_specs=[pl.BlockSpec((CAP, width), lambda q, j, s, w: (q, j))] * count,
        ),
        out_shape=[jax.ShapeDtypeStruct((groups * CAP, cols * width), BF16)] * count,
        compiler_params=params("arbitrary", "arbitrary"),
        cost_estimate=cost(
            count * groups * cols * 2 * tokens * WINDOW * width * 2,
            groups * cols * 2 * width * (tokens + count * CAP),
        ),
        name="compact",
    )(starts, where, pos_row.reshape(count, groups, 1, tokens), source)


def compact_scalars_kernel(start_ref, pos_ref, *refs):
    count = len(refs) // 2
    group = pl.program_id(0)
    row_of = lax.broadcasted_iota(jnp.int32, (WINDOW, BLOCK), 0)
    for number in range(count):
        refs[count + number][...] = jnp.zeros_like(refs[count + number])
    for number in range(pos_ref.shape[2] // BLOCK):
        start = pl.multiple_of(start_ref[group, number], EDGE)
        here = slice(number * BLOCK, (number + 1) * BLOCK)
        choice = row_of + start == pos_ref[0, :, here]
        for source, out in zip(refs[:count], refs[count:]):
            picked = jnp.sum(jnp.where(choice, source[0, :, here], 0.0), axis=1, keepdims=True)
            out[pl.ds(start, WINDOW), :] += picked


def compact_scalars(starts, pos_row, sources):
    groups, _, tokens = pos_row.shape
    block = pl.BlockSpec((1, 1, tokens), lambda q, s: (q, 0, 0))
    return pl.pallas_call(
        compact_scalars_kernel,
        grid_spec=pltpu.PrefetchScalarGridSpec(
            num_scalar_prefetch=1,
            grid=(groups,),
            in_specs=[block] * (1 + len(sources)),
            out_specs=[pl.BlockSpec((CAP, 1), lambda q, s: (q, 0))] * len(sources),
        ),
        out_shape=[jax.ShapeDtypeStruct((groups * CAP, 1), F32)] * len(sources),
        compiler_params=params("arbitrary"),
        cost_estimate=cost(0, 4 * groups * CAP * 128 * len(sources)),
        name="compact_scalars",
    )(starts, pos_row, *sources)


def expand_scalars_kernel(start_ref, pos_ref, *refs):
    count = len(refs) // 2
    group = pl.program_id(0)
    row_of = lax.broadcasted_iota(jnp.int32, (WINDOW, BLOCK), 0)
    for number in range(pos_ref.shape[2] // BLOCK):
        start = pl.multiple_of(start_ref[group, number], EDGE)
        here = slice(number * BLOCK, (number + 1) * BLOCK)
        choice = row_of + start == pos_ref[0, :, here]
        for source, out in zip(refs[:count], refs[count:]):
            held = source[pl.ds(start, WINDOW), :]
            out[0, :, here] = jnp.sum(jnp.where(choice, held, 0.0), axis=0, keepdims=True)


def expand_scalars(starts, pos_row, sources):
    groups, _, tokens = pos_row.shape
    block = pl.BlockSpec((1, 1, tokens), lambda q, s: (q, 0, 0))
    return pl.pallas_call(
        expand_scalars_kernel,
        grid_spec=pltpu.PrefetchScalarGridSpec(
            num_scalar_prefetch=1,
            grid=(groups,),
            in_specs=[block] + [pl.BlockSpec((CAP, 1), lambda q, s: (q, 0))] * len(sources),
            out_specs=[block] * len(sources),
        ),
        out_shape=[jax.ShapeDtypeStruct((groups, 1, tokens), F32)] * len(sources),
        compiler_params=params("arbitrary"),
        cost_estimate=cost(0, 4 * groups * CAP * 128 * len(sources)),
        name="expand_scalars",
    )(starts, pos_row, *sources)


def expand_kernel(sizes, count, start_ref, where_ref, pos_ref, *refs):
    group, groups = pl.program_id(0), pl.num_programs(0)
    sides = len(refs) // (count + len(sizes))
    sources, outs = refs[: count * sides], refs[count * sides :]
    column_of = lax.broadcasted_iota(jnp.int32, (BLOCK, WINDOW), 1)
    number = 0
    for part, size in enumerate(sizes):
        for step in range(size // BLOCK):
            totals = [None] * sides
            for expert in range(count):
                start = pl.multiple_of(start_ref[expert * groups + group, number], EDGE)
                place = pos_ref[expert, 0, number * BLOCK : (number + 1) * BLOCK, :]
                choice = jnp.where(column_of + start == place, 1.0, 0.0).astype(BF16)
                for side in range(sides):
                    held = sources[expert * sides + side][pl.ds(start, WINDOW), :]
                    rows = dot_of(choice, held, 1, 0)
                    totals[side] = rows if totals[side] is None else totals[side] + rows
            here = slice(step * BLOCK, (step + 1) * BLOCK)
            for side in range(sides):
                outs[part * sides + side][0, 0, here, :] = totals[side].astype(BF16)
            number += 1


def expand(starts, where, pos_col, sources, sizes, groups, cols):
    width = sources[0].shape[1] // cols
    tokens = sum(sizes)
    count = len(sources)

    def side(odd):
        return pl.BlockSpec((CAP, width), lambda q, j, s, w: (q, w[1] ^ (2 * j + odd)))

    outs = pl.pallas_call(
        functools.partial(expand_kernel, sizes, count),
        grid_spec=pltpu.PrefetchScalarGridSpec(
            num_scalar_prefetch=2,
            grid=(groups, cols // 2),
            in_specs=[pl.BlockSpec((count, 1, tokens, 1), lambda q, j, s, w: (0, q, 0, 0))]
            + [side(0), side(1)] * count,
            out_specs=[
                pl.BlockSpec((1, 1, size, width), lambda q, j, s, w: (q, j, 0, 0))
                for size in sizes
                for _ in range(2)
            ],
        ),
        out_shape=[
            jax.ShapeDtypeStruct((groups, cols // 2, size, width), BF16)
            for size in sizes
            for _ in range(2)
        ],
        compiler_params=params("arbitrary", "arbitrary"),
        cost_estimate=cost(
            4 * count * groups * cols * tokens * WINDOW * width,
            groups * cols * width * (2 * tokens + 2 * count * CAP),
        ),
        name="expand",
    )(
        starts,
        where,
        pos_col.reshape(count, groups, tokens, 1),
        *[source for source in sources for _ in range(2)],
    )
    return list(zip(outs[::2], outs[1::2]))


def expand_all(starts, where, pos_col, sources, groups, cols):
    width = sources[0].shape[1] // cols
    tokens = pos_col.shape[1]
    count = len(sources)
    return pl.pallas_call(
        functools.partial(expand_kernel, [tokens], count),
        grid_spec=pltpu.PrefetchScalarGridSpec(
            num_scalar_prefetch=2,
            grid=(groups, cols),
            in_specs=[pl.BlockSpec((count, 1, tokens, 1), lambda q, j, s, w: (0, q, 0, 0))]
            + [pl.BlockSpec((CAP, width), lambda q, j, s, w: (q, j))] * count,
            out_specs=pl.BlockSpec((1, 1, tokens, width), lambda q, j, s, w: (w[0] ^ q, j, 0, 0)),
        ),
        out_shape=jax.ShapeDtypeStruct((groups, cols, tokens, width), BF16),
        compiler_params=params("arbitrary", "arbitrary"),
        cost_estimate=cost(
            4 * count * groups * cols * tokens * WINDOW * width,
            groups * cols * width * (2 * tokens + 2 * count * CAP),
        ),
        name="expand_all",
    )(starts, where, pos_col.reshape(count, groups, tokens, 1), *sources)


def pack_kernel(where_ref, gate_ref, up_ref, down_ref, out_ref):
    hidden = gate_ref.shape[2]
    out_ref[0, :, :hidden] = gate_ref[0].astype(BF16)
    out_ref[0, :, hidden : 2 * hidden] = up_ref[0].astype(BF16)
    out_ref[0, :, 2 * hidden :] = down_ref[0].T.astype(BF16)


def pack_weights(where, gate, up, down, each):
    experts, depth, hidden = gate.shape

    def pick(shape):
        return pl.BlockSpec(shape, lambda q, w: ((w[0] ^ (q // each)) * each + q % each, 0, 0))

    return pl.pallas_call(
        pack_kernel,
        grid_spec=pltpu.PrefetchScalarGridSpec(
            num_scalar_prefetch=1,
            grid=(experts,),
            in_specs=[pick((1, depth, hidden)), pick((1, depth, hidden)), pick((1, hidden, depth))],
            out_specs=pl.BlockSpec((1, depth, 3 * hidden), lambda q, w: (q, 0, 0)),
        ),
        out_shape=jax.ShapeDtypeStruct((experts, depth, 3 * hidden), BF16),
        compiler_params=params("arbitrary"),
        cost_estimate=cost(0, 18 * experts * depth * hidden),
        name="pack_weights",
    )(where, gate, up, down)


def unpack_kernel(where_ref, *refs):
    sources, (gate_ref, up_ref, down_ref) = refs[:-3], refs[-3:]
    hidden = gate_ref.shape[2]
    for number, source in enumerate(sources):

        @pl.when(pl.program_id(0) == number)
        def _(source=source):
            gate_ref[0] = source[:, :hidden].astype(F32)
            up_ref[0] = source[:, hidden : 2 * hidden].astype(F32)
            down_ref[0] = source[:, 2 * hidden :].astype(F32).T


def unpack_grads(where, sources, each):
    count = len(sources)
    depth, wide = sources[0].shape
    hidden = wide // 3

    def pick(shape):
        return pl.BlockSpec(shape, lambda q, w: ((w[0] ^ (q // each)) * each + q % each, 0, 0))

    shapes = [(count, depth, hidden), (count, depth, hidden), (count, hidden, depth)]
    return pl.pallas_call(
        unpack_kernel,
        grid_spec=pltpu.PrefetchScalarGridSpec(
            num_scalar_prefetch=1,
            grid=(count,),
            in_specs=[pl.BlockSpec((depth, wide), lambda q, w: (0, 0))] * count,
            out_specs=[pick((1,) + shape[1:]) for shape in shapes],
        ),
        out_shape=[jax.ShapeDtypeStruct(shape, F32) for shape in shapes],
        compiler_params=params("arbitrary"),
        cost_estimate=cost(0, 18 * count * depth * hidden),
        name="unpack_grads",
    )(where, *sources)


def expert_kernel(count, hidden, row_ref, x_ref, m_ref, gate_ref, scale_ref, *refs):
    pieces = refs[:count]
    rows_ref, pre_ref, act_ref, cot_ref, inner_ref, result_ref, held, sems = refs[count:]
    depth = pieces[0].shape[0]

    @pl.when(pl.program_id(0) == 0)
    def _():
        copies = []
        for number, piece in enumerate(pieces):
            place = pl.ds(pl.multiple_of(row_ref[number] * depth, depth), depth)
            copies.append(pltpu.make_async_copy(piece, held.at[place, :], sems.at[number]))
        for copy in copies:
            copy.start()
        for copy in copies:
            copy.wait()

    gate = gate_ref[...]
    scale = scale_ref[...]
    wide = EXPERT_WIDE
    cot_ref[...] = jnp.zeros_like(cot_ref)
    inner_ref[...] = jnp.zeros_like(inner_ref)

    @pl.loop(0, hidden // wide, unroll=EXPERT_UNROLL)
    def _(step):
        first = pl.multiple_of(step * wide, wide)
        gate_pre = dot_of(x_ref[...], held[:, pl.ds(first, wide)], 1, 0) * scale
        up_pre = dot_of(x_ref[...], held[:, pl.ds(hidden + first, wide)], 1, 0) * scale
        back = dot_of(m_ref[...], held[:, pl.ds(2 * hidden + first, wide)], 1, 0)
        squash = 1.0 / (1.0 + jnp.exp(-gate_pre))
        silu = gate_pre * squash
        active = silu * up_pre
        cot_ref[...] += jnp.sum(active.astype(BF16).astype(F32) * back, axis=1, keepdims=True)
        act_ref[:, pl.ds(first, wide)] = (active * gate).astype(BF16)
        back = back * gate
        slope = squash * (1.0 + gate_pre * (1.0 - squash))
        gate_cot = back * up_pre * slope
        up_cot = back * silu
        inner_ref[...] += jnp.sum(gate_cot * gate_pre + up_cot * up_pre, axis=1, keepdims=True)
        pre_ref[:, pl.ds(first, wide)] = (gate_cot * scale).astype(BF16)
        pre_ref[:, pl.ds(hidden + first, wide)] = (up_cot * scale).astype(BF16)

    @pl.loop(0, held.shape[0] // wide, unroll=EXPERT_UNROLL)
    def _(step):
        first = pl.multiple_of(step * wide, wide)
        here = pl.ds(first, wide)
        rows_ref[:, here] = dot_of(pre_ref[...], held[here, : 2 * hidden], 1, 1).astype(BF16)
        result_ref[:, here] = dot_of(act_ref[...], held[here, 2 * hidden :], 1, 1).astype(BF16)


def expert_step(row_numbers, x, m, gate, scale, pieces):
    total, wide = x.shape
    hidden = pieces[0].shape[1] // 3
    count = len(pieces)

    def tile(columns):
        return pl.BlockSpec((TILE, columns), lambda i, r: (i, 0))

    return pl.pallas_call(
        functools.partial(expert_kernel, count, hidden),
        grid_spec=pltpu.PrefetchScalarGridSpec(
            num_scalar_prefetch=1,
            grid=(total // TILE,),
            in_specs=[tile(wide), tile(wide), tile(1), tile(1)]
            + [pl.BlockSpec(memory_space=ANY)] * count,
            out_specs=[tile(wide), tile(2 * hidden), tile(hidden), tile(1), tile(1), tile(wide)],
            scratch_shapes=[
                pltpu.VMEM((wide, 3 * hidden), BF16),
                pltpu.SemaphoreType.DMA((count,)),
            ],
        ),
        out_shape=[
            jax.ShapeDtypeStruct((total, wide), BF16),
            jax.ShapeDtypeStruct((total, 2 * hidden), BF16),
            jax.ShapeDtypeStruct((total, hidden), BF16),
            jax.ShapeDtypeStruct((total, 1), F32),
            jax.ShapeDtypeStruct((total, 1), F32),
            jax.ShapeDtypeStruct((total, wide), BF16),
        ],
        compiler_params=params("arbitrary"),
        cost_estimate=cost(
            2 * total * wide * hidden * 6, 2 * total * (4 * wide + 3 * hidden), total * hidden
        ),
        name="expert_step",
    )(row_numbers, x, m, gate, scale, *pieces)


def weight_grad_kernel(mids, place_ref, x_ref, m_ref, pre_ref, act_ref, out_ref, turned_ref):
    wide = GRAD_WIDE
    first = pre_ref.shape[1]
    depth = x_ref.shape[1] // mids
    turned_ref[0] = x_ref[...].T
    turned_ref[1] = m_ref[...].T
    mid = place_ref[place_ref.shape[0] - 1]

    def put(grad, here):
        for number in range(mids):
            block = grad[number * depth : (number + 1) * depth].astype(BF16)
            out_ref[0, number ^ mid, 0, :, here] = block

    @pl.loop(0, first // wide, unroll=GRAD_UNROLL)
    def _(step):
        here = pl.ds(pl.multiple_of(step * wide, wide), wide)
        put(dot_of(turned_ref[0], pre_ref[:, here], 1, 0), here)

    @pl.loop(0, act_ref.shape[1] // wide, unroll=GRAD_UNROLL)
    def _(step):
        here = pl.ds(pl.multiple_of(step * wide, wide), wide)
        there = pl.ds(pl.multiple_of(first + step * wide, wide), wide)
        put(dot_of(turned_ref[1], act_ref[:, here], 1, 0), there)


def weight_grads(places, x, m, pre, act, depth, groups, mids, high):
    total = x.shape[0]
    wide = pre.shape[1] + act.shape[1]

    def column(array):
        return pl.BlockSpec((total, mids * depth), lambda f, h, r: (0, r[f * high + h]))

    def whole(array):
        return pl.BlockSpec(array.shape, lambda f, h, r: (0, 0), pipeline_mode=pl.Buffered(1))

    return pl.pallas_call(
        functools.partial(weight_grad_kernel, mids),
        grid_spec=pltpu.PrefetchScalarGridSpec(
            num_scalar_prefetch=1,
            grid=(groups, high),
            in_specs=[column(x), column(m), whole(pre), whole(act)],
            out_specs=pl.BlockSpec(
                (1, mids, 1, depth, wide), lambda f, h, r: (f, 0, h, 0, 0)
            ),
            scratch_shapes=[pltpu.VMEM((2, mids * depth, total), BF16)],
        ),
        out_shape=jax.ShapeDtypeStruct((groups, mids, high, depth, wide), BF16),
        compiler_params=params("arbitrary", "arbitrary"),
        cost_estimate=cost(
            2 * total * depth * groups * mids * high * wide,
            2 * total * (2 * depth * groups * mids * high + wide),
        ),
        name="weight_grads",
    )(places, x, m, pre, act)


def bits_of(size):
    return [1 << n for n in range(size.bit_length() - 1)]


def swap(values, axis, bit):
    size = lax.axis_size(axis) if isinstance(axis, str) else math.prod(map(lax.axis_size, axis))
    return lax.ppermute(values, axis, [(n, n ^ bit) for n in range(size)])


class Flow:
    def __init__(self, steps):
        self.steps = steps
        self.result = None
        self.sends = next(steps)

    def advance(self, got):
        try:
            self.sends = self.steps.send(got)
        except StopIteration as stop:
            self.sends = None
            self.result = stop.value

    def step(self, count=1):
        for _ in range(count):
            if self.sends is not None:
                self.advance([swap(*send) for send in self.sends])
        return self

    def finish(self):
        while self.sends is not None:
            self.step()
        return self.result

    def holds(self):
        return self.result if self.sends is None else [send[0] for send in self.sends]

    def replace(self, arrays):
        if self.sends is None:
            self.result = arrays
        else:
            self.sends = [(array, *send[1:]) for array, send in zip(arrays, self.sends)]


def stage(live, flows=(), work=(), sync=()):
    flows = [flow for flow in flows if flow.sends is not None]
    got = [[swap(*send) for send in flow.sends] for flow in flows]
    done = [each() for each in work]
    held = [flow.holds() for flow in sync]
    got, done, held, kept = lax.optimization_barrier((got, done, held, dict(live)))
    live.update(kept)
    for flow, arrays in zip(flows, got):
        flow.advance(arrays)
    for flow, arrays in zip(sync, held):
        flow.replace(arrays)
    return done


def spread_steps(values, axis, bits):
    blocks = {0: values}
    for bit in bits:
        places = sorted(blocks)
        got = yield [(blocks[place], axis, bit) for place in places]
        blocks.update({place | bit: block for place, block in zip(places, got)})
    return [blocks[place] for place in sorted(blocks)]


def spread_rows_steps(values, row_bits, strides):
    held = values[None]
    places = [0]
    for axis, bit in row_bits:
        (got,) = yield [(held, axis, bit)]
        held = jnp.concatenate([held, got], axis=0)
        places += [place | (bit * strides[axis]) for place in places]
    return jnp.stack([held[places.index(place)] for place in range(len(places))])


def spread_cube_steps(values, groups, cols):
    held = values[None]
    for axis, bits in (("lo", bits_of(groups)), ("col", bits_of(cols))):
        for bit in bits:
            (got,) = yield [(held, axis, bit)]
            held = jnp.concatenate([held, got], axis=0)
    return jnp.swapaxes(held.reshape((cols, groups) + values.shape), 0, 1)


def col_reduce_steps(blocks, cols):
    held = dict(enumerate(blocks))
    for bit in bits_of(cols):
        away = [place for place in sorted(held) if place & bit]
        (got,) = yield [(jnp.stack([held[place].astype(BF16) for place in away]), "col", bit)]
        held = {
            place & ~bit: held[place & ~bit] + got[number].astype(F32)
            for number, place in enumerate(away)
        }
    return held[0]


def total_steps(values, axes):
    for axis in axes:
        size = math.prod(map(lax.axis_size, axis))
        got = yield [(values, axis, place) for place in range(1, size)]
        values = values + sum(got)
    return values


def row_reduce_steps(parts, row_bits):
    held = []
    for number, part in enumerate(parts):
        shape = (2,) * len(row_bits) + (part.shape[0] >> len(row_bits), part.shape[1])
        order = list(reversed(row_bits))
        if number % 2 and len(order) > 1:
            order[:2] = order[1::-1]
        held.append((part.reshape(shape), list(row_bits), order))
    for step in range(len(row_bits)):
        sends, rest = [], []
        for array, names, order in held:
            name = order[step]
            axis = names.index(name)
            mine = lax.axis_index(name[0]) // name[1] & 1
            away = lax.dynamic_index_in_dim(array, 1 - mine, axis, False)
            kept = lax.dynamic_index_in_dim(array, mine, axis, False)
            sends.append((away.astype(BF16), *name))
            rest.append((kept, [other for other in names if other != name], order))
        got = yield sends
        held = [
            (kept.astype(F32) + more.astype(F32), names, order)
            for (kept, names, order), more in zip(rest, got)
        ]
    return jnp.concatenate([array for array, _, _ in held], axis=1)


def links_of(groups, cols):
    return [("col", bit) for bit in bits_of(cols)[1:]] + [("lo", bit) for bit in bits_of(groups)]


def turned(links, number):
    number %= len(links)
    return links[number:] + links[:number]


def reduce_steps(parts, groups, cols):
    links = links_of(groups, cols)
    got = yield [(away, "col", 1) for _, away in parts]
    held = []
    for number, (keep, _) in enumerate(parts):
        shape = (2,) * len(links) + keep.shape[2:]
        names = [("lo", bit) for bit in reversed(bits_of(groups))]
        names += [("col", bit) for bit in reversed(bits_of(cols)[1:])]
        held.append((keep.reshape(shape), got[number].reshape(shape), names))
    for step in range(len(links)):
        sends, rest = [], []
        for number, (keep, more, names) in enumerate(held):
            link = turned(links, number)[step]
            axis = names.index(link)

            def half(place):
                total = lax.index_in_dim(keep, place, axis, False).astype(F32)
                return total + lax.index_in_dim(more, place, axis, False).astype(F32)

            sends.append((half(1).astype(BF16), *link))
            kept = half(0)
            rest.append(
                (
                    kept if step + 1 == len(links) else kept.astype(BF16),
                    [name for name in names if name != link],
                )
            )
        got = yield sends
        held = [(keep, more, names) for (keep, names), more in zip(rest, got)]
    return jnp.concatenate([keep.astype(F32) + more.astype(F32) for keep, more, _ in held], axis=0)


def part_sizes(tokens, count):
    whole = tokens // BLOCK
    return [BLOCK * ((whole + count - 1 - n) // count) for n in range(count)]


def expert_weight_steps(piece, far, bits):
    if far:
        (piece,) = yield [(piece, "lo", far)]
    held = {(): piece}
    fresh = [()]
    while True:
        ways = [
            (place, number)
            for place in fresh
            for number in range(place[-1] + 1 if place else 0, len(bits))
        ]
        if not ways:
            return held
        got = yield [(held[place], *bits[number]) for place, number in ways]
        fresh = [place + (number,) for place, number in ways]
        held.update(zip(fresh, got))


def expert_grad_steps(blocks, far, bits):
    for number in reversed(range(len(bits))):
        half = blocks.shape[0] // 2
        (got,) = yield [(blocks[half:], *bits[number])]
        blocks = blocks[:half].astype(F32) + got.astype(F32)
        if number or far:
            blocks = blocks.astype(BF16)
    total = blocks[0]
    if far:
        (total,) = yield [(total, "lo", far)]
    return total


def per_device(
    hidden_in,
    lengths,
    routes,
    attn_gain,
    query_gain,
    key_gain,
    query_weight,
    key_weight,
    value_weight,
    out_weight,
    moe_gain,
    router,
    gate_weight,
    up_weight,
    down_weight,
    cotangent,
):
    tok_rows, width = hidden_in.shape
    cols = lax.axis_size("col")
    groups = lax.axis_size("lo")
    high = lax.axis_size("hi")
    mids = lax.axis_size("mid")
    col = lax.axis_index("col")
    lo = lax.axis_index("lo")
    hi = lax.axis_index("hi")
    mid = lax.axis_index("mid")
    row = (hi * groups + lo) * mids + mid
    where = jnp.stack([lo, col])
    heads = width // HD
    seqs = lengths.shape[0]
    depth = gate_weight.shape[1]
    each = gate_weight.shape[0] // groups
    cube = ("lo", "col")
    rows_axes = ("hi", "lo", "mid")
    strides = {"hi": groups * mids, "lo": mids, "mid": 1}
    seq_rows = [slice(s * SEQ_LEN, (s + 1) * SEQ_LEN) for s in range(seqs)]
    links = links_of(groups, cols)
    col_bits = list(reversed(bits_of(cols)))
    hi_bits = [("hi", bit) for bit in bits_of(high)]
    mid_bits = [("mid", bit) for bit in bits_of(mids)]
    row_bits = hi_bits + [("lo", bit) for bit in bits_of(groups)] + mid_bits
    far_bits = hi_bits + mid_bits
    far_first_bits = hi_bits[::-1] + [("lo", bit) for bit in bits_of(groups)][::-1]
    far_first_bits += mid_bits[::-1]
    live = {}

    def row_of_set(place, far):
        other = row ^ (far * mids)
        for number in place:
            axis, bit = far_bits[number]
            other = other ^ (bit * strides[axis])
        return other

    hidden_flow = Flow(spread_steps(hidden_in, "col", col_bits))
    gain_flow = Flow(spread_steps(attn_gain, "col", col_bits))
    routes_flow = Flow(spread_steps(routes.T, "lo", bits_of(groups)))
    router_flow = Flow(spread_rows_steps(router.T.astype(BF16), row_bits, strides))
    out_flow = Flow(spread_rows_steps(out_weight.T.astype(BF16), row_bits, strides))
    qkv_local = jnp.concatenate([query_weight, key_weight, value_weight], axis=1).astype(BF16)
    qkv_full = lax.all_gather(qkv_local, rows_axes, axis=0, tiled=True)
    live_key = jnp.arange(SEQ_LEN)[None, :] < lengths[:, None]
    out_cot = jnp.where(live_key.reshape(tok_rows, 1), cotangent, jnp.zeros_like(cotangent))
    packed = pack_weights(where, gate_weight, up_weight, down_weight, each)
    units = [(expert, far) for expert in range(each) for far in range(groups)]
    live["packed"] = packed

    def rotary_tables():
        places = jnp.arange(SEQ_LEN).astype(F32)
        powers = jnp.arange(HD // 2).astype(F32) * (2.0 / HD)
        angles = places[:, None] * jnp.exp(-powers * math.log(rope_base))[None, :]
        cosine, sine = jnp.cos(angles), jnp.sin(angles)
        return (
            jnp.concatenate([cosine, cosine], axis=1),
            jnp.concatenate([-sine, sine], axis=1),
        )

    live["out_cot"] = out_cot
    (tables,) = stage(
        live,
        [hidden_flow, gain_flow, routes_flow, router_flow, out_flow],
        [rotary_tables],
    )

    hidden = hidden_in.astype(F32)

    def norm_attn():
        blocks = hidden_flow.finish()
        gains = gain_flow.finish()
        square = sum(jnp.sum(jnp.square(block.astype(F32)), axis=1) for block in blocks)
        inverse = lax.rsqrt(square / D + epsilon)[:, None]
        normed = jnp.zeros((tok_rows, D), BF16)
        for place, (block, gain) in enumerate(zip(blocks, gains)):
            piece = (block.astype(F32) * inverse * gain).astype(BF16)
            normed = lax.dynamic_update_slice_in_dim(normed, piece, (col ^ place) * width, 1)
        return normed, inverse

    def routing():
        rel = jnp.stack(routes_flow.finish())
        named = jnp.any(rel[:, :, None, :] == jnp.arange(EXPERTS)[None, None, :, None], axis=1)
        first = (col * groups + lo) * each
        member = lax.dynamic_slice_in_dim(named, first, each, 1)
        member = jnp.swapaxes(member, 0, 1).reshape(each * groups, tok_rows)
        count = member.astype(jnp.int32)
        rank = jnp.cumsum(count, axis=1) - count
        pos = jnp.where(member, rank, -(1 << 20))
        starts = jnp.minimum(rank[:, ::BLOCK] // EDGE * EDGE, CAP - WINDOW)
        return named, starts, pos[:, None, :], pos[:, :, None]

    live["qkv_full"] = qkv_full
    ((live["normed_attn"], attn_inverse),) = stage(live, [router_flow, out_flow], [norm_attn])
    weight_flows = {}

    def start_weights(expert):
        for far in range(groups):
            weight_flows[expert, far] = Flow(
                expert_weight_steps(live["packed"][far * each + expert], far, far_bits)
            )

    start_weights(0)
    hidden_blocks = hidden_flow.result
    query_scale, key_scale = query_gain[None, :], key_gain[None, :]

    def attend(s):
        return attend_forward(
            s, lengths[s : s + 1], live["qkv"], tables, query_scale, key_scale, heads
        )

    def project_and_attend():
        live["qkv"] = dot_of(live["normed_attn"], live["qkv_full"], 1, 0)
        return attend(0)

    firsts = [weight_flows[0, far] for far in range(1, groups)]
    (first_seq,) = stage(live, firsts + [router_flow], [project_and_attend])
    moe_cot = lax.all_gather(live["out_cot"], cube, axis=0, tiled=False)
    for expert in range(1, each):
        start_weights(expert)
    seconds = [weight_flows[unit] for unit in units if unit[0] == 1]
    named, starts, pos_row, pos_col = routing()

    span = width // depth

    def col_rows(blocks, place, axis):
        first = (col ^ place) * span
        return jnp.concatenate(
            [
                lax.dynamic_index_in_dim(blocks, (first + n) ^ row, 0, False)
                for n in range(span)
            ],
            axis=axis,
        )

    out_spread = out_flow.finish()
    out_rel = jnp.concatenate([col_rows(out_spread, place, 0) for place in range(cols)], axis=0)
    router_rows = col_rows(router_flow.finish(), 0, 1)

    def branch(mixture):
        partial = dot_of(mixture, out_rel, 1, 1)
        blocks = [partial[:, n * width : (n + 1) * width] for n in range(cols)]
        return Flow(col_reduce_steps(blocks, cols)).finish()

    def attend_rest():
        outs = [first_seq]
        sums = [branch(first_seq[0])]
        for s in range(1, seqs):
            outs.append(attend(s))
            sums.append(branch(outs[s][0]))
        return outs, sums

    ((attended, branches),) = stage(live, [weight_flows[0, 0]] + seconds[1:], [attend_rest])
    middle = hidden + jnp.concatenate(branches, axis=0)
    live["scaled_rows"] = (middle * moe_gain).astype(BF16)
    scaled_rows = live["scaled_rows"]
    moe_in = lax.all_gather(scaled_rows, cube, axis=0, tiled=False)
    square = jnp.sum(middle * middle, axis=1)[None, :]
    stat = jnp.concatenate([dot_of(router_rows, scaled_rows, 1, 1), square], axis=0)
    stat_flow = Flow(spread_cube_steps(stat, groups, cols))
    stage(live, [stat_flow], sync=[weight_flows[0, 0]] + firsts + seconds)
    (live["cot_rows"],) = stage(
        live,
        [stat_flow, weight_flows[0, 0]] + firsts,
        [lambda: compact(starts, where, pos_row, moe_cot, groups, cols)],
    )
    for flow in seconds[:1]:
        flow.step()
    stage(live, [stat_flow] + firsts)
    stat = stat_flow.finish()

    stat = jnp.sum(stat, axis=1)
    moe_inverse = lax.rsqrt(stat[:, EXPERTS] / D + epsilon)
    all_logits = stat[:, :EXPERTS] * moe_inverse[:, None, :]
    logits = jnp.where(named, all_logits, masked_score)
    shifted = jnp.where(named, jnp.exp(logits - jnp.max(logits, axis=1, keepdims=True)), 0.0)
    gates = shifted / jnp.sum(shifted, axis=1, keepdims=True)
    own_gate = lax.dynamic_slice_in_dim(gates, (col * groups + lo) * each, each, 1)
    own_gate = jnp.swapaxes(own_gate, 0, 1).reshape(each * groups, 1, tok_rows)
    row_gate, row_scale = compact_scalars(
        starts, pos_row, (own_gate, jnp.tile(moe_inverse, (each, 1))[:, None, :])
    )
    total_rows = groups * CAP

    live["moe_rows"] = compact(starts, where, pos_row, moe_in, groups, cols)

    def run_expert(expert):
        pieces, row_numbers = [], []
        for far in range(groups):
            for place, piece in weight_flows[expert, far].finish().items():
                pieces.append(piece)
                row_numbers.append(row_of_set(place, far))
        here = slice(expert * total_rows, (expert + 1) * total_rows)
        return expert_step(
            jnp.stack(row_numbers),
            live["moe_rows"][expert],
            live["cot_rows"][expert],
            row_gate[here],
            row_scale[here],
            pieces,
        )

    grad_places = jnp.stack(
        [
            (hi ^ above) * groups + (lo ^ far)
            for far in reversed(range(groups))
            for above in range(high)
        ]
        + [mid]
    )
    grad_flows = {}

    def start_grads(expert, outs):
        grads = weight_grads(
            grad_places,
            live["moe_rows"][expert],
            live["cot_rows"][expert],
            outs[1],
            outs[2],
            depth,
            groups,
            mids,
            high,
        )
        return grads.reshape((groups, mids * high) + grads.shape[3:])

    def grad_flow(expert, grads):
        for number, far in enumerate(reversed(range(groups))):
            grad_flows[expert, far] = Flow(expert_grad_steps(grads[number], far, far_bits))

    def running():
        return list(grad_flows.values())

    ran = []
    for expert in range(each):
        others = [flow for (number, _), flow in weight_flows.items() if number > expert]
        (outs,) = stage(
            live,
            others[1:] + running()[:1],
            [functools.partial(run_expert, expert)],
            sync=others[:1],
        )
        ran.append(outs)
        if expert + 1 < each:
            (grads,) = stage(live, others, [functools.partial(start_grads, expert, outs)])
            grad_flow(expert, grads)
    early = running()
    for flow in early:
        flow.step()
    live["result"] = [outs[5] for outs in ran]
    last = ran[-1]
    gate_cot = jnp.concatenate([outs[3] for outs in ran], axis=0)
    row_inner = jnp.concatenate([outs[4] for outs in ran], axis=0)
    sizes = part_sizes(tok_rows, len(links))
    live["scalars"] = (gate_cot, row_inner)
    (rows_parts,) = stage(
        live,
        [],
        [
            lambda: expand(
                starts, where, pos_col, [outs[0] for outs in ran], sizes, groups, cols
            )
        ],
    )
    gate_cot, row_inner = expand_scalars(starts, pos_row, live.pop("scalars"))
    gate_cot = gate_cot.reshape(each, groups, tok_rows)
    row_inner = jnp.sum(row_inner.reshape(each, groups, tok_rows), axis=0)[None]
    scalars = jnp.concatenate([gate_cot, row_inner], axis=0)
    scalars = scalars.reshape((each + 1) * groups, tok_rows)
    scalar_flow = Flow(spread_cube_steps(scalars, groups, cols))
    moe_in_flow = Flow(reduce_steps(rows_parts, groups, cols))
    (grads,) = stage(
        live,
        [moe_in_flow, scalar_flow],
        [functools.partial(start_grads, each - 1, last)],
        sync=early,
    )
    grad_flow(each - 1, grads)
    late = running()[len(early) :]
    (branch_parts,) = stage(
        live,
        [moe_in_flow, scalar_flow] + late[:1],
        [lambda: expand_all(starts, where, pos_col, live["result"], groups, cols)],
    )
    live["moe_branch"] = branch_parts.reshape(groups * cols, tok_rows, width)
    while moe_in_flow.sends is not None:
        stage(live, [moe_in_flow, scalar_flow], sync=early + late)
    scalar_all = scalar_flow.finish().reshape(groups, cols, each + 1, groups, tok_rows)
    scalar_all = jnp.stack([scalar_all[place, :, :, place] for place in range(groups)])
    by_expert = jnp.stack(
        [
            ((lo ^ (number // each % groups)) * cols + (col ^ (number // (each * groups)))) * each
            + number % each
            for number in range(EXPERTS)
        ]
    )
    gate_cot = jnp.take(scalar_all[:, :, :each].reshape(EXPERTS, tok_rows), by_expert, axis=0)
    my_gates, my_logits = gates[0], all_logits[0]
    logit_cot = my_gates * (gate_cot - jnp.sum(my_gates * gate_cot, axis=0, keepdims=True))
    inner = jnp.sum(scalar_all[:, :, each], axis=(0, 1)) + jnp.sum(logit_cot * my_logits, axis=0)
    scaled_logit = (logit_cot * moe_inverse[0][None, :]).astype(BF16)
    logit_cot = logit_cot.astype(BF16)
    my_inverse = moe_inverse[0][:, None]

    back = moe_in_flow.finish() + my_inverse * dot_of(logit_cot, router_rows, 0, 0)
    middle_cot = (
        out_cot.astype(F32)
        + back * moe_gain
        - middle * (my_inverse * my_inverse * (inner[:, None] / D))
    )
    cot_flow = Flow(spread_steps(middle_cot.astype(BF16), "col", col_bits))
    router_part, moe_gain_part = stage(
        live,
        [cot_flow] + early[1:] + late[1:],
        [
            lambda: dot_of(scaled_logit, scaled_rows, 1, 0),
            lambda: jnp.sum(back * middle, axis=0)[None],
        ],
    )
    cot_blocks = cot_flow.finish()
    moe_branch = lax.psum_scatter(
        live.pop("moe_branch"), cube, scatter_dimension=0, tiled=True
    )[0]

    def out_weight_grad():
        grad = jnp.zeros((D, width), F32)
        mixture = jnp.concatenate([each[0] for each in attended], axis=0)
        for place, block in enumerate(cot_blocks):
            piece = dot_of(block, mixture, 0, 0)
            grad = lax.dynamic_update_slice_in_dim(grad, piece, (col ^ place) * width, 0)
        return grad.astype(BF16)

    def row_sum(values):
        return lax.psum_scatter(values, rows_axes, scatter_dimension=0, tiled=True).astype(F32)

    out_sum = row_sum(out_weight_grad())

    def attend_back(s):
        rows = seq_rows[s]
        cots = jnp.concatenate([block[rows] for block in cot_blocks], axis=1)
        mixture_cot = dot_of(cots, out_rel, 1, 0).astype(BF16)
        *cots, query_part, key_part, token_inner = attend_backward(
            s,
            lengths[s : s + 1],
            attended[s][1:],
            mixture_cot,
            live["qkv"],
            tables,
            query_scale,
            key_scale,
            heads,
        )
        cots = jnp.concatenate(cots, axis=1)
        return cots, query_part, key_part, token_inner[:, 0]

    qkv_rel = jnp.concatenate(
        [
            lax.dynamic_slice_in_dim(live["qkv_full"], (col ^ place) * width, width, 0)
            for place in range(cols)
        ],
        axis=0,
    )
    done = stage(
        live,
        early[:1] + late[:1],
        [functools.partial(attend_back, s) for s in range(seqs)],
    )
    for flow in early + late:
        flow.finish()
    qkv_cot = jnp.concatenate([each[0] for each in done], axis=0)
    token_inner = jnp.concatenate([each[3] for each in done], axis=0)
    inner_flow = Flow(total_steps(token_inner, [("col",)]))
    live["qkv_cot"] = qkv_cot
    half = qkv_cot.shape[1] // 2
    grad_parts = stage(
        live,
        [],
        [
            lambda n=n: dot_of(
                live["normed_attn"], qkv_cot[:, n * half : (n + 1) * half], 0, 0
            ).astype(BF16)
            for n in range(2)
        ],
    )
    qkv_flow = Flow(row_reduce_steps(grad_parts, far_first_bits))
    (partial,) = stage(live, [qkv_flow], [lambda: dot_of(live["qkv_cot"], qkv_rel, 1, 1)])
    backs = [partial[:, n * width : (n + 1) * width] for n in range(cols)]
    attn_gain_parts = [
        jnp.sum(part * (block.astype(F32) * attn_inverse), axis=0)[None]
        for part, block in zip(backs, hidden_blocks)
    ]
    attn_flow = Flow(col_reduce_steps(backs, cols))

    def widen(blocks):
        full = jnp.zeros((blocks[0].shape[0], D), F32)
        for place, block in enumerate(blocks):
            full = lax.dynamic_update_slice_in_dim(full, block, (col ^ place) * width, 1)
        return full

    head_parts = jnp.concatenate([sum(each[1] for each in done), sum(each[2] for each in done)], 1)
    small = jnp.concatenate(
        [
            widen([router_part]),
            widen([moe_gain_part]),
            widen(attn_gain_parts),
            jnp.pad(head_parts, ((0, 0), (0, D - 2 * HD))),
        ],
        axis=0,
    )

    small_flow = Flow(total_steps(small, [("lo", "mid"), ("hi",), ("col",)]))
    flows = [attn_flow, inner_flow, small_flow, qkv_flow]
    stage(live, flows)
    live["moe_branch"] = moe_branch
    while any(flow.sends is not None for flow in flows):
        stage(live, flows)
    moe_branch = live["moe_branch"]
    weight_sum = qkv_flow.finish()

    input_grad = (
        middle_cot
        + attn_inverse * (attn_flow.finish() * attn_gain)
        - hidden * (attn_inverse * attn_inverse * (inner_flow.finish()[:, None] / D))
    )
    output = (middle + moe_branch.astype(F32)).astype(BF16)
    gate_grad, up_grad, down_grad = unpack_grads(
        where,
        [grad_flows[expert, far].finish() for far in range(groups) for expert in range(each)],
        each,
    )
    small = small_flow.finish()
    own = lax.dynamic_slice_in_dim(small, col * width, width, 1)
    router_grad = lax.dynamic_slice_in_dim(small[:EXPERTS], row * depth, depth, 1).T
    return (
        output,
        input_grad,
        own[EXPERTS + 1],
        small[EXPERTS + 2, :HD],
        small[EXPERTS + 2, HD : 2 * HD],
        weight_sum[:, :width],
        weight_sum[:, width : 2 * width],
        weight_sum[:, 2 * width : 3 * width],
        out_sum.T,
        own[EXPERTS],
        router_grad,
        gate_grad,
        up_grad,
        down_grad,
    )


def solution(mesh):
    row_count, col_count = mesh.shape["row"], mesh.shape["col"]
    groups = 2
    between = EXPERTS // col_count // groups
    shape = (row_count // (groups * between), groups, between, col_count)
    inner = Mesh(mesh.devices.reshape(shape), ("hi", "lo", "mid", "col"))
    row = ("hi", "lo", "mid")
    return jax.shard_map(
        per_device,
        mesh=inner,
        in_specs=(
            P(row, "col"),
            P(row),
            P(row, None),
            P("col"),
            P(),
            P(),
            P(row, "col"),
            P(row, "col"),
            P(row, "col"),
            P("col", row),
            P("col"),
            P(row, None),
            P("col", row, None),
            P("col", row, None),
            P("col", None, row),
            P(row, "col"),
        ),
        out_specs=(
            P(row, "col"),
            P(row, "col"),
            P("col"),
            P(),
            P(),
            P(row, "col"),
            P(row, "col"),
            P(row, "col"),
            P("col", row),
            P("col"),
            P(row, None),
            P("col", row, None),
            P("col", row, None),
            P("col", None, row),
        ),
        check_vma=False,
    )
```

```python
import functools
import math

import jax
import jax.numpy as jnp
from jax import lax
from jax.experimental import pallas as pl
from jax.experimental.pallas import tpu as pltpu
from jax.sharding import Mesh, PartitionSpec as P

D = 2048
HD = 128
EXPERTS = 16
SEQ_LEN = 1024
CAP = 1152

BLOCK = 128
WINDOW = 144
EDGE = 16
TILE = 384
COST_SHARE = 50
EXPERT_WIDE, EXPERT_UNROLL = 512, 2
GRAD_WIDE, GRAD_UNROLL = 512, 1

epsilon = 1e-06
rope_base = 10000.0
masked_score = -1e30

F32 = jnp.float32
BF16 = jnp.bfloat16
ANY = pl.ANY
VMEM_LIMIT = 56 * 1024 * 1024


def dot_of(a, b, da, db):
    return lax.dot_general(a, b, (((da,), (db,)), ((), ())), preferred_element_type=F32)


def params(*semantics):
    return pltpu.CompilerParams(
        vmem_limit_bytes=VMEM_LIMIT, dimension_semantics=semantics or None
    )


def cost(flops, bytes_accessed, transcendentals=0):
    return pl.CostEstimate(
        flops=int(flops) // COST_SHARE,
        bytes_accessed=int(bytes_accessed) // COST_SHARE,
        transcendentals=int(transcendentals) // COST_SHARE,
    )


def turn(values, cosine, sine):
    return values * cosine + pltpu.roll(values, HD // 2, 1) * sine


def attend_forward_kernel(
    live_ref, q_ref, k_ref, v_ref, cos_ref, sin_ref, qg_ref, kg_ref, mix_ref, ql_ref, kl_ref, vl_ref
):
    live = live_ref[0]
    cosine = cos_ref[...]
    sine = sin_ref[...]

    def normed(values, gain):
        inverse = lax.rsqrt(jnp.mean(values * values, axis=1, keepdims=True) + epsilon)
        return turn(values * inverse * gain, cosine, sine).astype(BF16)

    ql_ref[...] = normed(q_ref[...], qg_ref[...])
    kl_ref[...] = normed(k_ref[...], kg_ref[...])
    vl_ref[...] = v_ref[...].astype(BF16)
    keys = kl_ref[...]
    values = vl_ref[...]
    rows = 256
    place = lax.broadcasted_iota(jnp.int32, (rows, SEQ_LEN), 1)
    for part in range(SEQ_LEN // rows):
        here = pl.ds(part * rows, rows)
        scores = dot_of(ql_ref[here, :], keys, 1, 1) * (1.0 / math.sqrt(HD))
        scores = jnp.where(place < live, scores, masked_score)
        top = jnp.max(scores, axis=1, keepdims=True)
        shifted = jnp.exp(scores - top)
        total = jnp.sum(shifted, axis=1, keepdims=True)
        probs = (shifted * (1.0 / total)).astype(BF16)
        mix_ref[here, :] = dot_of(probs, values, 1, 0).astype(BF16)


def attend_forward(seq, live, qkv, tables, query_gain, key_gain, heads):
    width = heads * HD

    def pick(offset):
        return pl.BlockSpec((SEQ_LEN, HD), lambda h, live, o=offset: (seq, o + h))

    def whole(shape):
        return pl.BlockSpec(shape, lambda h, live: (0, 0))

    out = pl.BlockSpec((SEQ_LEN, HD), lambda h, live: (0, h))
    return pl.pallas_call(
        attend_forward_kernel,
        grid_spec=pltpu.PrefetchScalarGridSpec(
            num_scalar_prefetch=1,
            grid=(heads,),
            in_specs=[
                pick(0),
                pick(heads),
                pick(2 * heads),
                whole((SEQ_LEN, HD)),
                whole((SEQ_LEN, HD)),
                whole((1, HD)),
                whole((1, HD)),
            ],
            out_specs=[out] * 4,
        ),
        out_shape=[jax.ShapeDtypeStruct((SEQ_LEN, width), BF16)] * 4,
        compiler_params=params("arbitrary"),
        cost_estimate=cost(
            heads * 8 * SEQ_LEN * SEQ_LEN * HD, 20 * SEQ_LEN * width, heads * SEQ_LEN * SEQ_LEN
        ),
        name="attend_forward",
    )(live, qkv, qkv, qkv, tables[0], tables[1], query_gain, key_gain)


def attend_backward_kernel(
    live_ref,
    ql_ref,
    kl_ref,
    vl_ref,
    do_ref,
    q_ref,
    k_ref,
    cos_ref,
    sin_ref,
    qg_ref,
    kg_ref,
    qc_ref,
    kc_ref,
    vc_ref,
    qpart_ref,
    kpart_ref,
    inner_ref,
    dq_ref,
    dk_ref,
    dv_ref,
):
    head = pl.program_id(0)
    live = live_ref[0]
    scale = 1.0 / math.sqrt(HD)
    keys = kl_ref[...]
    values = vl_ref[...]
    rows = 256
    place = lax.broadcasted_iota(jnp.int32, (SEQ_LEN, rows), 0)
    for part in range(SEQ_LEN // rows):
        here = pl.ds(part * rows, rows)
        queries = ql_ref[here, :]
        incoming = do_ref[here, :]
        scores = dot_of(keys, queries, 1, 1) * scale
        scores = jnp.where(place < live, scores, masked_score)
        top = jnp.max(scores, axis=0, keepdims=True)
        shifted = jnp.exp(scores - top)
        total = jnp.sum(shifted, axis=0, keepdims=True)
        probs = shifted * (1.0 / total)
        dv = dot_of(probs.astype(BF16), incoming, 1, 0)
        probs_cot = dot_of(values, incoming, 1, 1)
        weighted = probs * probs_cot
        centre = jnp.sum(weighted, axis=0, keepdims=True)
        raw = ((weighted - probs * centre) * scale).astype(BF16)
        dk = dot_of(raw, queries, 1, 0)
        dq_ref[here, :] = dot_of(raw, keys, 0, 0)
        if part == 0:
            dv_ref[...] = dv
            dk_ref[...] = dk
        else:
            dv_ref[...] += dv
            dk_ref[...] += dk
    cosine = cos_ref[...]
    sine = -sin_ref[...]

    def back(values, gain, rotated_cot):
        incoming = turn(rotated_cot, cosine, sine)
        inverse = lax.rsqrt(jnp.mean(values * values, axis=1, keepdims=True) + epsilon)
        scaled = incoming * gain
        inner = jnp.mean(scaled * values, axis=1, keepdims=True)
        grad = inverse * scaled - values * (inverse * inverse * inverse * inner)
        part = jnp.sum(incoming * values * inverse, axis=0, keepdims=True)
        return grad.astype(BF16), part, jnp.sum(grad * values, axis=1, keepdims=True)

    qc_ref[...], qpart, inner = back(q_ref[...], qg_ref[...], dq_ref[...])
    kc_ref[...], kpart, key_inner = back(k_ref[...], kg_ref[...], dk_ref[...])
    vc_ref[...] = dv_ref[...].astype(BF16)
    inner += key_inner
    inner += jnp.sum(dv_ref[...] * values.astype(F32), axis=1, keepdims=True)

    @pl.when(head == 0)
    def _():
        qpart_ref[...] = qpart
        kpart_ref[...] = kpart
        inner_ref[...] = inner

    @pl.when(head > 0)
    def _():
        qpart_ref[...] += qpart
        kpart_ref[...] += kpart
        inner_ref[...] += inner


def attend_backward(seq, live, lows, mixture_cot, qkv, tables, query_gain, key_gain, heads):
    width = heads * HD
    block = pl.BlockSpec((SEQ_LEN, HD), lambda h, live: (0, h))

    def pick(offset):
        return pl.BlockSpec((SEQ_LEN, HD), lambda h, live, o=offset: (seq, o + h))

    def whole(shape):
        return pl.BlockSpec(shape, lambda h, live: (0, 0))

    return pl.pallas_call(
        attend_backward_kernel,
        grid_spec=pltpu.PrefetchScalarGridSpec(
            num_scalar_prefetch=1,
            grid=(heads,),
            in_specs=[block] * 4
            + [
                pick(0),
                pick(heads),
                whole((SEQ_LEN, HD)),
                whole((SEQ_LEN, HD)),
                whole((1, HD)),
                whole((1, HD)),
            ],
            out_specs=[block] * 3 + [whole((1, HD))] * 2 + [whole((SEQ_LEN, 1))],
            scratch_shapes=[pltpu.VMEM((SEQ_LEN, HD), F32)] * 3,
        ),
        out_shape=[jax.ShapeDtypeStruct((SEQ_LEN, width), BF16)] * 3
        + [jax.ShapeDtypeStruct((1, HD), F32)] * 2
        + [jax.ShapeDtypeStruct((SEQ_LEN, 1), F32)],
        compiler_params=params("arbitrary"),
        cost_estimate=cost(
            heads * 20 * SEQ_LEN * SEQ_LEN * HD, 24 * SEQ_LEN * width, heads * SEQ_LEN * SEQ_LEN
        ),
        name="attend_backward",
    )(live, *lows, mixture_cot, qkv, qkv, tables[0], tables[1], query_gain, key_gain)


def compact_kernel(start_ref, where_ref, pos_ref, source_ref, *outs):
    group, groups = pl.program_id(0), pl.num_programs(0)
    row_of = lax.broadcasted_iota(jnp.int32, (WINDOW, BLOCK), 0)
    for out in outs:
        out[...] = jnp.zeros_like(out)
    for number in range(source_ref.shape[1] // BLOCK):
        here = slice(number * BLOCK, (number + 1) * BLOCK)
        for expert, out in enumerate(outs):
            start = pl.multiple_of(start_ref[expert * groups + group, number], EDGE)
            place = pos_ref[expert, 0, :, here]
            choice = jnp.where(row_of + start == place, 1.0, 0.0).astype(BF16)
            rows = dot_of(choice, source_ref[0, here, :], 1, 0)
            out[pl.ds(start, WINDOW), :] += rows.astype(BF16)


def compact(starts, where, pos_row, source, groups, cols):
    tokens, width = source.shape[1:]
    count = pos_row.shape[0] // groups
    return pl.pallas_call(
        compact_kernel,
        grid_spec=pltpu.PrefetchScalarGridSpec(
            num_scalar_prefetch=2,
            grid=(groups, cols),
            in_specs=[
                pl.BlockSpec((count, 1, 1, tokens), lambda q, j, s, w: (0, q, 0, 0)),
                pl.BlockSpec(
                    (1, tokens, width), lambda q, j, s, w: ((w[0] ^ q) * cols + j, 0, 0)
                ),
            ],
            out_specs=[pl.BlockSpec((CAP, width), lambda q, j, s, w: (q, j))] * count,
        ),
        out_shape=[jax.ShapeDtypeStruct((groups * CAP, cols * width), BF16)] * count,
        compiler_params=params("arbitrary", "arbitrary"),
        cost_estimate=cost(
            count * groups * cols * 2 * tokens * WINDOW * width * 2,
            groups * cols * 2 * width * (tokens + count * CAP),
        ),
        name="compact",
    )(starts, where, pos_row.reshape(count, groups, 1, tokens), source)


def compact_scalars_kernel(start_ref, pos_ref, *refs):
    count = len(refs) // 2
    group = pl.program_id(0)
    row_of = lax.broadcasted_iota(jnp.int32, (WINDOW, BLOCK), 0)
    for number in range(count):
        refs[count + number][...] = jnp.zeros_like(refs[count + number])
    for number in range(pos_ref.shape[2] // BLOCK):
        start = pl.multiple_of(start_ref[group, number], EDGE)
        here = slice(number * BLOCK, (number + 1) * BLOCK)
        choice = row_of + start == pos_ref[0, :, here]
        for source, out in zip(refs[:count], refs[count:]):
            picked = jnp.sum(jnp.where(choice, source[0, :, here], 0.0), axis=1, keepdims=True)
            out[pl.ds(start, WINDOW), :] += picked


def compact_scalars(starts, pos_row, sources):
    groups, _, tokens = pos_row.shape
    block = pl.BlockSpec((1, 1, tokens), lambda q, s: (q, 0, 0))
    return pl.pallas_call(
        compact_scalars_kernel,
        grid_spec=pltpu.PrefetchScalarGridSpec(
            num_scalar_prefetch=1,
            grid=(groups,),
            in_specs=[block] * (1 + len(sources)),
            out_specs=[pl.BlockSpec((CAP, 1), lambda q, s: (q, 0))] * len(sources),
        ),
        out_shape=[jax.ShapeDtypeStruct((groups * CAP, 1), F32)] * len(sources),
        compiler_params=params("arbitrary"),
        cost_estimate=cost(0, 4 * groups * CAP * 128 * len(sources)),
        name="compact_scalars",
    )(starts, pos_row, *sources)


def expand_scalars_kernel(start_ref, pos_ref, *refs):
    count = len(refs) // 2
    group = pl.program_id(0)
    row_of = lax.broadcasted_iota(jnp.int32, (WINDOW, BLOCK), 0)
    for number in range(pos_ref.shape[2] // BLOCK):
        start = pl.multiple_of(start_ref[group, number], EDGE)
        here = slice(number * BLOCK, (number + 1) * BLOCK)
        choice = row_of + start == pos_ref[0, :, here]
        for source, out in zip(refs[:count], refs[count:]):
            held = source[pl.ds(start, WINDOW), :]
            out[0, :, here] = jnp.sum(jnp.where(choice, held, 0.0), axis=0, keepdims=True)


def expand_scalars(starts, pos_row, sources):
    groups, _, tokens = pos_row.shape
    block = pl.BlockSpec((1, 1, tokens), lambda q, s: (q, 0, 0))
    return pl.pallas_call(
        expand_scalars_kernel,
        grid_spec=pltpu.PrefetchScalarGridSpec(
            num_scalar_prefetch=1,
            grid=(groups,),
            in_specs=[block] + [pl.BlockSpec((CAP, 1), lambda q, s: (q, 0))] * len(sources),
            out_specs=[block] * len(sources),
        ),
        out_shape=[jax.ShapeDtypeStruct((groups, 1, tokens), F32)] * len(sources),
        compiler_params=params("arbitrary"),
        cost_estimate=cost(0, 4 * groups * CAP * 128 * len(sources)),
        name="expand_scalars",
    )(starts, pos_row, *sources)


def expand_kernel(sizes, count, start_ref, where_ref, pos_ref, *refs):
    group, groups = pl.program_id(0), pl.num_programs(0)
    sides = len(refs) // (count + len(sizes))
    sources, outs = refs[: count * sides], refs[count * sides :]
    column_of = lax.broadcasted_iota(jnp.int32, (BLOCK, WINDOW), 1)
    number = 0
    for part, size in enumerate(sizes):
        for step in range(size // BLOCK):
            totals = [None] * sides
            for expert in range(count):
                start = pl.multiple_of(start_ref[expert * groups + group, number], EDGE)
                place = pos_ref[expert, 0, number * BLOCK : (number + 1) * BLOCK, :]
                choice = jnp.where(column_of + start == place, 1.0, 0.0).astype(BF16)
                for side in range(sides):
                    held = sources[expert * sides + side][pl.ds(start, WINDOW), :]
                    rows = dot_of(choice, held, 1, 0)
                    totals[side] = rows if totals[side] is None else totals[side] + rows
            here = slice(step * BLOCK, (step + 1) * BLOCK)
            for side in range(sides):
                outs[part * sides + side][0, 0, here, :] = totals[side].astype(BF16)
            number += 1


def expand(starts, where, pos_col, sources, sizes, groups, cols):
    width = sources[0].shape[1] // cols
    tokens = sum(sizes)
    count = len(sources)

    def side(odd):
        return pl.BlockSpec((CAP, width), lambda q, j, s, w: (q, w[1] ^ (2 * j + odd)))

    outs = pl.pallas_call(
        functools.partial(expand_kernel, sizes, count),
        grid_spec=pltpu.PrefetchScalarGridSpec(
            num_scalar_prefetch=2,
            grid=(groups, cols // 2),
            in_specs=[pl.BlockSpec((count, 1, tokens, 1), lambda q, j, s, w: (0, q, 0, 0))]
            + [side(0), side(1)] * count,
            out_specs=[
                pl.BlockSpec((1, 1, size, width), lambda q, j, s, w: (q, j, 0, 0))
                for size in sizes
                for _ in range(2)
            ],
        ),
        out_shape=[
            jax.ShapeDtypeStruct((groups, cols // 2, size, width), BF16)
            for size in sizes
            for _ in range(2)
        ],
        compiler_params=params("arbitrary", "arbitrary"),
        cost_estimate=cost(
            4 * count * groups * cols * tokens * WINDOW * width,
            groups * cols * width * (2 * tokens + 2 * count * CAP),
        ),
        name="expand",
    )(
        starts,
        where,
        pos_col.reshape(count, groups, tokens, 1),
        *[source for source in sources for _ in range(2)],
    )
    return list(zip(outs[::2], outs[1::2]))


def expand_all(starts, where, pos_col, sources, groups, cols):
    width = sources[0].shape[1] // cols
    tokens = pos_col.shape[1]
    count = len(sources)
    return pl.pallas_call(
        functools.partial(expand_kernel, [tokens], count),
        grid_spec=pltpu.PrefetchScalarGridSpec(
            num_scalar_prefetch=2,
            grid=(groups, cols),
            in_specs=[pl.BlockSpec((count, 1, tokens, 1), lambda q, j, s, w: (0, q, 0, 0))]
            + [pl.BlockSpec((CAP, width), lambda q, j, s, w: (q, j))] * count,
            out_specs=pl.BlockSpec((1, 1, tokens, width), lambda q, j, s, w: (w[0] ^ q, j, 0, 0)),
        ),
        out_shape=jax.ShapeDtypeStruct((groups, cols, tokens, width), BF16),
        compiler_params=params("arbitrary", "arbitrary"),
        cost_estimate=cost(
            4 * count * groups * cols * tokens * WINDOW * width,
            groups * cols * width * (2 * tokens + 2 * count * CAP),
        ),
        name="expand_all",
    )(starts, where, pos_col.reshape(count, groups, tokens, 1), *sources)


def pack_kernel(where_ref, gate_ref, up_ref, down_ref, out_ref):
    hidden = gate_ref.shape[2]
    out_ref[0, :, :hidden] = gate_ref[0].astype(BF16)
    out_ref[0, :, hidden : 2 * hidden] = up_ref[0].astype(BF16)
    out_ref[0, :, 2 * hidden :] = down_ref[0].T.astype(BF16)


def pack_weights(where, gate, up, down, each):
    experts, depth, hidden = gate.shape

    def pick(shape):
        return pl.BlockSpec(shape, lambda q, w: ((w[0] ^ (q // each)) * each + q % each, 0, 0))

    return pl.pallas_call(
        pack_kernel,
        grid_spec=pltpu.PrefetchScalarGridSpec(
            num_scalar_prefetch=1,
            grid=(experts,),
            in_specs=[pick((1, depth, hidden)), pick((1, depth, hidden)), pick((1, hidden, depth))],
            out_specs=pl.BlockSpec((1, depth, 3 * hidden), lambda q, w: (q, 0, 0)),
        ),
        out_shape=jax.ShapeDtypeStruct((experts, depth, 3 * hidden), BF16),
        compiler_params=params("arbitrary"),
        cost_estimate=cost(0, 18 * experts * depth * hidden),
        name="pack_weights",
    )(where, gate, up, down)


def unpack_kernel(where_ref, *refs):
    sources, (gate_ref, up_ref, down_ref) = refs[:-3], refs[-3:]
    hidden = gate_ref.shape[2]
    for number, source in enumerate(sources):

        @pl.when(pl.program_id(0) == number)
        def _(source=source):
            gate_ref[0] = source[:, :hidden].astype(F32)
            up_ref[0] = source[:, hidden : 2 * hidden].astype(F32)
            down_ref[0] = source[:, 2 * hidden :].astype(F32).T


def unpack_grads(where, sources, each):
    count = len(sources)
    depth, wide = sources[0].shape
    hidden = wide // 3

    def pick(shape):
        return pl.BlockSpec(shape, lambda q, w: ((w[0] ^ (q // each)) * each + q % each, 0, 0))

    shapes = [(count, depth, hidden), (count, depth, hidden), (count, hidden, depth)]
    return pl.pallas_call(
        unpack_kernel,
        grid_spec=pltpu.PrefetchScalarGridSpec(
            num_scalar_prefetch=1,
            grid=(count,),
            in_specs=[pl.BlockSpec((depth, wide), lambda q, w: (0, 0))] * count,
            out_specs=[pick((1,) + shape[1:]) for shape in shapes],
        ),
        out_shape=[jax.ShapeDtypeStruct(shape, F32) for shape in shapes],
        compiler_params=params("arbitrary"),
        cost_estimate=cost(0, 18 * count * depth * hidden),
        name="unpack_grads",
    )(where, *sources)


def expert_kernel(count, hidden, row_ref, x_ref, m_ref, gate_ref, scale_ref, *refs):
    pieces = refs[:count]
    rows_ref, pre_ref, act_ref, cot_ref, inner_ref, result_ref, held, sems = refs[count:]
    depth = pieces[0].shape[0]

    @pl.when(pl.program_id(0) == 0)
    def _():
        copies = []
        for number, piece in enumerate(pieces):
            place = pl.ds(pl.multiple_of(row_ref[number] * depth, depth), depth)
            copies.append(pltpu.make_async_copy(piece, held.at[place, :], sems.at[number]))
        for copy in copies:
            copy.start()
        for copy in copies:
            copy.wait()

    gate = gate_ref[...]
    scale = scale_ref[...]
    wide = EXPERT_WIDE
    cot_ref[...] = jnp.zeros_like(cot_ref)
    inner_ref[...] = jnp.zeros_like(inner_ref)

    @pl.loop(0, hidden // wide, unroll=EXPERT_UNROLL)
    def _(step):
        first = pl.multiple_of(step * wide, wide)
        gate_pre = dot_of(x_ref[...], held[:, pl.ds(first, wide)], 1, 0) * scale
        up_pre = dot_of(x_ref[...], held[:, pl.ds(hidden + first, wide)], 1, 0) * scale
        back = dot_of(m_ref[...], held[:, pl.ds(2 * hidden + first, wide)], 1, 0)
        squash = 1.0 / (1.0 + jnp.exp(-gate_pre))
        silu = gate_pre * squash
        active = silu * up_pre
        cot_ref[...] += jnp.sum(active.astype(BF16).astype(F32) * back, axis=1, keepdims=True)
        act_ref[:, pl.ds(first, wide)] = (active * gate).astype(BF16)
        back = back * gate
        slope = squash * (1.0 + gate_pre * (1.0 - squash))
        gate_cot = back * up_pre * slope
        up_cot = back * silu
        inner_ref[...] += jnp.sum(gate_cot * gate_pre + up_cot * up_pre, axis=1, keepdims=True)
        pre_ref[:, pl.ds(first, wide)] = (gate_cot * scale).astype(BF16)
        pre_ref[:, pl.ds(hidden + first, wide)] = (up_cot * scale).astype(BF16)

    @pl.loop(0, held.shape[0] // wide, unroll=EXPERT_UNROLL)
    def _(step):
        first = pl.multiple_of(step * wide, wide)
        here = pl.ds(first, wide)
        rows_ref[:, here] = dot_of(pre_ref[...], held[here, : 2 * hidden], 1, 1).astype(BF16)
        result_ref[:, here] = dot_of(act_ref[...], held[here, 2 * hidden :], 1, 1).astype(BF16)


def expert_step(row_numbers, x, m, gate, scale, pieces):
    total, wide = x.shape
    hidden = pieces[0].shape[1] // 3
    count = len(pieces)

    def tile(columns):
        return pl.BlockSpec((TILE, columns), lambda i, r: (i, 0))

    return pl.pallas_call(
        functools.partial(expert_kernel, count, hidden),
        grid_spec=pltpu.PrefetchScalarGridSpec(
            num_scalar_prefetch=1,
            grid=(total // TILE,),
            in_specs=[tile(wide), tile(wide), tile(1), tile(1)]
            + [pl.BlockSpec(memory_space=ANY)] * count,
            out_specs=[tile(wide), tile(2 * hidden), tile(hidden), tile(1), tile(1), tile(wide)],
            scratch_shapes=[
                pltpu.VMEM((wide, 3 * hidden), BF16),
                pltpu.SemaphoreType.DMA((count,)),
            ],
        ),
        out_shape=[
            jax.ShapeDtypeStruct((total, wide), BF16),
            jax.ShapeDtypeStruct((total, 2 * hidden), BF16),
            jax.ShapeDtypeStruct((total, hidden), BF16),
            jax.ShapeDtypeStruct((total, 1), F32),
            jax.ShapeDtypeStruct((total, 1), F32),
            jax.ShapeDtypeStruct((total, wide), BF16),
        ],
        compiler_params=params("arbitrary"),
        cost_estimate=cost(
            2 * total * wide * hidden * 6, 2 * total * (4 * wide + 3 * hidden), total * hidden
        ),
        name="expert_step",
    )(row_numbers, x, m, gate, scale, *pieces)


def weight_grad_kernel(mids, place_ref, x_ref, m_ref, pre_ref, act_ref, out_ref, turned_ref):
    wide = GRAD_WIDE
    first = pre_ref.shape[1]
    depth = x_ref.shape[1] // mids
    turned_ref[0] = x_ref[...].T
    turned_ref[1] = m_ref[...].T
    mid = place_ref[place_ref.shape[0] - 1]

    def put(grad, here):
        for number in range(mids):
            block = grad[number * depth : (number + 1) * depth].astype(BF16)
            out_ref[0, number ^ mid, 0, :, here] = block

    @pl.loop(0, first // wide, unroll=GRAD_UNROLL)
    def _(step):
        here = pl.ds(pl.multiple_of(step * wide, wide), wide)
        put(dot_of(turned_ref[0], pre_ref[:, here], 1, 0), here)

    @pl.loop(0, act_ref.shape[1] // wide, unroll=GRAD_UNROLL)
    def _(step):
        here = pl.ds(pl.multiple_of(step * wide, wide), wide)
        there = pl.ds(pl.multiple_of(first + step * wide, wide), wide)
        put(dot_of(turned_ref[1], act_ref[:, here], 1, 0), there)


def weight_grads(places, x, m, pre, act, depth, groups, mids, high):
    total = x.shape[0]
    wide = pre.shape[1] + act.shape[1]

    def column(array):
        return pl.BlockSpec((total, mids * depth), lambda f, h, r: (0, r[f * high + h]))

    def whole(array):
        return pl.BlockSpec(array.shape, lambda f, h, r: (0, 0), pipeline_mode=pl.Buffered(1))

    return pl.pallas_call(
        functools.partial(weight_grad_kernel, mids),
        grid_spec=pltpu.PrefetchScalarGridSpec(
            num_scalar_prefetch=1,
            grid=(groups, high),
            in_specs=[column(x), column(m), whole(pre), whole(act)],
            out_specs=pl.BlockSpec(
                (1, mids, 1, depth, wide), lambda f, h, r: (f, 0, h, 0, 0)
            ),
            scratch_shapes=[pltpu.VMEM((2, mids * depth, total), BF16)],
        ),
        out_shape=jax.ShapeDtypeStruct((groups, mids, high, depth, wide), BF16),
        compiler_params=params("arbitrary", "arbitrary"),
        cost_estimate=cost(
            2 * total * depth * groups * mids * high * wide,
            2 * total * (2 * depth * groups * mids * high + wide),
        ),
        name="weight_grads",
    )(places, x, m, pre, act)


def bits_of(size):
    return [1 << n for n in range(size.bit_length() - 1)]


def swap(values, axis, bit):
    size = lax.axis_size(axis) if isinstance(axis, str) else math.prod(map(lax.axis_size, axis))
    return lax.ppermute(values, axis, [(n, n ^ bit) for n in range(size)])


class Flow:
    def __init__(self, steps):
        self.steps = steps
        self.result = None
        self.sends = next(steps)

    def advance(self, got):
        try:
            self.sends = self.steps.send(got)
        except StopIteration as stop:
            self.sends = None
            self.result = stop.value

    def step(self, count=1):
        for _ in range(count):
            if self.sends is not None:
                self.advance([swap(*send) for send in self.sends])
        return self

    def finish(self):
        while self.sends is not None:
            self.step()
        return self.result

    def holds(self):
        return self.result if self.sends is None else [send[0] for send in self.sends]

    def replace(self, arrays):
        if self.sends is None:
            self.result = arrays
        else:
            self.sends = [(array, *send[1:]) for array, send in zip(arrays, self.sends)]


def stage(live, flows=(), work=(), sync=()):
    flows = [flow for flow in flows if flow.sends is not None]
    got = [[swap(*send) for send in flow.sends] for flow in flows]
    done = [each() for each in work]
    held = [flow.holds() for flow in sync]
    got, done, held, kept = lax.optimization_barrier((got, done, held, dict(live)))
    live.update(kept)
    for flow, arrays in zip(flows, got):
        flow.advance(arrays)
    for flow, arrays in zip(sync, held):
        flow.replace(arrays)
    return done


def spread_steps(values, axis, bits):
    blocks = {0: values}
    for bit in bits:
        places = sorted(blocks)
        got = yield [(blocks[place], axis, bit) for place in places]
        blocks.update({place | bit: block for place, block in zip(places, got)})
    return [blocks[place] for place in sorted(blocks)]


def spread_rows_steps(values, row_bits, strides):
    held = values[None]
    places = [0]
    for axis, bit in row_bits:
        (got,) = yield [(held, axis, bit)]
        held = jnp.concatenate([held, got], axis=0)
        places += [place | (bit * strides[axis]) for place in places]
    return jnp.stack([held[places.index(place)] for place in range(len(places))])


def spread_cube_steps(values, groups, cols):
    held = values[None]
    for axis, bits in (("lo", bits_of(groups)), ("col", bits_of(cols))):
        for bit in bits:
            (got,) = yield [(held, axis, bit)]
            held = jnp.concatenate([held, got], axis=0)
    return jnp.swapaxes(held.reshape((cols, groups) + values.shape), 0, 1)


def col_reduce_steps(blocks, cols):
    held = dict(enumerate(blocks))
    for bit in bits_of(cols):
        away = [place for place in sorted(held) if place & bit]
        (got,) = yield [(jnp.stack([held[place].astype(BF16) for place in away]), "col", bit)]
        held = {
            place & ~bit: held[place & ~bit] + got[number].astype(F32)
            for number, place in enumerate(away)
        }
    return held[0]


def total_steps(values, axes):
    for axis in axes:
        size = math.prod(map(lax.axis_size, axis))
        got = yield [(values, axis, place) for place in range(1, size)]
        values = values + sum(got)
    return values


def row_reduce_steps(parts, row_bits):
    held = []
    for number, part in enumerate(parts):
        shape = (2,) * len(row_bits) + (part.shape[0] >> len(row_bits), part.shape[1])
        order = list(reversed(row_bits))
        if number % 2 and len(order) > 1:
            order[:2] = order[1::-1]
        held.append((part.reshape(shape), list(row_bits), order))
    for step in range(len(row_bits)):
        sends, rest = [], []
        for array, names, order in held:
            name = order[step]
            axis = names.index(name)
            mine = lax.axis_index(name[0]) // name[1] & 1
            away = lax.dynamic_index_in_dim(array, 1 - mine, axis, False)
            kept = lax.dynamic_index_in_dim(array, mine, axis, False)
            sends.append((away.astype(BF16), *name))
            rest.append((kept, [other for other in names if other != name], order))
        got = yield sends
        held = [
            (kept.astype(F32) + more.astype(F32), names, order)
            for (kept, names, order), more in zip(rest, got)
        ]
    return jnp.concatenate([array for array, _, _ in held], axis=1)


def links_of(groups, cols):
    return [("col", bit) for bit in bits_of(cols)[1:]] + [("lo", bit) for bit in bits_of(groups)]


def turned(links, number):
    number %= len(links)
    return links[number:] + links[:number]


def reduce_steps(parts, groups, cols):
    links = links_of(groups, cols)
    got = yield [(away, "col", 1) for _, away in parts]
    held = []
    for number, (keep, _) in enumerate(parts):
        shape = (2,) * len(links) + keep.shape[2:]
        names = [("lo", bit) for bit in reversed(bits_of(groups))]
        names += [("col", bit) for bit in reversed(bits_of(cols)[1:])]
        held.append((keep.reshape(shape), got[number].reshape(shape), names))
    for step in range(len(links)):
        sends, rest = [], []
        for number, (keep, more, names) in enumerate(held):
            link = turned(links, number)[step]
            axis = names.index(link)

            def half(place):
                total = lax.index_in_dim(keep, place, axis, False).astype(F32)
                return total + lax.index_in_dim(more, place, axis, False).astype(F32)

            sends.append((half(1).astype(BF16), *link))
            kept = half(0)
            rest.append(
                (
                    kept if step + 1 == len(links) else kept.astype(BF16),
                    [name for name in names if name != link],
                )
            )
        got = yield sends
        held = [(keep, more, names) for (keep, names), more in zip(rest, got)]
    return jnp.concatenate([keep.astype(F32) + more.astype(F32) for keep, more, _ in held], axis=0)


def part_sizes(tokens, count):
    whole = tokens // BLOCK
    return [BLOCK * ((whole + count - 1 - n) // count) for n in range(count)]


def expert_weight_steps(piece, far, bits):
    if far:
        (piece,) = yield [(piece, "lo", far)]
    held = {(): piece}
    fresh = [()]
    while True:
        ways = [
            (place, number)
            for place in fresh
            for number in range(place[-1] + 1 if place else 0, len(bits))
        ]
        if not ways:
            return held
        got = yield [(held[place], *bits[number]) for place, number in ways]
        fresh = [place + (number,) for place, number in ways]
        held.update(zip(fresh, got))


def expert_grad_steps(blocks, far, bits):
    for number in reversed(range(len(bits))):
        half = blocks.shape[0] // 2
        (got,) = yield [(blocks[half:], *bits[number])]
        blocks = blocks[:half].astype(F32) + got.astype(F32)
        if number or far:
            blocks = blocks.astype(BF16)
    total = blocks[0]
    if far:
        (total,) = yield [(total, "lo", far)]
    return total


def per_device(
    hidden_in,
    lengths,
    routes,
    attn_gain,
    query_gain,
    key_gain,
    query_weight,
    key_weight,
    value_weight,
    out_weight,
    moe_gain,
    router,
    gate_weight,
    up_weight,
    down_weight,
    cotangent,
):
    tok_rows, width = hidden_in.shape
    cols = lax.axis_size("col")
    groups = lax.axis_size("lo")
    high = lax.axis_size("hi")
    mids = lax.axis_size("mid")
    col = lax.axis_index("col")
    lo = lax.axis_index("lo")
    hi = lax.axis_index("hi")
    mid = lax.axis_index("mid")
    row = (hi * groups + lo) * mids + mid
    where = jnp.stack([lo, col])
    heads = width // HD
    seqs = lengths.shape[0]
    depth = gate_weight.shape[1]
    each = gate_weight.shape[0] // groups
    cube = ("lo", "col")
    rows_axes = ("hi", "lo", "mid")
    strides = {"hi": groups * mids, "lo": mids, "mid": 1}
    seq_rows = [slice(s * SEQ_LEN, (s + 1) * SEQ_LEN) for s in range(seqs)]
    links = links_of(groups, cols)
    col_bits = list(reversed(bits_of(cols)))
    hi_bits = [("hi", bit) for bit in bits_of(high)]
    mid_bits = [("mid", bit) for bit in bits_of(mids)]
    row_bits = hi_bits + [("lo", bit) for bit in bits_of(groups)] + mid_bits
    far_bits = hi_bits + mid_bits
    far_first_bits = hi_bits[::-1] + [("lo", bit) for bit in bits_of(groups)][::-1]
    far_first_bits += mid_bits[::-1]
    live = {}

    def row_of_set(place, far):
        other = row ^ (far * mids)
        for number in place:
            axis, bit = far_bits[number]
            other = other ^ (bit * strides[axis])
        return other

    hidden_flow = Flow(spread_steps(hidden_in, "col", col_bits))
    gain_flow = Flow(spread_steps(attn_gain, "col", col_bits))
    routes_flow = Flow(spread_steps(routes.T, "lo", bits_of(groups)))
    router_flow = Flow(spread_rows_steps(router.T.astype(BF16), row_bits, strides))
    out_flow = Flow(spread_rows_steps(out_weight.T.astype(BF16), row_bits, strides))
    qkv_local = jnp.concatenate([query_weight, key_weight, value_weight], axis=1).astype(BF16)
    qkv_full = lax.all_gather(qkv_local, rows_axes, axis=0, tiled=True)
    live_key = jnp.arange(SEQ_LEN)[None, :] < lengths[:, None]
    out_cot = jnp.where(live_key.reshape(tok_rows, 1), cotangent, jnp.zeros_like(cotangent))
    packed = pack_weights(where, gate_weight, up_weight, down_weight, each)
    units = [(expert, far) for expert in range(each) for far in range(groups)]
    live["packed"] = packed

    def rotary_tables():
        places = jnp.arange(SEQ_LEN).astype(F32)
        powers = jnp.arange(HD // 2).astype(F32) * (2.0 / HD)
        angles = places[:, None] * jnp.exp(-powers * math.log(rope_base))[None, :]
        cosine, sine = jnp.cos(angles), jnp.sin(angles)
        return (
            jnp.concatenate([cosine, cosine], axis=1),
            jnp.concatenate([-sine, sine], axis=1),
        )

    live["out_cot"] = out_cot
    (tables,) = stage(
        live,
        [hidden_flow, gain_flow, routes_flow, router_flow, out_flow],
        [rotary_tables],
    )

    hidden = hidden_in.astype(F32)

    def norm_attn():
        blocks = hidden_flow.finish()
        gains = gain_flow.finish()
        square = sum(jnp.sum(jnp.square(block.astype(F32)), axis=1) for block in blocks)
        inverse = lax.rsqrt(square / D + epsilon)[:, None]
        normed = jnp.zeros((tok_rows, D), BF16)
        for place, (block, gain) in enumerate(zip(blocks, gains)):
            piece = (block.astype(F32) * inverse * gain).astype(BF16)
            normed = lax.dynamic_update_slice_in_dim(normed, piece, (col ^ place) * width, 1)
        return normed, inverse

    def routing():
        rel = jnp.stack(routes_flow.finish())
        named = jnp.any(rel[:, :, None, :] == jnp.arange(EXPERTS)[None, None, :, None], axis=1)
        first = (col * groups + lo) * each
        member = lax.dynamic_slice_in_dim(named, first, each, 1)
        member = jnp.swapaxes(member, 0, 1).reshape(each * groups, tok_rows)
        count = member.astype(jnp.int32)
        rank = jnp.cumsum(count, axis=1) - count
        pos = jnp.where(member, rank, -(1 << 20))
        starts = jnp.minimum(rank[:, ::BLOCK] // EDGE * EDGE, CAP - WINDOW)
        return named, starts, pos[:, None, :], pos[:, :, None]

    live["qkv_full"] = qkv_full
    ((live["normed_attn"], attn_inverse),) = stage(live, [router_flow, out_flow], [norm_attn])
    weight_flows = {}

    def start_weights(expert):
        for far in range(groups):
            weight_flows[expert, far] = Flow(
                expert_weight_steps(live["packed"][far * each + expert], far, far_bits)
            )

    start_weights(0)
    hidden_blocks = hidden_flow.result
    query_scale, key_scale = query_gain[None, :], key_gain[None, :]

    def attend(s):
        return attend_forward(
            s, lengths[s : s + 1], live["qkv"], tables, query_scale, key_scale, heads
        )

    def project_and_attend():
        live["qkv"] = dot_of(live["normed_attn"], live["qkv_full"], 1, 0)
        return attend(0)

    firsts = [weight_flows[0, far] for far in range(1, groups)]
    (first_seq,) = stage(live, firsts + [router_flow, out_flow], [project_and_attend])
    moe_cot = lax.all_gather(live["out_cot"], cube, axis=0, tiled=False)
    for expert in range(1, each):
        start_weights(expert)
    seconds = [weight_flows[unit] for unit in units if unit[0] == 1]
    named, starts, pos_row, pos_col = routing()

    span = width // depth

    def col_rows(blocks, place, axis):
        first = (col ^ place) * span
        return jnp.concatenate(
            [
                lax.dynamic_index_in_dim(blocks, (first + n) ^ row, 0, False)
                for n in range(span)
            ],
            axis=axis,
        )

    out_spread = out_flow.finish()
    out_rel = jnp.concatenate([col_rows(out_spread, place, 0) for place in range(cols)], axis=0)
    router_rows = col_rows(router_flow.finish(), 0, 1)

    def branch(mixture):
        partial = dot_of(mixture, out_rel, 1, 1)
        blocks = [partial[:, n * width : (n + 1) * width] for n in range(cols)]
        return Flow(col_reduce_steps(blocks, cols)).finish()

    def attend_rest():
        outs = [first_seq]
        sums = [branch(first_seq[0])]
        for s in range(1, seqs):
            outs.append(attend(s))
            sums.append(branch(outs[s][0]))
        return outs, sums

    ((attended, branches),) = stage(live, [weight_flows[0, 0]] + seconds[1:], [attend_rest])
    middle = hidden + jnp.concatenate(branches, axis=0)
    live["scaled_rows"] = (middle * moe_gain).astype(BF16)
    scaled_rows = live["scaled_rows"]
    moe_in = lax.all_gather(scaled_rows, cube, axis=0, tiled=False)
    square = jnp.sum(middle * middle, axis=1)[None, :]
    stat = jnp.concatenate([dot_of(router_rows, scaled_rows, 1, 1), square], axis=0)
    stat_flow = Flow(spread_cube_steps(stat, groups, cols))
    stage(live, [stat_flow], sync=[weight_flows[0, 0]] + firsts + seconds)
    (live["cot_rows"],) = stage(
        live,
        [stat_flow, weight_flows[0, 0]] + firsts,
        [lambda: compact(starts, where, pos_row, moe_cot, groups, cols)],
    )
    stage(live, [stat_flow] + firsts)
    stat = stat_flow.finish()

    stat = jnp.sum(stat, axis=1)
    moe_inverse = lax.rsqrt(stat[:, EXPERTS] / D + epsilon)
    all_logits = stat[:, :EXPERTS] * moe_inverse[:, None, :]
    logits = jnp.where(named, all_logits, masked_score)
    shifted = jnp.where(named, jnp.exp(logits - jnp.max(logits, axis=1, keepdims=True)), 0.0)
    gates = shifted / jnp.sum(shifted, axis=1, keepdims=True)
    own_gate = lax.dynamic_slice_in_dim(gates, (col * groups + lo) * each, each, 1)
    own_gate = jnp.swapaxes(own_gate, 0, 1).reshape(each * groups, 1, tok_rows)
    row_gate, row_scale = compact_scalars(
        starts, pos_row, (own_gate, jnp.tile(moe_inverse, (each, 1))[:, None, :])
    )
    total_rows = groups * CAP

    live["moe_rows"] = compact(starts, where, pos_row, moe_in, groups, cols)

    def run_expert(expert):
        pieces, row_numbers = [], []
        for far in range(groups):
            for place, piece in weight_flows[expert, far].finish().items():
                pieces.append(piece)
                row_numbers.append(row_of_set(place, far))
        here = slice(expert * total_rows, (expert + 1) * total_rows)
        return expert_step(
            jnp.stack(row_numbers),
            live["moe_rows"][expert],
            live["cot_rows"][expert],
            row_gate[here],
            row_scale[here],
            pieces,
        )

    grad_places = jnp.stack(
        [
            (hi ^ above) * groups + (lo ^ far)
            for far in reversed(range(groups))
            for above in range(high)
        ]
        + [mid]
    )
    grad_flows = {}

    def start_grads(expert, outs):
        grads = weight_grads(
            grad_places,
            live["moe_rows"][expert],
            live["cot_rows"][expert],
            outs[1],
            outs[2],
            depth,
            groups,
            mids,
            high,
        )
        return grads.reshape((groups, mids * high) + grads.shape[3:])

    def grad_flow(expert, grads):
        for number, far in enumerate(reversed(range(groups))):
            grad_flows[expert, far] = Flow(expert_grad_steps(grads[number], far, far_bits))

    def running():
        return list(grad_flows.values())

    ran = []
    for expert in range(each):
        others = [flow for (number, _), flow in weight_flows.items() if number > expert]
        (outs,) = stage(
            live,
            others + running()[:1],
            [functools.partial(run_expert, expert)],
        )
        ran.append(outs)
        if expert + 1 < each:
            (grads,) = stage(live, others, [functools.partial(start_grads, expert, outs)])
            grad_flow(expert, grads)
    early = running()
    for flow in early:
        flow.step()
    live["result"] = [outs[5] for outs in ran]
    last = ran[-1]
    gate_cot = jnp.concatenate([outs[3] for outs in ran], axis=0)
    row_inner = jnp.concatenate([outs[4] for outs in ran], axis=0)
    sizes = part_sizes(tok_rows, len(links))
    live["scalars"] = (gate_cot, row_inner)
    (rows_parts,) = stage(
        live,
        [],
        [
            lambda: expand(
                starts, where, pos_col, [outs[0] for outs in ran], sizes, groups, cols
            )
        ],
    )
    gate_cot, row_inner = expand_scalars(starts, pos_row, live.pop("scalars"))
    gate_cot = gate_cot.reshape(each, groups, tok_rows)
    row_inner = jnp.sum(row_inner.reshape(each, groups, tok_rows), axis=0)[None]
    scalars = jnp.concatenate([gate_cot, row_inner], axis=0)
    scalars = scalars.reshape((each + 1) * groups, tok_rows)
    scalar_flow = Flow(spread_cube_steps(scalars, groups, cols))
    moe_in_flow = Flow(reduce_steps(rows_parts, groups, cols))
    (grads,) = stage(
        live,
        [moe_in_flow, scalar_flow],
        [functools.partial(start_grads, each - 1, last)],
        sync=early,
    )
    grad_flow(each - 1, grads)
    late = running()[len(early) :]
    (branch_parts,) = stage(
        live,
        [moe_in_flow, scalar_flow] + early[1:] + late[:1],
        [lambda: expand_all(starts, where, pos_col, live["result"], groups, cols)],
    )
    live["moe_branch"] = branch_parts.reshape(groups * cols, tok_rows, width)
    while moe_in_flow.sends is not None:
        stage(live, [moe_in_flow, scalar_flow], sync=early + late)
    scalar_all = scalar_flow.finish().reshape(groups, cols, each + 1, groups, tok_rows)
    scalar_all = jnp.stack([scalar_all[place, :, :, place] for place in range(groups)])
    by_expert = jnp.stack(
        [
            ((lo ^ (number // each % groups)) * cols + (col ^ (number // (each * groups)))) * each
            + number % each
            for number in range(EXPERTS)
        ]
    )
    gate_cot = jnp.take(scalar_all[:, :, :each].reshape(EXPERTS, tok_rows), by_expert, axis=0)
    my_gates, my_logits = gates[0], all_logits[0]
    logit_cot = my_gates * (gate_cot - jnp.sum(my_gates * gate_cot, axis=0, keepdims=True))
    inner = jnp.sum(scalar_all[:, :, each], axis=(0, 1)) + jnp.sum(logit_cot * my_logits, axis=0)
    scaled_logit = (logit_cot * moe_inverse[0][None, :]).astype(BF16)
    logit_cot = logit_cot.astype(BF16)
    my_inverse = moe_inverse[0][:, None]

    back = moe_in_flow.finish() + my_inverse * dot_of(logit_cot, router_rows, 0, 0)
    middle_cot = (
        out_cot.astype(F32)
        + back * moe_gain
        - middle * (my_inverse * my_inverse * (inner[:, None] / D))
    )
    cot_flow = Flow(spread_steps(middle_cot.astype(BF16), "col", col_bits))
    router_part, moe_gain_part = stage(
        live,
        [cot_flow] + early[:1],
        [
            lambda: dot_of(scaled_logit, scaled_rows, 1, 0),
            lambda: jnp.sum(back * middle, axis=0)[None],
        ],
    )
    cot_blocks = cot_flow.finish()
    moe_branch = lax.psum_scatter(
        live.pop("moe_branch"), cube, scatter_dimension=0, tiled=True
    )[0]

    def out_weight_grad():
        grad = jnp.zeros((D, width), F32)
        mixture = jnp.concatenate([each[0] for each in attended], axis=0)
        for place, block in enumerate(cot_blocks):
            piece = dot_of(block, mixture, 0, 0)
            grad = lax.dynamic_update_slice_in_dim(grad, piece, (col ^ place) * width, 0)
        return grad.astype(BF16)

    live["out_grad"] = out_weight_grad()

    def attend_back(s):
        rows = seq_rows[s]
        cots = jnp.concatenate([block[rows] for block in cot_blocks], axis=1)
        mixture_cot = dot_of(cots, out_rel, 1, 0).astype(BF16)
        *cots, query_part, key_part, token_inner = attend_backward(
            s,
            lengths[s : s + 1],
            attended[s][1:],
            mixture_cot,
            live["qkv"],
            tables,
            query_scale,
            key_scale,
            heads,
        )
        cots = jnp.concatenate(cots, axis=1)
        return cots, query_part, key_part, token_inner[:, 0]

    qkv_rel = jnp.concatenate(
        [
            lax.dynamic_slice_in_dim(live["qkv_full"], (col ^ place) * width, width, 0)
            for place in range(cols)
        ],
        axis=0,
    )
    done = stage(
        live,
        late,
        [functools.partial(attend_back, s) for s in range(seqs)],
    )
    for flow in early + late:
        flow.finish()
    qkv_cot = jnp.concatenate([each[0] for each in done], axis=0)
    token_inner = jnp.concatenate([each[3] for each in done], axis=0)
    inner_flow = Flow(total_steps(token_inner, [("col",)]))
    live["qkv_cot"] = qkv_cot
    half = qkv_cot.shape[1] // 2

    def projection_grads(number):
        grad = dot_of(live["normed_attn"], qkv_cot[:, number * half : (number + 1) * half], 0, 0)
        out_half = width // 2
        out = live["out_grad"][:, number * out_half : (number + 1) * out_half]
        return jnp.concatenate([grad.astype(BF16), out], axis=1)

    grad_parts = stage(live, [], [functools.partial(projection_grads, n) for n in range(2)])
    qkv_flow = Flow(row_reduce_steps(grad_parts, far_first_bits))
    (partial,) = stage(live, [qkv_flow], [lambda: dot_of(live["qkv_cot"], qkv_rel, 1, 1)])
    backs = [partial[:, n * width : (n + 1) * width] for n in range(cols)]
    attn_gain_parts = [
        jnp.sum(part * (block.astype(F32) * attn_inverse), axis=0)[None]
        for part, block in zip(backs, hidden_blocks)
    ]
    attn_flow = Flow(col_reduce_steps(backs, cols))

    def widen(blocks):
        full = jnp.zeros((blocks[0].shape[0], D), F32)
        for place, block in enumerate(blocks):
            full = lax.dynamic_update_slice_in_dim(full, block, (col ^ place) * width, 1)
        return full

    head_parts = jnp.concatenate([sum(each[1] for each in done), sum(each[2] for each in done)], 1)
    small = jnp.concatenate(
        [
            widen([router_part]),
            widen([moe_gain_part]),
            widen(attn_gain_parts),
            jnp.pad(head_parts, ((0, 0), (0, D - 2 * HD))),
        ],
        axis=0,
    )

    small_flow = Flow(total_steps(small, [("lo", "mid"), ("hi",), ("col",)]))
    flows = [attn_flow, inner_flow, small_flow, qkv_flow]
    stage(live, flows)
    live["moe_branch"] = moe_branch
    while any(flow.sends is not None for flow in flows):
        stage(live, flows)
    moe_branch = live["moe_branch"]
    first_sum, second_sum = jnp.split(qkv_flow.finish(), 2, axis=1)
    weight_sum = jnp.concatenate([first_sum[:, :half], second_sum[:, :half]], axis=1)
    out_sum = jnp.concatenate([first_sum[:, half:], second_sum[:, half:]], axis=1)

    input_grad = (
        middle_cot
        + attn_inverse * (attn_flow.finish() * attn_gain)
        - hidden * (attn_inverse * attn_inverse * (inner_flow.finish()[:, None] / D))
    )
    output = (middle + moe_branch.astype(F32)).astype(BF16)
    gate_grad, up_grad, down_grad = unpack_grads(
        where,
        [grad_flows[expert, far].finish() for far in range(groups) for expert in range(each)],
        each,
    )
    small = small_flow.finish()
    own = lax.dynamic_slice_in_dim(small, col * width, width, 1)
    router_grad = lax.dynamic_slice_in_dim(small[:EXPERTS], row * depth, depth, 1).T
    return (
        output,
        input_grad,
        own[EXPERTS + 1],
        small[EXPERTS + 2, :HD],
        small[EXPERTS + 2, HD : 2 * HD],
        weight_sum[:, :width],
        weight_sum[:, width : 2 * width],
        weight_sum[:, 2 * width : 3 * width],
        out_sum.T,
        own[EXPERTS],
        router_grad,
        gate_grad,
        up_grad,
        down_grad,
    )


def solution(mesh):
    row_count, col_count = mesh.shape["row"], mesh.shape["col"]
    groups = 2
    between = EXPERTS // col_count // groups
    shape = (row_count // (groups * between), groups, between, col_count)
    inner = Mesh(mesh.devices.reshape(shape), ("hi", "lo", "mid", "col"))
    row = ("hi", "lo", "mid")
    return jax.shard_map(
        per_device,
        mesh=inner,
        in_specs=(
            P(row, "col"),
            P(row),
            P(row, None),
            P("col"),
            P(),
            P(),
            P(row, "col"),
            P(row, "col"),
            P(row, "col"),
            P("col", row),
            P("col"),
            P(row, None),
            P("col", row, None),
            P("col", row, None),
            P("col", None, row),
            P(row, "col"),
        ),
        out_specs=(
            P(row, "col"),
            P(row, "col"),
            P("col"),
            P(),
            P(),
            P(row, "col"),
            P(row, "col"),
            P(row, "col"),
            P("col", row),
            P("col"),
            P(row, None),
            P("col", row, None),
            P("col", row, None),
            P("col", None, row),
        ),
        check_vma=False,
    )
```

```python
import functools
import math

import jax
import jax.numpy as jnp
from jax import lax
from jax.experimental import pallas as pl
from jax.experimental.pallas import tpu as pltpu
from jax.sharding import Mesh, PartitionSpec as P

D = 2048
HD = 128
EXPERTS = 16
SEQ_LEN = 1024
CAP = 1152

BLOCK = 128
WINDOW = 144
EDGE = 16
TILE = 384
COST_SHARE = 50
EXPERT_WIDE, EXPERT_UNROLL = 512, 2
GRAD_WIDE, GRAD_UNROLL = 512, 1

epsilon = 1e-06
rope_base = 10000.0
masked_score = -1e30

F32 = jnp.float32
BF16 = jnp.bfloat16
ANY = pl.ANY
VMEM_LIMIT = 56 * 1024 * 1024


def dot_of(a, b, da, db):
    return lax.dot_general(a, b, (((da,), (db,)), ((), ())), preferred_element_type=F32)


def params(*semantics):
    return pltpu.CompilerParams(
        vmem_limit_bytes=VMEM_LIMIT, dimension_semantics=semantics or None
    )


def cost(flops, bytes_accessed, transcendentals=0):
    return pl.CostEstimate(
        flops=int(flops) // COST_SHARE,
        bytes_accessed=int(bytes_accessed) // COST_SHARE,
        transcendentals=int(transcendentals) // COST_SHARE,
    )


def turn(values, cosine, sine):
    return values * cosine + pltpu.roll(values, HD // 2, 1) * sine


def attend_forward_kernel(
    live_ref, q_ref, k_ref, v_ref, cos_ref, sin_ref, qg_ref, kg_ref, mix_ref, ql_ref, kl_ref, vl_ref
):
    live = live_ref[0]
    cosine = cos_ref[...]
    sine = sin_ref[...]

    def normed(values, gain):
        inverse = lax.rsqrt(jnp.mean(values * values, axis=1, keepdims=True) + epsilon)
        return turn(values * inverse * gain, cosine, sine).astype(BF16)

    ql_ref[...] = normed(q_ref[...], qg_ref[...])
    kl_ref[...] = normed(k_ref[...], kg_ref[...])
    vl_ref[...] = v_ref[...].astype(BF16)
    keys = kl_ref[...]
    values = vl_ref[...]
    rows = 256
    place = lax.broadcasted_iota(jnp.int32, (rows, SEQ_LEN), 1)
    for part in range(SEQ_LEN // rows):
        here = pl.ds(part * rows, rows)
        scores = dot_of(ql_ref[here, :], keys, 1, 1) * (1.0 / math.sqrt(HD))
        scores = jnp.where(place < live, scores, masked_score)
        top = jnp.max(scores, axis=1, keepdims=True)
        shifted = jnp.exp(scores - top)
        total = jnp.sum(shifted, axis=1, keepdims=True)
        probs = (shifted * (1.0 / total)).astype(BF16)
        mix_ref[here, :] = dot_of(probs, values, 1, 0).astype(BF16)


def attend_forward(seq, live, qkv, tables, query_gain, key_gain, heads):
    width = heads * HD

    def pick(offset):
        return pl.BlockSpec((SEQ_LEN, HD), lambda h, live, o=offset: (seq, o + h))

    def whole(shape):
        return pl.BlockSpec(shape, lambda h, live: (0, 0))

    out = pl.BlockSpec((SEQ_LEN, HD), lambda h, live: (0, h))
    return pl.pallas_call(
        attend_forward_kernel,
        grid_spec=pltpu.PrefetchScalarGridSpec(
            num_scalar_prefetch=1,
            grid=(heads,),
            in_specs=[
                pick(0),
                pick(heads),
                pick(2 * heads),
                whole((SEQ_LEN, HD)),
                whole((SEQ_LEN, HD)),
                whole((1, HD)),
                whole((1, HD)),
            ],
            out_specs=[out] * 4,
        ),
        out_shape=[jax.ShapeDtypeStruct((SEQ_LEN, width), BF16)] * 4,
        compiler_params=params("arbitrary"),
        cost_estimate=cost(
            heads * 8 * SEQ_LEN * SEQ_LEN * HD, 20 * SEQ_LEN * width, heads * SEQ_LEN * SEQ_LEN
        ),
        name="attend_forward",
    )(live, qkv, qkv, qkv, tables[0], tables[1], query_gain, key_gain)


def attend_backward_kernel(
    live_ref,
    ql_ref,
    kl_ref,
    vl_ref,
    do_ref,
    q_ref,
    k_ref,
    cos_ref,
    sin_ref,
    qg_ref,
    kg_ref,
    qc_ref,
    kc_ref,
    vc_ref,
    qpart_ref,
    kpart_ref,
    inner_ref,
    dq_ref,
    dk_ref,
    dv_ref,
):
    head = pl.program_id(0)
    live = live_ref[0]
    scale = 1.0 / math.sqrt(HD)
    keys = kl_ref[...]
    values = vl_ref[...]
    rows = 256
    place = lax.broadcasted_iota(jnp.int32, (SEQ_LEN, rows), 0)
    for part in range(SEQ_LEN // rows):
        here = pl.ds(part * rows, rows)
        queries = ql_ref[here, :]
        incoming = do_ref[here, :]
        scores = dot_of(keys, queries, 1, 1) * scale
        scores = jnp.where(place < live, scores, masked_score)
        top = jnp.max(scores, axis=0, keepdims=True)
        shifted = jnp.exp(scores - top)
        total = jnp.sum(shifted, axis=0, keepdims=True)
        probs = shifted * (1.0 / total)
        dv = dot_of(probs.astype(BF16), incoming, 1, 0)
        probs_cot = dot_of(values, incoming, 1, 1)
        weighted = probs * probs_cot
        centre = jnp.sum(weighted, axis=0, keepdims=True)
        raw = ((weighted - probs * centre) * scale).astype(BF16)
        dk = dot_of(raw, queries, 1, 0)
        dq_ref[here, :] = dot_of(raw, keys, 0, 0)
        if part == 0:
            dv_ref[...] = dv
            dk_ref[...] = dk
        else:
            dv_ref[...] += dv
            dk_ref[...] += dk
    cosine = cos_ref[...]
    sine = -sin_ref[...]

    def back(values, gain, rotated_cot):
        incoming = turn(rotated_cot, cosine, sine)
        inverse = lax.rsqrt(jnp.mean(values * values, axis=1, keepdims=True) + epsilon)
        scaled = incoming * gain
        inner = jnp.mean(scaled * values, axis=1, keepdims=True)
        grad = inverse * scaled - values * (inverse * inverse * inverse * inner)
        part = jnp.sum(incoming * values * inverse, axis=0, keepdims=True)
        return grad.astype(BF16), part, jnp.sum(grad * values, axis=1, keepdims=True)

    qc_ref[...], qpart, inner = back(q_ref[...], qg_ref[...], dq_ref[...])
    kc_ref[...], kpart, key_inner = back(k_ref[...], kg_ref[...], dk_ref[...])
    vc_ref[...] = dv_ref[...].astype(BF16)
    inner += key_inner
    inner += jnp.sum(dv_ref[...] * values.astype(F32), axis=1, keepdims=True)

    @pl.when(head == 0)
    def _():
        qpart_ref[...] = qpart
        kpart_ref[...] = kpart
        inner_ref[...] = inner

    @pl.when(head > 0)
    def _():
        qpart_ref[...] += qpart
        kpart_ref[...] += kpart
        inner_ref[...] += inner


def attend_backward(seq, live, lows, mixture_cot, qkv, tables, query_gain, key_gain, heads):
    width = heads * HD
    block = pl.BlockSpec((SEQ_LEN, HD), lambda h, live: (0, h))

    def pick(offset):
        return pl.BlockSpec((SEQ_LEN, HD), lambda h, live, o=offset: (seq, o + h))

    def whole(shape):
        return pl.BlockSpec(shape, lambda h, live: (0, 0))

    return pl.pallas_call(
        attend_backward_kernel,
        grid_spec=pltpu.PrefetchScalarGridSpec(
            num_scalar_prefetch=1,
            grid=(heads,),
            in_specs=[block] * 4
            + [
                pick(0),
                pick(heads),
                whole((SEQ_LEN, HD)),
                whole((SEQ_LEN, HD)),
                whole((1, HD)),
                whole((1, HD)),
            ],
            out_specs=[block] * 3 + [whole((1, HD))] * 2 + [whole((SEQ_LEN, 1))],
            scratch_shapes=[pltpu.VMEM((SEQ_LEN, HD), F32)] * 3,
        ),
        out_shape=[jax.ShapeDtypeStruct((SEQ_LEN, width), BF16)] * 3
        + [jax.ShapeDtypeStruct((1, HD), F32)] * 2
        + [jax.ShapeDtypeStruct((SEQ_LEN, 1), F32)],
        compiler_params=params("arbitrary"),
        cost_estimate=cost(
            heads * 20 * SEQ_LEN * SEQ_LEN * HD, 24 * SEQ_LEN * width, heads * SEQ_LEN * SEQ_LEN
        ),
        name="attend_backward",
    )(live, *lows, mixture_cot, qkv, qkv, tables[0], tables[1], query_gain, key_gain)


def compact_kernel(start_ref, where_ref, pos_ref, source_ref, *outs):
    group, groups = pl.program_id(0), pl.num_programs(0)
    row_of = lax.broadcasted_iota(jnp.int32, (WINDOW, BLOCK), 0)
    for out in outs:
        out[...] = jnp.zeros_like(out)
    for number in range(source_ref.shape[1] // BLOCK):
        here = slice(number * BLOCK, (number + 1) * BLOCK)
        for expert, out in enumerate(outs):
            start = pl.multiple_of(start_ref[expert * groups + group, number], EDGE)
            place = pos_ref[expert, 0, :, here]
            choice = jnp.where(row_of + start == place, 1.0, 0.0).astype(BF16)
            rows = dot_of(choice, source_ref[0, here, :], 1, 0)
            out[pl.ds(start, WINDOW), :] += rows.astype(BF16)


def compact(starts, where, pos_row, source, groups, cols):
    tokens, width = source.shape[1:]
    count = pos_row.shape[0] // groups
    return pl.pallas_call(
        compact_kernel,
        grid_spec=pltpu.PrefetchScalarGridSpec(
            num_scalar_prefetch=2,
            grid=(groups, cols),
            in_specs=[
                pl.BlockSpec((count, 1, 1, tokens), lambda q, j, s, w: (0, q, 0, 0)),
                pl.BlockSpec(
                    (1, tokens, width), lambda q, j, s, w: ((w[0] ^ q) * cols + j, 0, 0)
                ),
            ],
            out_specs=[pl.BlockSpec((CAP, width), lambda q, j, s, w: (q, j))] * count,
        ),
        out_shape=[jax.ShapeDtypeStruct((groups * CAP, cols * width), BF16)] * count,
        compiler_params=params("arbitrary", "arbitrary"),
        cost_estimate=cost(
            count * groups * cols * 2 * tokens * WINDOW * width * 2,
            groups * cols * 2 * width * (tokens + count * CAP),
        ),
        name="compact",
    )(starts, where, pos_row.reshape(count, groups, 1, tokens), source)


def compact_scalars_kernel(start_ref, pos_ref, *refs):
    count = len(refs) // 2
    group = pl.program_id(0)
    row_of = lax.broadcasted_iota(jnp.int32, (WINDOW, BLOCK), 0)
    for number in range(count):
        refs[count + number][...] = jnp.zeros_like(refs[count + number])
    for number in range(pos_ref.shape[2] // BLOCK):
        start = pl.multiple_of(start_ref[group, number], EDGE)
        here = slice(number * BLOCK, (number + 1) * BLOCK)
        choice = row_of + start == pos_ref[0, :, here]
        for source, out in zip(refs[:count], refs[count:]):
            picked = jnp.sum(jnp.where(choice, source[0, :, here], 0.0), axis=1, keepdims=True)
            out[pl.ds(start, WINDOW), :] += picked


def compact_scalars(starts, pos_row, sources):
    groups, _, tokens = pos_row.shape
    block = pl.BlockSpec((1, 1, tokens), lambda q, s: (q, 0, 0))
    return pl.pallas_call(
        compact_scalars_kernel,
        grid_spec=pltpu.PrefetchScalarGridSpec(
            num_scalar_prefetch=1,
            grid=(groups,),
            in_specs=[block] * (1 + len(sources)),
            out_specs=[pl.BlockSpec((CAP, 1), lambda q, s: (q, 0))] * len(sources),
        ),
        out_shape=[jax.ShapeDtypeStruct((groups * CAP, 1), F32)] * len(sources),
        compiler_params=params("arbitrary"),
        cost_estimate=cost(0, 4 * groups * CAP * 128 * len(sources)),
        name="compact_scalars",
    )(starts, pos_row, *sources)


def expand_scalars_kernel(start_ref, pos_ref, *refs):
    count = len(refs) // 2
    group = pl.program_id(0)
    row_of = lax.broadcasted_iota(jnp.int32, (WINDOW, BLOCK), 0)
    for number in range(pos_ref.shape[2] // BLOCK):
        start = pl.multiple_of(start_ref[group, number], EDGE)
        here = slice(number * BLOCK, (number + 1) * BLOCK)
        choice = row_of + start == pos_ref[0, :, here]
        for source, out in zip(refs[:count], refs[count:]):
            held = source[pl.ds(start, WINDOW), :]
            out[0, :, here] = jnp.sum(jnp.where(choice, held, 0.0), axis=0, keepdims=True)


def expand_scalars(starts, pos_row, sources):
    groups, _, tokens = pos_row.shape
    block = pl.BlockSpec((1, 1, tokens), lambda q, s: (q, 0, 0))
    return pl.pallas_call(
        expand_scalars_kernel,
        grid_spec=pltpu.PrefetchScalarGridSpec(
            num_scalar_prefetch=1,
            grid=(groups,),
            in_specs=[block] + [pl.BlockSpec((CAP, 1), lambda q, s: (q, 0))] * len(sources),
            out_specs=[block] * len(sources),
        ),
        out_shape=[jax.ShapeDtypeStruct((groups, 1, tokens), F32)] * len(sources),
        compiler_params=params("arbitrary"),
        cost_estimate=cost(0, 4 * groups * CAP * 128 * len(sources)),
        name="expand_scalars",
    )(starts, pos_row, *sources)


def expand_kernel(sizes, count, start_ref, where_ref, pos_ref, *refs):
    group, groups = pl.program_id(0), pl.num_programs(0)
    sides = len(refs) // (count + len(sizes))
    sources, outs = refs[: count * sides], refs[count * sides :]
    column_of = lax.broadcasted_iota(jnp.int32, (BLOCK, WINDOW), 1)
    number = 0
    for part, size in enumerate(sizes):
        for step in range(size // BLOCK):
            totals = [None] * sides
            for expert in range(count):
                start = pl.multiple_of(start_ref[expert * groups + group, number], EDGE)
                place = pos_ref[expert, 0, number * BLOCK : (number + 1) * BLOCK, :]
                choice = jnp.where(column_of + start == place, 1.0, 0.0).astype(BF16)
                for side in range(sides):
                    held = sources[expert * sides + side][pl.ds(start, WINDOW), :]
                    rows = dot_of(choice, held, 1, 0)
                    totals[side] = rows if totals[side] is None else totals[side] + rows
            here = slice(step * BLOCK, (step + 1) * BLOCK)
            for side in range(sides):
                outs[part * sides + side][0, 0, here, :] = totals[side].astype(BF16)
            number += 1


def expand(starts, where, pos_col, sources, sizes, groups, cols):
    width = sources[0].shape[1] // cols
    tokens = sum(sizes)
    count = len(sources)

    def side(odd):
        return pl.BlockSpec((CAP, width), lambda q, j, s, w: (q, w[1] ^ (2 * j + odd)))

    outs = pl.pallas_call(
        functools.partial(expand_kernel, sizes, count),
        grid_spec=pltpu.PrefetchScalarGridSpec(
            num_scalar_prefetch=2,
            grid=(groups, cols // 2),
            in_specs=[pl.BlockSpec((count, 1, tokens, 1), lambda q, j, s, w: (0, q, 0, 0))]
            + [side(0), side(1)] * count,
            out_specs=[
                pl.BlockSpec((1, 1, size, width), lambda q, j, s, w: (q, j, 0, 0))
                for size in sizes
                for _ in range(2)
            ],
        ),
        out_shape=[
            jax.ShapeDtypeStruct((groups, cols // 2, size, width), BF16)
            for size in sizes
            for _ in range(2)
        ],
        compiler_params=params("arbitrary", "arbitrary"),
        cost_estimate=cost(
            4 * count * groups * cols * tokens * WINDOW * width,
            groups * cols * width * (2 * tokens + 2 * count * CAP),
        ),
        name="expand",
    )(
        starts,
        where,
        pos_col.reshape(count, groups, tokens, 1),
        *[source for source in sources for _ in range(2)],
    )
    return list(zip(outs[::2], outs[1::2]))


def expand_all(starts, where, pos_col, sources, groups, cols):
    width = sources[0].shape[1] // cols
    tokens = pos_col.shape[1]
    count = len(sources)
    return pl.pallas_call(
        functools.partial(expand_kernel, [tokens], count),
        grid_spec=pltpu.PrefetchScalarGridSpec(
            num_scalar_prefetch=2,
            grid=(groups, cols),
            in_specs=[pl.BlockSpec((count, 1, tokens, 1), lambda q, j, s, w: (0, q, 0, 0))]
            + [pl.BlockSpec((CAP, width), lambda q, j, s, w: (q, j))] * count,
            out_specs=pl.BlockSpec((1, 1, tokens, width), lambda q, j, s, w: (w[0] ^ q, j, 0, 0)),
        ),
        out_shape=jax.ShapeDtypeStruct((groups, cols, tokens, width), BF16),
        compiler_params=params("arbitrary", "arbitrary"),
        cost_estimate=cost(
            4 * count * groups * cols * tokens * WINDOW * width,
            groups * cols * width * (2 * tokens + 2 * count * CAP),
        ),
        name="expand_all",
    )(starts, where, pos_col.reshape(count, groups, tokens, 1), *sources)


def pack_kernel(where_ref, gate_ref, up_ref, down_ref, out_ref):
    hidden = gate_ref.shape[2]
    out_ref[0, :, :hidden] = gate_ref[0].astype(BF16)
    out_ref[0, :, hidden : 2 * hidden] = up_ref[0].astype(BF16)
    out_ref[0, :, 2 * hidden :] = down_ref[0].T.astype(BF16)


def pack_weights(where, gate, up, down, each):
    experts, depth, hidden = gate.shape

    def pick(shape):
        return pl.BlockSpec(shape, lambda q, w: ((w[0] ^ (q // each)) * each + q % each, 0, 0))

    return pl.pallas_call(
        pack_kernel,
        grid_spec=pltpu.PrefetchScalarGridSpec(
            num_scalar_prefetch=1,
            grid=(experts,),
            in_specs=[pick((1, depth, hidden)), pick((1, depth, hidden)), pick((1, hidden, depth))],
            out_specs=pl.BlockSpec((1, depth, 3 * hidden), lambda q, w: (q, 0, 0)),
        ),
        out_shape=jax.ShapeDtypeStruct((experts, depth, 3 * hidden), BF16),
        compiler_params=params("arbitrary"),
        cost_estimate=cost(0, 18 * experts * depth * hidden),
        name="pack_weights",
    )(where, gate, up, down)


def unpack_kernel(where_ref, *refs):
    sources, (gate_ref, up_ref, down_ref) = refs[:-3], refs[-3:]
    hidden = gate_ref.shape[2]
    for number, source in enumerate(sources):

        @pl.when(pl.program_id(0) == number)
        def _(source=source):
            gate_ref[0] = source[:, :hidden].astype(F32)
            up_ref[0] = source[:, hidden : 2 * hidden].astype(F32)
            down_ref[0] = source[:, 2 * hidden :].astype(F32).T


def unpack_grads(where, sources, each):
    count = len(sources)
    depth, wide = sources[0].shape
    hidden = wide // 3

    def pick(shape):
        return pl.BlockSpec(shape, lambda q, w: ((w[0] ^ (q // each)) * each + q % each, 0, 0))

    shapes = [(count, depth, hidden), (count, depth, hidden), (count, hidden, depth)]
    return pl.pallas_call(
        unpack_kernel,
        grid_spec=pltpu.PrefetchScalarGridSpec(
            num_scalar_prefetch=1,
            grid=(count,),
            in_specs=[pl.BlockSpec((depth, wide), lambda q, w: (0, 0))] * count,
            out_specs=[pick((1,) + shape[1:]) for shape in shapes],
        ),
        out_shape=[jax.ShapeDtypeStruct(shape, F32) for shape in shapes],
        compiler_params=params("arbitrary"),
        cost_estimate=cost(0, 18 * count * depth * hidden),
        name="unpack_grads",
    )(where, *sources)


def expert_kernel(count, hidden, row_ref, x_ref, m_ref, gate_ref, scale_ref, *refs):
    pieces = refs[:count]
    rows_ref, pre_ref, act_ref, cot_ref, inner_ref, result_ref, held, sems = refs[count:]
    depth = pieces[0].shape[0]

    @pl.when(pl.program_id(0) == 0)
    def _():
        copies = []
        for number, piece in enumerate(pieces):
            place = pl.ds(pl.multiple_of(row_ref[number] * depth, depth), depth)
            copies.append(pltpu.make_async_copy(piece, held.at[place, :], sems.at[number]))
        for copy in copies:
            copy.start()
        for copy in copies:
            copy.wait()

    gate = gate_ref[...]
    scale = scale_ref[...]
    wide = EXPERT_WIDE
    cot_ref[...] = jnp.zeros_like(cot_ref)
    inner_ref[...] = jnp.zeros_like(inner_ref)

    @pl.loop(0, hidden // wide, unroll=EXPERT_UNROLL)
    def _(step):
        first = pl.multiple_of(step * wide, wide)
        gate_pre = dot_of(x_ref[...], held[:, pl.ds(first, wide)], 1, 0) * scale
        up_pre = dot_of(x_ref[...], held[:, pl.ds(hidden + first, wide)], 1, 0) * scale
        back = dot_of(m_ref[...], held[:, pl.ds(2 * hidden + first, wide)], 1, 0)
        squash = 1.0 / (1.0 + jnp.exp(-gate_pre))
        silu = gate_pre * squash
        active = silu * up_pre
        cot_ref[...] += jnp.sum(active.astype(BF16).astype(F32) * back, axis=1, keepdims=True)
        act_ref[:, pl.ds(first, wide)] = (active * gate).astype(BF16)
        back = back * gate
        slope = squash * (1.0 + gate_pre * (1.0 - squash))
        gate_cot = back * up_pre * slope
        up_cot = back * silu
        inner_ref[...] += jnp.sum(gate_cot * gate_pre + up_cot * up_pre, axis=1, keepdims=True)
        pre_ref[:, pl.ds(first, wide)] = (gate_cot * scale).astype(BF16)
        pre_ref[:, pl.ds(hidden + first, wide)] = (up_cot * scale).astype(BF16)

    @pl.loop(0, held.shape[0] // wide, unroll=EXPERT_UNROLL)
    def _(step):
        first = pl.multiple_of(step * wide, wide)
        here = pl.ds(first, wide)
        rows_ref[:, here] = dot_of(pre_ref[...], held[here, : 2 * hidden], 1, 1).astype(BF16)
        result_ref[:, here] = dot_of(act_ref[...], held[here, 2 * hidden :], 1, 1).astype(BF16)


def expert_step(row_numbers, x, m, gate, scale, pieces):
    total, wide = x.shape
    hidden = pieces[0].shape[1] // 3
    count = len(pieces)

    def tile(columns):
        return pl.BlockSpec((TILE, columns), lambda i, r: (i, 0))

    return pl.pallas_call(
        functools.partial(expert_kernel, count, hidden),
        grid_spec=pltpu.PrefetchScalarGridSpec(
            num_scalar_prefetch=1,
            grid=(total // TILE,),
            in_specs=[tile(wide), tile(wide), tile(1), tile(1)]
            + [pl.BlockSpec(memory_space=ANY)] * count,
            out_specs=[tile(wide), tile(2 * hidden), tile(hidden), tile(1), tile(1), tile(wide)],
            scratch_shapes=[
                pltpu.VMEM((wide, 3 * hidden), BF16),
                pltpu.SemaphoreType.DMA((count,)),
            ],
        ),
        out_shape=[
            jax.ShapeDtypeStruct((total, wide), BF16),
            jax.ShapeDtypeStruct((total, 2 * hidden), BF16),
            jax.ShapeDtypeStruct((total, hidden), BF16),
            jax.ShapeDtypeStruct((total, 1), F32),
            jax.ShapeDtypeStruct((total, 1), F32),
            jax.ShapeDtypeStruct((total, wide), BF16),
        ],
        compiler_params=params("arbitrary"),
        cost_estimate=cost(
            2 * total * wide * hidden * 6, 2 * total * (4 * wide + 3 * hidden), total * hidden
        ),
        name="expert_step",
    )(row_numbers, x, m, gate, scale, *pieces)


def weight_grad_kernel(mids, place_ref, x_ref, m_ref, pre_ref, act_ref, out_ref, turned_ref):
    wide = GRAD_WIDE
    first = pre_ref.shape[1]
    depth = x_ref.shape[1] // mids
    turned_ref[0] = x_ref[...].T
    turned_ref[1] = m_ref[...].T
    mid = place_ref[place_ref.shape[0] - 1]

    def put(grad, here):
        for number in range(mids):
            block = grad[number * depth : (number + 1) * depth].astype(BF16)
            out_ref[0, number ^ mid, 0, :, here] = block

    @pl.loop(0, first // wide, unroll=GRAD_UNROLL)
    def _(step):
        here = pl.ds(pl.multiple_of(step * wide, wide), wide)
        put(dot_of(turned_ref[0], pre_ref[:, here], 1, 0), here)

    @pl.loop(0, act_ref.shape[1] // wide, unroll=GRAD_UNROLL)
    def _(step):
        here = pl.ds(pl.multiple_of(step * wide, wide), wide)
        there = pl.ds(pl.multiple_of(first + step * wide, wide), wide)
        put(dot_of(turned_ref[1], act_ref[:, here], 1, 0), there)


def weight_grads(places, x, m, pre, act, depth, groups, mids, high):
    total = x.shape[0]
    wide = pre.shape[1] + act.shape[1]

    def column(first):
        return pl.BlockSpec((total, mids * depth), lambda f, h, r: (0, r[first + f * high + h]))

    def whole(array):
        return pl.BlockSpec(array.shape, lambda f, h, r: (0, 0), pipeline_mode=pl.Buffered(1))

    return pl.pallas_call(
        functools.partial(weight_grad_kernel, mids),
        grid_spec=pltpu.PrefetchScalarGridSpec(
            num_scalar_prefetch=1,
            grid=(groups, high),
            in_specs=[column(0), column(groups * high), whole(pre), whole(act)],
            out_specs=pl.BlockSpec(
                (1, mids, 1, depth, wide), lambda f, h, r: (f, 0, h, 0, 0)
            ),
            scratch_shapes=[pltpu.VMEM((2, mids * depth, total), BF16)],
        ),
        out_shape=jax.ShapeDtypeStruct((groups, mids, high, depth, wide), BF16),
        compiler_params=params("arbitrary", "arbitrary"),
        cost_estimate=cost(
            2 * total * depth * groups * mids * high * wide,
            2 * total * (2 * depth * groups * mids * high + wide),
        ),
        name="weight_grads",
    )(places, x, m, pre, act)


def bits_of(size):
    return [1 << n for n in range(size.bit_length() - 1)]


def swap(values, axis, bit):
    size = lax.axis_size(axis) if isinstance(axis, str) else math.prod(map(lax.axis_size, axis))
    return lax.ppermute(values, axis, [(n, n ^ bit) for n in range(size)])


class Flow:
    def __init__(self, steps):
        self.steps = steps
        self.result = None
        self.sends = next(steps)

    def advance(self, got):
        try:
            self.sends = self.steps.send(got)
        except StopIteration as stop:
            self.sends = None
            self.result = stop.value

    def step(self, count=1):
        for _ in range(count):
            if self.sends is not None:
                self.advance([swap(*send) for send in self.sends])
        return self

    def finish(self):
        while self.sends is not None:
            self.step()
        return self.result

    def holds(self):
        return self.result if self.sends is None else [send[0] for send in self.sends]

    def replace(self, arrays):
        if self.sends is None:
            self.result = arrays
        else:
            self.sends = [(array, *send[1:]) for array, send in zip(arrays, self.sends)]


def stage(live, flows=(), work=(), sync=()):
    flows = [flow for flow in flows if flow.sends is not None]
    got = [[swap(*send) for send in flow.sends] for flow in flows]
    done = [each() for each in work]
    held = [flow.holds() for flow in sync]
    got, done, held, kept = lax.optimization_barrier((got, done, held, dict(live)))
    live.update(kept)
    for flow, arrays in zip(flows, got):
        flow.advance(arrays)
    for flow, arrays in zip(sync, held):
        flow.replace(arrays)
    return done


def spread_steps(values, axis, bits):
    blocks = {0: values}
    for bit in bits:
        places = sorted(blocks)
        got = yield [(blocks[place], axis, bit) for place in places]
        blocks.update({place | bit: block for place, block in zip(places, got)})
    return [blocks[place] for place in sorted(blocks)]


def spread_rows_steps(values, row_bits, strides):
    held = values[None]
    places = [0]
    for axis, bit in row_bits:
        (got,) = yield [(held, axis, bit)]
        held = jnp.concatenate([held, got], axis=0)
        places += [place | (bit * strides[axis]) for place in places]
    return jnp.stack([held[places.index(place)] for place in range(len(places))])


def spread_cube_steps(values, groups, cols):
    held = values[None]
    for axis, bits in (("lo", bits_of(groups)), ("col", bits_of(cols))):
        for bit in bits:
            (got,) = yield [(held, axis, bit)]
            held = jnp.concatenate([held, got], axis=0)
    return jnp.swapaxes(held.reshape((cols, groups) + values.shape), 0, 1)


def col_reduce_steps(blocks, cols):
    held = dict(enumerate(blocks))
    for bit in bits_of(cols):
        away = [place for place in sorted(held) if place & bit]
        (got,) = yield [(jnp.stack([held[place].astype(BF16) for place in away]), "col", bit)]
        held = {
            place & ~bit: held[place & ~bit] + got[number].astype(F32)
            for number, place in enumerate(away)
        }
    return held[0]


def total_steps(values, axes):
    for axis in axes:
        size = math.prod(map(lax.axis_size, axis))
        got = yield [(values, axis, place) for place in range(1, size)]
        values = values + sum(got)
    return values


def row_reduce_steps(grads, groups, mids, high):
    names = [("lo", bit) for bit in reversed(bits_of(groups))]
    names += [("mid", bit) for bit in reversed(bits_of(mids))]
    names += [("hi", bit) for bit in reversed(bits_of(high))]
    grads = grads.reshape((2,) * len(names) + grads.shape[3:])
    half = grads.shape[-1] // 2
    held = []
    for number in range(2):
        order = [name for name in names if name[0] != "hi"][:: 1 if number else -1]
        order += [name for name in reversed(names) if name[0] == "hi"]
        held.append((grads[..., number * half : (number + 1) * half], names, order))
    for step in range(len(names)):
        sends, rest = [], []
        for array, left, order in held:
            name = order[step]
            axis = left.index(name)
            away = 0 if name[0] == "lo" else 1
            sends.append((lax.index_in_dim(array, away, axis, False).astype(BF16), *name))
            kept = lax.index_in_dim(array, 1 - away, axis, False)
            rest.append((kept, [other for other in left if other != name], order))
        got = yield sends
        held = [
            (kept.astype(F32) + more.astype(F32), left, order)
            for (kept, left, order), more in zip(rest, got)
        ]
    return jnp.concatenate([array for array, _, _ in held], axis=1)


def links_of(groups, cols):
    return [("col", bit) for bit in bits_of(cols)[1:]] + [("lo", bit) for bit in bits_of(groups)]


def turned(links, number):
    number %= len(links)
    return links[number:] + links[:number]


def reduce_steps(parts, groups, cols):
    links = links_of(groups, cols)
    got = yield [(away, "col", 1) for _, away in parts]
    held = []
    for number, (keep, _) in enumerate(parts):
        shape = (2,) * len(links) + keep.shape[2:]
        names = [("lo", bit) for bit in reversed(bits_of(groups))]
        names += [("col", bit) for bit in reversed(bits_of(cols)[1:])]
        held.append((keep.reshape(shape), got[number].reshape(shape), names))
    for step in range(len(links)):
        sends, rest = [], []
        for number, (keep, more, names) in enumerate(held):
            link = turned(links, number)[step]
            axis = names.index(link)

            def half(place):
                total = lax.index_in_dim(keep, place, axis, False).astype(F32)
                return total + lax.index_in_dim(more, place, axis, False).astype(F32)

            sends.append((half(1).astype(BF16), *link))
            kept = half(0)
            rest.append(
                (
                    kept if step + 1 == len(links) else kept.astype(BF16),
                    [name for name in names if name != link],
                )
            )
        got = yield sends
        held = [(keep, more, names) for (keep, names), more in zip(rest, got)]
    return jnp.concatenate([keep.astype(F32) + more.astype(F32) for keep, more, _ in held], axis=0)


def part_sizes(tokens, count):
    whole = tokens // BLOCK
    return [BLOCK * ((whole + count - 1 - n) // count) for n in range(count)]


def expert_weight_steps(piece, far, bits):
    if far:
        (piece,) = yield [(piece, "lo", far)]
    held = {(): piece}
    fresh = [()]
    while True:
        ways = [
            (place, number)
            for place in fresh
            for number in range(place[-1] + 1 if place else 0, len(bits))
        ]
        if not ways:
            return held
        got = yield [(held[place], *bits[number]) for place, number in ways]
        fresh = [place + (number,) for place, number in ways]
        held.update(zip(fresh, got))


def expert_grad_steps(blocks, far, bits):
    for number in reversed(range(len(bits))):
        half = blocks.shape[0] // 2
        (got,) = yield [(blocks[half:], *bits[number])]
        blocks = blocks[:half].astype(F32) + got.astype(F32)
        if number or far:
            blocks = blocks.astype(BF16)
    total = blocks[0]
    if far:
        (total,) = yield [(total, "lo", far)]
    return total


def per_device(
    hidden_in,
    lengths,
    routes,
    attn_gain,
    query_gain,
    key_gain,
    query_weight,
    key_weight,
    value_weight,
    out_weight,
    moe_gain,
    router,
    gate_weight,
    up_weight,
    down_weight,
    cotangent,
):
    tok_rows, width = hidden_in.shape
    cols = lax.axis_size("col")
    groups = lax.axis_size("lo")
    high = lax.axis_size("hi")
    mids = lax.axis_size("mid")
    col = lax.axis_index("col")
    lo = lax.axis_index("lo")
    hi = lax.axis_index("hi")
    mid = lax.axis_index("mid")
    row = (hi * groups + lo) * mids + mid
    where = jnp.stack([lo, col])
    heads = width // HD
    seqs = lengths.shape[0]
    depth = gate_weight.shape[1]
    each = gate_weight.shape[0] // groups
    cube = ("lo", "col")
    rows_axes = ("hi", "lo", "mid")
    strides = {"hi": groups * mids, "lo": mids, "mid": 1}
    seq_rows = [slice(s * SEQ_LEN, (s + 1) * SEQ_LEN) for s in range(seqs)]
    links = links_of(groups, cols)
    col_bits = list(reversed(bits_of(cols)))
    hi_bits = [("hi", bit) for bit in bits_of(high)]
    mid_bits = [("mid", bit) for bit in bits_of(mids)]
    row_bits = hi_bits + [("lo", bit) for bit in bits_of(groups)] + mid_bits
    far_bits = hi_bits + mid_bits
    live = {}

    def row_of_set(place, far):
        other = row ^ (far * mids)
        for number in place:
            axis, bit = far_bits[number]
            other = other ^ (bit * strides[axis])
        return other

    hidden_flow = Flow(spread_steps(hidden_in, "col", col_bits))
    gain_flow = Flow(spread_steps(attn_gain, "col", col_bits))
    routes_flow = Flow(spread_steps(routes.T, "lo", bits_of(groups)))
    router_flow = Flow(spread_rows_steps(router.T.astype(BF16), row_bits, strides))
    out_flow = Flow(spread_rows_steps(out_weight.T.astype(BF16), row_bits, strides))
    qkv_local = jnp.concatenate([query_weight, key_weight, value_weight], axis=1).astype(BF16)
    qkv_full = lax.all_gather(qkv_local, rows_axes, axis=0, tiled=True)
    live_key = jnp.arange(SEQ_LEN)[None, :] < lengths[:, None]
    out_cot = jnp.where(live_key.reshape(tok_rows, 1), cotangent, jnp.zeros_like(cotangent))
    packed = pack_weights(where, gate_weight, up_weight, down_weight, each)
    units = [(expert, far) for expert in range(each) for far in range(groups)]
    live["packed"] = packed

    def rotary_tables():
        places = jnp.arange(SEQ_LEN).astype(F32)
        powers = jnp.arange(HD // 2).astype(F32) * (2.0 / HD)
        angles = places[:, None] * jnp.exp(-powers * math.log(rope_base))[None, :]
        cosine, sine = jnp.cos(angles), jnp.sin(angles)
        return (
            jnp.concatenate([cosine, cosine], axis=1),
            jnp.concatenate([-sine, sine], axis=1),
        )

    live["out_cot"] = out_cot
    (tables,) = stage(
        live,
        [hidden_flow, gain_flow, routes_flow, router_flow, out_flow],
        [rotary_tables],
    )

    hidden = hidden_in.astype(F32)

    def norm_attn():
        blocks = hidden_flow.finish()
        gains = gain_flow.finish()
        square = sum(jnp.sum(jnp.square(block.astype(F32)), axis=1) for block in blocks)
        inverse = lax.rsqrt(square / D + epsilon)[:, None]
        normed = jnp.zeros((tok_rows, D), BF16)
        for place, (block, gain) in enumerate(zip(blocks, gains)):
            piece = (block.astype(F32) * inverse * gain).astype(BF16)
            normed = lax.dynamic_update_slice_in_dim(normed, piece, (col ^ place) * width, 1)
        return normed, inverse

    def routing():
        rel = jnp.stack(routes_flow.finish())
        named = jnp.any(rel[:, :, None, :] == jnp.arange(EXPERTS)[None, None, :, None], axis=1)
        first = (col * groups + lo) * each
        member = lax.dynamic_slice_in_dim(named, first, each, 1)
        member = jnp.swapaxes(member, 0, 1).reshape(each * groups, tok_rows)
        count = member.astype(jnp.int32)
        rank = jnp.cumsum(count, axis=1) - count
        pos = jnp.where(member, rank, -(1 << 20))
        starts = jnp.minimum(rank[:, ::BLOCK] // EDGE * EDGE, CAP - WINDOW)
        return named, starts, pos[:, None, :], pos[:, :, None]

    live["qkv_full"] = qkv_full
    ((live["normed_attn"], attn_inverse),) = stage(live, [router_flow, out_flow], [norm_attn])
    weight_flows = {}

    def start_weights(expert):
        for far in range(groups):
            weight_flows[expert, far] = Flow(
                expert_weight_steps(live["packed"][far * each + expert], far, far_bits)
            )

    start_weights(0)
    moe_cot = lax.all_gather(live["out_cot"], cube, axis=0, tiled=False)
    hidden_blocks = hidden_flow.result
    query_scale, key_scale = query_gain[None, :], key_gain[None, :]

    def attend(s):
        return attend_forward(
            s, lengths[s : s + 1], live["qkv"], tables, query_scale, key_scale, heads
        )

    def project_and_attend():
        live["qkv"] = dot_of(live["normed_attn"], live["qkv_full"], 1, 0)
        return attend(0)

    firsts = [weight_flows[0, far] for far in range(1, groups)]
    (first_seq,) = stage(live, [router_flow, out_flow], [project_and_attend])
    for expert in range(1, each):
        start_weights(expert)
    seconds = [weight_flows[unit] for unit in units if unit[0] == 1]
    named, starts, pos_row, pos_col = routing()

    span = width // depth

    def col_rows(blocks, place, axis):
        first = (col ^ place) * span
        return jnp.concatenate(
            [
                lax.dynamic_index_in_dim(blocks, (first + n) ^ row, 0, False)
                for n in range(span)
            ],
            axis=axis,
        )

    out_spread = out_flow.finish()
    out_rel = jnp.concatenate([col_rows(out_spread, place, 0) for place in range(cols)], axis=0)
    router_rows = col_rows(router_flow.finish(), 0, 1)

    def branch(mixture):
        partial = dot_of(mixture, out_rel, 1, 1)
        blocks = [partial[:, n * width : (n + 1) * width] for n in range(cols)]
        return Flow(col_reduce_steps(blocks, cols)).finish()

    def attend_rest():
        outs = [first_seq]
        sums = [branch(first_seq[0])]
        for s in range(1, seqs):
            outs.append(attend(s))
            sums.append(branch(outs[s][0]))
        return outs, sums

    ((attended, branches),) = stage(live, [weight_flows[0, 0]] + firsts, [attend_rest])
    middle = hidden + jnp.concatenate(branches, axis=0)
    live["scaled_rows"] = (middle * moe_gain).astype(BF16)
    scaled_rows = live["scaled_rows"]
    moe_in = lax.all_gather(scaled_rows, cube, axis=0, tiled=False)
    square = jnp.sum(middle * middle, axis=1)[None, :]
    stat = jnp.concatenate([dot_of(router_rows, scaled_rows, 1, 1), square], axis=0)
    stat_flow = Flow(spread_cube_steps(stat, groups, cols))
    stage(live, [stat_flow], sync=[weight_flows[0, 0]] + firsts + seconds)
    (live["cot_rows"],) = stage(
        live,
        [stat_flow, weight_flows[0, 0]] + firsts + seconds[1:],
        [lambda: compact(starts, where, pos_row, moe_cot, groups, cols)],
    )
    stage(live, [stat_flow] + firsts)
    stat = stat_flow.finish()

    stat = jnp.sum(stat, axis=1)
    moe_inverse = lax.rsqrt(stat[:, EXPERTS] / D + epsilon)
    all_logits = stat[:, :EXPERTS] * moe_inverse[:, None, :]
    logits = jnp.where(named, all_logits, masked_score)
    shifted = jnp.where(named, jnp.exp(logits - jnp.max(logits, axis=1, keepdims=True)), 0.0)
    gates = shifted / jnp.sum(shifted, axis=1, keepdims=True)
    own_gate = lax.dynamic_slice_in_dim(gates, (col * groups + lo) * each, each, 1)
    own_gate = jnp.swapaxes(own_gate, 0, 1).reshape(each * groups, 1, tok_rows)
    row_gate, row_scale = compact_scalars(
        starts, pos_row, (own_gate, jnp.tile(moe_inverse, (each, 1))[:, None, :])
    )
    total_rows = groups * CAP

    live["moe_rows"] = compact(starts, where, pos_row, moe_in, groups, cols)

    def run_expert(expert):
        pieces, row_numbers = [], []
        for far in range(groups):
            for place, piece in weight_flows[expert, far].finish().items():
                pieces.append(piece)
                row_numbers.append(row_of_set(place, far))
        here = slice(expert * total_rows, (expert + 1) * total_rows)
        return expert_step(
            jnp.stack(row_numbers),
            live["moe_rows"][expert],
            live["cot_rows"][expert],
            row_gate[here],
            row_scale[here],
            pieces,
        )

    blocks_here = [
        (hi ^ above) * groups + (lo ^ far)
        for far in reversed(range(groups))
        for above in range(high)
    ]
    grad_places = jnp.stack(blocks_here + blocks_here + [mid])
    grad_flows = {}

    def start_grads(expert, outs):
        grads = weight_grads(
            grad_places,
            live["moe_rows"][expert],
            live["cot_rows"][expert],
            outs[1],
            outs[2],
            depth,
            groups,
            mids,
            high,
        )
        return grads.reshape((groups, mids * high) + grads.shape[3:])

    def grad_flow(expert, grads):
        for number, far in enumerate(reversed(range(groups))):
            grad_flows[expert, far] = Flow(expert_grad_steps(grads[number], far, far_bits))

    def running():
        return list(grad_flows.values())

    ran = []
    for expert in range(each):
        others = [flow for (number, _), flow in weight_flows.items() if number > expert]
        (outs,) = stage(
            live,
            others + running()[:1],
            [functools.partial(run_expert, expert)],
            sync=running()[1:],
        )
        ran.append(outs)
        if expert + 1 < each:
            (grads,) = stage(live, others, [functools.partial(start_grads, expert, outs)])
            grad_flow(expert, grads)
    early = running()
    live["result"] = [outs[5] for outs in ran]
    last = ran[-1]
    gate_cot = jnp.concatenate([outs[3] for outs in ran], axis=0)
    row_inner = jnp.concatenate([outs[4] for outs in ran], axis=0)
    sizes = part_sizes(tok_rows, len(links))
    live["scalars"] = (gate_cot, row_inner)
    (rows_parts,) = stage(
        live,
        [],
        [
            lambda: expand(
                starts, where, pos_col, [outs[0] for outs in ran], sizes, groups, cols
            )
        ],
    )
    gate_cot, row_inner = expand_scalars(starts, pos_row, live.pop("scalars"))
    gate_cot = gate_cot.reshape(each, groups, tok_rows)
    row_inner = jnp.sum(row_inner.reshape(each, groups, tok_rows), axis=0)[None]
    scalars = jnp.concatenate([gate_cot, row_inner], axis=0)
    scalars = scalars.reshape((each + 1) * groups, tok_rows)
    scalar_flow = Flow(spread_cube_steps(scalars, groups, cols))
    moe_in_flow = Flow(reduce_steps(rows_parts, groups, cols))
    (grads,) = stage(
        live,
        [moe_in_flow, scalar_flow] + early,
        [functools.partial(start_grads, each - 1, last)],
    )
    grad_flow(each - 1, grads)
    late = running()[len(early) :]
    scalar_flow.finish()
    (branch_parts,) = stage(
        live,
        [moe_in_flow] + early[1:] + late[:1],
        [lambda: expand_all(starts, where, pos_col, live["result"], groups, cols)],
        sync=[scalar_flow],
    )
    live["moe_branch"] = branch_parts.reshape(groups * cols, tok_rows, width)
    while moe_in_flow.sends is not None:
        stage(live, [moe_in_flow], sync=early + late)
    scalar_all = scalar_flow.finish().reshape(groups, cols, each + 1, groups, tok_rows)
    scalar_all = jnp.stack([scalar_all[place, :, :, place] for place in range(groups)])
    by_expert = jnp.stack(
        [
            ((lo ^ (number // each % groups)) * cols + (col ^ (number // (each * groups)))) * each
            + number % each
            for number in range(EXPERTS)
        ]
    )
    gate_cot = jnp.take(scalar_all[:, :, :each].reshape(EXPERTS, tok_rows), by_expert, axis=0)
    my_gates, my_logits = gates[0], all_logits[0]
    logit_cot = my_gates * (gate_cot - jnp.sum(my_gates * gate_cot, axis=0, keepdims=True))
    inner = jnp.sum(scalar_all[:, :, each], axis=(0, 1)) + jnp.sum(logit_cot * my_logits, axis=0)
    scaled_logit = (logit_cot * moe_inverse[0][None, :]).astype(BF16)
    logit_cot = logit_cot.astype(BF16)
    my_inverse = moe_inverse[0][:, None]

    back = moe_in_flow.finish() + my_inverse * dot_of(logit_cot, router_rows, 0, 0)
    middle_cot = (
        out_cot.astype(F32)
        + back * moe_gain
        - middle * (my_inverse * my_inverse * (inner[:, None] / D))
    )
    cot_flow = Flow(spread_steps(middle_cot.astype(BF16), "col", col_bits))
    router_part, moe_gain_part = stage(
        live,
        [cot_flow] + early[:1],
        [
            lambda: dot_of(scaled_logit, scaled_rows, 1, 0),
            lambda: jnp.sum(back * middle, axis=0)[None],
        ],
    )
    cot_blocks = cot_flow.finish()
    moe_branch = lax.psum_scatter(
        live.pop("moe_branch"), cube, scatter_dimension=0, tiled=True
    )[0]

    cot_all = jnp.concatenate(cot_blocks, axis=1)

    def attend_back(s):
        mixture_cot = dot_of(cot_all[seq_rows[s]], out_rel, 1, 0).astype(BF16)
        *cots, query_part, key_part, token_inner = attend_backward(
            s,
            lengths[s : s + 1],
            attended[s][1:],
            mixture_cot,
            live["qkv"],
            tables,
            query_scale,
            key_scale,
            heads,
        )
        cots = jnp.concatenate(cots, axis=1)
        return cots, query_part, key_part, token_inner[:, 0]

    qkv_rel = jnp.concatenate(
        [
            lax.dynamic_slice_in_dim(live["qkv_full"], (col ^ place) * width, width, 0)
            for place in range(cols)
        ],
        axis=0,
    )
    mixture = jnp.concatenate([outs[0] for outs in attended], axis=0)
    live.update(qkv_rel=qkv_rel, mixture=mixture, cot_all=cot_all)
    done = stage(
        live,
        late,
        [functools.partial(attend_back, s) for s in range(seqs)],
    )
    share = width // (mids * depth)
    cot_places = [((n // share) ^ col) * share + n % share for n in blocks_here]

    def projection_grads():
        cots = jnp.concatenate([outs[0] for outs in done], axis=0)
        grads = weight_grads(
            jnp.stack(blocks_here + cot_places + [mid]),
            live["normed_attn"],
            live["cot_all"],
            cots,
            live["mixture"],
            depth,
            groups,
            mids,
            high,
        )
        return grads, cots

    ((grads, live["qkv_cot"]),) = stage(live, [], [projection_grads])
    qkv_flow = Flow(row_reduce_steps(grads, groups, mids, high))

    def widen(blocks):
        full = jnp.zeros((blocks[0].shape[0], D), F32)
        for place, block in enumerate(blocks):
            full = lax.dynamic_update_slice_in_dim(full, block, (col ^ place) * width, 1)
        return full

    def input_cots():
        partial = dot_of(live["qkv_cot"], live["qkv_rel"], 1, 1)
        backs = [partial[:, n * width : (n + 1) * width] for n in range(cols)]
        attn_flow = Flow(col_reduce_steps(backs, cols)).step(len(bits_of(cols)) - 1)
        attn_gain_parts = [
            jnp.sum(part * (block.astype(F32) * attn_inverse), axis=0)[None]
            for part, block in zip(backs, hidden_blocks)
        ]
        token_inner = jnp.concatenate([outs[3] for outs in done], axis=0)
        inner_flow = Flow(total_steps(token_inner, [("col",)]))
        inner_flow.finish()
        query_part = sum(outs[1] for outs in done)
        key_part = sum(outs[2] for outs in done)
        head_parts = jnp.concatenate([query_part, key_part], 1)
        small = jnp.concatenate(
            [
                widen([router_part]),
                widen([moe_gain_part]),
                widen(attn_gain_parts),
                jnp.pad(head_parts, ((0, 0), (0, D - 2 * HD))),
            ],
            axis=0,
        )
        small_flow = Flow(total_steps(small, [("col",), ("lo", "mid"), ("hi",)])).step()
        flows.extend([attn_flow, inner_flow, small_flow])
        return [flow.holds() for flow in flows]

    flows = []
    (held,) = stage(live, [qkv_flow] + late[1:], [input_cots])
    for flow, arrays in zip(flows, held):
        flow.replace(arrays)
    attn_flow, inner_flow, small_flow = flows
    stage(live, flows + [qkv_flow] + early[:1] + late)
    live["moe_branch"] = moe_branch
    flows += [qkv_flow] + early + late
    while any(flow.sends is not None for flow in flows):
        stage(live, flows)
    moe_branch = live["moe_branch"]
    weight_sum = qkv_flow.finish()
    out_sum = weight_sum[:, 3 * width :]
    small = small_flow.finish()

    input_grad = (
        middle_cot
        + attn_inverse * (attn_flow.finish() * attn_gain)
        - hidden * (attn_inverse * attn_inverse * (inner_flow.finish()[:, None] / D))
    )
    output = (middle + moe_branch.astype(F32)).astype(BF16)
    gate_grad, up_grad, down_grad = unpack_grads(
        where,
        [grad_flows[expert, far].finish() for far in range(groups) for expert in range(each)],
        each,
    )
    own = lax.dynamic_slice_in_dim(small, col * width, width, 1)
    router_grad = lax.dynamic_slice_in_dim(small[:EXPERTS], row * depth, depth, 1).T
    return (
        output,
        input_grad,
        own[EXPERTS + 1],
        small[EXPERTS + 2, :HD],
        small[EXPERTS + 2, HD : 2 * HD],
        weight_sum[:, :width],
        weight_sum[:, width : 2 * width],
        weight_sum[:, 2 * width : 3 * width],
        out_sum.T,
        own[EXPERTS],
        router_grad,
        gate_grad,
        up_grad,
        down_grad,
    )


def solution(mesh):
    row_count, col_count = mesh.shape["row"], mesh.shape["col"]
    groups = 2
    between = EXPERTS // col_count // groups
    shape = (row_count // (groups * between), groups, between, col_count)
    inner = Mesh(mesh.devices.reshape(shape), ("hi", "lo", "mid", "col"))
    row = ("hi", "lo", "mid")
    return jax.shard_map(
        per_device,
        mesh=inner,
        in_specs=(
            P(row, "col"),
            P(row),
            P(row, None),
            P("col"),
            P(),
            P(),
            P(row, "col"),
            P(row, "col"),
            P(row, "col"),
            P("col", row),
            P("col"),
            P(row, None),
            P("col", row, None),
            P("col", row, None),
            P("col", None, row),
            P(row, "col"),
        ),
        out_specs=(
            P(row, "col"),
            P(row, "col"),
            P("col"),
            P(),
            P(),
            P(row, "col"),
            P(row, "col"),
            P(row, "col"),
            P("col", row),
            P("col"),
            P(row, None),
            P("col", row, None),
            P("col", row, None),
            P("col", None, row),
        ),
        check_vma=False,
    )
```

```python
import functools
import math

import jax
import jax.numpy as jnp
from jax import lax
from jax.experimental import pallas as pl
from jax.experimental.pallas import tpu as pltpu
from jax.sharding import Mesh, PartitionSpec as P

D = 2048
HD = 128
EXPERTS = 16
SEQ_LEN = 1024
CAP = 1152

BLOCK = 128
WINDOW = 144
EDGE = 16
TILE = 384
COST_SHARE = 50
EXPERT_WIDE, EXPERT_UNROLL = 512, 2
GRAD_WIDE, GRAD_UNROLL = 512, 1

epsilon = 1e-06
rope_base = 10000.0
masked_score = -1e30

F32 = jnp.float32
BF16 = jnp.bfloat16
ANY = pl.ANY
VMEM_LIMIT = 56 * 1024 * 1024


def dot_of(a, b, da, db):
    return lax.dot_general(a, b, (((da,), (db,)), ((), ())), preferred_element_type=F32)


def params(*semantics):
    return pltpu.CompilerParams(
        vmem_limit_bytes=VMEM_LIMIT, dimension_semantics=semantics or None
    )


def cost(flops, bytes_accessed, transcendentals=0):
    return pl.CostEstimate(
        flops=int(flops) // COST_SHARE,
        bytes_accessed=int(bytes_accessed) // COST_SHARE,
        transcendentals=int(transcendentals) // COST_SHARE,
    )


def turn(values, cosine, sine):
    return values * cosine + pltpu.roll(values, HD // 2, 1) * sine


def attend_forward_kernel(
    live_ref, q_ref, k_ref, v_ref, cos_ref, sin_ref, qg_ref, kg_ref, mix_ref, ql_ref, kl_ref, vl_ref
):
    live = live_ref[0]
    cosine = cos_ref[...]
    sine = sin_ref[...]

    def normed(values, gain):
        inverse = lax.rsqrt(jnp.mean(values * values, axis=1, keepdims=True) + epsilon)
        return turn(values * inverse * gain, cosine, sine).astype(BF16)

    ql_ref[...] = normed(q_ref[...], qg_ref[...])
    kl_ref[...] = normed(k_ref[...], kg_ref[...])
    vl_ref[...] = v_ref[...].astype(BF16)
    keys = kl_ref[...]
    values = vl_ref[...]
    rows = 256
    place = lax.broadcasted_iota(jnp.int32, (rows, SEQ_LEN), 1)
    for part in range(SEQ_LEN // rows):
        here = pl.ds(part * rows, rows)
        scores = dot_of(ql_ref[here, :], keys, 1, 1) * (1.0 / math.sqrt(HD))
        scores = jnp.where(place < live, scores, masked_score)
        top = jnp.max(scores, axis=1, keepdims=True)
        shifted = jnp.exp(scores - top)
        total = jnp.sum(shifted, axis=1, keepdims=True)
        probs = (shifted * (1.0 / total)).astype(BF16)
        mix_ref[here, :] = dot_of(probs, values, 1, 0).astype(BF16)


def attend_forward(seq, live, qkv, tables, query_gain, key_gain, heads):
    width = heads * HD

    def pick(offset):
        return pl.BlockSpec((SEQ_LEN, HD), lambda h, live, o=offset: (seq, o + h))

    def whole(shape):
        return pl.BlockSpec(shape, lambda h, live: (0, 0))

    out = pl.BlockSpec((SEQ_LEN, HD), lambda h, live: (0, h))
    return pl.pallas_call(
        attend_forward_kernel,
        grid_spec=pltpu.PrefetchScalarGridSpec(
            num_scalar_prefetch=1,
            grid=(heads,),
            in_specs=[
                pick(0),
                pick(heads),
                pick(2 * heads),
                whole((SEQ_LEN, HD)),
                whole((SEQ_LEN, HD)),
                whole((1, HD)),
                whole((1, HD)),
            ],
            out_specs=[out] * 4,
        ),
        out_shape=[jax.ShapeDtypeStruct((SEQ_LEN, width), BF16)] * 4,
        compiler_params=params("arbitrary"),
        cost_estimate=cost(
            heads * 8 * SEQ_LEN * SEQ_LEN * HD, 20 * SEQ_LEN * width, heads * SEQ_LEN * SEQ_LEN
        ),
        name="attend_forward",
    )(live, qkv, qkv, qkv, tables[0], tables[1], query_gain, key_gain)


def attend_backward_kernel(
    live_ref,
    ql_ref,
    kl_ref,
    vl_ref,
    do_ref,
    q_ref,
    k_ref,
    cos_ref,
    sin_ref,
    qg_ref,
    kg_ref,
    qc_ref,
    kc_ref,
    vc_ref,
    qpart_ref,
    kpart_ref,
    inner_ref,
    dq_ref,
    dk_ref,
    dv_ref,
):
    head = pl.program_id(0)
    live = live_ref[0]
    scale = 1.0 / math.sqrt(HD)
    keys = kl_ref[...]
    values = vl_ref[...]
    rows = 256
    place = lax.broadcasted_iota(jnp.int32, (SEQ_LEN, rows), 0)
    for part in range(SEQ_LEN // rows):
        here = pl.ds(part * rows, rows)
        queries = ql_ref[here, :]
        incoming = do_ref[here, :]
        scores = dot_of(keys, queries, 1, 1) * scale
        scores = jnp.where(place < live, scores, masked_score)
        top = jnp.max(scores, axis=0, keepdims=True)
        shifted = jnp.exp(scores - top)
        total = jnp.sum(shifted, axis=0, keepdims=True)
        probs = shifted * (1.0 / total)
        dv = dot_of(probs.astype(BF16), incoming, 1, 0)
        probs_cot = dot_of(values, incoming, 1, 1)
        weighted = probs * probs_cot
        centre = jnp.sum(weighted, axis=0, keepdims=True)
        raw = ((weighted - probs * centre) * scale).astype(BF16)
        dk = dot_of(raw, queries, 1, 0)
        dq_ref[here, :] = dot_of(raw, keys, 0, 0)
        if part == 0:
            dv_ref[...] = dv
            dk_ref[...] = dk
        else:
            dv_ref[...] += dv
            dk_ref[...] += dk
    cosine = cos_ref[...]
    sine = -sin_ref[...]

    def back(values, gain, rotated_cot):
        incoming = turn(rotated_cot, cosine, sine)
        inverse = lax.rsqrt(jnp.mean(values * values, axis=1, keepdims=True) + epsilon)
        scaled = incoming * gain
        inner = jnp.mean(scaled * values, axis=1, keepdims=True)
        grad = inverse * scaled - values * (inverse * inverse * inverse * inner)
        part = jnp.sum(incoming * values * inverse, axis=0, keepdims=True)
        return grad.astype(BF16), part, jnp.sum(grad * values, axis=1, keepdims=True)

    qc_ref[...], qpart, inner = back(q_ref[...], qg_ref[...], dq_ref[...])
    kc_ref[...], kpart, key_inner = back(k_ref[...], kg_ref[...], dk_ref[...])
    vc_ref[...] = dv_ref[...].astype(BF16)
    inner += key_inner
    inner += jnp.sum(dv_ref[...] * values.astype(F32), axis=1, keepdims=True)

    @pl.when(head == 0)
    def _():
        qpart_ref[...] = qpart
        kpart_ref[...] = kpart
        inner_ref[...] = inner

    @pl.when(head > 0)
    def _():
        qpart_ref[...] += qpart
        kpart_ref[...] += kpart
        inner_ref[...] += inner


def attend_backward(seq, live, lows, mixture_cot, qkv, tables, query_gain, key_gain, heads):
    width = heads * HD
    block = pl.BlockSpec((SEQ_LEN, HD), lambda h, live: (0, h))

    def pick(offset):
        return pl.BlockSpec((SEQ_LEN, HD), lambda h, live, o=offset: (seq, o + h))

    def whole(shape):
        return pl.BlockSpec(shape, lambda h, live: (0, 0))

    return pl.pallas_call(
        attend_backward_kernel,
        grid_spec=pltpu.PrefetchScalarGridSpec(
            num_scalar_prefetch=1,
            grid=(heads,),
            in_specs=[block] * 4
            + [
                pick(0),
                pick(heads),
                whole((SEQ_LEN, HD)),
                whole((SEQ_LEN, HD)),
                whole((1, HD)),
                whole((1, HD)),
            ],
            out_specs=[block] * 3 + [whole((1, HD))] * 2 + [whole((SEQ_LEN, 1))],
            scratch_shapes=[pltpu.VMEM((SEQ_LEN, HD), F32)] * 3,
        ),
        out_shape=[jax.ShapeDtypeStruct((SEQ_LEN, width), BF16)] * 3
        + [jax.ShapeDtypeStruct((1, HD), F32)] * 2
        + [jax.ShapeDtypeStruct((SEQ_LEN, 1), F32)],
        compiler_params=params("arbitrary"),
        cost_estimate=cost(
            heads * 20 * SEQ_LEN * SEQ_LEN * HD, 24 * SEQ_LEN * width, heads * SEQ_LEN * SEQ_LEN
        ),
        name="attend_backward",
    )(live, *lows, mixture_cot, qkv, qkv, tables[0], tables[1], query_gain, key_gain)


def compact_kernel(start_ref, where_ref, pos_ref, source_ref, *outs):
    group, groups = pl.program_id(0), pl.num_programs(0)
    row_of = lax.broadcasted_iota(jnp.int32, (WINDOW, BLOCK), 0)
    for out in outs:
        out[...] = jnp.zeros_like(out)
    for number in range(source_ref.shape[1] // BLOCK):
        here = slice(number * BLOCK, (number + 1) * BLOCK)
        for expert, out in enumerate(outs):
            start = pl.multiple_of(start_ref[expert * groups + group, number], EDGE)
            place = pos_ref[expert, 0, :, here]
            choice = jnp.where(row_of + start == place, 1.0, 0.0).astype(BF16)
            rows = dot_of(choice, source_ref[0, here, :], 1, 0)
            out[pl.ds(start, WINDOW), :] += rows.astype(BF16)


def compact(starts, where, pos_row, source, groups, cols):
    tokens, width = source.shape[1:]
    count = pos_row.shape[0] // groups
    return pl.pallas_call(
        compact_kernel,
        grid_spec=pltpu.PrefetchScalarGridSpec(
            num_scalar_prefetch=2,
            grid=(groups, cols),
            in_specs=[
                pl.BlockSpec((count, 1, 1, tokens), lambda q, j, s, w: (0, q, 0, 0)),
                pl.BlockSpec(
                    (1, tokens, width), lambda q, j, s, w: ((w[0] ^ q) * cols + j, 0, 0)
                ),
            ],
            out_specs=[pl.BlockSpec((CAP, width), lambda q, j, s, w: (q, j))] * count,
        ),
        out_shape=[jax.ShapeDtypeStruct((groups * CAP, cols * width), BF16)] * count,
        compiler_params=params("arbitrary", "arbitrary"),
        cost_estimate=cost(
            count * groups * cols * 2 * tokens * WINDOW * width * 2,
            groups * cols * 2 * width * (tokens + count * CAP),
        ),
        name="compact",
    )(starts, where, pos_row.reshape(count, groups, 1, tokens), source)


def compact_scalars_kernel(start_ref, pos_ref, *refs):
    count = len(refs) // 2
    group = pl.program_id(0)
    row_of = lax.broadcasted_iota(jnp.int32, (WINDOW, BLOCK), 0)
    for number in range(count):
        refs[count + number][...] = jnp.zeros_like(refs[count + number])
    for number in range(pos_ref.shape[2] // BLOCK):
        start = pl.multiple_of(start_ref[group, number], EDGE)
        here = slice(number * BLOCK, (number + 1) * BLOCK)
        choice = row_of + start == pos_ref[0, :, here]
        for source, out in zip(refs[:count], refs[count:]):
            picked = jnp.sum(jnp.where(choice, source[0, :, here], 0.0), axis=1, keepdims=True)
            out[pl.ds(start, WINDOW), :] += picked


def compact_scalars(starts, pos_row, sources):
    groups, _, tokens = pos_row.shape
    block = pl.BlockSpec((1, 1, tokens), lambda q, s: (q, 0, 0))
    return pl.pallas_call(
        compact_scalars_kernel,
        grid_spec=pltpu.PrefetchScalarGridSpec(
            num_scalar_prefetch=1,
            grid=(groups,),
            in_specs=[block] * (1 + len(sources)),
            out_specs=[pl.BlockSpec((CAP, 1), lambda q, s: (q, 0))] * len(sources),
        ),
        out_shape=[jax.ShapeDtypeStruct((groups * CAP, 1), F32)] * len(sources),
        compiler_params=params("arbitrary"),
        cost_estimate=cost(0, 4 * groups * CAP * 128 * len(sources)),
        name="compact_scalars",
    )(starts, pos_row, *sources)


def expand_scalars_kernel(start_ref, pos_ref, *refs):
    count = len(refs) // 2
    group = pl.program_id(0)
    row_of = lax.broadcasted_iota(jnp.int32, (WINDOW, BLOCK), 0)
    for number in range(pos_ref.shape[2] // BLOCK):
        start = pl.multiple_of(start_ref[group, number], EDGE)
        here = slice(number * BLOCK, (number + 1) * BLOCK)
        choice = row_of + start == pos_ref[0, :, here]
        for source, out in zip(refs[:count], refs[count:]):
            held = source[pl.ds(start, WINDOW), :]
            out[0, :, here] = jnp.sum(jnp.where(choice, held, 0.0), axis=0, keepdims=True)


def expand_scalars(starts, pos_row, sources):
    groups, _, tokens = pos_row.shape
    block = pl.BlockSpec((1, 1, tokens), lambda q, s: (q, 0, 0))
    return pl.pallas_call(
        expand_scalars_kernel,
        grid_spec=pltpu.PrefetchScalarGridSpec(
            num_scalar_prefetch=1,
            grid=(groups,),
            in_specs=[block] + [pl.BlockSpec((CAP, 1), lambda q, s: (q, 0))] * len(sources),
            out_specs=[block] * len(sources),
        ),
        out_shape=[jax.ShapeDtypeStruct((groups, 1, tokens), F32)] * len(sources),
        compiler_params=params("arbitrary"),
        cost_estimate=cost(0, 4 * groups * CAP * 128 * len(sources)),
        name="expand_scalars",
    )(starts, pos_row, *sources)


def expand_kernel(sizes, count, start_ref, where_ref, pos_ref, *refs):
    group, groups = pl.program_id(0), pl.num_programs(0)
    sides = len(refs) // (count + len(sizes))
    sources, outs = refs[: count * sides], refs[count * sides :]
    column_of = lax.broadcasted_iota(jnp.int32, (BLOCK, WINDOW), 1)
    number = 0
    for part, size in enumerate(sizes):
        for step in range(size // BLOCK):
            totals = [None] * sides
            for expert in range(count):
                start = pl.multiple_of(start_ref[expert * groups + group, number], EDGE)
                place = pos_ref[expert, 0, number * BLOCK : (number + 1) * BLOCK, :]
                choice = jnp.where(column_of + start == place, 1.0, 0.0).astype(BF16)
                for side in range(sides):
                    held = sources[expert * sides + side][pl.ds(start, WINDOW), :]
                    rows = dot_of(choice, held, 1, 0)
                    totals[side] = rows if totals[side] is None else totals[side] + rows
            here = slice(step * BLOCK, (step + 1) * BLOCK)
            for side in range(sides):
                outs[part * sides + side][0, 0, here, :] = totals[side].astype(BF16)
            number += 1


def expand(starts, where, pos_col, sources, sizes, groups, cols):
    width = sources[0].shape[1] // cols
    tokens = sum(sizes)
    count = len(sources)

    def side(odd):
        return pl.BlockSpec((CAP, width), lambda q, j, s, w: (q, w[1] ^ (2 * j + odd)))

    outs = pl.pallas_call(
        functools.partial(expand_kernel, sizes, count),
        grid_spec=pltpu.PrefetchScalarGridSpec(
            num_scalar_prefetch=2,
            grid=(groups, cols // 2),
            in_specs=[pl.BlockSpec((count, 1, tokens, 1), lambda q, j, s, w: (0, q, 0, 0))]
            + [side(0), side(1)] * count,
            out_specs=[
                pl.BlockSpec((1, 1, size, width), lambda q, j, s, w: (q, j, 0, 0))
                for size in sizes
                for _ in range(2)
            ],
        ),
        out_shape=[
            jax.ShapeDtypeStruct((groups, cols // 2, size, width), BF16)
            for size in sizes
            for _ in range(2)
        ],
        compiler_params=params("arbitrary", "arbitrary"),
        cost_estimate=cost(
            4 * count * groups * cols * tokens * WINDOW * width,
            groups * cols * width * (2 * tokens + 2 * count * CAP),
        ),
        name="expand",
    )(
        starts,
        where,
        pos_col.reshape(count, groups, tokens, 1),
        *[source for source in sources for _ in range(2)],
    )
    return list(zip(outs[::2], outs[1::2]))


def expand_all(starts, where, pos_col, sources, groups, cols):
    width = sources[0].shape[1] // cols
    tokens = pos_col.shape[1]
    count = len(sources)
    return pl.pallas_call(
        functools.partial(expand_kernel, [tokens], count),
        grid_spec=pltpu.PrefetchScalarGridSpec(
            num_scalar_prefetch=2,
            grid=(groups, cols),
            in_specs=[pl.BlockSpec((count, 1, tokens, 1), lambda q, j, s, w: (0, q, 0, 0))]
            + [pl.BlockSpec((CAP, width), lambda q, j, s, w: (q, j))] * count,
            out_specs=pl.BlockSpec((1, 1, tokens, width), lambda q, j, s, w: (w[0] ^ q, j, 0, 0)),
        ),
        out_shape=jax.ShapeDtypeStruct((groups, cols, tokens, width), BF16),
        compiler_params=params("arbitrary", "arbitrary"),
        cost_estimate=cost(
            4 * count * groups * cols * tokens * WINDOW * width,
            groups * cols * width * (2 * tokens + 2 * count * CAP),
        ),
        name="expand_all",
    )(starts, where, pos_col.reshape(count, groups, tokens, 1), *sources)


def pack_kernel(where_ref, gate_ref, up_ref, down_ref, out_ref):
    hidden = gate_ref.shape[2]
    out_ref[0, :, :hidden] = gate_ref[0].astype(BF16)
    out_ref[0, :, hidden : 2 * hidden] = up_ref[0].astype(BF16)
    out_ref[0, :, 2 * hidden :] = down_ref[0].T.astype(BF16)


def pack_weights(where, gate, up, down, each):
    experts, depth, hidden = gate.shape

    def pick(shape):
        return pl.BlockSpec(shape, lambda q, w: ((w[0] ^ (q // each)) * each + q % each, 0, 0))

    return pl.pallas_call(
        pack_kernel,
        grid_spec=pltpu.PrefetchScalarGridSpec(
            num_scalar_prefetch=1,
            grid=(experts,),
            in_specs=[pick((1, depth, hidden)), pick((1, depth, hidden)), pick((1, hidden, depth))],
            out_specs=pl.BlockSpec((1, depth, 3 * hidden), lambda q, w: (q, 0, 0)),
        ),
        out_shape=jax.ShapeDtypeStruct((experts, depth, 3 * hidden), BF16),
        compiler_params=params("arbitrary"),
        cost_estimate=cost(0, 18 * experts * depth * hidden),
        name="pack_weights",
    )(where, gate, up, down)


def unpack_kernel(where_ref, *refs):
    sources, (gate_ref, up_ref, down_ref) = refs[:-3], refs[-3:]
    hidden = gate_ref.shape[2]
    for number, source in enumerate(sources):

        @pl.when(pl.program_id(0) == number)
        def _(source=source):
            gate_ref[0] = source[:, :hidden].astype(F32)
            up_ref[0] = source[:, hidden : 2 * hidden].astype(F32)
            down_ref[0] = source[:, 2 * hidden :].astype(F32).T


def unpack_grads(where, sources, each):
    count = len(sources)
    depth, wide = sources[0].shape
    hidden = wide // 3

    def pick(shape):
        return pl.BlockSpec(shape, lambda q, w: ((w[0] ^ (q // each)) * each + q % each, 0, 0))

    shapes = [(count, depth, hidden), (count, depth, hidden), (count, hidden, depth)]
    return pl.pallas_call(
        unpack_kernel,
        grid_spec=pltpu.PrefetchScalarGridSpec(
            num_scalar_prefetch=1,
            grid=(count,),
            in_specs=[pl.BlockSpec((depth, wide), lambda q, w: (0, 0))] * count,
            out_specs=[pick((1,) + shape[1:]) for shape in shapes],
        ),
        out_shape=[jax.ShapeDtypeStruct(shape, F32) for shape in shapes],
        compiler_params=params("arbitrary"),
        cost_estimate=cost(0, 18 * count * depth * hidden),
        name="unpack_grads",
    )(where, *sources)


def expert_kernel(count, hidden, row_ref, x_ref, m_ref, gate_ref, scale_ref, *refs):
    pieces = refs[:count]
    rows_ref, pre_ref, act_ref, cot_ref, inner_ref, result_ref, held, sems = refs[count:]
    depth = pieces[0].shape[0]

    @pl.when(pl.program_id(0) == 0)
    def _():
        copies = []
        for number, piece in enumerate(pieces):
            place = pl.ds(pl.multiple_of(row_ref[number] * depth, depth), depth)
            copies.append(pltpu.make_async_copy(piece, held.at[place, :], sems.at[number]))
        for copy in copies:
            copy.start()
        for copy in copies:
            copy.wait()

    gate = gate_ref[...]
    scale = scale_ref[...]
    wide = EXPERT_WIDE
    cot_ref[...] = jnp.zeros_like(cot_ref)
    inner_ref[...] = jnp.zeros_like(inner_ref)

    @pl.loop(0, hidden // wide, unroll=EXPERT_UNROLL)
    def _(step):
        first = pl.multiple_of(step * wide, wide)
        gate_pre = dot_of(x_ref[...], held[:, pl.ds(first, wide)], 1, 0) * scale
        up_pre = dot_of(x_ref[...], held[:, pl.ds(hidden + first, wide)], 1, 0) * scale
        back = dot_of(m_ref[...], held[:, pl.ds(2 * hidden + first, wide)], 1, 0)
        squash = 1.0 / (1.0 + jnp.exp(-gate_pre))
        silu = gate_pre * squash
        active = silu * up_pre
        cot_ref[...] += jnp.sum(active.astype(BF16).astype(F32) * back, axis=1, keepdims=True)
        act_ref[:, pl.ds(first, wide)] = (active * gate).astype(BF16)
        back = back * gate
        slope = squash * (1.0 + gate_pre * (1.0 - squash))
        gate_cot = back * up_pre * slope
        up_cot = back * silu
        inner_ref[...] += jnp.sum(gate_cot * gate_pre + up_cot * up_pre, axis=1, keepdims=True)
        pre_ref[:, pl.ds(first, wide)] = (gate_cot * scale).astype(BF16)
        pre_ref[:, pl.ds(hidden + first, wide)] = (up_cot * scale).astype(BF16)

    @pl.loop(0, held.shape[0] // wide, unroll=EXPERT_UNROLL)
    def _(step):
        first = pl.multiple_of(step * wide, wide)
        here = pl.ds(first, wide)
        rows_ref[:, here] = dot_of(pre_ref[...], held[here, : 2 * hidden], 1, 1).astype(BF16)
        result_ref[:, here] = dot_of(act_ref[...], held[here, 2 * hidden :], 1, 1).astype(BF16)


def expert_step(row_numbers, x, m, gate, scale, pieces):
    total, wide = x.shape
    hidden = pieces[0].shape[1] // 3
    count = len(pieces)

    def tile(columns):
        return pl.BlockSpec((TILE, columns), lambda i, r: (i, 0))

    return pl.pallas_call(
        functools.partial(expert_kernel, count, hidden),
        grid_spec=pltpu.PrefetchScalarGridSpec(
            num_scalar_prefetch=1,
            grid=(total // TILE,),
            in_specs=[tile(wide), tile(wide), tile(1), tile(1)]
            + [pl.BlockSpec(memory_space=ANY)] * count,
            out_specs=[tile(wide), tile(2 * hidden), tile(hidden), tile(1), tile(1), tile(wide)],
            scratch_shapes=[
                pltpu.VMEM((wide, 3 * hidden), BF16),
                pltpu.SemaphoreType.DMA((count,)),
            ],
        ),
        out_shape=[
            jax.ShapeDtypeStruct((total, wide), BF16),
            jax.ShapeDtypeStruct((total, 2 * hidden), BF16),
            jax.ShapeDtypeStruct((total, hidden), BF16),
            jax.ShapeDtypeStruct((total, 1), F32),
            jax.ShapeDtypeStruct((total, 1), F32),
            jax.ShapeDtypeStruct((total, wide), BF16),
        ],
        compiler_params=params("arbitrary"),
        cost_estimate=cost(
            2 * total * wide * hidden * 6, 2 * total * (4 * wide + 3 * hidden), total * hidden
        ),
        name="expert_step",
    )(row_numbers, x, m, gate, scale, *pieces)


def weight_grad_kernel(mids, place_ref, x_ref, m_ref, pre_ref, act_ref, out_ref, turned_ref):
    wide = GRAD_WIDE
    first = pre_ref.shape[1]
    depth = x_ref.shape[1] // mids
    turned_ref[0] = x_ref[...].T
    turned_ref[1] = m_ref[...].T
    mid = place_ref[place_ref.shape[0] - 1]

    def put(grad, here):
        for number in range(mids):
            block = grad[number * depth : (number + 1) * depth].astype(BF16)
            out_ref[0, number ^ mid, 0, :, here] = block

    @pl.loop(0, first // wide, unroll=GRAD_UNROLL)
    def _(step):
        here = pl.ds(pl.multiple_of(step * wide, wide), wide)
        put(dot_of(turned_ref[0], pre_ref[:, here], 1, 0), here)

    @pl.loop(0, act_ref.shape[1] // wide, unroll=GRAD_UNROLL)
    def _(step):
        here = pl.ds(pl.multiple_of(step * wide, wide), wide)
        there = pl.ds(pl.multiple_of(first + step * wide, wide), wide)
        put(dot_of(turned_ref[1], act_ref[:, here], 1, 0), there)


def weight_grads(places, x, m, pre, act, depth, groups, mids, high):
    total = x.shape[0]
    wide = pre.shape[1] + act.shape[1]

    def column(first):
        return pl.BlockSpec((total, mids * depth), lambda f, h, r: (0, r[first + f * high + h]))

    def whole(array):
        return pl.BlockSpec(array.shape, lambda f, h, r: (0, 0), pipeline_mode=pl.Buffered(1))

    return pl.pallas_call(
        functools.partial(weight_grad_kernel, mids),
        grid_spec=pltpu.PrefetchScalarGridSpec(
            num_scalar_prefetch=1,
            grid=(groups, high),
            in_specs=[column(0), column(groups * high), whole(pre), whole(act)],
            out_specs=pl.BlockSpec(
                (1, mids, 1, depth, wide), lambda f, h, r: (f, 0, h, 0, 0)
            ),
            scratch_shapes=[pltpu.VMEM((2, mids * depth, total), BF16)],
        ),
        out_shape=jax.ShapeDtypeStruct((groups, mids, high, depth, wide), BF16),
        compiler_params=params("arbitrary", "arbitrary"),
        cost_estimate=cost(
            2 * total * depth * groups * mids * high * wide,
            2 * total * (2 * depth * groups * mids * high + wide),
        ),
        name="weight_grads",
    )(places, x, m, pre, act)


def bits_of(size):
    return [1 << n for n in range(size.bit_length() - 1)]


def swap(values, axis, bit):
    size = lax.axis_size(axis) if isinstance(axis, str) else math.prod(map(lax.axis_size, axis))
    return lax.ppermute(values, axis, [(n, n ^ bit) for n in range(size)])


class Flow:
    def __init__(self, steps):
        self.steps = steps
        self.result = None
        self.sends = next(steps)

    def advance(self, got):
        try:
            self.sends = self.steps.send(got)
        except StopIteration as stop:
            self.sends = None
            self.result = stop.value

    def step(self, count=1):
        for _ in range(count):
            if self.sends is not None:
                self.advance([swap(*send) for send in self.sends])
        return self

    def finish(self):
        while self.sends is not None:
            self.step()
        return self.result

    def holds(self):
        return self.result if self.sends is None else [send[0] for send in self.sends]

    def replace(self, arrays):
        if self.sends is None:
            self.result = arrays
        else:
            self.sends = [(array, *send[1:]) for array, send in zip(arrays, self.sends)]


def stage(live, flows=(), work=(), sync=()):
    flows = [flow for flow in flows if flow.sends is not None]
    got = [[swap(*send) for send in flow.sends] for flow in flows]
    done = [each() for each in work]
    held = [flow.holds() for flow in sync]
    got, done, held, kept = lax.optimization_barrier((got, done, held, dict(live)))
    live.update(kept)
    for flow, arrays in zip(flows, got):
        flow.advance(arrays)
    for flow, arrays in zip(sync, held):
        flow.replace(arrays)
    return done


def spread_steps(values, axis, bits):
    blocks = {0: values}
    for bit in bits:
        places = sorted(blocks)
        got = yield [(blocks[place], axis, bit) for place in places]
        blocks.update({place | bit: block for place, block in zip(places, got)})
    return [blocks[place] for place in sorted(blocks)]


def spread_rows_steps(values, row_bits, strides):
    held = values[None]
    places = [0]
    for axis, bit in row_bits:
        (got,) = yield [(held, axis, bit)]
        held = jnp.concatenate([held, got], axis=0)
        places += [place | (bit * strides[axis]) for place in places]
    return jnp.stack([held[places.index(place)] for place in range(len(places))])


def spread_cube_steps(values, groups, cols):
    held = values[None]
    for axis, bits in (("lo", bits_of(groups)), ("col", bits_of(cols))):
        for bit in bits:
            (got,) = yield [(held, axis, bit)]
            held = jnp.concatenate([held, got], axis=0)
    return jnp.swapaxes(held.reshape((cols, groups) + values.shape), 0, 1)


def col_reduce_steps(blocks, cols):
    held = dict(enumerate(blocks))
    for bit in bits_of(cols):
        away = [place for place in sorted(held) if place & bit]
        (got,) = yield [(jnp.stack([held[place].astype(BF16) for place in away]), "col", bit)]
        held = {
            place & ~bit: held[place & ~bit] + got[number].astype(F32)
            for number, place in enumerate(away)
        }
    return held[0]


def total_steps(values, axes):
    for axis in axes:
        size = math.prod(map(lax.axis_size, axis))
        got = yield [(values, axis, place) for place in range(1, size)]
        values = values + sum(got)
    return values


def row_reduce_steps(grads, groups, mids, high):
    names = [("lo", bit) for bit in reversed(bits_of(groups))]
    names += [("mid", bit) for bit in reversed(bits_of(mids))]
    names += [("hi", bit) for bit in reversed(bits_of(high))]
    grads = grads.reshape((2,) * len(names) + grads.shape[3:])
    half = grads.shape[-1] // 2
    held = []
    for number in range(2):
        order = [name for name in names if name[0] != "hi"][:: 1 if number else -1]
        order += [name for name in reversed(names) if name[0] == "hi"]
        held.append((grads[..., number * half : (number + 1) * half], names, order))
    for step in range(len(names)):
        sends, rest = [], []
        for array, left, order in held:
            name = order[step]
            axis = left.index(name)
            away = 0 if name[0] == "lo" else 1
            sends.append((lax.index_in_dim(array, away, axis, False).astype(BF16), *name))
            kept = lax.index_in_dim(array, 1 - away, axis, False)
            rest.append((kept, [other for other in left if other != name], order))
        got = yield sends
        held = [
            (kept.astype(F32) + more.astype(F32), left, order)
            for (kept, left, order), more in zip(rest, got)
        ]
    return jnp.concatenate([array for array, _, _ in held], axis=1)


def links_of(groups, cols):
    return [("col", bit) for bit in bits_of(cols)[1:]] + [("lo", bit) for bit in bits_of(groups)]


def turned(links, number):
    number %= len(links)
    return links[number:] + links[:number]


def reduce_steps(parts, groups, cols):
    links = links_of(groups, cols)
    got = yield [(away, "col", 1) for _, away in parts]
    held = []
    for number, (keep, _) in enumerate(parts):
        shape = (2,) * len(links) + keep.shape[2:]
        names = [("lo", bit) for bit in reversed(bits_of(groups))]
        names += [("col", bit) for bit in reversed(bits_of(cols)[1:])]
        held.append((keep.reshape(shape), got[number].reshape(shape), names))
    for step in range(len(links)):
        sends, rest = [], []
        for number, (keep, more, names) in enumerate(held):
            link = turned(links, number)[step]
            axis = names.index(link)

            def half(place):
                total = lax.index_in_dim(keep, place, axis, False).astype(F32)
                return total + lax.index_in_dim(more, place, axis, False).astype(F32)

            sends.append((half(1).astype(BF16), *link))
            kept = half(0)
            rest.append(
                (
                    kept if step + 1 == len(links) else kept.astype(BF16),
                    [name for name in names if name != link],
                )
            )
        got = yield sends
        held = [(keep, more, names) for (keep, names), more in zip(rest, got)]
    return jnp.concatenate([keep.astype(F32) + more.astype(F32) for keep, more, _ in held], axis=0)


def part_sizes(tokens, count):
    whole = tokens // BLOCK
    return [BLOCK * ((whole + count - 1 - n) // count) for n in range(count)]


def expert_weight_steps(piece, far, bits):
    if far:
        (piece,) = yield [(piece, "lo", far)]
    held = {(): piece}
    fresh = [()]
    while True:
        ways = [
            (place, number)
            for place in fresh
            for number in range(place[-1] + 1 if place else 0, len(bits))
        ]
        if not ways:
            return held
        got = yield [(held[place], *bits[number]) for place, number in ways]
        fresh = [place + (number,) for place, number in ways]
        held.update(zip(fresh, got))


def expert_grad_steps(blocks, far, bits):
    for number in reversed(range(len(bits))):
        half = blocks.shape[0] // 2
        (got,) = yield [(blocks[half:], *bits[number])]
        blocks = blocks[:half].astype(F32) + got.astype(F32)
        if number or far:
            blocks = blocks.astype(BF16)
    total = blocks[0]
    if far:
        (total,) = yield [(total, "lo", far)]
    return total


def per_device(
    hidden_in,
    lengths,
    routes,
    attn_gain,
    query_gain,
    key_gain,
    query_weight,
    key_weight,
    value_weight,
    out_weight,
    moe_gain,
    router,
    gate_weight,
    up_weight,
    down_weight,
    cotangent,
):
    tok_rows, width = hidden_in.shape
    cols = lax.axis_size("col")
    groups = lax.axis_size("lo")
    high = lax.axis_size("hi")
    mids = lax.axis_size("mid")
    col = lax.axis_index("col")
    lo = lax.axis_index("lo")
    hi = lax.axis_index("hi")
    mid = lax.axis_index("mid")
    row = (hi * groups + lo) * mids + mid
    where = jnp.stack([lo, col])
    heads = width // HD
    seqs = lengths.shape[0]
    depth = gate_weight.shape[1]
    each = gate_weight.shape[0] // groups
    cube = ("lo", "col")
    rows_axes = ("hi", "lo", "mid")
    strides = {"hi": groups * mids, "lo": mids, "mid": 1}
    seq_rows = [slice(s * SEQ_LEN, (s + 1) * SEQ_LEN) for s in range(seqs)]
    links = links_of(groups, cols)
    col_bits = list(reversed(bits_of(cols)))
    hi_bits = [("hi", bit) for bit in bits_of(high)]
    mid_bits = [("mid", bit) for bit in bits_of(mids)]
    row_bits = hi_bits + [("lo", bit) for bit in bits_of(groups)] + mid_bits
    far_bits = hi_bits + mid_bits
    live = {}

    def row_of_set(place, far):
        other = row ^ (far * mids)
        for number in place:
            axis, bit = far_bits[number]
            other = other ^ (bit * strides[axis])
        return other

    hidden_flow = Flow(spread_steps(hidden_in, "col", col_bits))
    gain_flow = Flow(spread_steps(attn_gain, "col", col_bits))
    routes_flow = Flow(spread_steps(routes.T, "lo", bits_of(groups)))
    router_flow = Flow(spread_rows_steps(router.T.astype(BF16), row_bits, strides))
    out_flow = Flow(spread_rows_steps(out_weight.T.astype(BF16), row_bits, strides))
    qkv_local = jnp.concatenate([query_weight, key_weight, value_weight], axis=1).astype(BF16)
    qkv_full = lax.all_gather(qkv_local, rows_axes, axis=0, tiled=True)
    live_key = jnp.arange(SEQ_LEN)[None, :] < lengths[:, None]
    out_cot = jnp.where(live_key.reshape(tok_rows, 1), cotangent, jnp.zeros_like(cotangent))
    packed = pack_weights(where, gate_weight, up_weight, down_weight, each)
    units = [(expert, far) for expert in range(each) for far in range(groups)]
    live["packed"] = packed

    def rotary_tables():
        places = jnp.arange(SEQ_LEN).astype(F32)
        powers = jnp.arange(HD // 2).astype(F32) * (2.0 / HD)
        angles = places[:, None] * jnp.exp(-powers * math.log(rope_base))[None, :]
        cosine, sine = jnp.cos(angles), jnp.sin(angles)
        return (
            jnp.concatenate([cosine, cosine], axis=1),
            jnp.concatenate([-sine, sine], axis=1),
        )

    live["out_cot"] = out_cot
    (tables,) = stage(
        live,
        [hidden_flow, gain_flow, routes_flow, router_flow, out_flow],
        [rotary_tables],
    )

    hidden = hidden_in.astype(F32)

    def norm_attn():
        blocks = hidden_flow.finish()
        gains = gain_flow.finish()
        square = sum(jnp.sum(jnp.square(block.astype(F32)), axis=1) for block in blocks)
        inverse = lax.rsqrt(square / D + epsilon)[:, None]
        normed = jnp.zeros((tok_rows, D), BF16)
        for place, (block, gain) in enumerate(zip(blocks, gains)):
            piece = (block.astype(F32) * inverse * gain).astype(BF16)
            normed = lax.dynamic_update_slice_in_dim(normed, piece, (col ^ place) * width, 1)
        return normed, inverse

    def routing():
        rel = jnp.stack(routes_flow.finish())
        named = jnp.any(rel[:, :, None, :] == jnp.arange(EXPERTS)[None, None, :, None], axis=1)
        first = (col * groups + lo) * each
        member = lax.dynamic_slice_in_dim(named, first, each, 1)
        member = jnp.swapaxes(member, 0, 1).reshape(each * groups, tok_rows)
        count = member.astype(jnp.int32)
        rank = jnp.cumsum(count, axis=1) - count
        pos = jnp.where(member, rank, -(1 << 20))
        starts = jnp.minimum(rank[:, ::BLOCK] // EDGE * EDGE, CAP - WINDOW)
        return named, starts, pos[:, None, :], pos[:, :, None]

    live["qkv_full"] = qkv_full
    ((live["normed_attn"], attn_inverse),) = stage(live, [router_flow, out_flow], [norm_attn])
    weight_flows = {}

    def start_weights(expert):
        for far in range(groups):
            weight_flows[expert, far] = Flow(
                expert_weight_steps(live["packed"][far * each + expert], far, far_bits)
            )

    start_weights(0)
    moe_cot = lax.all_gather(live["out_cot"], cube, axis=0, tiled=False)
    hidden_blocks = hidden_flow.result
    query_scale, key_scale = query_gain[None, :], key_gain[None, :]

    def attend(s):
        return attend_forward(
            s, lengths[s : s + 1], live["qkv"], tables, query_scale, key_scale, heads
        )

    def project_and_attend():
        live["qkv"] = dot_of(live["normed_attn"], live["qkv_full"], 1, 0)
        return attend(0)

    firsts = [weight_flows[0, far] for far in range(1, groups)]
    (first_seq,) = stage(live, [router_flow, out_flow], [project_and_attend])
    for expert in range(1, each):
        start_weights(expert)
    seconds = [weight_flows[unit] for unit in units if unit[0] == 1]
    named, starts, pos_row, pos_col = routing()

    span = width // depth

    def col_rows(blocks, place, axis):
        first = (col ^ place) * span
        return jnp.concatenate(
            [
                lax.dynamic_index_in_dim(blocks, (first + n) ^ row, 0, False)
                for n in range(span)
            ],
            axis=axis,
        )

    out_spread = out_flow.finish()
    out_rel = jnp.concatenate([col_rows(out_spread, place, 0) for place in range(cols)], axis=0)
    router_rows = col_rows(router_flow.finish(), 0, 1)

    def branch(mixture):
        partial = dot_of(mixture, out_rel, 1, 1)
        blocks = [partial[:, n * width : (n + 1) * width] for n in range(cols)]
        return Flow(col_reduce_steps(blocks, cols)).finish()

    def attend_rest():
        outs = [first_seq]
        sums = [branch(first_seq[0])]
        for s in range(1, seqs):
            outs.append(attend(s))
            sums.append(branch(outs[s][0]))
        return outs, sums

    ((attended, branches),) = stage(live, [weight_flows[0, 0]] + firsts, [attend_rest])
    middle = hidden + jnp.concatenate(branches, axis=0)
    live["scaled_rows"] = (middle * moe_gain).astype(BF16)
    scaled_rows = live["scaled_rows"]
    moe_in = lax.all_gather(scaled_rows, cube, axis=0, tiled=False)
    square = jnp.sum(middle * middle, axis=1)[None, :]
    stat = jnp.concatenate([dot_of(router_rows, scaled_rows, 1, 1), square], axis=0)
    stat_flow = Flow(spread_cube_steps(stat, groups, cols))
    stage(live, [stat_flow], sync=[weight_flows[0, 0]] + firsts + seconds)
    (live["cot_rows"],) = stage(
        live,
        [stat_flow, weight_flows[0, 0]] + firsts,
        [lambda: compact(starts, where, pos_row, moe_cot, groups, cols)],
    )
    stage(live, [stat_flow] + firsts + seconds[1:])
    stat = stat_flow.finish()

    stat = jnp.sum(stat, axis=1)
    moe_inverse = lax.rsqrt(stat[:, EXPERTS] / D + epsilon)
    all_logits = stat[:, :EXPERTS] * moe_inverse[:, None, :]
    logits = jnp.where(named, all_logits, masked_score)
    shifted = jnp.where(named, jnp.exp(logits - jnp.max(logits, axis=1, keepdims=True)), 0.0)
    gates = shifted / jnp.sum(shifted, axis=1, keepdims=True)
    own_gate = lax.dynamic_slice_in_dim(gates, (col * groups + lo) * each, each, 1)
    own_gate = jnp.swapaxes(own_gate, 0, 1).reshape(each * groups, 1, tok_rows)
    row_gate, row_scale = compact_scalars(
        starts, pos_row, (own_gate, jnp.tile(moe_inverse, (each, 1))[:, None, :])
    )
    total_rows = groups * CAP

    live["moe_rows"] = compact(starts, where, pos_row, moe_in, groups, cols)

    def run_expert(expert):
        pieces, row_numbers = [], []
        for far in range(groups):
            for place, piece in weight_flows[expert, far].finish().items():
                pieces.append(piece)
                row_numbers.append(row_of_set(place, far))
        here = slice(expert * total_rows, (expert + 1) * total_rows)
        return expert_step(
            jnp.stack(row_numbers),
            live["moe_rows"][expert],
            live["cot_rows"][expert],
            row_gate[here],
            row_scale[here],
            pieces,
        )

    blocks_here = [
        (hi ^ above) * groups + (lo ^ far)
        for far in reversed(range(groups))
        for above in range(high)
    ]
    grad_places = jnp.stack(blocks_here + blocks_here + [mid])
    grad_flows = {}

    def start_grads(expert, outs):
        grads = weight_grads(
            grad_places,
            live["moe_rows"][expert],
            live["cot_rows"][expert],
            outs[1],
            outs[2],
            depth,
            groups,
            mids,
            high,
        )
        return grads.reshape((groups, mids * high) + grads.shape[3:])

    def grad_flow(expert, grads):
        for number, far in enumerate(reversed(range(groups))):
            grad_flows[expert, far] = Flow(expert_grad_steps(grads[number], far, far_bits))

    def running():
        return list(grad_flows.values())

    ran = []
    for expert in range(each):
        others = [flow for (number, _), flow in weight_flows.items() if number > expert]
        (outs,) = stage(
            live,
            others + running()[:1],
            [functools.partial(run_expert, expert)],
            sync=running()[1:],
        )
        ran.append(outs)
        if expert + 1 < each:
            (grads,) = stage(live, others, [functools.partial(start_grads, expert, outs)])
            grad_flow(expert, grads)
    early = running()
    live["result"] = [outs[5] for outs in ran]
    last = ran[-1]
    gate_cot = jnp.concatenate([outs[3] for outs in ran], axis=0)
    row_inner = jnp.concatenate([outs[4] for outs in ran], axis=0)
    sizes = part_sizes(tok_rows, len(links))
    live["scalars"] = (gate_cot, row_inner)
    (rows_parts,) = stage(
        live,
        [],
        [
            lambda: expand(
                starts, where, pos_col, [outs[0] for outs in ran], sizes, groups, cols
            )
        ],
    )
    gate_cot, row_inner = expand_scalars(starts, pos_row, live.pop("scalars"))
    gate_cot = gate_cot.reshape(each, groups, tok_rows)
    row_inner = jnp.sum(row_inner.reshape(each, groups, tok_rows), axis=0)[None]
    scalars = jnp.concatenate([gate_cot, row_inner], axis=0)
    scalars = scalars.reshape((each + 1) * groups, tok_rows)
    scalar_flow = Flow(spread_cube_steps(scalars, groups, cols))
    moe_in_flow = Flow(reduce_steps(rows_parts, groups, cols))
    (grads,) = stage(
        live,
        [moe_in_flow, scalar_flow] + early,
        [functools.partial(start_grads, each - 1, last)],
    )
    grad_flow(each - 1, grads)
    late = running()[len(early) :]
    scalar_flow.finish()
    (branch_parts,) = stage(
        live,
        [moe_in_flow] + early[1:] + late[:1],
        [lambda: expand_all(starts, where, pos_col, live["result"], groups, cols)],
        sync=[scalar_flow],
    )
    live["moe_branch"] = branch_parts.reshape(groups * cols, tok_rows, width)
    while moe_in_flow.sends is not None:
        stage(live, [moe_in_flow], sync=early + late)
    scalar_all = scalar_flow.finish().reshape(groups, cols, each + 1, groups, tok_rows)
    scalar_all = jnp.stack([scalar_all[place, :, :, place] for place in range(groups)])
    by_expert = jnp.stack(
        [
            ((lo ^ (number // each % groups)) * cols + (col ^ (number // (each * groups)))) * each
            + number % each
            for number in range(EXPERTS)
        ]
    )
    gate_cot = jnp.take(scalar_all[:, :, :each].reshape(EXPERTS, tok_rows), by_expert, axis=0)
    my_gates, my_logits = gates[0], all_logits[0]
    logit_cot = my_gates * (gate_cot - jnp.sum(my_gates * gate_cot, axis=0, keepdims=True))
    inner = jnp.sum(scalar_all[:, :, each], axis=(0, 1)) + jnp.sum(logit_cot * my_logits, axis=0)
    scaled_logit = (logit_cot * moe_inverse[0][None, :]).astype(BF16)
    logit_cot = logit_cot.astype(BF16)
    my_inverse = moe_inverse[0][:, None]

    back = moe_in_flow.finish() + my_inverse * dot_of(logit_cot, router_rows, 0, 0)
    middle_cot = (
        out_cot.astype(F32)
        + back * moe_gain
        - middle * (my_inverse * my_inverse * (inner[:, None] / D))
    )
    cot_flow = Flow(spread_steps(middle_cot.astype(BF16), "col", col_bits))
    router_part, moe_gain_part = stage(
        live,
        [cot_flow] + early[:1],
        [
            lambda: dot_of(scaled_logit, scaled_rows, 1, 0),
            lambda: jnp.sum(back * middle, axis=0)[None],
        ],
    )
    cot_blocks = cot_flow.finish()
    moe_branch = lax.psum_scatter(
        live.pop("moe_branch"), cube, scatter_dimension=0, tiled=True
    )[0]

    cot_all = jnp.concatenate(cot_blocks, axis=1)

    def attend_back(s):
        mixture_cot = dot_of(cot_all[seq_rows[s]], out_rel, 1, 0).astype(BF16)
        *cots, query_part, key_part, token_inner = attend_backward(
            s,
            lengths[s : s + 1],
            attended[s][1:],
            mixture_cot,
            live["qkv"],
            tables,
            query_scale,
            key_scale,
            heads,
        )
        cots = jnp.concatenate(cots, axis=1)
        return cots, query_part, key_part, token_inner[:, 0]

    qkv_rel = jnp.concatenate(
        [
            lax.dynamic_slice_in_dim(live["qkv_full"], (col ^ place) * width, width, 0)
            for place in range(cols)
        ],
        axis=0,
    )
    mixture = jnp.concatenate([outs[0] for outs in attended], axis=0)
    live.update(qkv_rel=qkv_rel, mixture=mixture, cot_all=cot_all)
    done = stage(
        live,
        late,
        [functools.partial(attend_back, s) for s in range(seqs)],
    )
    share = width // (mids * depth)
    cot_places = [((n // share) ^ col) * share + n % share for n in blocks_here]

    live["qkv_cot"] = jnp.concatenate([outs[0] for outs in done], axis=0)

    def projection_grads():
        grads = weight_grads(
            jnp.stack(blocks_here + cot_places + [mid]),
            live["normed_attn"],
            live["cot_all"],
            live["qkv_cot"],
            live["mixture"],
            depth,
            groups,
            mids,
            high,
        )
        return grads

    def widen(blocks):
        full = jnp.zeros((blocks[0].shape[0], D), F32)
        for place, block in enumerate(blocks):
            full = lax.dynamic_update_slice_in_dim(full, block, (col ^ place) * width, 1)
        return full

    def input_cots():
        partial = dot_of(live["qkv_cot"], live["qkv_rel"], 1, 1)
        backs = [partial[:, n * width : (n + 1) * width] for n in range(cols)]
        attn_flow = Flow(col_reduce_steps(backs, cols)).step(len(bits_of(cols)) - 1)
        attn_gain_parts = [
            jnp.sum(part * (block.astype(F32) * attn_inverse), axis=0)[None]
            for part, block in zip(backs, hidden_blocks)
        ]
        token_inner = jnp.concatenate([outs[3] for outs in done], axis=0)
        inner_flow = Flow(total_steps(token_inner, [("col",)]))
        inner_flow.finish()
        query_part = sum(outs[1] for outs in done)
        key_part = sum(outs[2] for outs in done)
        head_parts = jnp.concatenate([query_part, key_part], 1)
        small = jnp.concatenate(
            [
                widen([router_part]),
                widen([moe_gain_part]),
                widen(attn_gain_parts),
                jnp.pad(head_parts, ((0, 0), (0, D - 2 * HD))),
            ],
            axis=0,
        )
        small_flow = Flow(total_steps(small, [("col",), ("lo", "mid"), ("hi",)])).step()
        flows.extend([attn_flow, inner_flow, small_flow])
        return [flow.holds() for flow in flows]

    flows = []
    late[1].step()
    (held,) = stage(live, [], [input_cots])
    for flow, arrays in zip(flows, held):
        flow.replace(arrays)
    attn_flow, inner_flow, small_flow = flows
    attn_flow.step()
    (grads,) = stage(live, [], [projection_grads])
    qkv_flow = Flow(row_reduce_steps(grads, groups, mids, high))
    stage(live, [qkv_flow, small_flow], sync=[attn_flow, late[1]])
    live["moe_branch"] = moe_branch

    def input_sums():
        return (
            middle_cot
            + attn_inverse * (attn_flow.finish() * attn_gain)
            - hidden * (attn_inverse * attn_inverse * (inner_flow.finish()[:, None] / D))
        )

    (input_grad,) = stage(live, [qkv_flow, small_flow] + early[:1] + late, [input_sums])
    flows = [qkv_flow, small_flow] + early + late
    while any(flow.sends is not None for flow in flows):
        stage(live, flows)
    moe_branch = live["moe_branch"]
    weight_sum = qkv_flow.finish()
    out_sum = weight_sum[:, 3 * width :]
    small = small_flow.finish()

    output = (middle + moe_branch.astype(F32)).astype(BF16)
    gate_grad, up_grad, down_grad = unpack_grads(
        where,
        [grad_flows[expert, far].finish() for far in range(groups) for expert in range(each)],
        each,
    )
    own = lax.dynamic_slice_in_dim(small, col * width, width, 1)
    router_grad = lax.dynamic_slice_in_dim(small[:EXPERTS], row * depth, depth, 1).T
    return (
        output,
        input_grad,
        own[EXPERTS + 1],
        small[EXPERTS + 2, :HD],
        small[EXPERTS + 2, HD : 2 * HD],
        weight_sum[:, :width],
        weight_sum[:, width : 2 * width],
        weight_sum[:, 2 * width : 3 * width],
        out_sum.T,
        own[EXPERTS],
        router_grad,
        gate_grad,
        up_grad,
        down_grad,
    )


def solution(mesh):
    row_count, col_count = mesh.shape["row"], mesh.shape["col"]
    groups = 2
    between = EXPERTS // col_count // groups
    shape = (row_count // (groups * between), groups, between, col_count)
    inner = Mesh(mesh.devices.reshape(shape), ("hi", "lo", "mid", "col"))
    row = ("hi", "lo", "mid")
    return jax.shard_map(
        per_device,
        mesh=inner,
        in_specs=(
            P(row, "col"),
            P(row),
            P(row, None),
            P("col"),
            P(),
            P(),
            P(row, "col"),
            P(row, "col"),
            P(row, "col"),
            P("col", row),
            P("col"),
            P(row, None),
            P("col", row, None),
            P("col", row, None),
            P("col", None, row),
            P(row, "col"),
        ),
        out_specs=(
            P(row, "col"),
            P(row, "col"),
            P("col"),
            P(),
            P(),
            P(row, "col"),
            P(row, "col"),
            P(row, "col"),
            P("col", row),
            P("col"),
            P(row, None),
            P("col", row, None),
            P("col", row, None),
            P("col", None, row),
        ),
        check_vma=False,
    )
```

```python
import functools
import math

import jax
import jax.numpy as jnp
from jax import lax
from jax.experimental import pallas as pl
from jax.experimental.pallas import tpu as pltpu
from jax.sharding import Mesh, PartitionSpec as P

D = 2048
HD = 128
EXPERTS = 16
SEQ_LEN = 1024
CAP = 1152

BLOCK = 128
WINDOW = 144
EDGE = 16
TILE = 384
COST_SHARE = 50
EXPERT_WIDE, EXPERT_UNROLL = 512, 2
GRAD_WIDE, GRAD_UNROLL = 512, 1

epsilon = 1e-06
rope_base = 10000.0
masked_score = -1e30

F32 = jnp.float32
BF16 = jnp.bfloat16
ANY = pl.ANY
VMEM_LIMIT = 56 * 1024 * 1024


def dot_of(a, b, da, db):
    return lax.dot_general(a, b, (((da,), (db,)), ((), ())), preferred_element_type=F32)


def params(*semantics):
    return pltpu.CompilerParams(
        vmem_limit_bytes=VMEM_LIMIT, dimension_semantics=semantics or None
    )


def cost(flops, bytes_accessed, transcendentals=0):
    return pl.CostEstimate(
        flops=int(flops) // COST_SHARE,
        bytes_accessed=int(bytes_accessed) // COST_SHARE,
        transcendentals=int(transcendentals) // COST_SHARE,
    )


def turn(values, cosine, sine):
    return values * cosine + pltpu.roll(values, HD // 2, 1) * sine


def attend_forward_kernel(
    live_ref, q_ref, k_ref, v_ref, cos_ref, sin_ref, qg_ref, kg_ref, mix_ref, ql_ref, kl_ref, vl_ref
):
    live = live_ref[0]
    cosine = cos_ref[...]
    sine = sin_ref[...]

    def normed(values, gain):
        inverse = lax.rsqrt(jnp.mean(values * values, axis=1, keepdims=True) + epsilon)
        return turn(values * inverse * gain, cosine, sine).astype(BF16)

    ql_ref[...] = normed(q_ref[...], qg_ref[...])
    kl_ref[...] = normed(k_ref[...], kg_ref[...])
    vl_ref[...] = v_ref[...].astype(BF16)
    keys = kl_ref[...]
    values = vl_ref[...]
    rows = 256
    place = lax.broadcasted_iota(jnp.int32, (rows, SEQ_LEN), 1)
    for part in range(SEQ_LEN // rows):
        here = pl.ds(part * rows, rows)
        scores = dot_of(ql_ref[here, :], keys, 1, 1) * (1.0 / math.sqrt(HD))
        scores = jnp.where(place < live, scores, masked_score)
        top = jnp.max(scores, axis=1, keepdims=True)
        shifted = jnp.exp(scores - top)
        total = jnp.sum(shifted, axis=1, keepdims=True)
        probs = (shifted * (1.0 / total)).astype(BF16)
        mix_ref[here, :] = dot_of(probs, values, 1, 0).astype(BF16)


def attend_forward(seq, live, qkv, tables, query_gain, key_gain, heads):
    width = heads * HD

    def pick(offset):
        return pl.BlockSpec((SEQ_LEN, HD), lambda h, live, o=offset: (seq, o + h))

    def whole(shape):
        return pl.BlockSpec(shape, lambda h, live: (0, 0))

    out = pl.BlockSpec((SEQ_LEN, HD), lambda h, live: (0, h))
    return pl.pallas_call(
        attend_forward_kernel,
        grid_spec=pltpu.PrefetchScalarGridSpec(
            num_scalar_prefetch=1,
            grid=(heads,),
            in_specs=[
                pick(0),
                pick(heads),
                pick(2 * heads),
                whole((SEQ_LEN, HD)),
                whole((SEQ_LEN, HD)),
                whole((1, HD)),
                whole((1, HD)),
            ],
            out_specs=[out] * 4,
        ),
        out_shape=[jax.ShapeDtypeStruct((SEQ_LEN, width), BF16)] * 4,
        compiler_params=params("arbitrary"),
        cost_estimate=cost(
            heads * 8 * SEQ_LEN * SEQ_LEN * HD, 20 * SEQ_LEN * width, heads * SEQ_LEN * SEQ_LEN
        ),
        name="attend_forward",
    )(live, qkv, qkv, qkv, tables[0], tables[1], query_gain, key_gain)


def attend_backward_kernel(
    live_ref,
    ql_ref,
    kl_ref,
    vl_ref,
    do_ref,
    q_ref,
    k_ref,
    cos_ref,
    sin_ref,
    qg_ref,
    kg_ref,
    qc_ref,
    kc_ref,
    vc_ref,
    qpart_ref,
    kpart_ref,
    inner_ref,
    dq_ref,
    dk_ref,
    dv_ref,
):
    head = pl.program_id(0)
    live = live_ref[0]
    scale = 1.0 / math.sqrt(HD)
    keys = kl_ref[...]
    values = vl_ref[...]
    rows = 256
    place = lax.broadcasted_iota(jnp.int32, (SEQ_LEN, rows), 0)
    for part in range(SEQ_LEN // rows):
        here = pl.ds(part * rows, rows)
        queries = ql_ref[here, :]
        incoming = do_ref[here, :]
        scores = dot_of(keys, queries, 1, 1) * scale
        scores = jnp.where(place < live, scores, masked_score)
        top = jnp.max(scores, axis=0, keepdims=True)
        shifted = jnp.exp(scores - top)
        total = jnp.sum(shifted, axis=0, keepdims=True)
        probs = shifted * (1.0 / total)
        dv = dot_of(probs.astype(BF16), incoming, 1, 0)
        probs_cot = dot_of(values, incoming, 1, 1)
        weighted = probs * probs_cot
        centre = jnp.sum(weighted, axis=0, keepdims=True)
        raw = ((weighted - probs * centre) * scale).astype(BF16)
        dk = dot_of(raw, queries, 1, 0)
        dq_ref[here, :] = dot_of(raw, keys, 0, 0)
        if part == 0:
            dv_ref[...] = dv
            dk_ref[...] = dk
        else:
            dv_ref[...] += dv
            dk_ref[...] += dk
    cosine = cos_ref[...]
    sine = -sin_ref[...]

    def back(values, gain, rotated_cot):
        incoming = turn(rotated_cot, cosine, sine)
        inverse = lax.rsqrt(jnp.mean(values * values, axis=1, keepdims=True) + epsilon)
        scaled = incoming * gain
        inner = jnp.mean(scaled * values, axis=1, keepdims=True)
        grad = inverse * scaled - values * (inverse * inverse * inverse * inner)
        part = jnp.sum(incoming * values * inverse, axis=0, keepdims=True)
        return grad.astype(BF16), part, jnp.sum(grad * values, axis=1, keepdims=True)

    qc_ref[...], qpart, inner = back(q_ref[...], qg_ref[...], dq_ref[...])
    kc_ref[...], kpart, key_inner = back(k_ref[...], kg_ref[...], dk_ref[...])
    vc_ref[...] = dv_ref[...].astype(BF16)
    inner += key_inner
    inner += jnp.sum(dv_ref[...] * values.astype(F32), axis=1, keepdims=True)

    @pl.when(head == 0)
    def _():
        qpart_ref[...] = qpart
        kpart_ref[...] = kpart
        inner_ref[...] = inner

    @pl.when(head > 0)
    def _():
        qpart_ref[...] += qpart
        kpart_ref[...] += kpart
        inner_ref[...] += inner


def attend_backward(seq, live, lows, mixture_cot, qkv, tables, query_gain, key_gain, heads):
    width = heads * HD
    block = pl.BlockSpec((SEQ_LEN, HD), lambda h, live: (0, h))

    def pick(offset):
        return pl.BlockSpec((SEQ_LEN, HD), lambda h, live, o=offset: (seq, o + h))

    def whole(shape):
        return pl.BlockSpec(shape, lambda h, live: (0, 0))

    return pl.pallas_call(
        attend_backward_kernel,
        grid_spec=pltpu.PrefetchScalarGridSpec(
            num_scalar_prefetch=1,
            grid=(heads,),
            in_specs=[block] * 4
            + [
                pick(0),
                pick(heads),
                whole((SEQ_LEN, HD)),
                whole((SEQ_LEN, HD)),
                whole((1, HD)),
                whole((1, HD)),
            ],
            out_specs=[block] * 3 + [whole((1, HD))] * 2 + [whole((SEQ_LEN, 1))],
            scratch_shapes=[pltpu.VMEM((SEQ_LEN, HD), F32)] * 3,
        ),
        out_shape=[jax.ShapeDtypeStruct((SEQ_LEN, width), BF16)] * 3
        + [jax.ShapeDtypeStruct((1, HD), F32)] * 2
        + [jax.ShapeDtypeStruct((SEQ_LEN, 1), F32)],
        compiler_params=params("arbitrary"),
        cost_estimate=cost(
            heads * 20 * SEQ_LEN * SEQ_LEN * HD, 24 * SEQ_LEN * width, heads * SEQ_LEN * SEQ_LEN
        ),
        name="attend_backward",
    )(live, *lows, mixture_cot, qkv, qkv, tables[0], tables[1], query_gain, key_gain)


def compact_kernel(start_ref, where_ref, pos_ref, source_ref, *outs):
    group, groups = pl.program_id(0), pl.num_programs(0)
    row_of = lax.broadcasted_iota(jnp.int32, (WINDOW, BLOCK), 0)
    for out in outs:
        out[...] = jnp.zeros_like(out)
    for number in range(source_ref.shape[1] // BLOCK):
        here = slice(number * BLOCK, (number + 1) * BLOCK)
        for expert, out in enumerate(outs):
            start = pl.multiple_of(start_ref[expert * groups + group, number], EDGE)
            place = pos_ref[expert, 0, :, here]
            choice = jnp.where(row_of + start == place, 1.0, 0.0).astype(BF16)
            rows = dot_of(choice, source_ref[0, here, :], 1, 0)
            out[pl.ds(start, WINDOW), :] += rows.astype(BF16)


def compact(starts, where, pos_row, source, groups, cols):
    tokens, width = source.shape[1:]
    count = pos_row.shape[0] // groups
    return pl.pallas_call(
        compact_kernel,
        grid_spec=pltpu.PrefetchScalarGridSpec(
            num_scalar_prefetch=2,
            grid=(groups, cols),
            in_specs=[
                pl.BlockSpec((count, 1, 1, tokens), lambda q, j, s, w: (0, q, 0, 0)),
                pl.BlockSpec(
                    (1, tokens, width), lambda q, j, s, w: ((w[0] ^ q) * cols + j, 0, 0)
                ),
            ],
            out_specs=[pl.BlockSpec((CAP, width), lambda q, j, s, w: (q, j))] * count,
        ),
        out_shape=[jax.ShapeDtypeStruct((groups * CAP, cols * width), BF16)] * count,
        compiler_params=params("arbitrary", "arbitrary"),
        cost_estimate=cost(
            count * groups * cols * 2 * tokens * WINDOW * width * 2,
            groups * cols * 2 * width * (tokens + count * CAP),
        ),
        name="compact",
    )(starts, where, pos_row.reshape(count, groups, 1, tokens), source)


def compact_scalars_kernel(start_ref, pos_ref, *refs):
    count = len(refs) // 2
    group = pl.program_id(0)
    row_of = lax.broadcasted_iota(jnp.int32, (WINDOW, BLOCK), 0)
    for number in range(count):
        refs[count + number][...] = jnp.zeros_like(refs[count + number])
    for number in range(pos_ref.shape[2] // BLOCK):
        start = pl.multiple_of(start_ref[group, number], EDGE)
        here = slice(number * BLOCK, (number + 1) * BLOCK)
        choice = row_of + start == pos_ref[0, :, here]
        for source, out in zip(refs[:count], refs[count:]):
            picked = jnp.sum(jnp.where(choice, source[0, :, here], 0.0), axis=1, keepdims=True)
            out[pl.ds(start, WINDOW), :] += picked


def compact_scalars(starts, pos_row, sources):
    groups, _, tokens = pos_row.shape
    block = pl.BlockSpec((1, 1, tokens), lambda q, s: (q, 0, 0))
    return pl.pallas_call(
        compact_scalars_kernel,
        grid_spec=pltpu.PrefetchScalarGridSpec(
            num_scalar_prefetch=1,
            grid=(groups,),
            in_specs=[block] * (1 + len(sources)),
            out_specs=[pl.BlockSpec((CAP, 1), lambda q, s: (q, 0))] * len(sources),
        ),
        out_shape=[jax.ShapeDtypeStruct((groups * CAP, 1), F32)] * len(sources),
        compiler_params=params("arbitrary"),
        cost_estimate=cost(0, 4 * groups * CAP * 128 * len(sources)),
        name="compact_scalars",
    )(starts, pos_row, *sources)


def expand_scalars_kernel(start_ref, pos_ref, *refs):
    count = len(refs) // 2
    group = pl.program_id(0)
    row_of = lax.broadcasted_iota(jnp.int32, (WINDOW, BLOCK), 0)
    for number in range(pos_ref.shape[2] // BLOCK):
        start = pl.multiple_of(start_ref[group, number], EDGE)
        here = slice(number * BLOCK, (number + 1) * BLOCK)
        choice = row_of + start == pos_ref[0, :, here]
        for source, out in zip(refs[:count], refs[count:]):
            held = source[pl.ds(start, WINDOW), :]
            out[0, :, here] = jnp.sum(jnp.where(choice, held, 0.0), axis=0, keepdims=True)


def expand_scalars(starts, pos_row, sources):
    groups, _, tokens = pos_row.shape
    block = pl.BlockSpec((1, 1, tokens), lambda q, s: (q, 0, 0))
    return pl.pallas_call(
        expand_scalars_kernel,
        grid_spec=pltpu.PrefetchScalarGridSpec(
            num_scalar_prefetch=1,
            grid=(groups,),
            in_specs=[block] + [pl.BlockSpec((CAP, 1), lambda q, s: (q, 0))] * len(sources),
            out_specs=[block] * len(sources),
        ),
        out_shape=[jax.ShapeDtypeStruct((groups, 1, tokens), F32)] * len(sources),
        compiler_params=params("arbitrary"),
        cost_estimate=cost(0, 4 * groups * CAP * 128 * len(sources)),
        name="expand_scalars",
    )(starts, pos_row, *sources)


def expand_kernel(sizes, count, start_ref, where_ref, pos_ref, *refs):
    group, groups = pl.program_id(0), pl.num_programs(0)
    sides = len(refs) // (count + len(sizes))
    sources, outs = refs[: count * sides], refs[count * sides :]
    column_of = lax.broadcasted_iota(jnp.int32, (BLOCK, WINDOW), 1)
    number = 0
    for part, size in enumerate(sizes):
        for step in range(size // BLOCK):
            totals = [None] * sides
            for expert in range(count):
                start = pl.multiple_of(start_ref[expert * groups + group, number], EDGE)
                place = pos_ref[expert, 0, number * BLOCK : (number + 1) * BLOCK, :]
                choice = jnp.where(column_of + start == place, 1.0, 0.0).astype(BF16)
                for side in range(sides):
                    held = sources[expert * sides + side][pl.ds(start, WINDOW), :]
                    rows = dot_of(choice, held, 1, 0)
                    totals[side] = rows if totals[side] is None else totals[side] + rows
            here = slice(step * BLOCK, (step + 1) * BLOCK)
            for side in range(sides):
                outs[part * sides + side][0, 0, here, :] = totals[side].astype(BF16)
            number += 1


def expand(starts, where, pos_col, sources, sizes, groups, cols):
    width = sources[0].shape[1] // cols
    tokens = sum(sizes)
    count = len(sources)

    def side(odd):
        return pl.BlockSpec((CAP, width), lambda q, j, s, w: (q, w[1] ^ (2 * j + odd)))

    outs = pl.pallas_call(
        functools.partial(expand_kernel, sizes, count),
        grid_spec=pltpu.PrefetchScalarGridSpec(
            num_scalar_prefetch=2,
            grid=(groups, cols // 2),
            in_specs=[pl.BlockSpec((count, 1, tokens, 1), lambda q, j, s, w: (0, q, 0, 0))]
            + [side(0), side(1)] * count,
            out_specs=[
                pl.BlockSpec((1, 1, size, width), lambda q, j, s, w: (q, j, 0, 0))
                for size in sizes
                for _ in range(2)
            ],
        ),
        out_shape=[
            jax.ShapeDtypeStruct((groups, cols // 2, size, width), BF16)
            for size in sizes
            for _ in range(2)
        ],
        compiler_params=params("arbitrary", "arbitrary"),
        cost_estimate=cost(
            4 * count * groups * cols * tokens * WINDOW * width,
            groups * cols * width * (2 * tokens + 2 * count * CAP),
        ),
        name="expand",
    )(
        starts,
        where,
        pos_col.reshape(count, groups, tokens, 1),
        *[source for source in sources for _ in range(2)],
    )
    return list(zip(outs[::2], outs[1::2]))


def expand_all(starts, where, pos_col, sources, groups, cols):
    width = sources[0].shape[1] // cols
    tokens = pos_col.shape[1]
    count = len(sources)
    return pl.pallas_call(
        functools.partial(expand_kernel, [tokens], count),
        grid_spec=pltpu.PrefetchScalarGridSpec(
            num_scalar_prefetch=2,
            grid=(groups, cols),
            in_specs=[pl.BlockSpec((count, 1, tokens, 1), lambda q, j, s, w: (0, q, 0, 0))]
            + [pl.BlockSpec((CAP, width), lambda q, j, s, w: (q, j))] * count,
            out_specs=pl.BlockSpec((1, 1, tokens, width), lambda q, j, s, w: (w[0] ^ q, j, 0, 0)),
        ),
        out_shape=jax.ShapeDtypeStruct((groups, cols, tokens, width), BF16),
        compiler_params=params("arbitrary", "arbitrary"),
        cost_estimate=cost(
            4 * count * groups * cols * tokens * WINDOW * width,
            groups * cols * width * (2 * tokens + 2 * count * CAP),
        ),
        name="expand_all",
    )(starts, where, pos_col.reshape(count, groups, tokens, 1), *sources)


def pack_kernel(where_ref, gate_ref, up_ref, down_ref, out_ref):
    hidden = gate_ref.shape[2]
    out_ref[0, :, :hidden] = gate_ref[0].astype(BF16)
    out_ref[0, :, hidden : 2 * hidden] = up_ref[0].astype(BF16)
    out_ref[0, :, 2 * hidden :] = down_ref[0].T.astype(BF16)


def pack_weights(where, gate, up, down, each):
    experts, depth, hidden = gate.shape

    def pick(shape):
        return pl.BlockSpec(shape, lambda q, w: ((w[0] ^ (q // each)) * each + q % each, 0, 0))

    return pl.pallas_call(
        pack_kernel,
        grid_spec=pltpu.PrefetchScalarGridSpec(
            num_scalar_prefetch=1,
            grid=(experts,),
            in_specs=[pick((1, depth, hidden)), pick((1, depth, hidden)), pick((1, hidden, depth))],
            out_specs=pl.BlockSpec((1, depth, 3 * hidden), lambda q, w: (q, 0, 0)),
        ),
        out_shape=jax.ShapeDtypeStruct((experts, depth, 3 * hidden), BF16),
        compiler_params=params("arbitrary"),
        cost_estimate=cost(0, 18 * experts * depth * hidden),
        name="pack_weights",
    )(where, gate, up, down)


def unpack_kernel(where_ref, *refs):
    sources, (gate_ref, up_ref, down_ref) = refs[:-3], refs[-3:]
    hidden = gate_ref.shape[2]
    for number, source in enumerate(sources):

        @pl.when(pl.program_id(0) == number)
        def _(source=source):
            gate_ref[0] = source[:, :hidden].astype(F32)
            up_ref[0] = source[:, hidden : 2 * hidden].astype(F32)
            down_ref[0] = source[:, 2 * hidden :].astype(F32).T


def unpack_grads(where, sources, each):
    count = len(sources)
    depth, wide = sources[0].shape
    hidden = wide // 3

    def pick(shape):
        return pl.BlockSpec(shape, lambda q, w: ((w[0] ^ (q // each)) * each + q % each, 0, 0))

    shapes = [(count, depth, hidden), (count, depth, hidden), (count, hidden, depth)]
    return pl.pallas_call(
        unpack_kernel,
        grid_spec=pltpu.PrefetchScalarGridSpec(
            num_scalar_prefetch=1,
            grid=(count,),
            in_specs=[pl.BlockSpec((depth, wide), lambda q, w: (0, 0))] * count,
            out_specs=[pick((1,) + shape[1:]) for shape in shapes],
        ),
        out_shape=[jax.ShapeDtypeStruct(shape, F32) for shape in shapes],
        compiler_params=params("arbitrary"),
        cost_estimate=cost(0, 18 * count * depth * hidden),
        name="unpack_grads",
    )(where, *sources)


def expert_kernel(count, hidden, row_ref, x_ref, m_ref, gate_ref, scale_ref, *refs):
    pieces = refs[:count]
    rows_ref, pre_ref, act_ref, cot_ref, inner_ref, result_ref, held, sems = refs[count:]
    depth = pieces[0].shape[0]

    @pl.when(pl.program_id(0) == 0)
    def _():
        copies = []
        for number, piece in enumerate(pieces):
            place = pl.ds(pl.multiple_of(row_ref[number] * depth, depth), depth)
            copies.append(pltpu.make_async_copy(piece, held.at[place, :], sems.at[number]))
        for copy in copies:
            copy.start()
        for copy in copies:
            copy.wait()

    gate = gate_ref[...]
    scale = scale_ref[...]
    wide = EXPERT_WIDE
    cot_ref[...] = jnp.zeros_like(cot_ref)
    inner_ref[...] = jnp.zeros_like(inner_ref)

    @pl.loop(0, hidden // wide, unroll=EXPERT_UNROLL)
    def _(step):
        first = pl.multiple_of(step * wide, wide)
        gate_pre = dot_of(x_ref[...], held[:, pl.ds(first, wide)], 1, 0) * scale
        up_pre = dot_of(x_ref[...], held[:, pl.ds(hidden + first, wide)], 1, 0) * scale
        back = dot_of(m_ref[...], held[:, pl.ds(2 * hidden + first, wide)], 1, 0)
        squash = 1.0 / (1.0 + jnp.exp(-gate_pre))
        silu = gate_pre * squash
        active = silu * up_pre
        cot_ref[...] += jnp.sum(active.astype(BF16).astype(F32) * back, axis=1, keepdims=True)
        act_ref[:, pl.ds(first, wide)] = (active * gate).astype(BF16)
        back = back * gate
        slope = squash * (1.0 + gate_pre * (1.0 - squash))
        gate_cot = back * up_pre * slope
        up_cot = back * silu
        inner_ref[...] += jnp.sum(gate_cot * gate_pre + up_cot * up_pre, axis=1, keepdims=True)
        pre_ref[:, pl.ds(first, wide)] = (gate_cot * scale).astype(BF16)
        pre_ref[:, pl.ds(hidden + first, wide)] = (up_cot * scale).astype(BF16)

    @pl.loop(0, held.shape[0] // wide, unroll=EXPERT_UNROLL)
    def _(step):
        first = pl.multiple_of(step * wide, wide)
        here = pl.ds(first, wide)
        rows_ref[:, here] = dot_of(pre_ref[...], held[here, : 2 * hidden], 1, 1).astype(BF16)
        result_ref[:, here] = dot_of(act_ref[...], held[here, 2 * hidden :], 1, 1).astype(BF16)


def expert_step(row_numbers, x, m, gate, scale, pieces):
    total, wide = x.shape
    hidden = pieces[0].shape[1] // 3
    count = len(pieces)

    def tile(columns):
        return pl.BlockSpec((TILE, columns), lambda i, r: (i, 0))

    return pl.pallas_call(
        functools.partial(expert_kernel, count, hidden),
        grid_spec=pltpu.PrefetchScalarGridSpec(
            num_scalar_prefetch=1,
            grid=(total // TILE,),
            in_specs=[tile(wide), tile(wide), tile(1), tile(1)]
            + [pl.BlockSpec(memory_space=ANY)] * count,
            out_specs=[tile(wide), tile(2 * hidden), tile(hidden), tile(1), tile(1), tile(wide)],
            scratch_shapes=[
                pltpu.VMEM((wide, 3 * hidden), BF16),
                pltpu.SemaphoreType.DMA((count,)),
            ],
        ),
        out_shape=[
            jax.ShapeDtypeStruct((total, wide), BF16),
            jax.ShapeDtypeStruct((total, 2 * hidden), BF16),
            jax.ShapeDtypeStruct((total, hidden), BF16),
            jax.ShapeDtypeStruct((total, 1), F32),
            jax.ShapeDtypeStruct((total, 1), F32),
            jax.ShapeDtypeStruct((total, wide), BF16),
        ],
        compiler_params=params("arbitrary"),
        cost_estimate=cost(
            2 * total * wide * hidden * 6, 2 * total * (4 * wide + 3 * hidden), total * hidden
        ),
        name="expert_step",
    )(row_numbers, x, m, gate, scale, *pieces)


def weight_grad_kernel(mids, place_ref, x_ref, m_ref, pre_ref, act_ref, out_ref, turned_ref):
    wide = GRAD_WIDE
    first = pre_ref.shape[1]
    depth = x_ref.shape[1] // mids
    turned_ref[0] = x_ref[...].T
    turned_ref[1] = m_ref[...].T
    mid = place_ref[place_ref.shape[0] - 1]

    def put(grad, here):
        for number in range(mids):
            block = grad[number * depth : (number + 1) * depth].astype(BF16)
            out_ref[0, number ^ mid, 0, :, here] = block

    @pl.loop(0, first // wide, unroll=GRAD_UNROLL)
    def _(step):
        here = pl.ds(pl.multiple_of(step * wide, wide), wide)
        put(dot_of(turned_ref[0], pre_ref[:, here], 1, 0), here)

    @pl.loop(0, act_ref.shape[1] // wide, unroll=GRAD_UNROLL)
    def _(step):
        here = pl.ds(pl.multiple_of(step * wide, wide), wide)
        there = pl.ds(pl.multiple_of(first + step * wide, wide), wide)
        put(dot_of(turned_ref[1], act_ref[:, here], 1, 0), there)


def weight_grads(places, x, m, pre, act, depth, groups, mids, high):
    total = x.shape[0]
    wide = pre.shape[1] + act.shape[1]

    def column(first):
        return pl.BlockSpec((total, mids * depth), lambda f, h, r: (0, r[first + f * high + h]))

    def whole(array):
        return pl.BlockSpec(array.shape, lambda f, h, r: (0, 0), pipeline_mode=pl.Buffered(1))

    return pl.pallas_call(
        functools.partial(weight_grad_kernel, mids),
        grid_spec=pltpu.PrefetchScalarGridSpec(
            num_scalar_prefetch=1,
            grid=(groups, high),
            in_specs=[column(0), column(groups * high), whole(pre), whole(act)],
            out_specs=pl.BlockSpec(
                (1, mids, 1, depth, wide), lambda f, h, r: (f, 0, h, 0, 0)
            ),
            scratch_shapes=[pltpu.VMEM((2, mids * depth, total), BF16)],
        ),
        out_shape=jax.ShapeDtypeStruct((groups, mids, high, depth, wide), BF16),
        compiler_params=params("arbitrary", "arbitrary"),
        cost_estimate=cost(
            2 * total * depth * groups * mids * high * wide,
            2 * total * (2 * depth * groups * mids * high + wide),
        ),
        name="weight_grads",
    )(places, x, m, pre, act)


def bits_of(size):
    return [1 << n for n in range(size.bit_length() - 1)]


def swap(values, axis, bit):
    size = lax.axis_size(axis) if isinstance(axis, str) else math.prod(map(lax.axis_size, axis))
    return lax.ppermute(values, axis, [(n, n ^ bit) for n in range(size)])


class Flow:
    def __init__(self, steps):
        self.steps = steps
        self.result = None
        self.sends = next(steps)

    def advance(self, got):
        try:
            self.sends = self.steps.send(got)
        except StopIteration as stop:
            self.sends = None
            self.result = stop.value

    def step(self, count=1):
        for _ in range(count):
            if self.sends is not None:
                self.advance([swap(*send) for send in self.sends])
        return self

    def finish(self):
        while self.sends is not None:
            self.step()
        return self.result

    def holds(self):
        return self.result if self.sends is None else [send[0] for send in self.sends]

    def replace(self, arrays):
        if self.sends is None:
            self.result = arrays
        else:
            self.sends = [(array, *send[1:]) for array, send in zip(arrays, self.sends)]


def stage(live, flows=(), work=(), sync=()):
    flows = [flow for flow in flows if flow.sends is not None]
    got = [[swap(*send) for send in flow.sends] for flow in flows]
    done = [each() for each in work]
    held = [flow.holds() for flow in sync]
    got, done, held, kept = lax.optimization_barrier((got, done, held, dict(live)))
    live.update(kept)
    for flow, arrays in zip(flows, got):
        flow.advance(arrays)
    for flow, arrays in zip(sync, held):
        flow.replace(arrays)
    return done


def spread_steps(values, axis, bits):
    blocks = {0: values}
    for bit in bits:
        places = sorted(blocks)
        got = yield [(blocks[place], axis, bit) for place in places]
        blocks.update({place | bit: block for place, block in zip(places, got)})
    return [blocks[place] for place in sorted(blocks)]


def spread_rows_steps(values, row_bits, strides):
    held = values[None]
    places = [0]
    for axis, bit in row_bits:
        (got,) = yield [(held, axis, bit)]
        held = jnp.concatenate([held, got], axis=0)
        places += [place | (bit * strides[axis]) for place in places]
    return jnp.stack([held[places.index(place)] for place in range(len(places))])


def spread_cube_steps(values, groups, cols):
    held = values[None]
    for axis, bits in (("lo", bits_of(groups)), ("col", bits_of(cols))):
        for bit in bits:
            (got,) = yield [(held, axis, bit)]
            held = jnp.concatenate([held, got], axis=0)
    return jnp.swapaxes(held.reshape((cols, groups) + values.shape), 0, 1)


def col_reduce_steps(blocks, cols):
    held = dict(enumerate(blocks))
    for bit in bits_of(cols):
        away = [place for place in sorted(held) if place & bit]
        (got,) = yield [(jnp.stack([held[place].astype(BF16) for place in away]), "col", bit)]
        held = {
            place & ~bit: held[place & ~bit] + got[number].astype(F32)
            for number, place in enumerate(away)
        }
    return held[0]


def total_steps(values, axes):
    for axis in axes:
        size = math.prod(map(lax.axis_size, axis))
        got = yield [(values, axis, place) for place in range(1, size)]
        values = values + sum(got)
    return values


def row_reduce_steps(grads, groups, mids, high):
    names = [("lo", bit) for bit in reversed(bits_of(groups))]
    names += [("mid", bit) for bit in reversed(bits_of(mids))]
    names += [("hi", bit) for bit in reversed(bits_of(high))]
    grads = grads.reshape((2,) * len(names) + grads.shape[3:])
    half = grads.shape[-1] // 2
    held = []
    for number in range(2):
        order = [name for name in names if name[0] != "hi"][:: 1 if number else -1]
        order += [name for name in reversed(names) if name[0] == "hi"]
        held.append((grads[..., number * half : (number + 1) * half], names, order))
    for step in range(len(names)):
        sends, rest = [], []
        for array, left, order in held:
            name = order[step]
            axis = left.index(name)
            away = 0 if name[0] == "lo" else 1
            sends.append((lax.index_in_dim(array, away, axis, False).astype(BF16), *name))
            kept = lax.index_in_dim(array, 1 - away, axis, False)
            rest.append((kept, [other for other in left if other != name], order))
        got = yield sends
        held = [
            (kept.astype(F32) + more.astype(F32), left, order)
            for (kept, left, order), more in zip(rest, got)
        ]
    return jnp.concatenate([array for array, _, _ in held], axis=1)


def links_of(groups, cols):
    return [("col", bit) for bit in bits_of(cols)[1:]] + [("lo", bit) for bit in bits_of(groups)]


def turned(links, number):
    number %= len(links)
    return links[number:] + links[:number]


def reduce_steps(parts, groups, cols):
    links = links_of(groups, cols)
    got = yield [(away, "col", 1) for _, away in parts]
    held = []
    for number, (keep, _) in enumerate(parts):
        shape = (2,) * len(links) + keep.shape[2:]
        names = [("lo", bit) for bit in reversed(bits_of(groups))]
        names += [("col", bit) for bit in reversed(bits_of(cols)[1:])]
        held.append((keep.reshape(shape), got[number].reshape(shape), names))
    for step in range(len(links)):
        sends, rest = [], []
        for number, (keep, more, names) in enumerate(held):
            link = turned(links, number)[step]
            axis = names.index(link)

            def half(place):
                total = lax.index_in_dim(keep, place, axis, False).astype(F32)
                return total + lax.index_in_dim(more, place, axis, False).astype(F32)

            sends.append((half(1).astype(BF16), *link))
            kept = half(0)
            rest.append(
                (
                    kept if step + 1 == len(links) else kept.astype(BF16),
                    [name for name in names if name != link],
                )
            )
        got = yield sends
        held = [(keep, more, names) for (keep, names), more in zip(rest, got)]
    return jnp.concatenate([keep.astype(F32) + more.astype(F32) for keep, more, _ in held], axis=0)


def part_sizes(tokens, count):
    whole = tokens // BLOCK
    return [BLOCK * ((whole + count - 1 - n) // count) for n in range(count)]


def expert_weight_steps(piece, far, bits):
    if far:
        (piece,) = yield [(piece, "lo", far)]
    held = {(): piece}
    fresh = [()]
    while True:
        ways = [
            (place, number)
            for place in fresh
            for number in range(place[-1] + 1 if place else 0, len(bits))
        ]
        if not ways:
            return held
        got = yield [(held[place], *bits[number]) for place, number in ways]
        fresh = [place + (number,) for place, number in ways]
        held.update(zip(fresh, got))


def expert_grad_steps(blocks, far, bits):
    for number in reversed(range(len(bits))):
        half = blocks.shape[0] // 2
        (got,) = yield [(blocks[half:], *bits[number])]
        blocks = blocks[:half].astype(F32) + got.astype(F32)
        if number or far:
            blocks = blocks.astype(BF16)
    total = blocks[0]
    if far:
        (total,) = yield [(total, "lo", far)]
    return total


def per_device(
    hidden_in,
    lengths,
    routes,
    attn_gain,
    query_gain,
    key_gain,
    query_weight,
    key_weight,
    value_weight,
    out_weight,
    moe_gain,
    router,
    gate_weight,
    up_weight,
    down_weight,
    cotangent,
):
    tok_rows, width = hidden_in.shape
    cols = lax.axis_size("col")
    groups = lax.axis_size("lo")
    high = lax.axis_size("hi")
    mids = lax.axis_size("mid")
    col = lax.axis_index("col")
    lo = lax.axis_index("lo")
    hi = lax.axis_index("hi")
    mid = lax.axis_index("mid")
    row = (hi * groups + lo) * mids + mid
    where = jnp.stack([lo, col])
    heads = width // HD
    seqs = lengths.shape[0]
    depth = gate_weight.shape[1]
    each = gate_weight.shape[0] // groups
    cube = ("lo", "col")
    rows_axes = ("hi", "lo", "mid")
    strides = {"hi": groups * mids, "lo": mids, "mid": 1}
    seq_rows = [slice(s * SEQ_LEN, (s + 1) * SEQ_LEN) for s in range(seqs)]
    links = links_of(groups, cols)
    col_bits = list(reversed(bits_of(cols)))
    hi_bits = [("hi", bit) for bit in bits_of(high)]
    mid_bits = [("mid", bit) for bit in bits_of(mids)]
    row_bits = hi_bits + [("lo", bit) for bit in bits_of(groups)] + mid_bits
    far_bits = hi_bits + mid_bits
    live = {}

    def row_of_set(place, far):
        other = row ^ (far * mids)
        for number in place:
            axis, bit = far_bits[number]
            other = other ^ (bit * strides[axis])
        return other

    hidden_flow = Flow(spread_steps(hidden_in, "col", col_bits))
    gain_flow = Flow(spread_steps(attn_gain, "col", col_bits))
    routes_flow = Flow(spread_steps(routes.T, "lo", bits_of(groups)))
    router_flow = Flow(spread_rows_steps(router.T.astype(BF16), row_bits, strides))
    out_flow = Flow(spread_rows_steps(out_weight.T.astype(BF16), row_bits, strides))
    qkv_local = jnp.concatenate([query_weight, key_weight, value_weight], axis=1).astype(BF16)
    qkv_full = lax.all_gather(qkv_local, rows_axes, axis=0, tiled=True)
    live_key = jnp.arange(SEQ_LEN)[None, :] < lengths[:, None]
    out_cot = jnp.where(live_key.reshape(tok_rows, 1), cotangent, jnp.zeros_like(cotangent))
    packed = pack_weights(where, gate_weight, up_weight, down_weight, each)
    units = [(expert, far) for expert in range(each) for far in range(groups)]
    live["packed"] = packed

    def rotary_tables():
        places = jnp.arange(SEQ_LEN).astype(F32)
        powers = jnp.arange(HD // 2).astype(F32) * (2.0 / HD)
        angles = places[:, None] * jnp.exp(-powers * math.log(rope_base))[None, :]
        cosine, sine = jnp.cos(angles), jnp.sin(angles)
        return (
            jnp.concatenate([cosine, cosine], axis=1),
            jnp.concatenate([-sine, sine], axis=1),
        )

    live["out_cot"] = out_cot
    (tables,) = stage(
        live,
        [hidden_flow, gain_flow, routes_flow, router_flow, out_flow],
        [rotary_tables],
    )

    hidden = hidden_in.astype(F32)

    def norm_attn():
        blocks = hidden_flow.finish()
        gains = gain_flow.finish()
        square = sum(jnp.sum(jnp.square(block.astype(F32)), axis=1) for block in blocks)
        inverse = lax.rsqrt(square / D + epsilon)[:, None]
        normed = jnp.zeros((tok_rows, D), BF16)
        for place, (block, gain) in enumerate(zip(blocks, gains)):
            piece = (block.astype(F32) * inverse * gain).astype(BF16)
            normed = lax.dynamic_update_slice_in_dim(normed, piece, (col ^ place) * width, 1)
        return normed, inverse

    def routing():
        rel = jnp.stack(routes_flow.finish())
        named = jnp.any(rel[:, :, None, :] == jnp.arange(EXPERTS)[None, None, :, None], axis=1)
        first = (col * groups + lo) * each
        member = lax.dynamic_slice_in_dim(named, first, each, 1)
        member = jnp.swapaxes(member, 0, 1).reshape(each * groups, tok_rows)
        count = member.astype(jnp.int32)
        rank = jnp.cumsum(count, axis=1) - count
        pos = jnp.where(member, rank, -(1 << 20))
        starts = jnp.minimum(rank[:, ::BLOCK] // EDGE * EDGE, CAP - WINDOW)
        return named, starts, pos[:, None, :], pos[:, :, None]

    live["qkv_full"] = qkv_full
    ((live["normed_attn"], attn_inverse),) = stage(live, [router_flow, out_flow], [norm_attn])
    weight_flows = {}

    def start_weights(expert):
        for far in range(groups):
            weight_flows[expert, far] = Flow(
                expert_weight_steps(live["packed"][far * each + expert], far, far_bits)
            )

    start_weights(0)
    moe_cot = lax.all_gather(live["out_cot"], cube, axis=0, tiled=False)
    hidden_blocks = hidden_flow.result
    query_scale, key_scale = query_gain[None, :], key_gain[None, :]

    def attend(s):
        return attend_forward(
            s, lengths[s : s + 1], live["qkv"], tables, query_scale, key_scale, heads
        )

    def project_and_attend():
        live["qkv"] = dot_of(live["normed_attn"], live["qkv_full"], 1, 0)
        return attend(0)

    firsts = [weight_flows[0, far] for far in range(1, groups)]
    (first_seq,) = stage(live, [router_flow, out_flow], [project_and_attend])
    for expert in range(1, each):
        start_weights(expert)
    seconds = [weight_flows[unit] for unit in units if unit[0] == 1]
    named, starts, pos_row, pos_col = routing()

    span = width // depth

    def col_rows(blocks, place, axis):
        first = (col ^ place) * span
        return jnp.concatenate(
            [
                lax.dynamic_index_in_dim(blocks, (first + n) ^ row, 0, False)
                for n in range(span)
            ],
            axis=axis,
        )

    out_spread = out_flow.finish()
    out_rel = jnp.concatenate([col_rows(out_spread, place, 0) for place in range(cols)], axis=0)
    router_rows = col_rows(router_flow.finish(), 0, 1)

    def branch(mixture):
        partial = dot_of(mixture, out_rel, 1, 1)
        blocks = [partial[:, n * width : (n + 1) * width] for n in range(cols)]
        return Flow(col_reduce_steps(blocks, cols)).finish()

    def attend_rest():
        outs = [first_seq]
        sums = [branch(first_seq[0])]
        for s in range(1, seqs):
            outs.append(attend(s))
            sums.append(branch(outs[s][0]))
        return outs, sums

    ((attended, branches),) = stage(live, [weight_flows[0, 0]] + firsts, [attend_rest])
    middle = hidden + jnp.concatenate(branches, axis=0)
    live["scaled_rows"] = (middle * moe_gain).astype(BF16)
    scaled_rows = live["scaled_rows"]
    moe_in = lax.all_gather(scaled_rows, cube, axis=0, tiled=False)
    square = jnp.sum(middle * middle, axis=1)[None, :]
    stat = jnp.concatenate([dot_of(router_rows, scaled_rows, 1, 1), square], axis=0)
    stat_flow = Flow(spread_cube_steps(stat, groups, cols))
    stage(live, [stat_flow], sync=[weight_flows[0, 0]] + firsts + seconds)
    (live["cot_rows"],) = stage(
        live,
        [stat_flow, weight_flows[0, 0]] + firsts,
        [lambda: compact(starts, where, pos_row, moe_cot, groups, cols)],
        sync=seconds[:1],
    )
    for flow in seconds[:1]:
        flow.step(2)
    stage(live, [stat_flow] + firsts + seconds[1:])
    stat = stat_flow.finish()

    stat = jnp.sum(stat, axis=1)
    moe_inverse = lax.rsqrt(stat[:, EXPERTS] / D + epsilon)
    all_logits = stat[:, :EXPERTS] * moe_inverse[:, None, :]
    logits = jnp.where(named, all_logits, masked_score)
    shifted = jnp.where(named, jnp.exp(logits - jnp.max(logits, axis=1, keepdims=True)), 0.0)
    gates = shifted / jnp.sum(shifted, axis=1, keepdims=True)
    own_gate = lax.dynamic_slice_in_dim(gates, (col * groups + lo) * each, each, 1)
    own_gate = jnp.swapaxes(own_gate, 0, 1).reshape(each * groups, 1, tok_rows)
    row_gate, row_scale = compact_scalars(
        starts, pos_row, (own_gate, jnp.tile(moe_inverse, (each, 1))[:, None, :])
    )
    total_rows = groups * CAP

    live["moe_rows"] = compact(starts, where, pos_row, moe_in, groups, cols)

    def run_expert(expert):
        pieces, row_numbers = [], []
        for far in range(groups):
            for place, piece in weight_flows[expert, far].finish().items():
                pieces.append(piece)
                row_numbers.append(row_of_set(place, far))
        here = slice(expert * total_rows, (expert + 1) * total_rows)
        return expert_step(
            jnp.stack(row_numbers),
            live["moe_rows"][expert],
            live["cot_rows"][expert],
            row_gate[here],
            row_scale[here],
            pieces,
        )

    blocks_here = [
        (hi ^ above) * groups + (lo ^ far)
        for far in reversed(range(groups))
        for above in range(high)
    ]
    grad_places = jnp.stack(blocks_here + blocks_here + [mid])
    grad_flows = {}

    def start_grads(expert, outs):
        grads = weight_grads(
            grad_places,
            live["moe_rows"][expert],
            live["cot_rows"][expert],
            outs[1],
            outs[2],
            depth,
            groups,
            mids,
            high,
        )
        return grads.reshape((groups, mids * high) + grads.shape[3:])

    def grad_flow(expert, grads):
        for number, far in enumerate(reversed(range(groups))):
            grad_flows[expert, far] = Flow(expert_grad_steps(grads[number], far, far_bits))

    def running():
        return list(grad_flows.values())

    ran = []
    for expert in range(each):
        others = [flow for (number, _), flow in weight_flows.items() if number > expert]
        (outs,) = stage(
            live,
            others[1:] + running()[:1],
            [functools.partial(run_expert, expert)],
            sync=others[:1] + running()[1:],
        )
        ran.append(outs)
        if expert + 1 < each:
            (grads,) = stage(live, others, [functools.partial(start_grads, expert, outs)])
            grad_flow(expert, grads)
    early = running()
    live["result"] = [outs[5] for outs in ran]
    last = ran[-1]
    gate_cot = jnp.concatenate([outs[3] for outs in ran], axis=0)
    row_inner = jnp.concatenate([outs[4] for outs in ran], axis=0)
    sizes = part_sizes(tok_rows, len(links))
    live["scalars"] = (gate_cot, row_inner)
    (rows_parts,) = stage(
        live,
        [],
        [
            lambda: expand(
                starts, where, pos_col, [outs[0] for outs in ran], sizes, groups, cols
            )
        ],
    )
    gate_cot, row_inner = expand_scalars(starts, pos_row, live.pop("scalars"))
    gate_cot = gate_cot.reshape(each, groups, tok_rows)
    row_inner = jnp.sum(row_inner.reshape(each, groups, tok_rows), axis=0)[None]
    scalars = jnp.concatenate([gate_cot, row_inner], axis=0)
    scalars = scalars.reshape((each + 1) * groups, tok_rows)
    scalar_flow = Flow(spread_cube_steps(scalars, groups, cols))
    moe_in_flow = Flow(reduce_steps(rows_parts, groups, cols))
    (grads,) = stage(
        live,
        [moe_in_flow, scalar_flow] + early,
        [functools.partial(start_grads, each - 1, last)],
    )
    grad_flow(each - 1, grads)
    late = running()[len(early) :]
    scalar_flow.finish()
    for flow in late[:1]:
        flow.step()
    (branch_parts,) = stage(
        live,
        [moe_in_flow],
        [lambda: expand_all(starts, where, pos_col, live["result"], groups, cols)],
        sync=[scalar_flow] + early,
    )
    for flow in early[1:]:
        flow.step()
    live["moe_branch"] = branch_parts.reshape(groups * cols, tok_rows, width)
    while moe_in_flow.sends is not None:
        stage(live, [moe_in_flow], sync=late)
    scalar_all = scalar_flow.finish().reshape(groups, cols, each + 1, groups, tok_rows)
    scalar_all = jnp.stack([scalar_all[place, :, :, place] for place in range(groups)])
    by_expert = jnp.stack(
        [
            ((lo ^ (number // each % groups)) * cols + (col ^ (number // (each * groups)))) * each
            + number % each
            for number in range(EXPERTS)
        ]
    )
    gate_cot = jnp.take(scalar_all[:, :, :each].reshape(EXPERTS, tok_rows), by_expert, axis=0)
    my_gates, my_logits = gates[0], all_logits[0]
    logit_cot = my_gates * (gate_cot - jnp.sum(my_gates * gate_cot, axis=0, keepdims=True))
    inner = jnp.sum(scalar_all[:, :, each], axis=(0, 1)) + jnp.sum(logit_cot * my_logits, axis=0)
    scaled_logit = (logit_cot * moe_inverse[0][None, :]).astype(BF16)
    logit_cot = logit_cot.astype(BF16)
    my_inverse = moe_inverse[0][:, None]

    back = moe_in_flow.finish() + my_inverse * dot_of(logit_cot, router_rows, 0, 0)
    middle_cot = (
        out_cot.astype(F32)
        + back * moe_gain
        - middle * (my_inverse * my_inverse * (inner[:, None] / D))
    )
    cot_flow = Flow(spread_steps(middle_cot.astype(BF16), "col", col_bits))
    router_part, moe_gain_part = stage(
        live,
        [cot_flow],
        [
            lambda: dot_of(scaled_logit, scaled_rows, 1, 0),
            lambda: jnp.sum(back * middle, axis=0)[None],
        ],
        sync=early[1:],
    )
    cot_blocks = cot_flow.finish()
    moe_branch = lax.psum_scatter(
        live.pop("moe_branch"), cube, scatter_dimension=0, tiled=True
    )[0]

    cot_all = jnp.concatenate(cot_blocks, axis=1)

    def attend_back(s):
        mixture_cot = dot_of(cot_all[seq_rows[s]], out_rel, 1, 0).astype(BF16)
        *cots, query_part, key_part, token_inner = attend_backward(
            s,
            lengths[s : s + 1],
            attended[s][1:],
            mixture_cot,
            live["qkv"],
            tables,
            query_scale,
            key_scale,
            heads,
        )
        cots = jnp.concatenate(cots, axis=1)
        return cots, query_part, key_part, token_inner[:, 0]

    qkv_rel = jnp.concatenate(
        [
            lax.dynamic_slice_in_dim(live["qkv_full"], (col ^ place) * width, width, 0)
            for place in range(cols)
        ],
        axis=0,
    )
    mixture = jnp.concatenate([outs[0] for outs in attended], axis=0)
    live.update(qkv_rel=qkv_rel, mixture=mixture, cot_all=cot_all)
    done = stage(
        live,
        early[:1] + late,
        [functools.partial(attend_back, s) for s in range(seqs)],
    )
    share = width // (mids * depth)
    cot_places = [((n // share) ^ col) * share + n % share for n in blocks_here]

    live["qkv_cot"] = jnp.concatenate([outs[0] for outs in done], axis=0)

    def projection_grads():
        grads = weight_grads(
            jnp.stack(blocks_here + cot_places + [mid]),
            live["normed_attn"],
            live["cot_all"],
            live["qkv_cot"],
            live["mixture"],
            depth,
            groups,
            mids,
            high,
        )
        return grads

    def widen(blocks):
        full = jnp.zeros((blocks[0].shape[0], D), F32)
        for place, block in enumerate(blocks):
            full = lax.dynamic_update_slice_in_dim(full, block, (col ^ place) * width, 1)
        return full

    for flow in late:
        flow.step()
    (partial,) = stage(live, [], [lambda: dot_of(live["qkv_cot"], live["qkv_rel"], 1, 1)])
    backs = [partial[:, n * width : (n + 1) * width] for n in range(cols)]
    attn_flow = Flow(col_reduce_steps(backs, cols))

    def gain_sums():
        attn_gain_parts = [
            jnp.sum(part * (block.astype(F32) * attn_inverse), axis=0)[None]
            for part, block in zip(backs, hidden_blocks)
        ]
        query_part = sum(outs[1] for outs in done)
        key_part = sum(outs[2] for outs in done)
        head_parts = jnp.concatenate([query_part, key_part], 1)
        return jnp.concatenate(
            [
                widen([router_part]),
                widen([moe_gain_part]),
                widen(attn_gain_parts),
                jnp.pad(head_parts, ((0, 0), (0, D - 2 * HD))),
            ],
            axis=0,
        )

    token_inner = jnp.concatenate([outs[3] for outs in done], axis=0)
    inner_flow = Flow(total_steps(token_inner, [("col",)]))
    (grads,) = stage(live, [attn_flow, inner_flow], [projection_grads])
    qkv_flow = Flow(row_reduce_steps(grads, groups, mids, high))
    for _ in bits_of(cols)[2:]:
        stage(live, [attn_flow])
    small_flows = []

    def small_sums():
        flow = Flow(total_steps(gain_sums(), [("col",), ("lo", "mid"), ("hi",)])).step()
        small_flows.append(flow)
        return flow.holds()

    (held,) = stage(live, [attn_flow, qkv_flow], [small_sums], sync=[late[1]])
    (small_flow,) = small_flows
    small_flow.replace(held)
    live["moe_branch"] = moe_branch

    def input_sums():
        return (
            middle_cot
            + attn_inverse * (attn_flow.finish() * attn_gain)
            - hidden * (attn_inverse * attn_inverse * (inner_flow.finish()[:, None] / D))
        )

    (input_grad,) = stage(live, [qkv_flow, small_flow], [input_sums])
    flows = [qkv_flow, small_flow] + early + late
    while any(flow.sends is not None for flow in flows):
        stage(live, flows)
    moe_branch = live["moe_branch"]
    weight_sum = qkv_flow.finish()
    out_sum = weight_sum[:, 3 * width :]
    small = small_flow.finish()

    output = (middle + moe_branch.astype(F32)).astype(BF16)
    gate_grad, up_grad, down_grad = unpack_grads(
        where,
        [grad_flows[expert, far].finish() for far in range(groups) for expert in range(each)],
        each,
    )
    own = lax.dynamic_slice_in_dim(small, col * width, width, 1)
    router_grad = lax.dynamic_slice_in_dim(small[:EXPERTS], row * depth, depth, 1).T
    return (
        output,
        input_grad,
        own[EXPERTS + 1],
        small[EXPERTS + 2, :HD],
        small[EXPERTS + 2, HD : 2 * HD],
        weight_sum[:, :width],
        weight_sum[:, width : 2 * width],
        weight_sum[:, 2 * width : 3 * width],
        out_sum.T,
        own[EXPERTS],
        router_grad,
        gate_grad,
        up_grad,
        down_grad,
    )


def solution(mesh):
    row_count, col_count = mesh.shape["row"], mesh.shape["col"]
    groups = 2
    between = EXPERTS // col_count // groups
    shape = (row_count // (groups * between), groups, between, col_count)
    inner = Mesh(mesh.devices.reshape(shape), ("hi", "lo", "mid", "col"))
    row = ("hi", "lo", "mid")
    return jax.shard_map(
        per_device,
        mesh=inner,
        in_specs=(
            P(row, "col"),
            P(row),
            P(row, None),
            P("col"),
            P(),
            P(),
            P(row, "col"),
            P(row, "col"),
            P(row, "col"),
            P("col", row),
            P("col"),
            P(row, None),
            P("col", row, None),
            P("col", row, None),
            P("col", None, row),
            P(row, "col"),
        ),
        out_specs=(
            P(row, "col"),
            P(row, "col"),
            P("col"),
            P(),
            P(),
            P(row, "col"),
            P(row, "col"),
            P(row, "col"),
            P("col", row),
            P("col"),
            P(row, None),
            P("col", row, None),
            P("col", row, None),
            P("col", None, row),
        ),
        check_vma=False,
    )
```

```python
import functools
import math

import jax
import jax.numpy as jnp
from jax import lax
from jax.experimental import pallas as pl
from jax.experimental.pallas import tpu as pltpu
from jax.sharding import Mesh, PartitionSpec as P

D = 2048
HD = 128
EXPERTS = 16
SEQ_LEN = 1024
CAP = 1152

BLOCK = 128
WINDOW = 144
EDGE = 16
TILE = 384
COST_SHARE = 50
EXPERT_WIDE, EXPERT_UNROLL = 512, 2
GRAD_WIDE, GRAD_UNROLL = 512, 1

epsilon = 1e-06
rope_base = 10000.0
masked_score = -1e30

F32 = jnp.float32
BF16 = jnp.bfloat16
ANY = pl.ANY
VMEM_LIMIT = 56 * 1024 * 1024


def dot_of(a, b, da, db):
    return lax.dot_general(a, b, (((da,), (db,)), ((), ())), preferred_element_type=F32)


def params(*semantics):
    return pltpu.CompilerParams(
        vmem_limit_bytes=VMEM_LIMIT, dimension_semantics=semantics or None
    )


def cost(flops, bytes_accessed, transcendentals=0):
    return pl.CostEstimate(
        flops=int(flops) // COST_SHARE,
        bytes_accessed=int(bytes_accessed) // COST_SHARE,
        transcendentals=int(transcendentals) // COST_SHARE,
    )


def turn(values, cosine, sine):
    return values * cosine + pltpu.roll(values, HD // 2, 1) * sine


def attend_forward_kernel(
    live_ref, q_ref, k_ref, v_ref, cos_ref, sin_ref, qg_ref, kg_ref, mix_ref, ql_ref, kl_ref, vl_ref
):
    live = live_ref[0]
    cosine = cos_ref[...]
    sine = sin_ref[...]

    def normed(values, gain):
        inverse = lax.rsqrt(jnp.mean(values * values, axis=1, keepdims=True) + epsilon)
        return turn(values * inverse * gain, cosine, sine).astype(BF16)

    ql_ref[...] = normed(q_ref[...], qg_ref[...])
    kl_ref[...] = normed(k_ref[...], kg_ref[...])
    vl_ref[...] = v_ref[...].astype(BF16)
    keys = kl_ref[...]
    values = vl_ref[...]
    rows = 256
    place = lax.broadcasted_iota(jnp.int32, (rows, SEQ_LEN), 1)
    for part in range(SEQ_LEN // rows):
        here = pl.ds(part * rows, rows)
        scores = dot_of(ql_ref[here, :], keys, 1, 1) * (1.0 / math.sqrt(HD))
        scores = jnp.where(place < live, scores, masked_score)
        top = jnp.max(scores, axis=1, keepdims=True)
        shifted = jnp.exp(scores - top)
        total = jnp.sum(shifted, axis=1, keepdims=True)
        probs = (shifted * (1.0 / total)).astype(BF16)
        mix_ref[here, :] = dot_of(probs, values, 1, 0).astype(BF16)


def attend_forward(seq, live, qkv, tables, query_gain, key_gain, heads):
    width = heads * HD

    def pick(offset):
        return pl.BlockSpec((SEQ_LEN, HD), lambda h, live, o=offset: (seq, o + h))

    def whole(shape):
        return pl.BlockSpec(shape, lambda h, live: (0, 0))

    out = pl.BlockSpec((SEQ_LEN, HD), lambda h, live: (0, h))
    return pl.pallas_call(
        attend_forward_kernel,
        grid_spec=pltpu.PrefetchScalarGridSpec(
            num_scalar_prefetch=1,
            grid=(heads,),
            in_specs=[
                pick(0),
                pick(heads),
                pick(2 * heads),
                whole((SEQ_LEN, HD)),
                whole((SEQ_LEN, HD)),
                whole((1, HD)),
                whole((1, HD)),
            ],
            out_specs=[out] * 4,
        ),
        out_shape=[jax.ShapeDtypeStruct((SEQ_LEN, width), BF16)] * 4,
        compiler_params=params("arbitrary"),
        cost_estimate=cost(
            heads * 8 * SEQ_LEN * SEQ_LEN * HD, 20 * SEQ_LEN * width, heads * SEQ_LEN * SEQ_LEN
        ),
        name="attend_forward",
    )(live, qkv, qkv, qkv, tables[0], tables[1], query_gain, key_gain)


def attend_backward_kernel(
    live_ref,
    ql_ref,
    kl_ref,
    vl_ref,
    do_ref,
    q_ref,
    k_ref,
    cos_ref,
    sin_ref,
    qg_ref,
    kg_ref,
    qc_ref,
    kc_ref,
    vc_ref,
    qpart_ref,
    kpart_ref,
    inner_ref,
    dq_ref,
    dk_ref,
    dv_ref,
):
    head = pl.program_id(0)
    live = live_ref[0]
    scale = 1.0 / math.sqrt(HD)
    keys = kl_ref[...]
    values = vl_ref[...]
    rows = 256
    place = lax.broadcasted_iota(jnp.int32, (SEQ_LEN, rows), 0)
    for part in range(SEQ_LEN // rows):
        here = pl.ds(part * rows, rows)
        queries = ql_ref[here, :]
        incoming = do_ref[here, :]
        scores = dot_of(keys, queries, 1, 1) * scale
        scores = jnp.where(place < live, scores, masked_score)
        top = jnp.max(scores, axis=0, keepdims=True)
        shifted = jnp.exp(scores - top)
        total = jnp.sum(shifted, axis=0, keepdims=True)
        probs = shifted * (1.0 / total)
        dv = dot_of(probs.astype(BF16), incoming, 1, 0)
        probs_cot = dot_of(values, incoming, 1, 1)
        weighted = probs * probs_cot
        centre = jnp.sum(weighted, axis=0, keepdims=True)
        raw = ((weighted - probs * centre) * scale).astype(BF16)
        dk = dot_of(raw, queries, 1, 0)
        dq_ref[here, :] = dot_of(raw, keys, 0, 0)
        if part == 0:
            dv_ref[...] = dv
            dk_ref[...] = dk
        else:
            dv_ref[...] += dv
            dk_ref[...] += dk
    cosine = cos_ref[...]
    sine = -sin_ref[...]

    def back(values, gain, rotated_cot):
        incoming = turn(rotated_cot, cosine, sine)
        inverse = lax.rsqrt(jnp.mean(values * values, axis=1, keepdims=True) + epsilon)
        scaled = incoming * gain
        inner = jnp.mean(scaled * values, axis=1, keepdims=True)
        grad = inverse * scaled - values * (inverse * inverse * inverse * inner)
        part = jnp.sum(incoming * values * inverse, axis=0, keepdims=True)
        return grad.astype(BF16), part, jnp.sum(grad * values, axis=1, keepdims=True)

    qc_ref[...], qpart, inner = back(q_ref[...], qg_ref[...], dq_ref[...])
    kc_ref[...], kpart, key_inner = back(k_ref[...], kg_ref[...], dk_ref[...])
    vc_ref[...] = dv_ref[...].astype(BF16)
    inner += key_inner
    inner += jnp.sum(dv_ref[...] * values.astype(F32), axis=1, keepdims=True)

    @pl.when(head == 0)
    def _():
        qpart_ref[...] = qpart
        kpart_ref[...] = kpart
        inner_ref[...] = inner

    @pl.when(head > 0)
    def _():
        qpart_ref[...] += qpart
        kpart_ref[...] += kpart
        inner_ref[...] += inner


def attend_backward(seq, live, lows, mixture_cot, qkv, tables, query_gain, key_gain, heads):
    width = heads * HD
    block = pl.BlockSpec((SEQ_LEN, HD), lambda h, live: (0, h))

    def pick(offset):
        return pl.BlockSpec((SEQ_LEN, HD), lambda h, live, o=offset: (seq, o + h))

    def whole(shape):
        return pl.BlockSpec(shape, lambda h, live: (0, 0))

    return pl.pallas_call(
        attend_backward_kernel,
        grid_spec=pltpu.PrefetchScalarGridSpec(
            num_scalar_prefetch=1,
            grid=(heads,),
            in_specs=[block] * 4
            + [
                pick(0),
                pick(heads),
                whole((SEQ_LEN, HD)),
                whole((SEQ_LEN, HD)),
                whole((1, HD)),
                whole((1, HD)),
            ],
            out_specs=[block] * 3 + [whole((1, HD))] * 2 + [whole((SEQ_LEN, 1))],
            scratch_shapes=[pltpu.VMEM((SEQ_LEN, HD), F32)] * 3,
        ),
        out_shape=[jax.ShapeDtypeStruct((SEQ_LEN, width), BF16)] * 3
        + [jax.ShapeDtypeStruct((1, HD), F32)] * 2
        + [jax.ShapeDtypeStruct((SEQ_LEN, 1), F32)],
        compiler_params=params("arbitrary"),
        cost_estimate=cost(
            heads * 20 * SEQ_LEN * SEQ_LEN * HD, 24 * SEQ_LEN * width, heads * SEQ_LEN * SEQ_LEN
        ),
        name="attend_backward",
    )(live, *lows, mixture_cot, qkv, qkv, tables[0], tables[1], query_gain, key_gain)


def compact_kernel(start_ref, where_ref, pos_ref, source_ref, *outs):
    group, groups = pl.program_id(0), pl.num_programs(0)
    row_of = lax.broadcasted_iota(jnp.int32, (WINDOW, BLOCK), 0)
    for out in outs:
        out[...] = jnp.zeros_like(out)
    for number in range(source_ref.shape[1] // BLOCK):
        here = slice(number * BLOCK, (number + 1) * BLOCK)
        for expert, out in enumerate(outs):
            start = pl.multiple_of(start_ref[expert * groups + group, number], EDGE)
            place = pos_ref[expert, 0, :, here]
            choice = jnp.where(row_of + start == place, 1.0, 0.0).astype(BF16)
            rows = dot_of(choice, source_ref[0, here, :], 1, 0)
            out[pl.ds(start, WINDOW), :] += rows.astype(BF16)


def compact(starts, where, pos_row, source, groups, cols):
    tokens, width = source.shape[1:]
    count = pos_row.shape[0] // groups
    return pl.pallas_call(
        compact_kernel,
        grid_spec=pltpu.PrefetchScalarGridSpec(
            num_scalar_prefetch=2,
            grid=(groups, cols),
            in_specs=[
                pl.BlockSpec((count, 1, 1, tokens), lambda q, j, s, w: (0, q, 0, 0)),
                pl.BlockSpec(
                    (1, tokens, width), lambda q, j, s, w: ((w[0] ^ q) * cols + j, 0, 0)
                ),
            ],
            out_specs=[pl.BlockSpec((CAP, width), lambda q, j, s, w: (q, j))] * count,
        ),
        out_shape=[jax.ShapeDtypeStruct((groups * CAP, cols * width), BF16)] * count,
        compiler_params=params("arbitrary", "arbitrary"),
        cost_estimate=cost(
            count * groups * cols * 2 * tokens * WINDOW * width * 2,
            groups * cols * 2 * width * (tokens + count * CAP),
        ),
        name="compact",
    )(starts, where, pos_row.reshape(count, groups, 1, tokens), source)


def compact_scalars_kernel(start_ref, pos_ref, *refs):
    count = len(refs) // 2
    group = pl.program_id(0)
    row_of = lax.broadcasted_iota(jnp.int32, (WINDOW, BLOCK), 0)
    for number in range(count):
        refs[count + number][...] = jnp.zeros_like(refs[count + number])
    for number in range(pos_ref.shape[2] // BLOCK):
        start = pl.multiple_of(start_ref[group, number], EDGE)
        here = slice(number * BLOCK, (number + 1) * BLOCK)
        choice = row_of + start == pos_ref[0, :, here]
        for source, out in zip(refs[:count], refs[count:]):
            picked = jnp.sum(jnp.where(choice, source[0, :, here], 0.0), axis=1, keepdims=True)
            out[pl.ds(start, WINDOW), :] += picked


def compact_scalars(starts, pos_row, sources):
    groups, _, tokens = pos_row.shape
    block = pl.BlockSpec((1, 1, tokens), lambda q, s: (q, 0, 0))
    return pl.pallas_call(
        compact_scalars_kernel,
        grid_spec=pltpu.PrefetchScalarGridSpec(
            num_scalar_prefetch=1,
            grid=(groups,),
            in_specs=[block] * (1 + len(sources)),
            out_specs=[pl.BlockSpec((CAP, 1), lambda q, s: (q, 0))] * len(sources),
        ),
        out_shape=[jax.ShapeDtypeStruct((groups * CAP, 1), F32)] * len(sources),
        compiler_params=params("arbitrary"),
        cost_estimate=cost(0, 4 * groups * CAP * 128 * len(sources)),
        name="compact_scalars",
    )(starts, pos_row, *sources)


def expand_scalars_kernel(start_ref, pos_ref, *refs):
    count = len(refs) // 2
    group = pl.program_id(0)
    row_of = lax.broadcasted_iota(jnp.int32, (WINDOW, BLOCK), 0)
    for number in range(pos_ref.shape[2] // BLOCK):
        start = pl.multiple_of(start_ref[group, number], EDGE)
        here = slice(number * BLOCK, (number + 1) * BLOCK)
        choice = row_of + start == pos_ref[0, :, here]
        for source, out in zip(refs[:count], refs[count:]):
            held = source[pl.ds(start, WINDOW), :]
            out[0, :, here] = jnp.sum(jnp.where(choice, held, 0.0), axis=0, keepdims=True)


def expand_scalars(starts, pos_row, sources):
    groups, _, tokens = pos_row.shape
    block = pl.BlockSpec((1, 1, tokens), lambda q, s: (q, 0, 0))
    return pl.pallas_call(
        expand_scalars_kernel,
        grid_spec=pltpu.PrefetchScalarGridSpec(
            num_scalar_prefetch=1,
            grid=(groups,),
            in_specs=[block] + [pl.BlockSpec((CAP, 1), lambda q, s: (q, 0))] * len(sources),
            out_specs=[block] * len(sources),
        ),
        out_shape=[jax.ShapeDtypeStruct((groups, 1, tokens), F32)] * len(sources),
        compiler_params=params("arbitrary"),
        cost_estimate=cost(0, 4 * groups * CAP * 128 * len(sources)),
        name="expand_scalars",
    )(starts, pos_row, *sources)


def expand_kernel(sizes, count, start_ref, where_ref, pos_ref, *refs):
    group, groups = pl.program_id(0), pl.num_programs(0)
    sides = len(refs) // (count + len(sizes))
    sources, outs = refs[: count * sides], refs[count * sides :]
    column_of = lax.broadcasted_iota(jnp.int32, (BLOCK, WINDOW), 1)
    number = 0
    for part, size in enumerate(sizes):
        for step in range(size // BLOCK):
            totals = [None] * sides
            for expert in range(count):
                start = pl.multiple_of(start_ref[expert * groups + group, number], EDGE)
                place = pos_ref[expert, 0, number * BLOCK : (number + 1) * BLOCK, :]
                choice = jnp.where(column_of + start == place, 1.0, 0.0).astype(BF16)
                for side in range(sides):
                    held = sources[expert * sides + side][pl.ds(start, WINDOW), :]
                    rows = dot_of(choice, held, 1, 0)
                    totals[side] = rows if totals[side] is None else totals[side] + rows
            here = slice(step * BLOCK, (step + 1) * BLOCK)
            for side in range(sides):
                outs[part * sides + side][0, 0, here, :] = totals[side].astype(BF16)
            number += 1


def expand(starts, where, pos_col, sources, sizes, groups, cols):
    width = sources[0].shape[1] // cols
    tokens = sum(sizes)
    count = len(sources)

    def side(odd):
        return pl.BlockSpec((CAP, width), lambda q, j, s, w: (q, w[1] ^ (2 * j + odd)))

    outs = pl.pallas_call(
        functools.partial(expand_kernel, sizes, count),
        grid_spec=pltpu.PrefetchScalarGridSpec(
            num_scalar_prefetch=2,
            grid=(groups, cols // 2),
            in_specs=[pl.BlockSpec((count, 1, tokens, 1), lambda q, j, s, w: (0, q, 0, 0))]
            + [side(0), side(1)] * count,
            out_specs=[
                pl.BlockSpec((1, 1, size, width), lambda q, j, s, w: (q, j, 0, 0))
                for size in sizes
                for _ in range(2)
            ],
        ),
        out_shape=[
            jax.ShapeDtypeStruct((groups, cols // 2, size, width), BF16)
            for size in sizes
            for _ in range(2)
        ],
        compiler_params=params("arbitrary", "arbitrary"),
        cost_estimate=cost(
            4 * count * groups * cols * tokens * WINDOW * width,
            groups * cols * width * (2 * tokens + 2 * count * CAP),
        ),
        name="expand",
    )(
        starts,
        where,
        pos_col.reshape(count, groups, tokens, 1),
        *[source for source in sources for _ in range(2)],
    )
    return list(zip(outs[::2], outs[1::2]))


def expand_all(starts, where, pos_col, sources, groups, cols):
    width = sources[0].shape[1] // cols
    tokens = pos_col.shape[1]
    count = len(sources)
    return pl.pallas_call(
        functools.partial(expand_kernel, [tokens], count),
        grid_spec=pltpu.PrefetchScalarGridSpec(
            num_scalar_prefetch=2,
            grid=(groups, cols),
            in_specs=[pl.BlockSpec((count, 1, tokens, 1), lambda q, j, s, w: (0, q, 0, 0))]
            + [pl.BlockSpec((CAP, width), lambda q, j, s, w: (q, j))] * count,
            out_specs=pl.BlockSpec((1, 1, tokens, width), lambda q, j, s, w: (w[0] ^ q, j, 0, 0)),
        ),
        out_shape=jax.ShapeDtypeStruct((groups, cols, tokens, width), BF16),
        compiler_params=params("arbitrary", "arbitrary"),
        cost_estimate=cost(
            4 * count * groups * cols * tokens * WINDOW * width,
            groups * cols * width * (2 * tokens + 2 * count * CAP),
        ),
        name="expand_all",
    )(starts, where, pos_col.reshape(count, groups, tokens, 1), *sources)


def pack_kernel(where_ref, gate_ref, up_ref, down_ref, out_ref):
    hidden = gate_ref.shape[2]
    out_ref[0, :, :hidden] = gate_ref[0].astype(BF16)
    out_ref[0, :, hidden : 2 * hidden] = up_ref[0].astype(BF16)
    out_ref[0, :, 2 * hidden :] = down_ref[0].T.astype(BF16)


def pack_weights(where, gate, up, down, each):
    experts, depth, hidden = gate.shape

    def pick(shape):
        return pl.BlockSpec(shape, lambda q, w: ((w[0] ^ (q // each)) * each + q % each, 0, 0))

    return pl.pallas_call(
        pack_kernel,
        grid_spec=pltpu.PrefetchScalarGridSpec(
            num_scalar_prefetch=1,
            grid=(experts,),
            in_specs=[pick((1, depth, hidden)), pick((1, depth, hidden)), pick((1, hidden, depth))],
            out_specs=pl.BlockSpec((1, depth, 3 * hidden), lambda q, w: (q, 0, 0)),
        ),
        out_shape=jax.ShapeDtypeStruct((experts, depth, 3 * hidden), BF16),
        compiler_params=params("arbitrary"),
        cost_estimate=cost(0, 18 * experts * depth * hidden),
        name="pack_weights",
    )(where, gate, up, down)


def unpack_kernel(where_ref, *refs):
    sources, (gate_ref, up_ref, down_ref) = refs[:-3], refs[-3:]
    hidden = gate_ref.shape[2]
    for number, source in enumerate(sources):

        @pl.when(pl.program_id(0) == number)
        def _(source=source):
            gate_ref[0] = source[:, :hidden].astype(F32)
            up_ref[0] = source[:, hidden : 2 * hidden].astype(F32)
            down_ref[0] = source[:, 2 * hidden :].astype(F32).T


def unpack_grads(where, sources, each):
    count = len(sources)
    depth, wide = sources[0].shape
    hidden = wide // 3

    def pick(shape):
        return pl.BlockSpec(shape, lambda q, w: ((w[0] ^ (q // each)) * each + q % each, 0, 0))

    shapes = [(count, depth, hidden), (count, depth, hidden), (count, hidden, depth)]
    return pl.pallas_call(
        unpack_kernel,
        grid_spec=pltpu.PrefetchScalarGridSpec(
            num_scalar_prefetch=1,
            grid=(count,),
            in_specs=[pl.BlockSpec((depth, wide), lambda q, w: (0, 0))] * count,
            out_specs=[pick((1,) + shape[1:]) for shape in shapes],
        ),
        out_shape=[jax.ShapeDtypeStruct(shape, F32) for shape in shapes],
        compiler_params=params("arbitrary"),
        cost_estimate=cost(0, 18 * count * depth * hidden),
        name="unpack_grads",
    )(where, *sources)


def expert_kernel(count, hidden, row_ref, x_ref, m_ref, gate_ref, scale_ref, *refs):
    pieces = refs[:count]
    rows_ref, pre_ref, act_ref, cot_ref, inner_ref, result_ref, held, sems = refs[count:]
    depth = pieces[0].shape[0]

    @pl.when(pl.program_id(0) == 0)
    def _():
        copies = []
        for number, piece in enumerate(pieces):
            place = pl.ds(pl.multiple_of(row_ref[number] * depth, depth), depth)
            copies.append(pltpu.make_async_copy(piece, held.at[place, :], sems.at[number]))
        for copy in copies:
            copy.start()
        for copy in copies:
            copy.wait()

    gate = gate_ref[...]
    scale = scale_ref[...]
    wide = EXPERT_WIDE
    cot_ref[...] = jnp.zeros_like(cot_ref)
    inner_ref[...] = jnp.zeros_like(inner_ref)

    @pl.loop(0, hidden // wide, unroll=EXPERT_UNROLL)
    def _(step):
        first = pl.multiple_of(step * wide, wide)
        gate_pre = dot_of(x_ref[...], held[:, pl.ds(first, wide)], 1, 0) * scale
        up_pre = dot_of(x_ref[...], held[:, pl.ds(hidden + first, wide)], 1, 0) * scale
        back = dot_of(m_ref[...], held[:, pl.ds(2 * hidden + first, wide)], 1, 0)
        squash = 1.0 / (1.0 + jnp.exp(-gate_pre))
        silu = gate_pre * squash
        active = silu * up_pre
        cot_ref[...] += jnp.sum(active.astype(BF16).astype(F32) * back, axis=1, keepdims=True)
        act_ref[:, pl.ds(first, wide)] = (active * gate).astype(BF16)
        back = back * gate
        slope = squash * (1.0 + gate_pre * (1.0 - squash))
        gate_cot = back * up_pre * slope
        up_cot = back * silu
        inner_ref[...] += jnp.sum(gate_cot * gate_pre + up_cot * up_pre, axis=1, keepdims=True)
        pre_ref[:, pl.ds(first, wide)] = (gate_cot * scale).astype(BF16)
        pre_ref[:, pl.ds(hidden + first, wide)] = (up_cot * scale).astype(BF16)

    @pl.loop(0, held.shape[0] // wide, unroll=EXPERT_UNROLL)
    def _(step):
        first = pl.multiple_of(step * wide, wide)
        here = pl.ds(first, wide)
        rows_ref[:, here] = dot_of(pre_ref[...], held[here, : 2 * hidden], 1, 1).astype(BF16)
        result_ref[:, here] = dot_of(act_ref[...], held[here, 2 * hidden :], 1, 1).astype(BF16)


def expert_step(row_numbers, x, m, gate, scale, pieces):
    total, wide = x.shape
    hidden = pieces[0].shape[1] // 3
    count = len(pieces)

    def tile(columns):
        return pl.BlockSpec((TILE, columns), lambda i, r: (i, 0))

    return pl.pallas_call(
        functools.partial(expert_kernel, count, hidden),
        grid_spec=pltpu.PrefetchScalarGridSpec(
            num_scalar_prefetch=1,
            grid=(total // TILE,),
            in_specs=[tile(wide), tile(wide), tile(1), tile(1)]
            + [pl.BlockSpec(memory_space=ANY)] * count,
            out_specs=[tile(wide), tile(2 * hidden), tile(hidden), tile(1), tile(1), tile(wide)],
            scratch_shapes=[
                pltpu.VMEM((wide, 3 * hidden), BF16),
                pltpu.SemaphoreType.DMA((count,)),
            ],
        ),
        out_shape=[
            jax.ShapeDtypeStruct((total, wide), BF16),
            jax.ShapeDtypeStruct((total, 2 * hidden), BF16),
            jax.ShapeDtypeStruct((total, hidden), BF16),
            jax.ShapeDtypeStruct((total, 1), F32),
            jax.ShapeDtypeStruct((total, 1), F32),
            jax.ShapeDtypeStruct((total, wide), BF16),
        ],
        compiler_params=params("arbitrary"),
        cost_estimate=cost(
            2 * total * wide * hidden * 6, 2 * total * (4 * wide + 3 * hidden), total * hidden
        ),
        name="expert_step",
    )(row_numbers, x, m, gate, scale, *pieces)


def weight_grad_kernel(mids, place_ref, x_ref, m_ref, pre_ref, act_ref, out_ref, turned_ref):
    wide = GRAD_WIDE
    first = pre_ref.shape[1]
    depth = x_ref.shape[1] // mids
    turned_ref[0] = x_ref[...].T
    turned_ref[1] = m_ref[...].T
    mid = place_ref[place_ref.shape[0] - 1]

    def put(grad, here):
        for number in range(mids):
            block = grad[number * depth : (number + 1) * depth].astype(BF16)
            out_ref[0, number ^ mid, 0, :, here] = block

    @pl.loop(0, first // wide, unroll=GRAD_UNROLL)
    def _(step):
        here = pl.ds(pl.multiple_of(step * wide, wide), wide)
        put(dot_of(turned_ref[0], pre_ref[:, here], 1, 0), here)

    @pl.loop(0, act_ref.shape[1] // wide, unroll=GRAD_UNROLL)
    def _(step):
        here = pl.ds(pl.multiple_of(step * wide, wide), wide)
        there = pl.ds(pl.multiple_of(first + step * wide, wide), wide)
        put(dot_of(turned_ref[1], act_ref[:, here], 1, 0), there)


def weight_grads(places, x, m, pre, act, depth, groups, mids, high):
    total = x.shape[0]
    wide = pre.shape[1] + act.shape[1]

    def column(first):
        return pl.BlockSpec((total, mids * depth), lambda f, h, r: (0, r[first + f * high + h]))

    def whole(array):
        return pl.BlockSpec(array.shape, lambda f, h, r: (0, 0), pipeline_mode=pl.Buffered(1))

    return pl.pallas_call(
        functools.partial(weight_grad_kernel, mids),
        grid_spec=pltpu.PrefetchScalarGridSpec(
            num_scalar_prefetch=1,
            grid=(groups, high),
            in_specs=[column(0), column(groups * high), whole(pre), whole(act)],
            out_specs=pl.BlockSpec(
                (1, mids, 1, depth, wide), lambda f, h, r: (f, 0, h, 0, 0)
            ),
            scratch_shapes=[pltpu.VMEM((2, mids * depth, total), BF16)],
        ),
        out_shape=jax.ShapeDtypeStruct((groups, mids, high, depth, wide), BF16),
        compiler_params=params("arbitrary", "arbitrary"),
        cost_estimate=cost(
            2 * total * depth * groups * mids * high * wide,
            2 * total * (2 * depth * groups * mids * high + wide),
        ),
        name="weight_grads",
    )(places, x, m, pre, act)


def bits_of(size):
    return [1 << n for n in range(size.bit_length() - 1)]


def swap(values, axis, bit):
    size = lax.axis_size(axis) if isinstance(axis, str) else math.prod(map(lax.axis_size, axis))
    return lax.ppermute(values, axis, [(n, n ^ bit) for n in range(size)])


class Flow:
    def __init__(self, steps):
        self.steps = steps
        self.result = None
        self.sends = next(steps)

    def advance(self, got):
        try:
            self.sends = self.steps.send(got)
        except StopIteration as stop:
            self.sends = None
            self.result = stop.value

    def step(self, count=1):
        for _ in range(count):
            if self.sends is not None:
                self.advance([swap(*send) for send in self.sends])
        return self

    def finish(self):
        while self.sends is not None:
            self.step()
        return self.result

    def holds(self):
        return self.result if self.sends is None else [send[0] for send in self.sends]

    def replace(self, arrays):
        if self.sends is None:
            self.result = arrays
        else:
            self.sends = [(array, *send[1:]) for array, send in zip(arrays, self.sends)]


def stage(live, flows=(), work=(), sync=()):
    flows = [flow for flow in flows if flow.sends is not None]
    got = [[swap(*send) for send in flow.sends] for flow in flows]
    done = [each() for each in work]
    held = [flow.holds() for flow in sync]
    got, done, held, kept = lax.optimization_barrier((got, done, held, dict(live)))
    live.update(kept)
    for flow, arrays in zip(flows, got):
        flow.advance(arrays)
    for flow, arrays in zip(sync, held):
        flow.replace(arrays)
    return done


def spread_steps(values, axis, bits):
    blocks = {0: values}
    for bit in bits:
        places = sorted(blocks)
        got = yield [(blocks[place], axis, bit) for place in places]
        blocks.update({place | bit: block for place, block in zip(places, got)})
    return [blocks[place] for place in sorted(blocks)]


def spread_rows_steps(values, row_bits, strides):
    held = values[None]
    places = [0]
    for axis, bit in row_bits:
        (got,) = yield [(held, axis, bit)]
        held = jnp.concatenate([held, got], axis=0)
        places += [place | (bit * strides[axis]) for place in places]
    return jnp.stack([held[places.index(place)] for place in range(len(places))])


def spread_cube_steps(values, groups, cols):
    held = values[None]
    for axis, bits in (("lo", bits_of(groups)), ("col", bits_of(cols))):
        for bit in bits:
            (got,) = yield [(held, axis, bit)]
            held = jnp.concatenate([held, got], axis=0)
    return jnp.swapaxes(held.reshape((cols, groups) + values.shape), 0, 1)


def col_reduce_steps(blocks, cols):
    held = dict(enumerate(blocks))
    for bit in bits_of(cols):
        away = [place for place in sorted(held) if place & bit]
        (got,) = yield [(jnp.stack([held[place].astype(BF16) for place in away]), "col", bit)]
        held = {
            place & ~bit: held[place & ~bit] + got[number].astype(F32)
            for number, place in enumerate(away)
        }
    return held[0]


def total_steps(values, axes):
    for axis in axes:
        size = math.prod(map(lax.axis_size, axis))
        got = yield [(values, axis, place) for place in range(1, size)]
        values = values + sum(got)
    return values


def row_reduce_steps(grads, groups, mids, high):
    names = [("lo", bit) for bit in reversed(bits_of(groups))]
    names += [("mid", bit) for bit in reversed(bits_of(mids))]
    names += [("hi", bit) for bit in reversed(bits_of(high))]
    grads = grads.reshape((2,) * len(names) + grads.shape[3:])
    half = grads.shape[-1] // 2
    held = []
    for number in range(2):
        order = [name for name in names if name[0] != "hi"][:: 1 if number else -1]
        order += [name for name in reversed(names) if name[0] == "hi"]
        held.append((grads[..., number * half : (number + 1) * half], names, order))
    for step in range(len(names)):
        sends, rest = [], []
        for array, left, order in held:
            name = order[step]
            axis = left.index(name)
            away = 0 if name[0] == "lo" else 1
            sends.append((lax.index_in_dim(array, away, axis, False).astype(BF16), *name))
            kept = lax.index_in_dim(array, 1 - away, axis, False)
            rest.append((kept, [other for other in left if other != name], order))
        got = yield sends
        held = [
            (kept.astype(F32) + more.astype(F32), left, order)
            for (kept, left, order), more in zip(rest, got)
        ]
    return jnp.concatenate([array for array, _, _ in held], axis=1)


def links_of(groups, cols):
    return [("col", bit) for bit in bits_of(cols)[1:]] + [("lo", bit) for bit in bits_of(groups)]


def turned(links, number):
    number %= len(links)
    return links[number:] + links[:number]


def reduce_steps(parts, groups, cols):
    links = links_of(groups, cols)
    got = yield [(away, "col", 1) for _, away in parts]
    held = []
    for number, (keep, _) in enumerate(parts):
        shape = (2,) * len(links) + keep.shape[2:]
        names = [("lo", bit) for bit in reversed(bits_of(groups))]
        names += [("col", bit) for bit in reversed(bits_of(cols)[1:])]
        held.append((keep.reshape(shape), got[number].reshape(shape), names))
    for step in range(len(links)):
        sends, rest = [], []
        for number, (keep, more, names) in enumerate(held):
            link = turned(links, number)[step]
            axis = names.index(link)

            def half(place):
                total = lax.index_in_dim(keep, place, axis, False).astype(F32)
                return total + lax.index_in_dim(more, place, axis, False).astype(F32)

            sends.append((half(1).astype(BF16), *link))
            kept = half(0)
            rest.append(
                (
                    kept if step + 1 == len(links) else kept.astype(BF16),
                    [name for name in names if name != link],
                )
            )
        got = yield sends
        held = [(keep, more, names) for (keep, names), more in zip(rest, got)]
    return jnp.concatenate([keep.astype(F32) + more.astype(F32) for keep, more, _ in held], axis=0)


def part_sizes(tokens, count):
    whole = tokens // BLOCK
    return [BLOCK * ((whole + count - 1 - n) // count) for n in range(count)]


def expert_weight_steps(piece, far, bits):
    if far:
        (piece,) = yield [(piece, "lo", far)]
    held = {(): piece}
    fresh = [()]
    while True:
        ways = [
            (place, number)
            for place in fresh
            for number in range(place[-1] + 1 if place else 0, len(bits))
        ]
        if not ways:
            return held
        got = yield [(held[place], *bits[number]) for place, number in ways]
        fresh = [place + (number,) for place, number in ways]
        held.update(zip(fresh, got))


def expert_grad_steps(blocks, far, bits):
    for number in reversed(range(len(bits))):
        half = blocks.shape[0] // 2
        (got,) = yield [(blocks[half:], *bits[number])]
        blocks = blocks[:half].astype(F32) + got.astype(F32)
        if number or far:
            blocks = blocks.astype(BF16)
    total = blocks[0]
    if far:
        (total,) = yield [(total, "lo", far)]
    return total


def per_device(
    hidden_in,
    lengths,
    routes,
    attn_gain,
    query_gain,
    key_gain,
    query_weight,
    key_weight,
    value_weight,
    out_weight,
    moe_gain,
    router,
    gate_weight,
    up_weight,
    down_weight,
    cotangent,
):
    tok_rows, width = hidden_in.shape
    cols = lax.axis_size("col")
    groups = lax.axis_size("lo")
    high = lax.axis_size("hi")
    mids = lax.axis_size("mid")
    col = lax.axis_index("col")
    lo = lax.axis_index("lo")
    hi = lax.axis_index("hi")
    mid = lax.axis_index("mid")
    row = (hi * groups + lo) * mids + mid
    where = jnp.stack([lo, col])
    heads = width // HD
    seqs = lengths.shape[0]
    depth = gate_weight.shape[1]
    each = gate_weight.shape[0] // groups
    cube = ("lo", "col")
    rows_axes = ("hi", "lo", "mid")
    strides = {"hi": groups * mids, "lo": mids, "mid": 1}
    seq_rows = [slice(s * SEQ_LEN, (s + 1) * SEQ_LEN) for s in range(seqs)]
    links = links_of(groups, cols)
    col_bits = list(reversed(bits_of(cols)))
    hi_bits = [("hi", bit) for bit in bits_of(high)]
    mid_bits = [("mid", bit) for bit in bits_of(mids)]
    row_bits = hi_bits + [("lo", bit) for bit in bits_of(groups)] + mid_bits
    far_bits = hi_bits + mid_bits
    live = {}

    def row_of_set(place, far):
        other = row ^ (far * mids)
        for number in place:
            axis, bit = far_bits[number]
            other = other ^ (bit * strides[axis])
        return other

    hidden_flow = Flow(spread_steps(hidden_in, "col", col_bits))
    gain_flow = Flow(spread_steps(attn_gain, "col", col_bits))
    routes_flow = Flow(spread_steps(routes.T, "lo", bits_of(groups)))
    router_flow = Flow(spread_rows_steps(router.T.astype(BF16), row_bits, strides))
    out_flow = Flow(spread_rows_steps(out_weight.T.astype(BF16), row_bits, strides))
    qkv_local = jnp.concatenate([query_weight, key_weight, value_weight], axis=1).astype(BF16)
    qkv_full = lax.all_gather(qkv_local, rows_axes, axis=0, tiled=True)
    live_key = jnp.arange(SEQ_LEN)[None, :] < lengths[:, None]
    out_cot = jnp.where(live_key.reshape(tok_rows, 1), cotangent, jnp.zeros_like(cotangent))
    packed = pack_weights(where, gate_weight, up_weight, down_weight, each)
    units = [(expert, far) for expert in range(each) for far in range(groups)]
    live["packed"] = packed

    def rotary_tables():
        places = jnp.arange(SEQ_LEN).astype(F32)
        powers = jnp.arange(HD // 2).astype(F32) * (2.0 / HD)
        angles = places[:, None] * jnp.exp(-powers * math.log(rope_base))[None, :]
        cosine, sine = jnp.cos(angles), jnp.sin(angles)
        return (
            jnp.concatenate([cosine, cosine], axis=1),
            jnp.concatenate([-sine, sine], axis=1),
        )

    live["out_cot"] = out_cot
    (tables,) = stage(
        live,
        [hidden_flow, gain_flow, routes_flow, router_flow, out_flow],
        [rotary_tables],
    )

    hidden = hidden_in.astype(F32)

    def norm_attn():
        blocks = hidden_flow.finish()
        gains = gain_flow.finish()
        square = sum(jnp.sum(jnp.square(block.astype(F32)), axis=1) for block in blocks)
        inverse = lax.rsqrt(square / D + epsilon)[:, None]
        normed = jnp.zeros((tok_rows, D), BF16)
        for place, (block, gain) in enumerate(zip(blocks, gains)):
            piece = (block.astype(F32) * inverse * gain).astype(BF16)
            normed = lax.dynamic_update_slice_in_dim(normed, piece, (col ^ place) * width, 1)
        return normed, inverse

    def routing():
        rel = jnp.stack(routes_flow.finish())
        named = jnp.any(rel[:, :, None, :] == jnp.arange(EXPERTS)[None, None, :, None], axis=1)
        first = (col * groups + lo) * each
        member = lax.dynamic_slice_in_dim(named, first, each, 1)
        member = jnp.swapaxes(member, 0, 1).reshape(each * groups, tok_rows)
        count = member.astype(jnp.int32)
        rank = jnp.cumsum(count, axis=1) - count
        pos = jnp.where(member, rank, -(1 << 20))
        starts = jnp.minimum(rank[:, ::BLOCK] // EDGE * EDGE, CAP - WINDOW)
        return named, starts, pos[:, None, :], pos[:, :, None]

    live["qkv_full"] = qkv_full
    ((live["normed_attn"], attn_inverse),) = stage(live, [router_flow, out_flow], [norm_attn])
    weight_flows = {}

    def start_weights(expert):
        for far in range(groups):
            weight_flows[expert, far] = Flow(
                expert_weight_steps(live["packed"][far * each + expert], far, far_bits)
            )

    start_weights(0)
    moe_cot = lax.all_gather(live["out_cot"], cube, axis=0, tiled=False)
    hidden_blocks = hidden_flow.result
    query_scale, key_scale = query_gain[None, :], key_gain[None, :]

    def attend(s):
        return attend_forward(
            s, lengths[s : s + 1], live["qkv"], tables, query_scale, key_scale, heads
        )

    def project_and_attend():
        live["qkv"] = dot_of(live["normed_attn"], live["qkv_full"], 1, 0)
        return attend(0)

    firsts = [weight_flows[0, far] for far in range(1, groups)]
    (first_seq,) = stage(live, [router_flow, out_flow], [project_and_attend])
    for expert in range(1, each):
        start_weights(expert)
    seconds = [weight_flows[unit] for unit in units if unit[0] == 1]
    named, starts, pos_row, pos_col = routing()

    span = width // depth

    def col_rows(blocks, place, axis):
        first = (col ^ place) * span
        return jnp.concatenate(
            [
                lax.dynamic_index_in_dim(blocks, (first + n) ^ row, 0, False)
                for n in range(span)
            ],
            axis=axis,
        )

    out_spread = out_flow.finish()
    out_rel = jnp.concatenate([col_rows(out_spread, place, 0) for place in range(cols)], axis=0)
    router_rows = col_rows(router_flow.finish(), 0, 1)

    def branch(mixture):
        partial = dot_of(mixture, out_rel, 1, 1)
        blocks = [partial[:, n * width : (n + 1) * width] for n in range(cols)]
        return Flow(col_reduce_steps(blocks, cols)).finish()

    def attend_rest():
        outs = [first_seq]
        sums = [branch(first_seq[0])]
        for s in range(1, seqs):
            outs.append(attend(s))
            sums.append(branch(outs[s][0]))
        return outs, sums

    ((attended, branches),) = stage(live, [weight_flows[0, 0]] + firsts, [attend_rest])
    middle = hidden + jnp.concatenate(branches, axis=0)
    live["scaled_rows"] = (middle * moe_gain).astype(BF16)
    scaled_rows = live["scaled_rows"]
    moe_in = lax.all_gather(scaled_rows, cube, axis=0, tiled=False)
    square = jnp.sum(middle * middle, axis=1)[None, :]
    stat = jnp.concatenate([dot_of(router_rows, scaled_rows, 1, 1), square], axis=0)
    stat_flow = Flow(spread_cube_steps(stat, groups, cols))
    stage(live, [stat_flow], sync=[weight_flows[0, 0]] + firsts + seconds)
    (live["cot_rows"],) = stage(
        live,
        [stat_flow, weight_flows[0, 0]] + firsts,
        [lambda: compact(starts, where, pos_row, moe_cot, groups, cols)],
        sync=seconds,
    )
    for flow in seconds[:1]:
        flow.step(2)
    stage(live, [stat_flow] + firsts + seconds[1:])
    stat = stat_flow.finish()

    stat = jnp.sum(stat, axis=1)
    moe_inverse = lax.rsqrt(stat[:, EXPERTS] / D + epsilon)
    all_logits = stat[:, :EXPERTS] * moe_inverse[:, None, :]
    logits = jnp.where(named, all_logits, masked_score)
    shifted = jnp.where(named, jnp.exp(logits - jnp.max(logits, axis=1, keepdims=True)), 0.0)
    gates = shifted / jnp.sum(shifted, axis=1, keepdims=True)
    own_gate = lax.dynamic_slice_in_dim(gates, (col * groups + lo) * each, each, 1)
    own_gate = jnp.swapaxes(own_gate, 0, 1).reshape(each * groups, 1, tok_rows)
    row_gate, row_scale = compact_scalars(
        starts, pos_row, (own_gate, jnp.tile(moe_inverse, (each, 1))[:, None, :])
    )
    total_rows = groups * CAP

    live["moe_rows"] = compact(starts, where, pos_row, moe_in, groups, cols)

    def run_expert(expert):
        pieces, row_numbers = [], []
        for far in range(groups):
            for place, piece in weight_flows[expert, far].finish().items():
                pieces.append(piece)
                row_numbers.append(row_of_set(place, far))
        here = slice(expert * total_rows, (expert + 1) * total_rows)
        return expert_step(
            jnp.stack(row_numbers),
            live["moe_rows"][expert],
            live["cot_rows"][expert],
            row_gate[here],
            row_scale[here],
            pieces,
        )

    blocks_here = [
        (hi ^ above) * groups + (lo ^ far)
        for far in reversed(range(groups))
        for above in range(high)
    ]
    grad_places = jnp.stack(blocks_here + blocks_here + [mid])
    grad_flows = {}

    def start_grads(expert, outs):
        grads = weight_grads(
            grad_places,
            live["moe_rows"][expert],
            live["cot_rows"][expert],
            outs[1],
            outs[2],
            depth,
            groups,
            mids,
            high,
        )
        return grads.reshape((groups, mids * high) + grads.shape[3:])

    def grad_flow(expert, grads):
        for number, far in enumerate(reversed(range(groups))):
            grad_flows[expert, far] = Flow(expert_grad_steps(grads[number], far, far_bits))

    def running():
        return list(grad_flows.values())

    ran = []
    for expert in range(each):
        others = [flow for (number, _), flow in weight_flows.items() if number > expert]
        (outs,) = stage(
            live,
            others[1:] + running()[:1],
            [functools.partial(run_expert, expert)],
            sync=others[:1] + running()[1:],
        )
        ran.append(outs)
        if expert + 1 < each:
            (grads,) = stage(live, others, [functools.partial(start_grads, expert, outs)])
            grad_flow(expert, grads)
    early = running()
    live["result"] = [outs[5] for outs in ran]
    last = ran[-1]
    gate_cot = jnp.concatenate([outs[3] for outs in ran], axis=0)
    row_inner = jnp.concatenate([outs[4] for outs in ran], axis=0)
    sizes = part_sizes(tok_rows, len(links))
    live["scalars"] = (gate_cot, row_inner)
    (rows_parts,) = stage(
        live,
        [],
        [
            lambda: expand(
                starts, where, pos_col, [outs[0] for outs in ran], sizes, groups, cols
            )
        ],
    )
    gate_cot, row_inner = expand_scalars(starts, pos_row, live.pop("scalars"))
    gate_cot = gate_cot.reshape(each, groups, tok_rows)
    row_inner = jnp.sum(row_inner.reshape(each, groups, tok_rows), axis=0)[None]
    scalars = jnp.concatenate([gate_cot, row_inner], axis=0)
    scalars = scalars.reshape((each + 1) * groups, tok_rows)
    scalar_flow = Flow(spread_cube_steps(scalars, groups, cols))
    moe_in_flow = Flow(reduce_steps(rows_parts, groups, cols))
    (grads,) = stage(
        live,
        [moe_in_flow, scalar_flow] + early,
        [functools.partial(start_grads, each - 1, last)],
    )
    grad_flow(each - 1, grads)
    late = running()[len(early) :]
    scalar_flow.finish()
    for flow in late[:1]:
        flow.step()
    (branch_parts,) = stage(
        live,
        [moe_in_flow],
        [lambda: expand_all(starts, where, pos_col, live["result"], groups, cols)],
        sync=[scalar_flow] + early,
    )
    live["moe_branch"] = branch_parts.reshape(groups * cols, tok_rows, width)
    while moe_in_flow.sends is not None:
        stage(live, [moe_in_flow], sync=early + late)
    for flow in early[1:]:
        flow.step()
    scalar_all = scalar_flow.finish().reshape(groups, cols, each + 1, groups, tok_rows)
    scalar_all = jnp.stack([scalar_all[place, :, :, place] for place in range(groups)])
    by_expert = jnp.stack(
        [
            ((lo ^ (number // each % groups)) * cols + (col ^ (number // (each * groups)))) * each
            + number % each
            for number in range(EXPERTS)
        ]
    )
    gate_cot = jnp.take(scalar_all[:, :, :each].reshape(EXPERTS, tok_rows), by_expert, axis=0)
    my_gates, my_logits = gates[0], all_logits[0]
    logit_cot = my_gates * (gate_cot - jnp.sum(my_gates * gate_cot, axis=0, keepdims=True))
    inner = jnp.sum(scalar_all[:, :, each], axis=(0, 1)) + jnp.sum(logit_cot * my_logits, axis=0)
    scaled_logit = (logit_cot * moe_inverse[0][None, :]).astype(BF16)
    logit_cot = logit_cot.astype(BF16)
    my_inverse = moe_inverse[0][:, None]

    back = moe_in_flow.finish() + my_inverse * dot_of(logit_cot, router_rows, 0, 0)
    middle_cot = (
        out_cot.astype(F32)
        + back * moe_gain
        - middle * (my_inverse * my_inverse * (inner[:, None] / D))
    )
    cot_flow = Flow(spread_steps(middle_cot.astype(BF16), "col", col_bits))
    router_part, moe_gain_part = stage(
        live,
        [cot_flow],
        [
            lambda: dot_of(scaled_logit, scaled_rows, 1, 0),
            lambda: jnp.sum(back * middle, axis=0)[None],
        ],
    )
    cot_blocks = cot_flow.finish()
    moe_branch = lax.psum_scatter(
        live.pop("moe_branch"), cube, scatter_dimension=0, tiled=True
    )[0]

    cot_all = jnp.concatenate(cot_blocks, axis=1)

    def attend_back(s):
        mixture_cot = dot_of(cot_all[seq_rows[s]], out_rel, 1, 0).astype(BF16)
        *cots, query_part, key_part, token_inner = attend_backward(
            s,
            lengths[s : s + 1],
            attended[s][1:],
            mixture_cot,
            live["qkv"],
            tables,
            query_scale,
            key_scale,
            heads,
        )
        cots = jnp.concatenate(cots, axis=1)
        return cots, query_part, key_part, token_inner[:, 0]

    qkv_rel = jnp.concatenate(
        [
            lax.dynamic_slice_in_dim(live["qkv_full"], (col ^ place) * width, width, 0)
            for place in range(cols)
        ],
        axis=0,
    )
    mixture = jnp.concatenate([outs[0] for outs in attended], axis=0)
    live.update(qkv_rel=qkv_rel, mixture=mixture, cot_all=cot_all)
    done = stage(
        live,
        early[:1] + late,
        [functools.partial(attend_back, s) for s in range(seqs)],
        sync=early[1:],
    )
    share = width // (mids * depth)
    cot_places = [((n // share) ^ col) * share + n % share for n in blocks_here]

    live["qkv_cot"] = jnp.concatenate([outs[0] for outs in done], axis=0)

    def projection_grads():
        grads = weight_grads(
            jnp.stack(blocks_here + cot_places + [mid]),
            live["normed_attn"],
            live["cot_all"],
            live["qkv_cot"],
            live["mixture"],
            depth,
            groups,
            mids,
            high,
        )
        return grads

    def widen(blocks):
        full = jnp.zeros((blocks[0].shape[0], D), F32)
        for place, block in enumerate(blocks):
            full = lax.dynamic_update_slice_in_dim(full, block, (col ^ place) * width, 1)
        return full

    for flow in late:
        flow.step()
    (partial,) = stage(live, [], [lambda: dot_of(live["qkv_cot"], live["qkv_rel"], 1, 1)])
    backs = [partial[:, n * width : (n + 1) * width] for n in range(cols)]
    attn_flow = Flow(col_reduce_steps(backs, cols))

    def gain_sums():
        attn_gain_parts = [
            jnp.sum(part * (block.astype(F32) * attn_inverse), axis=0)[None]
            for part, block in zip(backs, hidden_blocks)
        ]
        query_part = sum(outs[1] for outs in done)
        key_part = sum(outs[2] for outs in done)
        head_parts = jnp.concatenate([query_part, key_part], 1)
        return jnp.concatenate(
            [
                widen([router_part]),
                widen([moe_gain_part]),
                widen(attn_gain_parts),
                jnp.pad(head_parts, ((0, 0), (0, D - 2 * HD))),
            ],
            axis=0,
        )

    token_inner = jnp.concatenate([outs[3] for outs in done], axis=0)
    inner_flow = Flow(total_steps(token_inner, [("col",)]))
    (grads,) = stage(live, [attn_flow, inner_flow], [projection_grads])
    qkv_flow = Flow(row_reduce_steps(grads, groups, mids, high))
    for _ in bits_of(cols)[2:]:
        stage(live, [attn_flow])
    small_flows = []

    def small_sums():
        flow = Flow(total_steps(gain_sums(), [("col",), ("lo", "mid"), ("hi",)])).step()
        small_flows.append(flow)
        return flow.holds()

    (held,) = stage(live, [attn_flow, qkv_flow], [small_sums], sync=[late[1]])
    (small_flow,) = small_flows
    small_flow.replace(held)
    live["moe_branch"] = moe_branch

    def input_sums():
        return (
            middle_cot
            + attn_inverse * (attn_flow.finish() * attn_gain)
            - hidden * (attn_inverse * attn_inverse * (inner_flow.finish()[:, None] / D))
        )

    (input_grad,) = stage(live, [qkv_flow, small_flow], [input_sums])
    flows = [qkv_flow, small_flow] + early + late
    while any(flow.sends is not None for flow in flows):
        stage(live, flows)
    moe_branch = live["moe_branch"]
    weight_sum = qkv_flow.finish()
    out_sum = weight_sum[:, 3 * width :]
    small = small_flow.finish()

    output = (middle + moe_branch.astype(F32)).astype(BF16)
    gate_grad, up_grad, down_grad = unpack_grads(
        where,
        [grad_flows[expert, far].finish() for far in range(groups) for expert in range(each)],
        each,
    )
    own = lax.dynamic_slice_in_dim(small, col * width, width, 1)
    router_grad = lax.dynamic_slice_in_dim(small[:EXPERTS], row * depth, depth, 1).T
    return (
        output,
        input_grad,
        own[EXPERTS + 1],
        small[EXPERTS + 2, :HD],
        small[EXPERTS + 2, HD : 2 * HD],
        weight_sum[:, :width],
        weight_sum[:, width : 2 * width],
        weight_sum[:, 2 * width : 3 * width],
        out_sum.T,
        own[EXPERTS],
        router_grad,
        gate_grad,
        up_grad,
        down_grad,
    )


def solution(mesh):
    row_count, col_count = mesh.shape["row"], mesh.shape["col"]
    groups = 2
    between = EXPERTS // col_count // groups
    shape = (row_count // (groups * between), groups, between, col_count)
    inner = Mesh(mesh.devices.reshape(shape), ("hi", "lo", "mid", "col"))
    row = ("hi", "lo", "mid")
    return jax.shard_map(
        per_device,
        mesh=inner,
        in_specs=(
            P(row, "col"),
            P(row),
            P(row, None),
            P("col"),
            P(),
            P(),
            P(row, "col"),
            P(row, "col"),
            P(row, "col"),
            P("col", row),
            P("col"),
            P(row, None),
            P("col", row, None),
            P("col", row, None),
            P("col", None, row),
            P(row, "col"),
        ),
        out_specs=(
            P(row, "col"),
            P(row, "col"),
            P("col"),
            P(),
            P(),
            P(row, "col"),
            P(row, "col"),
            P(row, "col"),
            P("col", row),
            P("col"),
            P(row, None),
            P("col", row, None),
            P("col", row, None),
            P("col", None, row),
        ),
        check_vma=False,
    )
```

```python
import functools
import math

import jax
import jax.numpy as jnp
from jax import lax
from jax.experimental import pallas as pl
from jax.experimental.pallas import tpu as pltpu
from jax.sharding import Mesh, PartitionSpec as P

D = 2048
HD = 128
EXPERTS = 16
SEQ_LEN = 1024
CAP = 1152

BLOCK = 128
WINDOW = 144
EDGE = 16
TILE = 384
COST_SHARE = 50
EXPERT_WIDE, EXPERT_UNROLL = 512, 2
GRAD_WIDE, GRAD_UNROLL = 512, 1

epsilon = 1e-06
rope_base = 10000.0
masked_score = -1e30

F32 = jnp.float32
BF16 = jnp.bfloat16
ANY = pl.ANY
VMEM_LIMIT = 56 * 1024 * 1024


def dot_of(a, b, da, db):
    return lax.dot_general(a, b, (((da,), (db,)), ((), ())), preferred_element_type=F32)


def params(*semantics):
    return pltpu.CompilerParams(
        vmem_limit_bytes=VMEM_LIMIT, dimension_semantics=semantics or None
    )


def cost(flops, bytes_accessed, transcendentals=0):
    return pl.CostEstimate(
        flops=int(flops) // COST_SHARE,
        bytes_accessed=int(bytes_accessed) // COST_SHARE,
        transcendentals=int(transcendentals) // COST_SHARE,
    )


def turn(values, cosine, sine):
    return values * cosine + pltpu.roll(values, HD // 2, 1) * sine


def attend_forward_kernel(
    live_ref, q_ref, k_ref, v_ref, cos_ref, sin_ref, qg_ref, kg_ref, mix_ref, ql_ref, kl_ref, vl_ref
):
    live = live_ref[0]
    cosine = cos_ref[...]
    sine = sin_ref[...]

    def normed(values, gain):
        inverse = lax.rsqrt(jnp.mean(values * values, axis=1, keepdims=True) + epsilon)
        return turn(values * inverse * gain, cosine, sine).astype(BF16)

    ql_ref[...] = normed(q_ref[...], qg_ref[...])
    kl_ref[...] = normed(k_ref[...], kg_ref[...])
    vl_ref[...] = v_ref[...].astype(BF16)
    keys = kl_ref[...]
    values = vl_ref[...]
    rows = 256
    place = lax.broadcasted_iota(jnp.int32, (rows, SEQ_LEN), 1)
    for part in range(SEQ_LEN // rows):
        here = pl.ds(part * rows, rows)
        scores = dot_of(ql_ref[here, :], keys, 1, 1) * (1.0 / math.sqrt(HD))
        scores = jnp.where(place < live, scores, masked_score)
        top = jnp.max(scores, axis=1, keepdims=True)
        shifted = jnp.exp(scores - top)
        total = jnp.sum(shifted, axis=1, keepdims=True)
        probs = (shifted * (1.0 / total)).astype(BF16)
        mix_ref[here, :] = dot_of(probs, values, 1, 0).astype(BF16)


def attend_forward(seq, live, qkv, tables, query_gain, key_gain, heads):
    width = heads * HD

    def pick(offset):
        return pl.BlockSpec((SEQ_LEN, HD), lambda h, live, o=offset: (seq, o + h))

    def whole(shape):
        return pl.BlockSpec(shape, lambda h, live: (0, 0))

    out = pl.BlockSpec((SEQ_LEN, HD), lambda h, live: (0, h))
    return pl.pallas_call(
        attend_forward_kernel,
        grid_spec=pltpu.PrefetchScalarGridSpec(
            num_scalar_prefetch=1,
            grid=(heads,),
            in_specs=[
                pick(0),
                pick(heads),
                pick(2 * heads),
                whole((SEQ_LEN, HD)),
                whole((SEQ_LEN, HD)),
                whole((1, HD)),
                whole((1, HD)),
            ],
            out_specs=[out] * 4,
        ),
        out_shape=[jax.ShapeDtypeStruct((SEQ_LEN, width), BF16)] * 4,
        compiler_params=params("arbitrary"),
        cost_estimate=cost(
            heads * 8 * SEQ_LEN * SEQ_LEN * HD, 20 * SEQ_LEN * width, heads * SEQ_LEN * SEQ_LEN
        ),
        name="attend_forward",
    )(live, qkv, qkv, qkv, tables[0], tables[1], query_gain, key_gain)


def attend_backward_kernel(
    live_ref,
    ql_ref,
    kl_ref,
    vl_ref,
    do_ref,
    q_ref,
    k_ref,
    cos_ref,
    sin_ref,
    qg_ref,
    kg_ref,
    qc_ref,
    kc_ref,
    vc_ref,
    qpart_ref,
    kpart_ref,
    inner_ref,
    dq_ref,
    dk_ref,
    dv_ref,
):
    head = pl.program_id(0)
    live = live_ref[0]
    scale = 1.0 / math.sqrt(HD)
    keys = kl_ref[...]
    values = vl_ref[...]
    rows = 256
    place = lax.broadcasted_iota(jnp.int32, (SEQ_LEN, rows), 0)
    for part in range(SEQ_LEN // rows):
        here = pl.ds(part * rows, rows)
        queries = ql_ref[here, :]
        incoming = do_ref[here, :]
        scores = dot_of(keys, queries, 1, 1) * scale
        scores = jnp.where(place < live, scores, masked_score)
        top = jnp.max(scores, axis=0, keepdims=True)
        shifted = jnp.exp(scores - top)
        total = jnp.sum(shifted, axis=0, keepdims=True)
        probs = shifted * (1.0 / total)
        dv = dot_of(probs.astype(BF16), incoming, 1, 0)
        probs_cot = dot_of(values, incoming, 1, 1)
        weighted = probs * probs_cot
        centre = jnp.sum(weighted, axis=0, keepdims=True)
        raw = ((weighted - probs * centre) * scale).astype(BF16)
        dk = dot_of(raw, queries, 1, 0)
        dq_ref[here, :] = dot_of(raw, keys, 0, 0)
        if part == 0:
            dv_ref[...] = dv
            dk_ref[...] = dk
        else:
            dv_ref[...] += dv
            dk_ref[...] += dk
    cosine = cos_ref[...]
    sine = -sin_ref[...]

    def back(values, gain, rotated_cot):
        incoming = turn(rotated_cot, cosine, sine)
        inverse = lax.rsqrt(jnp.mean(values * values, axis=1, keepdims=True) + epsilon)
        scaled = incoming * gain
        inner = jnp.mean(scaled * values, axis=1, keepdims=True)
        grad = inverse * scaled - values * (inverse * inverse * inverse * inner)
        part = jnp.sum(incoming * values * inverse, axis=0, keepdims=True)
        return grad.astype(BF16), part, jnp.sum(grad * values, axis=1, keepdims=True)

    qc_ref[...], qpart, inner = back(q_ref[...], qg_ref[...], dq_ref[...])
    kc_ref[...], kpart, key_inner = back(k_ref[...], kg_ref[...], dk_ref[...])
    vc_ref[...] = dv_ref[...].astype(BF16)
    inner += key_inner
    inner += jnp.sum(dv_ref[...] * values.astype(F32), axis=1, keepdims=True)

    @pl.when(head == 0)
    def _():
        qpart_ref[...] = qpart
        kpart_ref[...] = kpart
        inner_ref[...] = inner

    @pl.when(head > 0)
    def _():
        qpart_ref[...] += qpart
        kpart_ref[...] += kpart
        inner_ref[...] += inner


def attend_backward(seq, live, lows, mixture_cot, qkv, tables, query_gain, key_gain, heads):
    width = heads * HD
    block = pl.BlockSpec((SEQ_LEN, HD), lambda h, live: (0, h))

    def pick(offset):
        return pl.BlockSpec((SEQ_LEN, HD), lambda h, live, o=offset: (seq, o + h))

    def whole(shape):
        return pl.BlockSpec(shape, lambda h, live: (0, 0))

    return pl.pallas_call(
        attend_backward_kernel,
        grid_spec=pltpu.PrefetchScalarGridSpec(
            num_scalar_prefetch=1,
            grid=(heads,),
            in_specs=[block] * 4
            + [
                pick(0),
                pick(heads),
                whole((SEQ_LEN, HD)),
                whole((SEQ_LEN, HD)),
                whole((1, HD)),
                whole((1, HD)),
            ],
            out_specs=[block] * 3 + [whole((1, HD))] * 2 + [whole((SEQ_LEN, 1))],
            scratch_shapes=[pltpu.VMEM((SEQ_LEN, HD), F32)] * 3,
        ),
        out_shape=[jax.ShapeDtypeStruct((SEQ_LEN, width), BF16)] * 3
        + [jax.ShapeDtypeStruct((1, HD), F32)] * 2
        + [jax.ShapeDtypeStruct((SEQ_LEN, 1), F32)],
        compiler_params=params("arbitrary"),
        cost_estimate=cost(
            heads * 20 * SEQ_LEN * SEQ_LEN * HD, 24 * SEQ_LEN * width, heads * SEQ_LEN * SEQ_LEN
        ),
        name="attend_backward",
    )(live, *lows, mixture_cot, qkv, qkv, tables[0], tables[1], query_gain, key_gain)


def compact_kernel(start_ref, where_ref, pos_ref, source_ref, *outs):
    group, groups = pl.program_id(0), pl.num_programs(0)
    row_of = lax.broadcasted_iota(jnp.int32, (WINDOW, BLOCK), 0)
    for out in outs:
        out[...] = jnp.zeros_like(out)
    for number in range(source_ref.shape[1] // BLOCK):
        here = slice(number * BLOCK, (number + 1) * BLOCK)
        for expert, out in enumerate(outs):
            start = pl.multiple_of(start_ref[expert * groups + group, number], EDGE)
            place = pos_ref[expert, 0, :, here]
            choice = jnp.where(row_of + start == place, 1.0, 0.0).astype(BF16)
            rows = dot_of(choice, source_ref[0, here, :], 1, 0)
            out[pl.ds(start, WINDOW), :] += rows.astype(BF16)


def compact(starts, where, pos_row, source, groups, cols):
    tokens, width = source.shape[1:]
    count = pos_row.shape[0] // groups
    return pl.pallas_call(
        compact_kernel,
        grid_spec=pltpu.PrefetchScalarGridSpec(
            num_scalar_prefetch=2,
            grid=(groups, cols),
            in_specs=[
                pl.BlockSpec((count, 1, 1, tokens), lambda q, j, s, w: (0, q, 0, 0)),
                pl.BlockSpec(
                    (1, tokens, width), lambda q, j, s, w: ((w[0] ^ q) * cols + j, 0, 0)
                ),
            ],
            out_specs=[pl.BlockSpec((CAP, width), lambda q, j, s, w: (q, j))] * count,
        ),
        out_shape=[jax.ShapeDtypeStruct((groups * CAP, cols * width), BF16)] * count,
        compiler_params=params("arbitrary", "arbitrary"),
        cost_estimate=cost(
            count * groups * cols * 2 * tokens * WINDOW * width * 2,
            groups * cols * 2 * width * (tokens + count * CAP),
        ),
        name="compact",
    )(starts, where, pos_row.reshape(count, groups, 1, tokens), source)


def compact_scalars_kernel(start_ref, pos_ref, *refs):
    count = len(refs) // 2
    group = pl.program_id(0)
    row_of = lax.broadcasted_iota(jnp.int32, (WINDOW, BLOCK), 0)
    for number in range(count):
        refs[count + number][...] = jnp.zeros_like(refs[count + number])
    for number in range(pos_ref.shape[2] // BLOCK):
        start = pl.multiple_of(start_ref[group, number], EDGE)
        here = slice(number * BLOCK, (number + 1) * BLOCK)
        choice = row_of + start == pos_ref[0, :, here]
        for source, out in zip(refs[:count], refs[count:]):
            picked = jnp.sum(jnp.where(choice, source[0, :, here], 0.0), axis=1, keepdims=True)
            out[pl.ds(start, WINDOW), :] += picked


def compact_scalars(starts, pos_row, sources):
    groups, _, tokens = pos_row.shape
    block = pl.BlockSpec((1, 1, tokens), lambda q, s: (q, 0, 0))
    return pl.pallas_call(
        compact_scalars_kernel,
        grid_spec=pltpu.PrefetchScalarGridSpec(
            num_scalar_prefetch=1,
            grid=(groups,),
            in_specs=[block] * (1 + len(sources)),
            out_specs=[pl.BlockSpec((CAP, 1), lambda q, s: (q, 0))] * len(sources),
        ),
        out_shape=[jax.ShapeDtypeStruct((groups * CAP, 1), F32)] * len(sources),
        compiler_params=params("arbitrary"),
        cost_estimate=cost(0, 4 * groups * CAP * 128 * len(sources)),
        name="compact_scalars",
    )(starts, pos_row, *sources)


def expand_scalars_kernel(start_ref, pos_ref, *refs):
    count = len(refs) // 2
    group = pl.program_id(0)
    row_of = lax.broadcasted_iota(jnp.int32, (WINDOW, BLOCK), 0)
    for number in range(pos_ref.shape[2] // BLOCK):
        start = pl.multiple_of(start_ref[group, number], EDGE)
        here = slice(number * BLOCK, (number + 1) * BLOCK)
        choice = row_of + start == pos_ref[0, :, here]
        for source, out in zip(refs[:count], refs[count:]):
            held = source[pl.ds(start, WINDOW), :]
            out[0, :, here] = jnp.sum(jnp.where(choice, held, 0.0), axis=0, keepdims=True)


def expand_scalars(starts, pos_row, sources):
    groups, _, tokens = pos_row.shape
    block = pl.BlockSpec((1, 1, tokens), lambda q, s: (q, 0, 0))
    return pl.pallas_call(
        expand_scalars_kernel,
        grid_spec=pltpu.PrefetchScalarGridSpec(
            num_scalar_prefetch=1,
            grid=(groups,),
            in_specs=[block] + [pl.BlockSpec((CAP, 1), lambda q, s: (q, 0))] * len(sources),
            out_specs=[block] * len(sources),
        ),
        out_shape=[jax.ShapeDtypeStruct((groups, 1, tokens), F32)] * len(sources),
        compiler_params=params("arbitrary"),
        cost_estimate=cost(0, 4 * groups * CAP * 128 * len(sources)),
        name="expand_scalars",
    )(starts, pos_row, *sources)


def expand_kernel(sizes, count, start_ref, where_ref, pos_ref, *refs):
    group, groups = pl.program_id(0), pl.num_programs(0)
    sides = len(refs) // (count + len(sizes))
    sources, outs = refs[: count * sides], refs[count * sides :]
    column_of = lax.broadcasted_iota(jnp.int32, (BLOCK, WINDOW), 1)
    number = 0
    for part, size in enumerate(sizes):
        for step in range(size // BLOCK):
            totals = [None] * sides
            for expert in range(count):
                start = pl.multiple_of(start_ref[expert * groups + group, number], EDGE)
                place = pos_ref[expert, 0, number * BLOCK : (number + 1) * BLOCK, :]
                choice = jnp.where(column_of + start == place, 1.0, 0.0).astype(BF16)
                for side in range(sides):
                    held = sources[expert * sides + side][pl.ds(start, WINDOW), :]
                    rows = dot_of(choice, held, 1, 0)
                    totals[side] = rows if totals[side] is None else totals[side] + rows
            here = slice(step * BLOCK, (step + 1) * BLOCK)
            for side in range(sides):
                outs[part * sides + side][0, 0, here, :] = totals[side].astype(BF16)
            number += 1


def expand(starts, where, pos_col, sources, sizes, groups, cols):
    width = sources[0].shape[1] // cols
    tokens = sum(sizes)
    count = len(sources)

    def side(odd):
        return pl.BlockSpec((CAP, width), lambda q, j, s, w: (q, w[1] ^ (2 * j + odd)))

    outs = pl.pallas_call(
        functools.partial(expand_kernel, sizes, count),
        grid_spec=pltpu.PrefetchScalarGridSpec(
            num_scalar_prefetch=2,
            grid=(groups, cols // 2),
            in_specs=[pl.BlockSpec((count, 1, tokens, 1), lambda q, j, s, w: (0, q, 0, 0))]
            + [side(0), side(1)] * count,
            out_specs=[
                pl.BlockSpec((1, 1, size, width), lambda q, j, s, w: (q, j, 0, 0))
                for size in sizes
                for _ in range(2)
            ],
        ),
        out_shape=[
            jax.ShapeDtypeStruct((groups, cols // 2, size, width), BF16)
            for size in sizes
            for _ in range(2)
        ],
        compiler_params=params("arbitrary", "arbitrary"),
        cost_estimate=cost(
            4 * count * groups * cols * tokens * WINDOW * width,
            groups * cols * width * (2 * tokens + 2 * count * CAP),
        ),
        name="expand",
    )(
        starts,
        where,
        pos_col.reshape(count, groups, tokens, 1),
        *[source for source in sources for _ in range(2)],
    )
    return list(zip(outs[::2], outs[1::2]))


def expand_all(starts, where, pos_col, sources, groups, cols):
    width = sources[0].shape[1] // cols
    tokens = pos_col.shape[1]
    count = len(sources)
    return pl.pallas_call(
        functools.partial(expand_kernel, [tokens], count),
        grid_spec=pltpu.PrefetchScalarGridSpec(
            num_scalar_prefetch=2,
            grid=(groups, cols),
            in_specs=[pl.BlockSpec((count, 1, tokens, 1), lambda q, j, s, w: (0, q, 0, 0))]
            + [pl.BlockSpec((CAP, width), lambda q, j, s, w: (q, j))] * count,
            out_specs=pl.BlockSpec((1, 1, tokens, width), lambda q, j, s, w: (w[0] ^ q, j, 0, 0)),
        ),
        out_shape=jax.ShapeDtypeStruct((groups, cols, tokens, width), BF16),
        compiler_params=params("arbitrary", "arbitrary"),
        cost_estimate=cost(
            4 * count * groups * cols * tokens * WINDOW * width,
            groups * cols * width * (2 * tokens + 2 * count * CAP),
        ),
        name="expand_all",
    )(starts, where, pos_col.reshape(count, groups, tokens, 1), *sources)


def pack_kernel(where_ref, gate_ref, up_ref, down_ref, out_ref):
    hidden = gate_ref.shape[2]
    out_ref[0, :, :hidden] = gate_ref[0].astype(BF16)
    out_ref[0, :, hidden : 2 * hidden] = up_ref[0].astype(BF16)
    out_ref[0, :, 2 * hidden :] = down_ref[0].T.astype(BF16)


def pack_weights(where, gate, up, down, each):
    experts, depth, hidden = gate.shape

    def pick(shape):
        return pl.BlockSpec(shape, lambda q, w: ((w[0] ^ (q // each)) * each + q % each, 0, 0))

    return pl.pallas_call(
        pack_kernel,
        grid_spec=pltpu.PrefetchScalarGridSpec(
            num_scalar_prefetch=1,
            grid=(experts,),
            in_specs=[pick((1, depth, hidden)), pick((1, depth, hidden)), pick((1, hidden, depth))],
            out_specs=pl.BlockSpec((1, depth, 3 * hidden), lambda q, w: (q, 0, 0)),
        ),
        out_shape=jax.ShapeDtypeStruct((experts, depth, 3 * hidden), BF16),
        compiler_params=params("arbitrary"),
        cost_estimate=cost(0, 18 * experts * depth * hidden),
        name="pack_weights",
    )(where, gate, up, down)


def unpack_kernel(where_ref, *refs):
    sources, (gate_ref, up_ref, down_ref) = refs[:-3], refs[-3:]
    hidden = gate_ref.shape[2]
    for number, source in enumerate(sources):

        @pl.when(pl.program_id(0) == number)
        def _(source=source):
            gate_ref[0] = source[:, :hidden].astype(F32)
            up_ref[0] = source[:, hidden : 2 * hidden].astype(F32)
            down_ref[0] = source[:, 2 * hidden :].astype(F32).T


def unpack_grads(where, sources, each):
    count = len(sources)
    depth, wide = sources[0].shape
    hidden = wide // 3

    def pick(shape):
        return pl.BlockSpec(shape, lambda q, w: ((w[0] ^ (q // each)) * each + q % each, 0, 0))

    shapes = [(count, depth, hidden), (count, depth, hidden), (count, hidden, depth)]
    return pl.pallas_call(
        unpack_kernel,
        grid_spec=pltpu.PrefetchScalarGridSpec(
            num_scalar_prefetch=1,
            grid=(count,),
            in_specs=[pl.BlockSpec((depth, wide), lambda q, w: (0, 0))] * count,
            out_specs=[pick((1,) + shape[1:]) for shape in shapes],
        ),
        out_shape=[jax.ShapeDtypeStruct(shape, F32) for shape in shapes],
        compiler_params=params("arbitrary"),
        cost_estimate=cost(0, 18 * count * depth * hidden),
        name="unpack_grads",
    )(where, *sources)


def expert_kernel(count, hidden, row_ref, x_ref, m_ref, gate_ref, scale_ref, *refs):
    pieces = refs[:count]
    rows_ref, pre_ref, act_ref, cot_ref, inner_ref, result_ref, held, sems = refs[count:]
    depth = pieces[0].shape[0]

    @pl.when(pl.program_id(0) == 0)
    def _():
        copies = []
        for number, piece in enumerate(pieces):
            place = pl.ds(pl.multiple_of(row_ref[number] * depth, depth), depth)
            copies.append(pltpu.make_async_copy(piece, held.at[place, :], sems.at[number]))
        for copy in copies:
            copy.start()
        for copy in copies:
            copy.wait()

    gate = gate_ref[...]
    scale = scale_ref[...]
    wide = EXPERT_WIDE
    cot_ref[...] = jnp.zeros_like(cot_ref)
    inner_ref[...] = jnp.zeros_like(inner_ref)

    @pl.loop(0, hidden // wide, unroll=EXPERT_UNROLL)
    def _(step):
        first = pl.multiple_of(step * wide, wide)
        gate_pre = dot_of(x_ref[...], held[:, pl.ds(first, wide)], 1, 0) * scale
        up_pre = dot_of(x_ref[...], held[:, pl.ds(hidden + first, wide)], 1, 0) * scale
        back = dot_of(m_ref[...], held[:, pl.ds(2 * hidden + first, wide)], 1, 0)
        squash = 1.0 / (1.0 + jnp.exp(-gate_pre))
        silu = gate_pre * squash
        active = silu * up_pre
        cot_ref[...] += jnp.sum(active.astype(BF16).astype(F32) * back, axis=1, keepdims=True)
        act_ref[:, pl.ds(first, wide)] = (active * gate).astype(BF16)
        back = back * gate
        slope = squash * (1.0 + gate_pre * (1.0 - squash))
        gate_cot = back * up_pre * slope
        up_cot = back * silu
        inner_ref[...] += jnp.sum(gate_cot * gate_pre + up_cot * up_pre, axis=1, keepdims=True)
        pre_ref[:, pl.ds(first, wide)] = (gate_cot * scale).astype(BF16)
        pre_ref[:, pl.ds(hidden + first, wide)] = (up_cot * scale).astype(BF16)

    @pl.loop(0, held.shape[0] // wide, unroll=EXPERT_UNROLL)
    def _(step):
        first = pl.multiple_of(step * wide, wide)
        here = pl.ds(first, wide)
        rows_ref[:, here] = dot_of(pre_ref[...], held[here, : 2 * hidden], 1, 1).astype(BF16)
        result_ref[:, here] = dot_of(act_ref[...], held[here, 2 * hidden :], 1, 1).astype(BF16)


def expert_step(row_numbers, x, m, gate, scale, pieces):
    total, wide = x.shape
    hidden = pieces[0].shape[1] // 3
    count = len(pieces)

    def tile(columns):
        return pl.BlockSpec((TILE, columns), lambda i, r: (i, 0))

    return pl.pallas_call(
        functools.partial(expert_kernel, count, hidden),
        grid_spec=pltpu.PrefetchScalarGridSpec(
            num_scalar_prefetch=1,
            grid=(total // TILE,),
            in_specs=[tile(wide), tile(wide), tile(1), tile(1)]
            + [pl.BlockSpec(memory_space=ANY)] * count,
            out_specs=[tile(wide), tile(2 * hidden), tile(hidden), tile(1), tile(1), tile(wide)],
            scratch_shapes=[
                pltpu.VMEM((wide, 3 * hidden), BF16),
                pltpu.SemaphoreType.DMA((count,)),
            ],
        ),
        out_shape=[
            jax.ShapeDtypeStruct((total, wide), BF16),
            jax.ShapeDtypeStruct((total, 2 * hidden), BF16),
            jax.ShapeDtypeStruct((total, hidden), BF16),
            jax.ShapeDtypeStruct((total, 1), F32),
            jax.ShapeDtypeStruct((total, 1), F32),
            jax.ShapeDtypeStruct((total, wide), BF16),
        ],
        compiler_params=params("arbitrary"),
        cost_estimate=cost(
            2 * total * wide * hidden * 6, 2 * total * (4 * wide + 3 * hidden), total * hidden
        ),
        name="expert_step",
    )(row_numbers, x, m, gate, scale, *pieces)


def weight_grad_kernel(mids, place_ref, x_ref, m_ref, pre_ref, act_ref, out_ref, turned_ref):
    wide = GRAD_WIDE
    first = pre_ref.shape[1]
    depth = x_ref.shape[1] // mids
    turned_ref[0] = x_ref[...].T
    turned_ref[1] = m_ref[...].T
    mid = place_ref[place_ref.shape[0] - 1]

    def put(grad, here):
        for number in range(mids):
            block = grad[number * depth : (number + 1) * depth].astype(BF16)
            out_ref[0, number ^ mid, 0, :, here] = block

    @pl.loop(0, first // wide, unroll=GRAD_UNROLL)
    def _(step):
        here = pl.ds(pl.multiple_of(step * wide, wide), wide)
        put(dot_of(turned_ref[0], pre_ref[:, here], 1, 0), here)

    @pl.loop(0, act_ref.shape[1] // wide, unroll=GRAD_UNROLL)
    def _(step):
        here = pl.ds(pl.multiple_of(step * wide, wide), wide)
        there = pl.ds(pl.multiple_of(first + step * wide, wide), wide)
        put(dot_of(turned_ref[1], act_ref[:, here], 1, 0), there)


def weight_grads(places, x, m, pre, act, depth, groups, mids, high):
    total = x.shape[0]
    wide = pre.shape[1] + act.shape[1]

    def column(first):
        return pl.BlockSpec((total, mids * depth), lambda f, h, r: (0, r[first + f * high + h]))

    def whole(array):
        return pl.BlockSpec(array.shape, lambda f, h, r: (0, 0), pipeline_mode=pl.Buffered(1))

    return pl.pallas_call(
        functools.partial(weight_grad_kernel, mids),
        grid_spec=pltpu.PrefetchScalarGridSpec(
            num_scalar_prefetch=1,
            grid=(groups, high),
            in_specs=[column(0), column(groups * high), whole(pre), whole(act)],
            out_specs=pl.BlockSpec(
                (1, mids, 1, depth, wide), lambda f, h, r: (f, 0, h, 0, 0)
            ),
            scratch_shapes=[pltpu.VMEM((2, mids * depth, total), BF16)],
        ),
        out_shape=jax.ShapeDtypeStruct((groups, mids, high, depth, wide), BF16),
        compiler_params=params("arbitrary", "arbitrary"),
        cost_estimate=cost(
            2 * total * depth * groups * mids * high * wide,
            2 * total * (2 * depth * groups * mids * high + wide),
        ),
        name="weight_grads",
    )(places, x, m, pre, act)


def bits_of(size):
    return [1 << n for n in range(size.bit_length() - 1)]


def swap(values, axis, bit):
    size = lax.axis_size(axis) if isinstance(axis, str) else math.prod(map(lax.axis_size, axis))
    return lax.ppermute(values, axis, [(n, n ^ bit) for n in range(size)])


class Flow:
    def __init__(self, steps):
        self.steps = steps
        self.result = None
        self.sends = next(steps)

    def advance(self, got):
        try:
            self.sends = self.steps.send(got)
        except StopIteration as stop:
            self.sends = None
            self.result = stop.value

    def step(self, count=1):
        for _ in range(count):
            if self.sends is not None:
                self.advance([swap(*send) for send in self.sends])
        return self

    def finish(self):
        while self.sends is not None:
            self.step()
        return self.result

    def holds(self):
        return self.result if self.sends is None else [send[0] for send in self.sends]

    def replace(self, arrays):
        if self.sends is None:
            self.result = arrays
        else:
            self.sends = [(array, *send[1:]) for array, send in zip(arrays, self.sends)]


def stage(live, flows=(), work=(), sync=()):
    flows = [flow for flow in flows if flow.sends is not None]
    got = [[swap(*send) for send in flow.sends] for flow in flows]
    done = [each() for each in work]
    held = [flow.holds() for flow in sync]
    got, done, held, kept = lax.optimization_barrier((got, done, held, dict(live)))
    live.update(kept)
    for flow, arrays in zip(flows, got):
        flow.advance(arrays)
    for flow, arrays in zip(sync, held):
        flow.replace(arrays)
    return done


def spread_steps(values, axis, bits):
    blocks = {0: values}
    for bit in bits:
        places = sorted(blocks)
        got = yield [(blocks[place], axis, bit) for place in places]
        blocks.update({place | bit: block for place, block in zip(places, got)})
    return [blocks[place] for place in sorted(blocks)]


def spread_rows_steps(values, row_bits, strides):
    held = values[None]
    places = [0]
    for axis, bit in row_bits:
        (got,) = yield [(held, axis, bit)]
        held = jnp.concatenate([held, got], axis=0)
        places += [place | (bit * strides[axis]) for place in places]
    return jnp.stack([held[places.index(place)] for place in range(len(places))])


def spread_cube_steps(values, groups, cols):
    held = values[None]
    for axis, bits in (("lo", bits_of(groups)), ("col", bits_of(cols))):
        for bit in bits:
            (got,) = yield [(held, axis, bit)]
            held = jnp.concatenate([held, got], axis=0)
    return jnp.swapaxes(held.reshape((cols, groups) + values.shape), 0, 1)


def col_reduce_steps(blocks, cols):
    held = dict(enumerate(blocks))
    for bit in bits_of(cols):
        away = [place for place in sorted(held) if place & bit]
        (got,) = yield [(jnp.stack([held[place].astype(BF16) for place in away]), "col", bit)]
        held = {
            place & ~bit: held[place & ~bit] + got[number].astype(F32)
            for number, place in enumerate(away)
        }
    return held[0]


def total_steps(values, axes):
    for axis in axes:
        size = math.prod(map(lax.axis_size, axis))
        got = yield [(values, axis, place) for place in range(1, size)]
        values = values + sum(got)
    return values


def row_reduce_steps(grads, groups, mids, high):
    names = [("lo", bit) for bit in reversed(bits_of(groups))]
    names += [("mid", bit) for bit in reversed(bits_of(mids))]
    names += [("hi", bit) for bit in reversed(bits_of(high))]
    grads = grads.reshape((2,) * len(names) + grads.shape[3:])
    half = grads.shape[-1] // 2
    held = []
    for number in range(2):
        order = [name for name in names if name[0] != "hi"][:: 1 if number else -1]
        order += [name for name in reversed(names) if name[0] == "hi"]
        held.append((grads[..., number * half : (number + 1) * half], names, order))
    for step in range(len(names)):
        sends, rest = [], []
        for array, left, order in held:
            name = order[step]
            axis = left.index(name)
            away = 0 if name[0] == "lo" else 1
            sends.append((lax.index_in_dim(array, away, axis, False).astype(BF16), *name))
            kept = lax.index_in_dim(array, 1 - away, axis, False)
            rest.append((kept, [other for other in left if other != name], order))
        got = yield sends
        held = [
            (kept.astype(F32) + more.astype(F32), left, order)
            for (kept, left, order), more in zip(rest, got)
        ]
    return jnp.concatenate([array for array, _, _ in held], axis=1)


def links_of(groups, cols):
    return [("col", bit) for bit in bits_of(cols)[1:]] + [("lo", bit) for bit in bits_of(groups)]


def turned(links, number):
    number %= len(links)
    return links[number:] + links[:number]


def reduce_steps(parts, groups, cols):
    links = links_of(groups, cols)
    got = yield [(away, "col", 1) for _, away in parts]
    held = []
    for number, (keep, _) in enumerate(parts):
        shape = (2,) * len(links) + keep.shape[2:]
        names = [("lo", bit) for bit in reversed(bits_of(groups))]
        names += [("col", bit) for bit in reversed(bits_of(cols)[1:])]
        held.append((keep.reshape(shape), got[number].reshape(shape), names))
    for step in range(len(links)):
        sends, rest = [], []
        for number, (keep, more, names) in enumerate(held):
            link = turned(links, number)[step]
            axis = names.index(link)

            def half(place):
                total = lax.index_in_dim(keep, place, axis, False).astype(F32)
                return total + lax.index_in_dim(more, place, axis, False).astype(F32)

            sends.append((half(1).astype(BF16), *link))
            kept = half(0)
            rest.append(
                (
                    kept if step + 1 == len(links) else kept.astype(BF16),
                    [name for name in names if name != link],
                )
            )
        got = yield sends
        held = [(keep, more, names) for (keep, names), more in zip(rest, got)]
    return jnp.concatenate([keep.astype(F32) + more.astype(F32) for keep, more, _ in held], axis=0)


def part_sizes(tokens, count):
    whole = tokens // BLOCK
    return [BLOCK * ((whole + count - 1 - n) // count) for n in range(count)]


def expert_weight_steps(piece, far, bits):
    if far:
        (piece,) = yield [(piece, "lo", far)]
    held = {(): piece}
    fresh = [()]
    while True:
        ways = [
            (place, number)
            for place in fresh
            for number in range(place[-1] + 1 if place else 0, len(bits))
        ]
        if not ways:
            return held
        got = yield [(held[place], *bits[number]) for place, number in ways]
        fresh = [place + (number,) for place, number in ways]
        held.update(zip(fresh, got))


def expert_grad_steps(blocks, far, bits):
    for number in reversed(range(len(bits))):
        half = blocks.shape[0] // 2
        (got,) = yield [(blocks[half:], *bits[number])]
        blocks = blocks[:half].astype(F32) + got.astype(F32)
        if number or far:
            blocks = blocks.astype(BF16)
    total = blocks[0]
    if far:
        (total,) = yield [(total, "lo", far)]
    return total


def per_device(
    hidden_in,
    lengths,
    routes,
    attn_gain,
    query_gain,
    key_gain,
    query_weight,
    key_weight,
    value_weight,
    out_weight,
    moe_gain,
    router,
    gate_weight,
    up_weight,
    down_weight,
    cotangent,
):
    tok_rows, width = hidden_in.shape
    cols = lax.axis_size("col")
    groups = lax.axis_size("lo")
    high = lax.axis_size("hi")
    mids = lax.axis_size("mid")
    col = lax.axis_index("col")
    lo = lax.axis_index("lo")
    hi = lax.axis_index("hi")
    mid = lax.axis_index("mid")
    row = (hi * groups + lo) * mids + mid
    where = jnp.stack([lo, col])
    heads = width // HD
    seqs = lengths.shape[0]
    depth = gate_weight.shape[1]
    each = gate_weight.shape[0] // groups
    cube = ("lo", "col")
    rows_axes = ("hi", "lo", "mid")
    strides = {"hi": groups * mids, "lo": mids, "mid": 1}
    seq_rows = [slice(s * SEQ_LEN, (s + 1) * SEQ_LEN) for s in range(seqs)]
    links = links_of(groups, cols)
    col_bits = list(reversed(bits_of(cols)))
    hi_bits = [("hi", bit) for bit in bits_of(high)]
    mid_bits = [("mid", bit) for bit in bits_of(mids)]
    row_bits = hi_bits + [("lo", bit) for bit in bits_of(groups)] + mid_bits
    far_bits = hi_bits + mid_bits
    live = {}

    def row_of_set(place, far):
        other = row ^ (far * mids)
        for number in place:
            axis, bit = far_bits[number]
            other = other ^ (bit * strides[axis])
        return other

    hidden_flow = Flow(spread_steps(hidden_in, "col", col_bits))
    gain_flow = Flow(spread_steps(attn_gain, "col", col_bits))
    routes_flow = Flow(spread_steps(routes.T, "lo", bits_of(groups)))
    router_flow = Flow(spread_rows_steps(router.T.astype(BF16), row_bits, strides))
    out_flow = Flow(spread_rows_steps(out_weight.T.astype(BF16), row_bits, strides))
    qkv_local = jnp.concatenate([query_weight, key_weight, value_weight], axis=1).astype(BF16)
    qkv_full = lax.all_gather(qkv_local, rows_axes, axis=0, tiled=True)
    live_key = jnp.arange(SEQ_LEN)[None, :] < lengths[:, None]
    out_cot = jnp.where(live_key.reshape(tok_rows, 1), cotangent, jnp.zeros_like(cotangent))
    packed = pack_weights(where, gate_weight, up_weight, down_weight, each)
    units = [(expert, far) for expert in range(each) for far in range(groups)]
    live["packed"] = packed

    def rotary_tables():
        places = jnp.arange(SEQ_LEN).astype(F32)
        powers = jnp.arange(HD // 2).astype(F32) * (2.0 / HD)
        angles = places[:, None] * jnp.exp(-powers * math.log(rope_base))[None, :]
        cosine, sine = jnp.cos(angles), jnp.sin(angles)
        return (
            jnp.concatenate([cosine, cosine], axis=1),
            jnp.concatenate([-sine, sine], axis=1),
        )

    live["out_cot"] = out_cot
    (tables,) = stage(
        live,
        [hidden_flow, gain_flow, routes_flow, router_flow, out_flow],
        [rotary_tables],
    )

    hidden = hidden_in.astype(F32)

    def norm_attn():
        blocks = hidden_flow.finish()
        gains = gain_flow.finish()
        square = sum(jnp.sum(jnp.square(block.astype(F32)), axis=1) for block in blocks)
        inverse = lax.rsqrt(square / D + epsilon)[:, None]
        normed = jnp.zeros((tok_rows, D), BF16)
        for place, (block, gain) in enumerate(zip(blocks, gains)):
            piece = (block.astype(F32) * inverse * gain).astype(BF16)
            normed = lax.dynamic_update_slice_in_dim(normed, piece, (col ^ place) * width, 1)
        return normed, inverse

    def routing():
        rel = jnp.stack(routes_flow.finish())
        named = jnp.any(rel[:, :, None, :] == jnp.arange(EXPERTS)[None, None, :, None], axis=1)
        first = (col * groups + lo) * each
        member = lax.dynamic_slice_in_dim(named, first, each, 1)
        member = jnp.swapaxes(member, 0, 1).reshape(each * groups, tok_rows)
        count = member.astype(jnp.int32)
        rank = jnp.cumsum(count, axis=1) - count
        pos = jnp.where(member, rank, -(1 << 20))
        starts = jnp.minimum(rank[:, ::BLOCK] // EDGE * EDGE, CAP - WINDOW)
        return named, starts, pos[:, None, :], pos[:, :, None]

    live["qkv_full"] = qkv_full
    ((live["normed_attn"], attn_inverse),) = stage(live, [router_flow, out_flow], [norm_attn])
    weight_flows = {}

    def start_weights(expert):
        for far in range(groups):
            weight_flows[expert, far] = Flow(
                expert_weight_steps(live["packed"][far * each + expert], far, far_bits)
            )

    start_weights(0)
    moe_cot = lax.all_gather(live["out_cot"], cube, axis=0, tiled=False)
    hidden_blocks = hidden_flow.result
    query_scale, key_scale = query_gain[None, :], key_gain[None, :]

    def attend(s):
        return attend_forward(
            s, lengths[s : s + 1], live["qkv"], tables, query_scale, key_scale, heads
        )

    def project_and_attend():
        live["qkv"] = dot_of(live["normed_attn"], live["qkv_full"], 1, 0)
        return attend(0)

    firsts = [weight_flows[0, far] for far in range(1, groups)]
    (first_seq,) = stage(live, [router_flow, out_flow], [project_and_attend])
    for expert in range(1, each):
        start_weights(expert)
    seconds = [weight_flows[unit] for unit in units if unit[0] == 1]
    named, starts, pos_row, pos_col = routing()

    span = width // depth

    def col_rows(blocks, place, axis):
        first = (col ^ place) * span
        return jnp.concatenate(
            [
                lax.dynamic_index_in_dim(blocks, (first + n) ^ row, 0, False)
                for n in range(span)
            ],
            axis=axis,
        )

    out_spread = out_flow.finish()
    out_rel = jnp.concatenate([col_rows(out_spread, place, 0) for place in range(cols)], axis=0)
    router_rows = col_rows(router_flow.finish(), 0, 1)

    def branch(mixture):
        partial = dot_of(mixture, out_rel, 1, 1)
        blocks = [partial[:, n * width : (n + 1) * width] for n in range(cols)]
        return Flow(col_reduce_steps(blocks, cols)).finish()

    def attend_rest():
        outs = [first_seq]
        sums = [branch(first_seq[0])]
        for s in range(1, seqs):
            outs.append(attend(s))
            sums.append(branch(outs[s][0]))
        return outs, sums

    ((attended, branches),) = stage(live, [weight_flows[0, 0]] + firsts, [attend_rest])
    middle = hidden + jnp.concatenate(branches, axis=0)
    live["scaled_rows"] = (middle * moe_gain).astype(BF16)
    scaled_rows = live["scaled_rows"]
    moe_in = lax.all_gather(scaled_rows, cube, axis=0, tiled=False)
    square = jnp.sum(middle * middle, axis=1)[None, :]
    stat = jnp.concatenate([dot_of(router_rows, scaled_rows, 1, 1), square], axis=0)
    stat_flow = Flow(spread_cube_steps(stat, groups, cols))
    stage(live, [stat_flow], sync=[weight_flows[0, 0]] + firsts + seconds)
    (live["cot_rows"],) = stage(
        live,
        [stat_flow, weight_flows[0, 0]] + firsts,
        [lambda: compact(starts, where, pos_row, moe_cot, groups, cols)],
        sync=seconds[:1],
    )
    for flow in seconds[:1]:
        flow.step(2)
    stage(live, [stat_flow] + firsts + seconds[1:])
    stat = stat_flow.finish()

    stat = jnp.sum(stat, axis=1)
    moe_inverse = lax.rsqrt(stat[:, EXPERTS] / D + epsilon)
    all_logits = stat[:, :EXPERTS] * moe_inverse[:, None, :]
    logits = jnp.where(named, all_logits, masked_score)
    shifted = jnp.where(named, jnp.exp(logits - jnp.max(logits, axis=1, keepdims=True)), 0.0)
    gates = shifted / jnp.sum(shifted, axis=1, keepdims=True)
    own_gate = lax.dynamic_slice_in_dim(gates, (col * groups + lo) * each, each, 1)
    own_gate = jnp.swapaxes(own_gate, 0, 1).reshape(each * groups, 1, tok_rows)
    row_gate, row_scale = compact_scalars(
        starts, pos_row, (own_gate, jnp.tile(moe_inverse, (each, 1))[:, None, :])
    )
    total_rows = groups * CAP

    live["moe_rows"] = compact(starts, where, pos_row, moe_in, groups, cols)

    def run_expert(expert):
        pieces, row_numbers = [], []
        for far in range(groups):
            for place, piece in weight_flows[expert, far].finish().items():
                pieces.append(piece)
                row_numbers.append(row_of_set(place, far))
        here = slice(expert * total_rows, (expert + 1) * total_rows)
        return expert_step(
            jnp.stack(row_numbers),
            live["moe_rows"][expert],
            live["cot_rows"][expert],
            row_gate[here],
            row_scale[here],
            pieces,
        )

    blocks_here = [
        (hi ^ above) * groups + (lo ^ far)
        for far in reversed(range(groups))
        for above in range(high)
    ]
    grad_places = jnp.stack(blocks_here + blocks_here + [mid])
    grad_flows = {}

    def start_grads(expert, outs):
        grads = weight_grads(
            grad_places,
            live["moe_rows"][expert],
            live["cot_rows"][expert],
            outs[1],
            outs[2],
            depth,
            groups,
            mids,
            high,
        )
        return grads.reshape((groups, mids * high) + grads.shape[3:])

    def grad_flow(expert, grads):
        for number, far in enumerate(reversed(range(groups))):
            grad_flows[expert, far] = Flow(expert_grad_steps(grads[number], far, far_bits))

    def running():
        return list(grad_flows.values())

    ran = []
    for expert in range(each):
        others = [flow for (number, _), flow in weight_flows.items() if number > expert]
        (outs,) = stage(
            live,
            others[1:] + running()[:1],
            [functools.partial(run_expert, expert)],
            sync=others[:1] + running()[1:],
        )
        ran.append(outs)
        if expert + 1 < each:
            (grads,) = stage(live, others, [functools.partial(start_grads, expert, outs)])
            grad_flow(expert, grads)
    early = running()
    live["result"] = [outs[5] for outs in ran]
    last = ran[-1]
    gate_cot = jnp.concatenate([outs[3] for outs in ran], axis=0)
    row_inner = jnp.concatenate([outs[4] for outs in ran], axis=0)
    sizes = part_sizes(tok_rows, len(links))
    live["scalars"] = (gate_cot, row_inner)
    (rows_parts,) = stage(
        live,
        [],
        [
            lambda: expand(
                starts, where, pos_col, [outs[0] for outs in ran], sizes, groups, cols
            )
        ],
    )
    gate_cot, row_inner = expand_scalars(starts, pos_row, live.pop("scalars"))
    gate_cot = gate_cot.reshape(each, groups, tok_rows)
    row_inner = jnp.sum(row_inner.reshape(each, groups, tok_rows), axis=0)[None]
    scalars = jnp.concatenate([gate_cot, row_inner], axis=0)
    scalars = scalars.reshape((each + 1) * groups, tok_rows)
    scalar_flow = Flow(spread_cube_steps(scalars, groups, cols))
    moe_in_flow = Flow(reduce_steps(rows_parts, groups, cols))
    (grads,) = stage(
        live,
        [moe_in_flow, scalar_flow] + early,
        [functools.partial(start_grads, each - 1, last)],
    )
    grad_flow(each - 1, grads)
    late = running()[len(early) :]
    scalar_flow.finish()
    for flow in late[:1]:
        flow.step()
    (branch_parts,) = stage(
        live,
        [moe_in_flow],
        [lambda: expand_all(starts, where, pos_col, live["result"], groups, cols)],
        sync=[scalar_flow] + early,
    )
    live["moe_branch"] = branch_parts.reshape(groups * cols, tok_rows, width)
    while moe_in_flow.sends is not None:
        stage(live, [moe_in_flow], sync=late)
    scalar_all = scalar_flow.finish().reshape(groups, cols, each + 1, groups, tok_rows)
    scalar_all = jnp.stack([scalar_all[place, :, :, place] for place in range(groups)])
    by_expert = jnp.stack(
        [
            ((lo ^ (number // each % groups)) * cols + (col ^ (number // (each * groups)))) * each
            + number % each
            for number in range(EXPERTS)
        ]
    )
    gate_cot = jnp.take(scalar_all[:, :, :each].reshape(EXPERTS, tok_rows), by_expert, axis=0)
    my_gates, my_logits = gates[0], all_logits[0]
    logit_cot = my_gates * (gate_cot - jnp.sum(my_gates * gate_cot, axis=0, keepdims=True))
    inner = jnp.sum(scalar_all[:, :, each], axis=(0, 1)) + jnp.sum(logit_cot * my_logits, axis=0)
    scaled_logit = (logit_cot * moe_inverse[0][None, :]).astype(BF16)
    logit_cot = logit_cot.astype(BF16)
    my_inverse = moe_inverse[0][:, None]

    back = moe_in_flow.finish() + my_inverse * dot_of(logit_cot, router_rows, 0, 0)
    middle_cot = (
        out_cot.astype(F32)
        + back * moe_gain
        - middle * (my_inverse * my_inverse * (inner[:, None] / D))
    )
    cot_flow = Flow(spread_steps(middle_cot.astype(BF16), "col", col_bits))
    router_part, moe_gain_part = stage(
        live,
        [cot_flow],
        [
            lambda: dot_of(scaled_logit, scaled_rows, 1, 0),
            lambda: jnp.sum(back * middle, axis=0)[None],
        ],
    )
    cot_blocks = cot_flow.finish()
    moe_branch = lax.psum_scatter(
        live.pop("moe_branch"), cube, scatter_dimension=0, tiled=True
    )[0]

    cot_all = jnp.concatenate(cot_blocks, axis=1)

    def attend_back(s):
        mixture_cot = dot_of(cot_all[seq_rows[s]], out_rel, 1, 0).astype(BF16)
        *cots, query_part, key_part, token_inner = attend_backward(
            s,
            lengths[s : s + 1],
            attended[s][1:],
            mixture_cot,
            live["qkv"],
            tables,
            query_scale,
            key_scale,
            heads,
        )
        cots = jnp.concatenate(cots, axis=1)
        return cots, query_part, key_part, token_inner[:, 0]

    qkv_rel = jnp.concatenate(
        [
            lax.dynamic_slice_in_dim(live["qkv_full"], (col ^ place) * width, width, 0)
            for place in range(cols)
        ],
        axis=0,
    )
    mixture = jnp.concatenate([outs[0] for outs in attended], axis=0)
    live.update(qkv_rel=qkv_rel, mixture=mixture, cot_all=cot_all)
    done = stage(
        live,
        early[:1] + late,
        [functools.partial(attend_back, s) for s in range(seqs)],
        sync=early[1:],
    )
    share = width // (mids * depth)
    cot_places = [((n // share) ^ col) * share + n % share for n in blocks_here]

    live["qkv_cot"] = jnp.concatenate([outs[0] for outs in done], axis=0)

    def projection_grads():
        grads = weight_grads(
            jnp.stack(blocks_here + cot_places + [mid]),
            live["normed_attn"],
            live["cot_all"],
            live["qkv_cot"],
            live["mixture"],
            depth,
            groups,
            mids,
            high,
        )
        return grads

    def widen(blocks):
        full = jnp.zeros((blocks[0].shape[0], D), F32)
        for place, block in enumerate(blocks):
            full = lax.dynamic_update_slice_in_dim(full, block, (col ^ place) * width, 1)
        return full

    for flow in late + early[1:]:
        flow.step()
    (partial,) = stage(live, [], [lambda: dot_of(live["qkv_cot"], live["qkv_rel"], 1, 1)])
    backs = [partial[:, n * width : (n + 1) * width] for n in range(cols)]
    attn_flow = Flow(col_reduce_steps(backs, cols))

    def gain_sums():
        attn_gain_parts = [
            jnp.sum(part * (block.astype(F32) * attn_inverse), axis=0)[None]
            for part, block in zip(backs, hidden_blocks)
        ]
        query_part = sum(outs[1] for outs in done)
        key_part = sum(outs[2] for outs in done)
        head_parts = jnp.concatenate([query_part, key_part], 1)
        return jnp.concatenate(
            [
                widen([router_part]),
                widen([moe_gain_part]),
                widen(attn_gain_parts),
                jnp.pad(head_parts, ((0, 0), (0, D - 2 * HD))),
            ],
            axis=0,
        )

    token_inner = jnp.concatenate([outs[3] for outs in done], axis=0)
    inner_flow = Flow(total_steps(token_inner, [("col",)]))
    (grads,) = stage(live, [attn_flow, inner_flow], [projection_grads])
    qkv_flow = Flow(row_reduce_steps(grads, groups, mids, high))
    for _ in bits_of(cols)[2:]:
        stage(live, [attn_flow])
    small_flows = []

    def small_sums():
        flow = Flow(total_steps(gain_sums(), [("col",), ("lo", "mid"), ("hi",)])).step()
        small_flows.append(flow)
        return flow.holds()

    (held,) = stage(live, [attn_flow, qkv_flow], [small_sums])
    (small_flow,) = small_flows
    small_flow.replace(held)
    live["moe_branch"] = moe_branch

    def input_sums():
        return (
            middle_cot
            + attn_inverse * (attn_flow.finish() * attn_gain)
            - hidden * (attn_inverse * attn_inverse * (inner_flow.finish()[:, None] / D))
        )

    (input_grad,) = stage(
        live, [qkv_flow, small_flow], [input_sums], sync=late[1:] + early[1:]
    )
    flows = [qkv_flow, small_flow] + early + late
    while any(flow.sends is not None for flow in flows):
        stage(live, flows)
    moe_branch = live["moe_branch"]
    weight_sum = qkv_flow.finish()
    out_sum = weight_sum[:, 3 * width :]
    small = small_flow.finish()

    output = (middle + moe_branch.astype(F32)).astype(BF16)
    gate_grad, up_grad, down_grad = unpack_grads(
        where,
        [grad_flows[expert, far].finish() for far in range(groups) for expert in range(each)],
        each,
    )
    own = lax.dynamic_slice_in_dim(small, col * width, width, 1)
    router_grad = lax.dynamic_slice_in_dim(small[:EXPERTS], row * depth, depth, 1).T
    return (
        output,
        input_grad,
        own[EXPERTS + 1],
        small[EXPERTS + 2, :HD],
        small[EXPERTS + 2, HD : 2 * HD],
        weight_sum[:, :width],
        weight_sum[:, width : 2 * width],
        weight_sum[:, 2 * width : 3 * width],
        out_sum.T,
        own[EXPERTS],
        router_grad,
        gate_grad,
        up_grad,
        down_grad,
    )


def solution(mesh):
    row_count, col_count = mesh.shape["row"], mesh.shape["col"]
    groups = 2
    between = EXPERTS // col_count // groups
    shape = (row_count // (groups * between), groups, between, col_count)
    inner = Mesh(mesh.devices.reshape(shape), ("hi", "lo", "mid", "col"))
    row = ("hi", "lo", "mid")
    return jax.shard_map(
        per_device,
        mesh=inner,
        in_specs=(
            P(row, "col"),
            P(row),
            P(row, None),
            P("col"),
            P(),
            P(),
            P(row, "col"),
            P(row, "col"),
            P(row, "col"),
            P("col", row),
            P("col"),
            P(row, None),
            P("col", row, None),
            P("col", row, None),
            P("col", None, row),
            P(row, "col"),
        ),
        out_specs=(
            P(row, "col"),
            P(row, "col"),
            P("col"),
            P(),
            P(),
            P(row, "col"),
            P(row, "col"),
            P(row, "col"),
            P("col", row),
            P("col"),
            P(row, None),
            P("col", row, None),
            P("col", row, None),
            P("col", None, row),
        ),
        check_vma=False,
    )
```
